32 devices in a mesh: groups: 2 (over y), patient: 4 (over x, core), feature: 4 (over z).
Axes of the slice: x: 2, y: 2, z: 4, core: 2. Of those that a mesh axis runs over, the one named last changes fastest.
Arguments:
- visits: bfloat16 [256, 256, 4096], P(('groups', 'patient'), None, 'feature'), parts along dimension 0, may hold values from -6 to 6
- visit_counts: int32 [256], P(('groups', 'patient')), parts along dimension 0, may hold values from 16 to 256, as said below
- h_start: float32 [64, 64], replicated, may hold values from -0.75 to 0.75
- v_start: bfloat16 [4096, 64], P('feature'), may hold values from -0.09375 to 0.09375
- w_start: float32 [256, 64], P(('groups', 'patient')), parts along dimension 0, may hold values from -5 to 5
Outputs:
- h_next: float32 [64, 128], P(None, 'groups'), parts along dimension 1
- v_next: float32 [4096, 128], P('feature', 'groups'), parts along dimension 1
- w_next: float32 [128, 128], P('patient', 'groups'), parts along dimension 1
The draws below stay inside these ranges and needn't reach their ends.
There are 2 independent parts, one for each index of `groups`. The reference program is written for one: setup_inputs(seed, part) draws one part's arguments, and reference() takes and returns one part's arrays. A program takes and returns all parts, laid end to end along the dimension named above; an argument that names none is the same for every part. Nothing has to cross between parts.
Inputs may be any that keep to these rules, and one draw needn't show every extreme that they name: `visit_counts`: in each block of 32 patients that lie on one index of patient, one patient has exactly 256 visits.
All inputs are finite; a program needn't handle non-finite values.
Results may differ from the reference program's by a relative error of at most 0.0015.
Values may be sent and summed in bfloat16 or wider, within the bound.
No kernel may reach another device: no remote copies, remote signals or barrier semaphores. Data moves between devices by JAX's collectives and lax.ppermute only.
A program may use at most 128 MiB of HBM per device.

```python
import jax
import jax.numpy as jnp
from jax import lax

RANK = 64
FEATURES = 4096
MOST = 256
NS_STEPS = 12
P_DEV = 32
PATIENTS = 128


def draw_visit_counts(key, part):
    key = jax.random.fold_in(key, 5)
    first_key, second_key = jax.random.split(key)
    lowest = min(16, MOST)
    counts = jax.random.randint(first_key, (PATIENTS // P_DEV, P_DEV), lowest, MOST + 1)
    picked = jax.random.randint(second_key, (PATIENTS // P_DEV, 1), 0, P_DEV)
    filled = jnp.arange(P_DEV, dtype=jnp.int32)[None, :] == picked
    counts = jnp.where(filled, MOST, counts)
    return counts.reshape(PATIENTS).astype(jnp.int32)


def level_of(rng, shape, pieces, low, top_value):
    def one(dim, parts):
        heights = jax.random.uniform(jax.random.fold_in(jax.random.fold_in(rng, 6), dim), (parts,), jnp.float32, low / len(pieces), top_value / len(pieces))
        return jnp.repeat(jnp.exp(heights), shape[dim] // parts).reshape((-1,) + (1,) * (len(shape) - dim - 1))

    loudness = one(*pieces[0])
    for cut in pieces[1:]:
        loudness = loudness * one(*cut)
    return loudness


def centred(stream_key, extent, scale, most, cuts=(), held_as=jnp.bfloat16):
    entries = scale * jax.random.normal(stream_key, extent, jnp.float32)
    if cuts:
        entries = entries * level_of(stream_key, extent, cuts, -0.22, 0.18)
    return jnp.clip(entries, -most, most).astype(held_as)


def setup_inputs(seed: int = 0, part: int = 0) -> dict:
    streams_of = jax.random.split(jax.random.key(seed), 6)
    part_splits = jax.random.split(jax.random.fold_in(streams_of[5], part), 6)
    return {
        "visits": centred(part_splits[0], (PATIENTS, MOST, FEATURES), 1.0, 6.0, ((0, 4), (2, 4))),
        "visit_counts": draw_visit_counts(jax.random.fold_in(jax.random.fold_in(streams_of[5], part), 71), part),
        "h_start": centred(streams_of[2], (RANK, RANK), RANK ** -0.5, 0.75, (), jnp.float32),
        "v_start": centred(streams_of[3], (FEATURES, RANK), FEATURES ** -0.5, 0.09375, ((0, 4),)),
        "w_start": centred(part_splits[4], (PATIENTS, RANK), 1.0, 5.0, ((0, 4),), jnp.float32),
    }


epsilon = 1e-06
HIGH = lax.Precision.HIGHEST

def polar_factor(proj, weights, counts, h_start):
    slots = jnp.arange(MOST, dtype=jnp.int32)
    keep = (slots[None, :] < counts[:, None]).astype(jnp.float32)
    mixed = jnp.einsum('rc,kcm->krm', h_start, proj * weights[:, :, None], precision=HIGH) * keep[:, None, :]
    scale = lax.rsqrt(lax.optimization_barrier(jnp.sum(mixed * mixed, axis=(1, 2))) + epsilon)
    frames = mixed * scale[:, None, None]

    def sweep(step, frames):
        gram = jnp.einsum('krm,ksm->krs', frames, frames, precision=HIGH)
        return 1.5 * frames - 0.5 * jnp.einsum('ksr,ksm->krm', gram, frames, precision=HIGH)
    frames = lax.fori_loop(0, NS_STEPS, sweep, frames)
    return frames.astype(jnp.bfloat16)

def solve_right(terms, gram):
    return jnp.linalg.solve(gram, terms.T).T

def reference(visits, visit_counts, h_start, v_start, w_start):
    blocks = PATIENTS // P_DEV
    v_full = v_start.astype(jnp.float32)

    def one_block(index):
        start = (index * P_DEV).astype(jnp.int32)
        piece = lax.dynamic_slice_in_dim(visits, start, P_DEV, 0).astype(jnp.float32)
        weights = lax.dynamic_slice_in_dim(w_start, start, P_DEV, 0)
        counts = lax.dynamic_slice_in_dim(visit_counts, start, P_DEV, 0)
        proj = jnp.einsum('kmj,jr->krm', piece, v_full, precision=HIGH)
        frames = polar_factor(proj, weights, counts, h_start)
        return jnp.einsum('krm,kmj->krj', frames.astype(jnp.float32), piece, precision=HIGH)
    projected = lax.map(one_block, jnp.arange(blocks, dtype=jnp.int32)).reshape(PATIENTS, RANK, FEATURES)
    v_gram = jnp.dot(v_full.T, v_full, precision=HIGH)
    w_gram = jnp.dot(w_start.T, w_start, precision=HIGH)
    inner = jnp.einsum('krj,jc->krc', projected, v_full, precision=HIGH)
    h_terms = jnp.einsum('krc,kc->rc', inner, w_start, precision=HIGH)
    h_next = solve_right(h_terms, w_gram * v_gram)
    h_gram = jnp.dot(h_next.T, h_next, precision=HIGH)
    factor = h_next[None, :, :] * w_start[:, None, :]
    v_terms = jnp.einsum('krj,krc->jc', projected, factor, precision=HIGH)
    v_next = solve_right(v_terms, h_gram * w_gram)
    second = jnp.einsum('krj,jc->krc', projected, v_next, precision=HIGH)
    w_terms = jnp.einsum('krc,rc->kc', second, h_next, precision=HIGH)
    v_gram_next = jnp.dot(v_next.T, v_next, precision=HIGH)
    w_next = solve_right(w_terms, h_gram * v_gram_next)
    return (h_next, v_next, w_next)
```

```python
import functools

import jax
import jax.numpy as jnp
from jax import lax
from jax.experimental import pallas as pl
from jax.experimental.pallas import tpu as pltpu
from jax.sharding import PartitionSpec as P

NS_STEPS = 12
LANES = 128
LEVELS = 32000.0

epsilon = 1e-06
HIGH = lax.Precision.HIGHEST
F32 = jnp.float32
BF16 = jnp.bfloat16
MIB = 1024 * 1024

ROWS_BY_COLS = (((1,), (0,)), ((), ()))
ROWS_BY_ROWS = (((1,), (1,)), ((), ()))
COLS_BY_COLS = (((0,), (0,)), ((), ()))


def low_dot(a, b, dims=ROWS_BY_COLS):
    return lax.dot_general(a, b, dims, preferred_element_type=F32)


def high_dot(a, b, dims=ROWS_BY_COLS):
    return lax.dot_general(a, b, dims, precision=HIGH, preferred_element_type=F32)


def two_parts(x):
    first = x.astype(BF16)
    return first, (x - first.astype(F32)).astype(BF16)


def three_parts(x):
    first = x.astype(BF16)
    rest = x - first.astype(F32)
    second = rest.astype(BF16)
    return first, second, (rest - second.astype(F32)).astype(BF16)


def lane_numbers(shape):
    return lax.broadcasted_iota(jnp.int32, shape, len(shape) - 1)


def project_piece(visits, frame):
    return low_dot(frame, visits, ROWS_BY_ROWS)


def send_projection_kernel(slot, batch, place, v_ref, visits_ref, coded_ref, scale_ref, frame):
    step = pl.program_id(0)

    @pl.when(step == 0)
    def _():
        frame[...] = v_ref[...].astype(F32).T.astype(BF16)
        scale_ref[...] = jnp.zeros_like(scale_ref)

    scales = scale_ref[...].astype(F32)
    lanes = lane_numbers(scales.shape)
    for p in range(batch):
        proj = project_piece(visits_ref[0, p], frame[...])
        top = jnp.max(jnp.abs(proj), axis=1, keepdims=True)
        scale = (jnp.maximum(top, 1e-30) * 1.0078125).astype(BF16).astype(F32)
        coded = jnp.floor(proj * (LEVELS / scale) + 0.5)
        coded_ref[p] = coded.astype(jnp.int32).astype(jnp.int16)
        scales = jnp.where(lanes == step * batch + p, scale, scales)
    scale_ref[...] = scales.astype(BF16)


def own_projection_kernel(batch, place, v_ref, w_ref, visits_ref, proj_ref, v_gram_ref, w_gram_ref, frame):
    step = pl.program_id(0)

    @pl.when(step == 0)
    def _():
        frame[...] = v_ref[...].astype(F32).T.astype(BF16)
        v_gram_ref[...] = low_dot(frame[...], frame[...], ROWS_BY_ROWS)
        w_gram_ref[...] = high_dot(w_ref[...], w_ref[...], COLS_BY_COLS)

    for p in range(batch):
        proj_ref[p] = project_piece(visits_ref[0, p], frame[...])


def batch_of(share):
    return 2 if share % 2 == 0 else 1


def visits_spec(slot, batch, slots, width):
    return pl.BlockSpec((1, batch, slots, width), lambda i, place: (place[0] ^ slot, i, 0, 0))


def whole(shape):
    return pl.BlockSpec(shape, lambda i, place: (0,) * len(shape))


def cost(flops, size):
    return pl.CostEstimate(flops=int(flops), bytes_accessed=int(size), transcendentals=0)


def project_for(slot, place, visits, v_start):
    _, share, slots, width = visits.shape
    rank = v_start.shape[1]
    batch = batch_of(share)
    return pl.pallas_call(
        functools.partial(send_projection_kernel, slot, batch),
        grid_spec=pltpu.PrefetchScalarGridSpec(
            num_scalar_prefetch=1,
            grid=(share // batch,),
            in_specs=[whole(v_start.shape), visits_spec(slot, batch, slots, width)],
            out_specs=[
                pl.BlockSpec((batch, rank, slots), lambda i, place: (i, 0, 0)),
                whole((rank, LANES)),
            ],
            scratch_shapes=[pltpu.VMEM((rank, width), BF16)],
        ),
        out_shape=[
            jax.ShapeDtypeStruct((share, rank, slots), jnp.int16),
            jax.ShapeDtypeStruct((rank, LANES), BF16),
        ],
        cost_estimate=cost(2 * share * rank * slots * width, 2 * share * slots * width),
        name="project_send",
    )(place, v_start, visits)


def project_own(place, visits, v_start, w_start):
    _, share, slots, width = visits.shape
    rank = v_start.shape[1]
    batch = batch_of(share)
    gram = (rank, rank)
    return pl.pallas_call(
        functools.partial(own_projection_kernel, batch),
        grid_spec=pltpu.PrefetchScalarGridSpec(
            num_scalar_prefetch=1,
            grid=(share // batch,),
            in_specs=[whole(v_start.shape), whole(w_start.shape), visits_spec(0, batch, slots, width)],
            out_specs=[
                pl.BlockSpec((batch, rank, slots), lambda i, place: (i, 0, 0)),
                whole(gram),
                whole(gram),
            ],
            scratch_shapes=[pltpu.VMEM((rank, width), BF16)],
        ),
        out_shape=[
            jax.ShapeDtypeStruct((share, rank, slots), F32),
            jax.ShapeDtypeStruct(gram, F32),
            jax.ShapeDtypeStruct(gram, F32),
        ],
        cost_estimate=cost(2 * share * rank * slots * width, 2 * share * slots * width),
        name="project_own",
    )(place, v_start, w_start, visits)


def eliminate(table, rank):
    rows = lax.broadcasted_iota(jnp.int32, table.shape, 0)
    for i in range(rank):
        pivot_row = table[i : i + 1, :] / table[i : i + 1, i : i + 1]
        column = table[:, i : i + 1]
        table = jnp.where(rows == i, pivot_row, table - column * pivot_row)
    return table


def inverse_of(gram):
    rank = gram.shape[0]
    eye = (lax.broadcasted_iota(jnp.int32, gram.shape, 0) == lane_numbers(gram.shape)).astype(F32)
    return eliminate(jnp.concatenate([gram, eye], axis=1), rank)[:, rank:]


def total(refs):
    out = refs[0][...]
    for ref in refs[1:]:
        out = out + ref[...]
    return out


def first_inverse_kernel(n_v, n_w, *refs):
    v_refs, w_refs = refs[:n_v], refs[n_v : n_v + n_w]
    w_gram_ref, inverse_ref = refs[n_v + n_w :]
    w_gram = total(w_refs)
    w_gram_ref[...] = w_gram
    inverse_ref[...] = inverse_of(w_gram * total(v_refs))


def first_inverse(v_grams, w_grams):
    out = jax.ShapeDtypeStruct(w_grams[0].shape, F32)
    return pl.pallas_call(
        functools.partial(first_inverse_kernel, len(v_grams), len(w_grams)),
        out_shape=[out, out],
        cost_estimate=cost(12_000_000_000, 64),
        name="first_inverse",
    )(*v_grams, *w_grams)


def frames_kernel(share, n_slots, place, counts_ref, h_ref, w_ref, own_ref, *refs):
    coded, scales = refs[: n_slots - 1], refs[n_slots - 1 : 2 * n_slots - 2]
    frames_ref, terms_ref, proj, frames = refs[2 * n_slots - 2 :]
    first = place[0] * share
    rank, slots = frames.shape[1:]
    for p in range(share):
        piece = own_ref[p]
        for code, scale in zip(coded, scales):
            step = scale[:, p : p + 1].astype(F32) * (1.0 / LEVELS)
            piece = piece + code[p].astype(jnp.int32).astype(F32) * step
        proj[p] = piece
        weights = w_ref[pl.ds(first + p, 1), :]
        mixed = high_dot(h_ref[...] * weights, piece)
        mixed = jnp.where(lane_numbers((rank, slots)) < counts_ref[first + p], mixed, 0.0)
        energy = jnp.sum(jnp.sum(mixed * mixed, axis=1, keepdims=True), axis=0, keepdims=True)
        frames[p] = mixed * lax.rsqrt(energy + epsilon)

    def sweep(step, carry):
        for p in range(share):
            frame = frames[p]
            first_part, second_part = two_parts(frame)
            both = low_dot(jnp.concatenate([first_part, second_part], axis=0), first_part, ROWS_BY_ROWS)
            gram = both[:rank] + both[rank:] + low_dot(first_part, second_part, ROWS_BY_ROWS)
            gram_first, gram_second = two_parts(gram)
            moved = low_dot(jnp.concatenate([gram_first, gram_second], axis=0), first_part)
            moved = moved[:rank] + moved[rank:] + low_dot(gram_first, second_part)
            frames[p] = 1.5 * frame - 0.5 * moved
        return carry

    lax.fori_loop(0, NS_STEPS, sweep, 0)
    terms = jnp.zeros((rank, rank), F32)
    for p in range(share):
        low = frames[p].astype(BF16)
        frames_ref[p] = low
        parts = three_parts(proj[p])
        product = low_dot(low, parts[0], ROWS_BY_ROWS)
        for part in parts[1:]:
            product = product + low_dot(low, part, ROWS_BY_ROWS)
        terms = terms + product * w_ref[pl.ds(first + p, 1), :]
    terms_ref[...] = terms


VMEM_SPEC = pl.BlockSpec(memory_space=pltpu.VMEM)
SMEM_SPEC = pl.BlockSpec(memory_space=pltpu.SMEM)


def own_frames(place, counts, h_start, w_start, own, coded, scales):
    share, rank, slots = own.shape
    return pl.pallas_call(
        functools.partial(frames_kernel, share, len(coded) + 1),
        in_specs=[SMEM_SPEC] * 2 + [VMEM_SPEC] * (3 + len(coded) + len(scales)),
        out_specs=[VMEM_SPEC] * 2,
        out_shape=[
            jax.ShapeDtypeStruct(own.shape, BF16),
            jax.ShapeDtypeStruct((rank, rank), F32),
        ],
        scratch_shapes=[pltpu.VMEM(own.shape, F32)] * 2,
        compiler_params=pltpu.CompilerParams(vmem_limit_bytes=32 * MIB),
        cost_estimate=cost(10_000_000_000, 4 * share * rank * slots),
        name="own_frames",
    )(place, counts, h_start, w_start, own, *coded, *scales)


def next_h_kernel(n_terms, *refs):
    inverse_ref, w_gram_ref, h_ref, gram_ref, product_ref = refs[n_terms:]
    h_next = high_dot(total(refs[:n_terms]), inverse_ref[...])
    gram = high_dot(h_next, h_next, COLS_BY_COLS)
    h_ref[...] = h_next
    gram_ref[...] = gram
    product_ref[...] = gram * w_gram_ref[...]


def next_h(terms, inverse, w_gram):
    out = jax.ShapeDtypeStruct(w_gram.shape, F32)
    return pl.pallas_call(
        functools.partial(next_h_kernel, len(terms)),
        out_shape=[out] * 3,
        cost_estimate=cost(2_000_000_000, 64),
        name="next_h",
    )(*terms, inverse, w_gram)


def inverse_kernel(gram_ref, inverse_ref):
    inverse_ref[...] = inverse_of(gram_ref[...])


def inverse(gram):
    return pl.pallas_call(
        inverse_kernel,
        out_shape=jax.ShapeDtypeStruct(gram.shape, F32),
        cost_estimate=cost(12_000_000_000, 64),
        name="inverse",
    )(gram)


def v_terms_kernel(slot, batch, share, resumed, place, h_ref, w_ref, frames_ref, visits_ref, *refs):
    if resumed:
        before_ref, _, terms_ref, mixed_ref, h_parts = refs
    else:
        terms_ref, mixed_ref, h_parts = refs
    step = pl.program_id(0)
    rank, slots = frames_ref.shape[1:]

    @pl.when(step == 0)
    def _():
        h_parts[...] = jnp.concatenate(three_parts(h_ref[...].T), axis=0)
        terms_ref[...] = before_ref[...] if resumed else jnp.zeros_like(terms_ref)

    joined = jnp.concatenate([frames_ref[p] for p in range(batch)], axis=1)
    mixed = low_dot(h_parts[...], joined)
    mixed = mixed[:rank] + mixed[rank : 2 * rank] + mixed[2 * rank :]
    first = (place[0] ^ slot) * share + step * batch
    w_columns = w_ref[...]
    patients = lane_numbers(w_columns.shape)
    weighted = []
    for p in range(batch):
        piece = mixed[:, p * slots : (p + 1) * slots]
        mixed_ref[0, p] = piece
        weight = jnp.sum(jnp.where(patients == first + p, w_columns, 0.0), axis=1, keepdims=True)
        weighted.append(piece * weight)
    parts = jnp.concatenate(three_parts(jnp.concatenate(weighted, axis=1)), axis=0)
    pieces = visits_ref[0].reshape(batch * slots, visits_ref.shape[3])
    terms = low_dot(parts, pieces)
    terms_ref[...] += terms[:rank] + terms[rank : 2 * rank] + terms[2 * rank :]


def add_v_terms(slot, place, h_next, w_columns, frames, visits, before):
    n_slots, share, slots, width = visits.shape
    rank = h_next.shape[0]
    batch = batch_of(share)
    terms_shape = (rank, width)
    mixed_shape = (n_slots, share, rank, slots)
    in_specs = [
        whole(h_next.shape),
        whole(w_columns.shape),
        pl.BlockSpec((batch, rank, slots), lambda i, place: (i, 0, 0)),
        visits_spec(slot, batch, slots, width),
    ]
    operands = [h_next, w_columns, frames, visits]
    aliases = {}
    if before is not None:
        in_specs += [whole(terms_shape), pl.BlockSpec(memory_space=pl.ANY)]
        operands += before
        aliases = {6: 1}
    return pl.pallas_call(
        functools.partial(v_terms_kernel, slot, batch, share, before is not None),
        grid_spec=pltpu.PrefetchScalarGridSpec(
            num_scalar_prefetch=1,
            grid=(share // batch,),
            in_specs=in_specs,
            out_specs=[
                whole(terms_shape),
                pl.BlockSpec((1, batch, rank, slots), lambda i, place: (slot, i, 0, 0)),
            ],
            scratch_shapes=[pltpu.VMEM((3 * rank, rank), BF16)],
        ),
        out_shape=[
            jax.ShapeDtypeStruct(terms_shape, F32),
            jax.ShapeDtypeStruct(mixed_shape, F32),
        ],
        input_output_aliases=aliases,
        cost_estimate=cost(8 * share * rank * slots * width, 2 * share * slots * width),
        name="v_terms",
    )(place, *operands)


def next_v_kernel(n_terms, batch, share, place, *refs):
    terms_refs, (inverse_ref, mixed_ref, visits_ref, v_ref, sums_ref, v_parts) = refs[:n_terms], refs[n_terms:]
    step = pl.program_id(0)
    rank = inverse_ref.shape[0]

    @pl.when(step == 0)
    def _():
        v_columns = high_dot(inverse_ref[...], total(terms_refs))
        v_ref[...] = v_columns.T
        v_parts[...] = jnp.concatenate(three_parts(v_columns), axis=0)
        gram = high_dot(v_columns, v_columns, ROWS_BY_ROWS)
        sums_ref[...] = jnp.concatenate([gram, jnp.zeros((rank, LANES - rank), F32)], axis=1)

    sums = sums_ref[...]
    lanes = lane_numbers(sums.shape)
    for p in range(batch):
        seen = low_dot(v_parts[...], visits_ref[p], ROWS_BY_ROWS)
        seen = seen[:rank] + seen[rank : 2 * rank] + seen[2 * rank :]
        column = jnp.sum(seen * mixed_ref[0, p], axis=1, keepdims=True)
        sums = jnp.where(lanes == rank + step * batch + p, column, sums)
    sums_ref[...] = sums


def next_v(place, terms, inverse, mixed, visits):
    patients, slots, width = visits.shape
    _, share, rank, _ = mixed.shape
    batch = batch_of(share)
    per_owner = share // batch
    return pl.pallas_call(
        functools.partial(next_v_kernel, len(terms), batch, share),
        grid_spec=pltpu.PrefetchScalarGridSpec(
            num_scalar_prefetch=1,
            grid=(patients // batch,),
            in_specs=[whole((rank, width))] * len(terms)
            + [
                whole((rank, rank)),
                pl.BlockSpec(
                    (1, batch, rank, slots),
                    lambda i, place: (place[0] ^ (i // per_owner), i % per_owner, 0, 0),
                ),
                pl.BlockSpec((batch, slots, width), lambda i, place: (i, 0, 0)),
            ],
            out_specs=[whole((width, rank)), whole((rank, LANES))],
            scratch_shapes=[pltpu.VMEM((3 * rank, width), BF16)],
        ),
        out_shape=[
            jax.ShapeDtypeStruct((width, rank), F32),
            jax.ShapeDtypeStruct((rank, LANES), F32),
        ],
        compiler_params=pltpu.CompilerParams(vmem_limit_bytes=32 * MIB),
        cost_estimate=cost(8 * patients * rank * slots * width, 2 * patients * slots * width),
        name="next_v",
    )(place, *terms, inverse, mixed, visits)


def next_w_kernel(n_sums, *refs):
    gram_ref, w_ref = refs[n_sums:]
    patients, rank = w_ref.shape
    sums = total(refs[:n_sums])
    table = jnp.concatenate([sums[:, :rank] * gram_ref[...], sums[:, rank:]], axis=1)
    solved = eliminate(table, rank)
    w_ref[...] = solved.T[rank : rank + patients]


def next_w(sums, h_gram, patients):
    rank = h_gram.shape[0]
    return pl.pallas_call(
        functools.partial(next_w_kernel, len(sums)),
        out_shape=jax.ShapeDtypeStruct((patients, rank), F32),
        cost_estimate=cost(12_000_000_000, 64),
        name="next_w",
    )(*sums, h_gram)


def swap(x, axis, slot):
    pairs = [(i, i ^ slot) for i in range(lax.axis_size(axis))]
    return lax.ppermute(x, axis, pairs)


def all_terms(x, axis):
    n = lax.axis_size(axis)
    if n > 4:
        return [lax.psum(x, axis)]
    return [x] + [swap(x, axis, s) for s in range(1, n)]


def staged_terms(x, axis):
    n = lax.axis_size(axis)
    step = 1
    while 2 * step < n:
        x = x + swap(x, axis, step)
        step *= 2
    return [x, swap(x, axis, step)]


def on_device(visits, visit_counts, h_start, v_start, w_start):
    n = lax.axis_size("feature")
    patients, slots, width = visits.shape
    share = patients // n
    place = lax.axis_index("feature").astype(jnp.int32).reshape(1)
    by_owner = visits.reshape(n, share, slots, width)

    coded, scales = [], []
    for slot in range(n - 1, 0, -1):
        code, scale = project_for(slot, place, by_owner, v_start)
        coded.append(swap(code, "feature", slot))
        scales.append(swap(scale, "feature", slot))
    own, v_local, w_local = project_own(place, by_owner, v_start, w_start)
    w_gram, first = first_inverse(all_terms(v_local, "feature"), all_terms(w_local, "patient"))

    frames, h_local = own_frames(place, visit_counts, h_start, w_start, own, coded, scales)
    h_terms = all_terms(sum(all_terms(h_local, "feature")), "patient")
    all_frames = [frames] + [swap(frames, "feature", slot) for slot in range(1, n)]
    h_next, h_gram, product = next_h(h_terms, first, w_gram)

    w_columns = w_start.T
    before = None
    for slot in range(n):
        before = add_v_terms(slot, place, h_next, w_columns, all_frames[slot], by_owner, before)
    terms, mixed = before
    v_terms = staged_terms(terms, "patient")
    v_next, sums = next_v(place, v_terms, inverse(product), mixed, visits)
    w_next = next_w(all_terms(sums, "feature"), h_gram, patients)
    return (h_next, v_next, w_next)


def solution(mesh):
    return jax.shard_map(
        on_device,
        mesh=mesh,
        in_specs=(
            P(("groups", "patient"), None, "feature"),
            P(("groups", "patient")),
            P(),
            P("feature", None),
            P(("groups", "patient"), None),
        ),
        out_specs=(P(None, "groups"), P("feature", "groups"), P("patient", "groups")),
        check_vma=False,
    )
```

```python
import functools

import jax
import jax.numpy as jnp
from jax import lax
from jax.experimental import pallas as pl
from jax.experimental.pallas import tpu as pltpu
from jax.sharding import PartitionSpec as P

NS_STEPS = 12
LANES = 128
LEVELS = 32000.0
COARSE_STEPS = 3
SHORT = pl.CostEstimate(flops=1000, bytes_accessed=1000, transcendentals=0)

epsilon = 1e-06
HIGH = lax.Precision.HIGHEST
F32 = jnp.float32
BF16 = jnp.bfloat16
MIB = 1024 * 1024

ROWS_BY_COLS = (((1,), (0,)), ((), ()))
ROWS_BY_ROWS = (((1,), (1,)), ((), ()))
COLS_BY_COLS = (((0,), (0,)), ((), ()))


def low_dot(a, b, dims=ROWS_BY_COLS):
    return lax.dot_general(a, b, dims, preferred_element_type=F32)


def high_dot(a, b, dims=ROWS_BY_COLS):
    return lax.dot_general(a, b, dims, precision=HIGH, preferred_element_type=F32)


def two_parts(x):
    first = x.astype(BF16)
    return first, (x - first.astype(F32)).astype(BF16)


def three_parts(x):
    first = x.astype(BF16)
    rest = x - first.astype(F32)
    second = rest.astype(BF16)
    return first, second, (rest - second.astype(F32)).astype(BF16)


def lane_numbers(shape):
    return lax.broadcasted_iota(jnp.int32, shape, len(shape) - 1)


def batch_of(share):
    return 2 if share % 2 == 0 else 1


def whole(shape):
    return pl.BlockSpec(shape, lambda *place: (0,) * len(shape))


def parameters(mib):
    return pltpu.CompilerParams(vmem_limit_bytes=mib * MIB)


STREAM = 50
SMALL = 16
VMEM_SPEC = pl.BlockSpec(memory_space=pltpu.VMEM)
SMEM_SPEC = pl.BlockSpec(memory_space=pltpu.SMEM)


def exponent_rows(share):
    return -(-share // 16) * 16


def encode(proj, coded_ref, first_row, exponents, patient):
    top = jnp.max(jnp.abs(proj), axis=1, keepdims=True)
    exponent = jnp.ceil(jnp.log2(jnp.maximum(top, 1e-30)))
    coded = jnp.floor(proj * (LEVELS / jnp.exp2(exponent)) + 0.5)
    coded_ref[pl.ds(first_row, proj.shape[0]), :] = coded.astype(jnp.int32).astype(jnp.int16)
    return jnp.where(lane_numbers(exponents.shape) == patient, exponent, exponents)


def encode_batch(step, batch, share, v_ref, visits_ref, coded_ref, exponents_ref):
    rank = v_ref.shape[0]
    exponents = exponents_ref[...]
    for p in range(batch):
        proj = low_dot(v_ref[...], visits_ref[0, p], ROWS_BY_ROWS)
        row = pl.multiple_of((step * batch + p) * rank, rank)
        exponents = encode(proj, coded_ref, row, exponents, step * batch + p)
    exponents_ref[...] = exponents

    @pl.when(step == share // batch - 1)
    def _():
        rows = exponent_rows(share)
        last = exponents.T[:rows]
        last = jnp.concatenate([last, jnp.zeros((rows, coded_ref.shape[1] - rank), F32)], axis=1)
        coded_ref[pl.ds(share * rank, rows), :] = last.astype(jnp.int32).astype(jnp.int16)


def decode(coded_ref, share, rank):
    rows = exponent_rows(share)
    exponents = coded_ref[pl.ds(share * rank, rows), :LANES].astype(jnp.int32).astype(F32).T
    steps = jnp.exp2(exponents[:rank]) * (1.0 / LEVELS)
    return [
        coded_ref[pl.ds(p * rank, rank), :].astype(jnp.int32).astype(F32) * steps[:, p : p + 1]
        for p in range(share)
    ]


def send_projection_kernel(batch, share, place, v_ref, visits_ref, coded_ref, exponents_ref):
    step = pl.program_id(0)

    @pl.when(step == 0)
    def _():
        exponents_ref[...] = jnp.zeros_like(exponents_ref)

    encode_batch(step, batch, share, v_ref, visits_ref, coded_ref, exponents_ref)


def last_projection_kernel(
    batch, share, place, v_ref, w_ref, visits_ref, coded_ref, proj_ref, v_gram_ref, w_gram_ref, exponents_ref
):
    own = pl.program_id(0)
    step = pl.program_id(1)

    @pl.when((own == 0) & (step == 0))
    def _():
        exponents_ref[...] = jnp.zeros_like(exponents_ref)
        v_gram_ref[...] = low_dot(v_ref[...], v_ref[...], ROWS_BY_ROWS)
        w_gram_ref[...] = high_dot(w_ref[...], w_ref[...], COLS_BY_COLS)

    @pl.when(own == 0)
    def _():
        encode_batch(step, batch, share, v_ref, visits_ref, coded_ref, exponents_ref)

    @pl.when(own == 1)
    def _():
        for p in range(batch):
            proj_ref[p] = low_dot(v_ref[...], visits_ref[0, p], ROWS_BY_ROWS)


def project_for(slot, place, visits, v_rows):
    _, share, slots, width = visits.shape
    rank = v_rows.shape[0]
    batch = batch_of(share)
    coded = (share * rank + exponent_rows(share), slots)
    return pl.pallas_call(
        functools.partial(send_projection_kernel, batch, share),
        grid_spec=pltpu.PrefetchScalarGridSpec(
            num_scalar_prefetch=1,
            grid=(share // batch,),
            in_specs=[
                whole(v_rows.shape),
                pl.BlockSpec((1, batch, slots, width), lambda i, place: (place[0] ^ slot, i, 0, 0)),
            ],
            out_specs=whole(coded),
            scratch_shapes=[pltpu.VMEM((rank, LANES), F32)],
        ),
        out_shape=jax.ShapeDtypeStruct(coded, jnp.int16),
        compiler_params=parameters(STREAM),
        cost_estimate=SHORT,
        name="project_send",
    )(place, v_rows, visits)


def project_last(place, visits, v_rows, w_start):
    _, share, slots, width = visits.shape
    rank = v_rows.shape[0]
    batch = batch_of(share)
    coded = (share * rank + exponent_rows(share), slots)
    gram = (rank, rank)
    return pl.pallas_call(
        functools.partial(last_projection_kernel, batch, share),
        grid_spec=pltpu.PrefetchScalarGridSpec(
            num_scalar_prefetch=1,
            grid=(2, share // batch),
            in_specs=[
                whole(v_rows.shape),
                whole(w_start.shape),
                pl.BlockSpec((1, batch, slots, width), lambda own, i, place: (place[0] ^ (1 - own), i, 0, 0)),
            ],
            out_specs=[
                whole(coded),
                pl.BlockSpec((batch, rank, slots), lambda own, i, place: (i * own, 0, 0)),
                whole(gram),
                whole(gram),
            ],
            scratch_shapes=[pltpu.VMEM((rank, LANES), F32)],
        ),
        out_shape=[
            jax.ShapeDtypeStruct(coded, jnp.int16),
            jax.ShapeDtypeStruct((share, rank, slots), F32),
            jax.ShapeDtypeStruct(gram, F32),
            jax.ShapeDtypeStruct(gram, F32),
        ],
        compiler_params=parameters(STREAM),
        cost_estimate=SHORT,
        name="project_last",
    )(place, v_rows, w_start, visits)


def eliminate(table, rank):
    rows = lax.broadcasted_iota(jnp.int32, table.shape, 0)
    for i in range(0, rank, 2):
        first = jnp.broadcast_to(table[:, i : i + 1], table.shape)
        second = jnp.broadcast_to(table[:, i + 1 : i + 2], table.shape)
        row_first, row_second = table[i : i + 1], table[i + 1 : i + 2]
        a, b = first[i : i + 1], second[i : i + 1]
        c, d = first[i + 1 : i + 2], second[i + 1 : i + 2]
        scale = 1.0 / (a * d - b * c)
        new_first = (d * row_first - b * row_second) * scale
        new_second = (a * row_second - c * row_first) * scale
        table = table - first * new_first - second * new_second
        table = jnp.where(rows == i, new_first, jnp.where(rows == i + 1, new_second, table))
    return table


def inverse_of(gram):
    rank = gram.shape[0]
    eye = (lax.broadcasted_iota(jnp.int32, gram.shape, 0) == lane_numbers(gram.shape)).astype(F32)
    return eliminate(jnp.concatenate([gram, eye], axis=1), rank)[:, rank:]


def total(refs):
    out = refs[0][...]
    for ref in refs[1:]:
        out = out + ref[...]
    return out


def first_inverse_kernel(n_v, *refs):
    w_gram_ref, inverse_ref = refs[-2:]
    w_gram = total(refs[n_v:-2])
    w_gram_ref[...] = w_gram
    inverse_ref[...] = inverse_of(w_gram * total(refs[:n_v]))


def first_inverse(v_grams, w_grams):
    out = jax.ShapeDtypeStruct(w_grams[0].shape, F32)
    return pl.pallas_call(
        functools.partial(first_inverse_kernel, len(v_grams)),
        out_shape=[out, out],
        compiler_params=parameters(SMALL),
        cost_estimate=SHORT,
        name="first_inverse",
    )(*v_grams, *w_grams)


def sweep_once(frames, p, rank, fine):
    frame = frames[p]
    first, second = two_parts(frame)
    if fine:
        both = low_dot(jnp.concatenate([first, second], axis=0), first, ROWS_BY_ROWS)
        gram = both[:rank] + both[rank:] + low_dot(first, second, ROWS_BY_ROWS)
        gram_first, gram_second = two_parts(gram)
        moved = low_dot(jnp.concatenate([gram_first, gram_second], axis=0), first)
        moved = moved[:rank] + moved[rank:] + low_dot(gram_first, second)
    else:
        moved = low_dot(low_dot(first, first, ROWS_BY_ROWS).astype(BF16), first)
    frames[p] = 1.5 * frame - 0.5 * moved


def frames_kernel(share, n_slots, place, counts_ref, h_ref, w_ref, own_ref, *refs):
    coded = refs[: n_slots - 1]
    frames_ref, terms_ref, proj, frames = refs[n_slots - 1 :]
    first = place[0] * share
    rank, slots = frames.shape[1:]
    pieces = [own_ref[p] for p in range(share)]
    for code in coded:
        pieces = [a + b for a, b in zip(pieces, decode(code, share, rank))]
    for p, piece in enumerate(pieces):
        proj[p] = piece
        mixed = high_dot(h_ref[...] * w_ref[pl.ds(first + p, 1), :], piece)
        mixed = jnp.where(lane_numbers((rank, slots)) < counts_ref[first + p], mixed, 0.0)
        energy = jnp.sum(jnp.sum(mixed * mixed, axis=1, keepdims=True), axis=0, keepdims=True)
        frames[p] = mixed * lax.rsqrt(energy + epsilon)

    def sweep(fine, step, carry):
        for p in range(share):
            sweep_once(frames, p, rank, fine)
        return carry

    lax.fori_loop(0, COARSE_STEPS, functools.partial(sweep, False), 0)
    lax.fori_loop(COARSE_STEPS, NS_STEPS, functools.partial(sweep, True), 0)
    terms = jnp.zeros((rank, rank), F32)
    for p in range(share):
        low = frames[p].astype(BF16)
        frames_ref[p] = low
        parts = three_parts(proj[p])
        product = low_dot(low, parts[0], ROWS_BY_ROWS)
        for part in parts[1:]:
            product = product + low_dot(low, part, ROWS_BY_ROWS)
        terms = terms + product * w_ref[pl.ds(first + p, 1), :]
    terms_ref[...] = terms


def own_frames(place, counts, h_start, w_start, own, coded):
    share, rank, slots = own.shape
    return pl.pallas_call(
        functools.partial(frames_kernel, share, len(coded) + 1),
        in_specs=[SMEM_SPEC] * 2 + [VMEM_SPEC] * (3 + len(coded)),
        out_specs=[VMEM_SPEC] * 2,
        out_shape=[
            jax.ShapeDtypeStruct(own.shape, BF16),
            jax.ShapeDtypeStruct((rank, rank), F32),
        ],
        scratch_shapes=[pltpu.VMEM(own.shape, F32)] * 2,
        compiler_params=parameters(SMALL),
        cost_estimate=SHORT,
        name="own_frames",
    )(place, counts, h_start, w_start, own, *coded)


def projected_kernel(batch, place, frames_ref, visits_ref, *refs):
    first_ref, second_ref = refs[-2:]
    rank = frames_ref.shape[1]
    for p in range(batch):
        rows = slice(p * rank, (p + 1) * rank)
        first_ref[0, rows], second_ref[0, rows] = two_parts(low_dot(frames_ref[p], visits_ref[0, p]))


def project_frames(slot, place, frames, visits, before):
    n_slots, share, slots, width = visits.shape
    rank = frames.shape[1]
    batch = batch_of(share)
    out = jax.ShapeDtypeStruct((n_slots, share * rank, width), BF16)
    return pl.pallas_call(
        functools.partial(projected_kernel, batch),
        grid_spec=pltpu.PrefetchScalarGridSpec(
            num_scalar_prefetch=1,
            grid=(share // batch,),
            in_specs=[
                pl.BlockSpec((batch, rank, slots), lambda i, place: (i, 0, 0)),
                pl.BlockSpec((1, batch, slots, width), lambda i, place: (place[0] ^ slot, i, 0, 0)),
            ]
            + [pl.BlockSpec(memory_space=pl.ANY)] * len(before),
            out_specs=[pl.BlockSpec((1, batch * rank, width), lambda i, place: (slot, i, 0))] * 2,
        ),
        out_shape=[out] * 2,
        input_output_aliases={3: 0, 4: 1} if before else {},
        compiler_params=parameters(STREAM),
        cost_estimate=SHORT,
        name="project_frames",
    )(place, frames, visits, *before)


def next_h_kernel(n_terms, n_slots, place, *refs):
    inverse_ref, w_ref, h_ref, factor_ref = refs[n_terms:]
    h_next = high_dot(total(refs[:n_terms]), inverse_ref[...])
    h_ref[...] = h_next
    rank = h_next.shape[0]
    patients = w_ref.shape[0]
    share = patients // n_slots
    h_rows = h_next.T
    w_rows = jnp.concatenate([w_ref[...], jnp.zeros((LANES - patients, rank), F32)], axis=0)
    w_columns = w_rows.T
    for slot in range(n_slots):
        first = (place[0] ^ slot) * share
        columns = pltpu.roll(w_columns, jnp.where(first == 0, 0, LANES - first), 1)
        factor = jnp.concatenate([h_rows * columns[:, p : p + 1] for p in range(share)], axis=1)
        factor_ref[slot] = jnp.concatenate(three_parts(factor), axis=0)


def next_h(place, terms, inverse, w_start, n_slots):
    patients, rank = w_start.shape
    share = patients // n_slots
    return pl.pallas_call(
        functools.partial(next_h_kernel, len(terms), n_slots),
        in_specs=[SMEM_SPEC] + [VMEM_SPEC] * (len(terms) + 2),
        out_specs=[VMEM_SPEC] * 2,
        out_shape=[
            jax.ShapeDtypeStruct(inverse.shape, F32),
            jax.ShapeDtypeStruct((n_slots, 3 * rank, share * rank), BF16),
        ],
        compiler_params=parameters(SMALL),
        cost_estimate=SHORT,
        name="next_h",
    )(place, *terms, inverse, w_start)


def second_inverse_kernel(h_ref, w_gram_ref, gram_ref, inverse_ref):
    gram = high_dot(h_ref[...], h_ref[...], COLS_BY_COLS)
    gram_ref[...] = gram
    inverse_ref[...] = inverse_of(gram * w_gram_ref[...])


def second_inverse(h_next, w_gram):
    out = jax.ShapeDtypeStruct(w_gram.shape, F32)
    return pl.pallas_call(
        second_inverse_kernel,
        out_shape=[out, out],
        compiler_params=parameters(SMALL),
        cost_estimate=SHORT,
        name="second_inverse",
    )(h_next, w_gram)


def v_terms_kernel(factor_ref, first_ref, second_ref, terms_ref):
    step = pl.program_id(0)
    rank = terms_ref.shape[0]
    large = low_dot(factor_ref[0], first_ref[0])
    small = low_dot(factor_ref[0, : 2 * rank], second_ref[0])
    terms = large[:rank] + (large[rank : 2 * rank] + small[:rank]) + (large[2 * rank :] + small[rank:])

    @pl.when(step == 0)
    def _():
        terms_ref[...] = terms

    @pl.when(step > 0)
    def _():
        terms_ref[...] += terms


def all_v_terms(factor, first, second):
    n_slots, rows, width = first.shape
    rank = factor.shape[1] // 3
    return pl.pallas_call(
        v_terms_kernel,
        grid=(n_slots,),
        in_specs=[
            pl.BlockSpec((1, 3 * rank, rows), lambda i: (i, 0, 0)),
            pl.BlockSpec((1, rows, width), lambda i: (i, 0, 0)),
            pl.BlockSpec((1, rows, width), lambda i: (i, 0, 0)),
        ],
        out_specs=whole((rank, width)),
        out_shape=jax.ShapeDtypeStruct((rank, width), F32),
        compiler_params=parameters(STREAM),
        cost_estimate=SHORT,
        name="v_terms",
    )(factor, first, second)


def next_v_kernel(n_terms, share, place, *refs):
    inverse_ref, h_ref, first_ref, second_ref, v_ref, sums_ref, v_parts, weights = refs[n_terms:]
    slot = pl.program_id(0)
    rank = inverse_ref.shape[0]

    @pl.when(slot == 0)
    def _():
        v_rows = high_dot(inverse_ref[...], total(refs[:n_terms]))
        v_ref[...] = v_rows
        v_parts[...] = jnp.concatenate(two_parts(v_rows), axis=0)
        weights[...] = jnp.concatenate([h_ref[...]] * 2, axis=1)
        gram = high_dot(v_rows, v_rows, ROWS_BY_ROWS)
        sums_ref[...] = jnp.concatenate([jnp.zeros((rank, rank), F32), gram], axis=1)

    seen = low_dot(first_ref[0], v_parts[...], ROWS_BY_ROWS) + low_dot(second_ref[0], v_parts[...], ROWS_BY_ROWS)
    first = (place[0] ^ slot) * share
    for p in range(share):
        row = jnp.sum(seen[p * rank : (p + 1) * rank] * weights[...], axis=0, keepdims=True)
        sums_ref[pl.ds(first + p, 1), :rank] = row[:, :rank] + row[:, rank:]


def next_v(place, terms, inverse, h_next, first, second):
    n_slots, rows, width = first.shape
    rank = inverse.shape[0]
    return pl.pallas_call(
        functools.partial(next_v_kernel, len(terms), rows // rank),
        grid_spec=pltpu.PrefetchScalarGridSpec(
            num_scalar_prefetch=1,
            grid=(n_slots,),
            in_specs=[whole((rank, width))] * len(terms)
            + [whole((rank, rank))] * 2
            + [pl.BlockSpec((1, rows, width), lambda i, place: (i, 0, 0))] * 2,
            out_specs=[whole((rank, width)), whole((rank, 2 * rank))],
            scratch_shapes=[pltpu.VMEM((2 * rank, width), BF16), pltpu.VMEM((rank, 2 * rank), F32)],
        ),
        out_shape=[
            jax.ShapeDtypeStruct((rank, width), F32),
            jax.ShapeDtypeStruct((rank, 2 * rank), F32),
        ],
        compiler_params=parameters(STREAM),
        cost_estimate=SHORT,
        name="next_v",
    )(place, *terms, inverse, h_next, first, second)


def next_w_kernel(n_sums, *refs):
    gram_ref, w_ref = refs[n_sums:]
    patients, rank = w_ref.shape
    sums = total(refs[:n_sums])
    table = jnp.concatenate([sums[:, rank:] * gram_ref[...], sums.T[:rank]], axis=1)
    w_ref[...] = eliminate(table, rank).T[rank : rank + patients]


def next_w(sums, h_gram, patients):
    rank = h_gram.shape[0]
    return pl.pallas_call(
        functools.partial(next_w_kernel, len(sums)),
        out_shape=jax.ShapeDtypeStruct((patients, rank), F32),
        compiler_params=parameters(SMALL),
        cost_estimate=SHORT,
        name="next_w",
    )(*sums, h_gram)


def swap(x, axis, slot):
    pairs = [(i, i ^ slot) for i in range(lax.axis_size(axis))]
    return lax.ppermute(x, axis, pairs)


def all_terms(x, axis):
    n = lax.axis_size(axis)
    if n > 4:
        return [lax.psum(x, axis)]
    return [x] + [swap(x, axis, s) for s in range(1, n)]


def staged_terms(x, axis):
    n = lax.axis_size(axis)
    step = 1
    while 2 * step < n:
        x = x + swap(x, axis, step)
        step *= 2
    return [x, swap(x, axis, step)]


def on_device(visits, visit_counts, h_start, v_start, w_start):
    n = lax.axis_size("feature")
    patients, slots, width = visits.shape
    share = patients // n
    place = lax.axis_index("feature").astype(jnp.int32).reshape(1)
    by_owner = visits.reshape(n, share, slots, width)
    v_rows = v_start.T

    coded = [swap(project_for(slot, place, by_owner, v_rows), "feature", slot) for slot in range(n - 1, 1, -1)]
    code, own, v_local, w_local = project_last(place, by_owner, v_rows, w_start)
    coded.append(swap(code, "feature", 1))
    w_gram, first = first_inverse(all_terms(v_local, "feature"), all_terms(w_local, "patient"))

    frames, h_local = own_frames(place, visit_counts, h_start, w_start, own, coded)
    order = list(range(n - 1, 0, -1))
    all_frames = {0: frames} | {slot: swap(frames, "feature", slot) for slot in order}
    h_terms = all_terms(sum(all_terms(h_local, "feature")), "patient")
    h_next, factor = next_h(place, h_terms, first, w_start, n)

    before = []
    for slot in [0, 1] + order[:-1]:
        before = project_frames(slot, place, all_frames[slot], by_owner, before)
    v_terms = staged_terms(all_v_terms(factor, *before), "patient")
    h_gram, second = second_inverse(h_next, w_gram)
    v_next, sums = next_v(place, v_terms, second, h_next, *before)
    w_next = next_w(all_terms(sums, "feature"), h_gram, patients)
    return (h_next, v_next.T, w_next)


def solution(mesh):
    return jax.shard_map(
        on_device,
        mesh=mesh,
        in_specs=(
            P(("groups", "patient"), None, "feature"),
            P(("groups", "patient")),
            P(),
            P("feature", None),
            P(("groups", "patient"), None),
        ),
        out_specs=(P(None, "groups"), P("feature", "groups"), P("patient", "groups")),
        check_vma=False,
    )
```

```python
import functools

import jax
import jax.numpy as jnp
from jax import lax
from jax.experimental import pallas as pl
from jax.experimental.pallas import tpu as pltpu
from jax.sharding import PartitionSpec as P

NS_STEPS = 12
LANES = 128
LEVELS = 32000.0
COARSE_STEPS = 3
SHORT = pl.CostEstimate(flops=1000, bytes_accessed=1000, transcendentals=0)

epsilon = 1e-06
HIGH = lax.Precision.HIGHEST
F32 = jnp.float32
BF16 = jnp.bfloat16
MIB = 1024 * 1024

ROWS_BY_COLS = (((1,), (0,)), ((), ()))
ROWS_BY_ROWS = (((1,), (1,)), ((), ()))
COLS_BY_COLS = (((0,), (0,)), ((), ()))


def low_dot(a, b, dims=ROWS_BY_COLS):
    return lax.dot_general(a, b, dims, preferred_element_type=F32)


def high_dot(a, b, dims=ROWS_BY_COLS):
    return lax.dot_general(a, b, dims, precision=HIGH, preferred_element_type=F32)


def two_parts(x):
    first = x.astype(BF16)
    return first, (x - first.astype(F32)).astype(BF16)


def three_parts(x):
    first = x.astype(BF16)
    rest = x - first.astype(F32)
    second = rest.astype(BF16)
    return first, second, (rest - second.astype(F32)).astype(BF16)


def lane_numbers(shape):
    return lax.broadcasted_iota(jnp.int32, shape, len(shape) - 1)


def batch_of(share):
    return 4 if share % 4 == 0 else share


ANY_SPEC = pl.BlockSpec(memory_space=pl.ANY)


def whole(shape):
    return pl.BlockSpec(shape, lambda *place: (0,) * len(shape))


def parameters(mib):
    return pltpu.CompilerParams(vmem_limit_bytes=mib * MIB)


STREAM = 50
SMALL = 16
VMEM_SPEC = pl.BlockSpec(memory_space=pltpu.VMEM)
SMEM_SPEC = pl.BlockSpec(memory_space=pltpu.SMEM)


def exponent_rows(share):
    return -(-(share + 1) // 16) * 16


def payload_shape(share, rank, slots):
    return (share * rank + rank // 2 + exponent_rows(share), slots)


def row_exponent(x):
    top = jnp.max(jnp.abs(x), axis=1, keepdims=True)
    return jnp.ceil(jnp.log2(jnp.maximum(top, 1e-30)))


def encode_batch(step, batch, v_ref, visits_refs, coded_ref, exponents_ref):
    rank = v_ref.shape[0]
    exponents = exponents_ref[...]
    lanes = lane_numbers(exponents.shape)
    for p in range(batch):
        proj = low_dot(v_ref[...], visits_refs[p][0, 0], ROWS_BY_ROWS)
        exponent = row_exponent(proj)
        coded = jnp.floor(proj * (LEVELS / jnp.exp2(exponent)) + 0.5)
        row = pl.multiple_of((step * batch + p) * rank, rank)
        coded_ref[pl.ds(row, rank), :] = coded.astype(jnp.int32).astype(jnp.int16)
        exponents = jnp.where(lanes == step * batch + p, exponent, exponents)
    exponents_ref[...] = exponents


def encode_rest(share, v_ref, coded_ref, exponents_ref):
    rank = v_ref.shape[0]
    gram = low_dot(v_ref[...], v_ref[...], ROWS_BY_ROWS)
    exponent = row_exponent(gram)
    scaled = gram * (LEVELS / jnp.exp2(exponent))
    first = jnp.floor(scaled + 0.5)
    second = jnp.floor((scaled - first) * (2 * LEVELS) + 0.5)
    digits = jnp.concatenate([first, second], axis=1)
    digits = jnp.concatenate([digits[: rank // 2], digits[rank // 2 :]], axis=1)
    coded_ref[pl.ds(share * rank, rank // 2), :] = digits.astype(jnp.int32).astype(jnp.int16)
    exponents = exponents_ref[...]
    exponents = jnp.where(lane_numbers(exponents.shape) == share, exponent, exponents)
    rows = exponent_rows(share)
    last = exponents.T[:rows]
    last = jnp.concatenate([last, jnp.zeros((rows, coded_ref.shape[1] - rank), F32)], axis=1)
    coded_ref[pl.ds(share * rank + rank // 2, rows), :] = last.astype(jnp.int32).astype(jnp.int16)


def decode(coded_ref, share, rank):
    def rows(first, count):
        return coded_ref[pl.ds(first, count), :].astype(jnp.int32).astype(F32)

    exponents = rows(share * rank + rank // 2, exponent_rows(share))[:, :LANES].T
    steps = jnp.exp2(exponents[:rank]) * (1.0 / LEVELS)
    digits = rows(share * rank, rank // 2)
    digits = jnp.concatenate([digits[:, : 2 * rank], digits[:, 2 * rank :]], axis=0)
    gram = (digits[:, :rank] + digits[:, rank:] * (0.5 / LEVELS)) * steps[:, share : share + 1]
    return [rows(p * rank, rank) * steps[:, p : p + 1] for p in range(share)], gram


def send_projection_kernel(batch, share, place, v_ref, *refs):
    visits_refs = refs[:batch]
    coded_ref, exponents_ref = refs[batch:]
    step = pl.program_id(0)

    @pl.when(step == 0)
    def _():
        exponents_ref[...] = jnp.zeros_like(exponents_ref)

    encode_batch(step, batch, v_ref, visits_refs, coded_ref, exponents_ref)

    @pl.when(step == share // batch - 1)
    def _():
        encode_rest(share, v_ref, coded_ref, exponents_ref)


def own_projection_kernel(batch, place, v_ref, w_ref, *refs):
    visits_refs = refs[:batch]
    proj_ref, v_gram_ref, w_gram_ref = refs[batch:]

    @pl.when(pl.program_id(0) == 0)
    def _():
        v_gram_ref[...] = low_dot(v_ref[...], v_ref[...], ROWS_BY_ROWS)
        w_gram_ref[...] = high_dot(w_ref[...], w_ref[...], COLS_BY_COLS)

    for p in range(batch):
        proj_ref[p] = low_dot(v_ref[...], visits_refs[p][0, 0], ROWS_BY_ROWS)


def visits_specs(slot, batch, slots, width):
    return [
        pl.BlockSpec((1, 1, slots, width), lambda i, place, p=p: (place[0] ^ slot, i * batch + p, 0, 0))
        for p in range(batch)
    ]


def project_for(slot, place, visits, v_rows):
    _, share, slots, width = visits.shape
    rank = v_rows.shape[0]
    batch = batch_of(share)
    coded = payload_shape(share, rank, slots)
    return pl.pallas_call(
        functools.partial(send_projection_kernel, batch, share),
        grid_spec=pltpu.PrefetchScalarGridSpec(
            num_scalar_prefetch=1,
            grid=(share // batch,),
            in_specs=[whole(v_rows.shape)] + visits_specs(slot, batch, slots, width),
            out_specs=whole(coded),
            scratch_shapes=[pltpu.VMEM((rank, LANES), F32)],
        ),
        out_shape=jax.ShapeDtypeStruct(coded, jnp.int16),
        compiler_params=parameters(STREAM),
        cost_estimate=SHORT,
        name="project_send",
    )(place, v_rows, *[visits] * batch)


def project_own(place, visits, v_rows, w_start):
    _, share, slots, width = visits.shape
    rank = v_rows.shape[0]
    batch = batch_of(share)
    gram = (rank, rank)
    return pl.pallas_call(
        functools.partial(own_projection_kernel, batch),
        grid_spec=pltpu.PrefetchScalarGridSpec(
            num_scalar_prefetch=1,
            grid=(share // batch,),
            in_specs=[whole(v_rows.shape), whole(w_start.shape)] + visits_specs(0, batch, slots, width),
            out_specs=[
                pl.BlockSpec((batch, rank, slots), lambda i, place: (i, 0, 0)),
                whole(gram),
                whole(gram),
            ],
        ),
        out_shape=[
            jax.ShapeDtypeStruct((share, rank, slots), F32),
            jax.ShapeDtypeStruct(gram, F32),
            jax.ShapeDtypeStruct(gram, F32),
        ],
        compiler_params=parameters(STREAM),
        cost_estimate=SHORT,
        name="project_own",
    )(place, v_rows, w_start, *[visits] * batch)


def eliminate(table, rank):
    rows = lax.broadcasted_iota(jnp.int32, table.shape, 0)
    for i in range(0, rank, 2):
        first = jnp.broadcast_to(table[:, i : i + 1], table.shape)
        second = jnp.broadcast_to(table[:, i + 1 : i + 2], table.shape)
        row_first, row_second = table[i : i + 1], table[i + 1 : i + 2]
        a, b = first[i : i + 1], second[i : i + 1]
        c, d = first[i + 1 : i + 2], second[i + 1 : i + 2]
        scale = 1.0 / (a * d - b * c)
        new_first = (d * row_first - b * row_second) * scale
        new_second = (a * row_second - c * row_first) * scale
        table = table - first * new_first - second * new_second
        table = jnp.where(rows == i, new_first, jnp.where(rows == i + 1, new_second, table))
    return table


def inverse_of(gram):
    rank = gram.shape[0]
    eye = (lax.broadcasted_iota(jnp.int32, gram.shape, 0) == lane_numbers(gram.shape)).astype(F32)
    return eliminate(jnp.concatenate([gram, eye], axis=1), rank)[:, rank:]


def total(refs):
    out = refs[0][...]
    for ref in refs[1:]:
        out = out + ref[...]
    return out


def first_inverse_kernel(v_gram_ref, w_gram_ref, after_ref, inverse_ref):
    inverse_ref[...] = inverse_of(w_gram_ref[...] * v_gram_ref[...])


def first_inverse(v_gram, w_gram, after):
    return pl.pallas_call(
        first_inverse_kernel,
        in_specs=[VMEM_SPEC] * 2 + [ANY_SPEC],
        out_specs=VMEM_SPEC,
        out_shape=jax.ShapeDtypeStruct(w_gram.shape, F32),
        compiler_params=parameters(SMALL),
        cost_estimate=SHORT,
        name="first_inverse",
    )(v_gram, w_gram, after)


def sum_h_kernel(n_terms, *refs):
    h_ref, w_gram_ref = refs[n_terms + 1 :]
    rank = h_ref.shape[0]
    both = total(refs[:n_terms])
    h_ref[...] = both[:, :rank]
    w_gram_ref[...] = both[:, rank:]


def sum_h(terms, after):
    rank = terms[0].shape[0]
    return pl.pallas_call(
        functools.partial(sum_h_kernel, len(terms)),
        in_specs=[VMEM_SPEC] * len(terms) + [ANY_SPEC],
        out_specs=[VMEM_SPEC] * 2,
        out_shape=[jax.ShapeDtypeStruct((rank, rank), F32)] * 2,
        compiler_params=parameters(SMALL),
        cost_estimate=SHORT,
        name="sum_h",
    )(*terms, after)


def sweep_once(frames, p, rank, fine):
    frame = frames[p]
    first, second = two_parts(frame)
    if fine:
        both = low_dot(jnp.concatenate([first, second], axis=0), first, ROWS_BY_ROWS)
        gram = both[:rank] + both[rank:] + low_dot(first, second, ROWS_BY_ROWS)
        gram_first, gram_second = two_parts(gram)
        moved = low_dot(jnp.concatenate([gram_first, gram_second], axis=0), first)
        moved = moved[:rank] + moved[rank:] + low_dot(gram_first, second)
    else:
        moved = low_dot(low_dot(first, first, ROWS_BY_ROWS).astype(BF16), first)
    frames[p] = 1.5 * frame - 0.5 * moved


def frames_kernel(share, n_coded, place, counts_ref, h_ref, w_ref, v_gram_ref, w_gram_ref, own_ref, *refs):
    coded = refs[:n_coded]
    frames_ref, terms_ref, v_total_ref, proj, frames = refs[n_coded:]
    first = place[0] * share
    rank, slots = frames.shape[1:]
    pieces = [own_ref[p] for p in range(share)]
    v_gram = v_gram_ref[...]
    for code in coded:
        arrived, gram = decode(code, share, rank)
        pieces = [a + b for a, b in zip(pieces, arrived)]
        v_gram = v_gram + gram
    v_total_ref[...] = v_gram
    for p, piece in enumerate(pieces):
        proj[p] = piece
        mixed = high_dot(h_ref[...] * w_ref[pl.ds(first + p, 1), :], piece)
        mixed = jnp.where(lane_numbers((rank, slots)) < counts_ref[first + p], mixed, 0.0)
        energy = jnp.sum(jnp.sum(mixed * mixed, axis=1, keepdims=True), axis=0, keepdims=True)
        frames[p] = mixed * lax.rsqrt(energy + epsilon)

    def sweep(fine, step, carry):
        for p in range(share):
            sweep_once(frames, p, rank, fine)
        return carry

    lax.fori_loop(0, COARSE_STEPS, functools.partial(sweep, False), 0)
    lax.fori_loop(COARSE_STEPS, NS_STEPS, functools.partial(sweep, True), 0)
    terms = jnp.zeros((rank, rank), F32)
    for p in range(share):
        low = frames[p].astype(BF16)
        frames_ref[p] = low
        parts = three_parts(proj[p])
        product = low_dot(low, parts[0], ROWS_BY_ROWS)
        for part in parts[1:]:
            product = product + low_dot(low, part, ROWS_BY_ROWS)
        terms = terms + product * w_ref[pl.ds(first + p, 1), :]
    terms_ref[...] = jnp.concatenate([terms, w_gram_ref[...]], axis=1)


def own_frames(place, counts, h_start, w_start, v_gram, w_gram, own, coded):
    share, rank, slots = own.shape
    return pl.pallas_call(
        functools.partial(frames_kernel, share, len(coded)),
        in_specs=[SMEM_SPEC] * 2 + [VMEM_SPEC] * (5 + len(coded)),
        out_specs=[VMEM_SPEC] * 3,
        out_shape=[
            jax.ShapeDtypeStruct(own.shape, BF16),
            jax.ShapeDtypeStruct((rank, 2 * rank), F32),
            jax.ShapeDtypeStruct((rank, rank), F32),
        ],
        scratch_shapes=[pltpu.VMEM(own.shape, F32)] * 2,
        compiler_params=parameters(SMALL),
        cost_estimate=SHORT,
        name="own_frames",
    )(place, counts, h_start, w_start, v_gram, w_gram, own, *coded)


def projected_kernel(batch, place, frames_ref, *refs):
    first_ref, second_ref, token_ref = refs[-3:]
    rank = frames_ref.shape[1]
    token_ref[...] = jnp.zeros_like(token_ref)
    for p in range(batch):
        rows = slice(p * rank, (p + 1) * rank)
        first_ref[0, rows], second_ref[0, rows] = two_parts(low_dot(frames_ref[p], refs[p][0, 0]))


def project_frames(slot, place, frames, visits, before):
    n_slots, share, slots, width = visits.shape
    rank = frames.shape[1]
    batch = batch_of(share)
    out = jax.ShapeDtypeStruct((n_slots, share * rank, width), BF16)
    aliases = {batch + 2: 0, batch + 3: 1} if before else {}
    *before, token = pl.pallas_call(
        functools.partial(projected_kernel, batch),
        grid_spec=pltpu.PrefetchScalarGridSpec(
            num_scalar_prefetch=1,
            grid=(share // batch,),
            in_specs=[pl.BlockSpec((batch, rank, slots), lambda i, place: (i, 0, 0))]
            + visits_specs(slot, batch, slots, width)
            + [ANY_SPEC] * len(before),
            out_specs=[pl.BlockSpec((1, batch * rank, width), lambda i, place: (slot, i, 0))] * 2 + [whole((8, LANES))],
        ),
        out_shape=[out, out, jax.ShapeDtypeStruct((8, LANES), F32)],
        input_output_aliases=aliases,
        compiler_params=parameters(STREAM),
        cost_estimate=SHORT,
        name="project_frames",
    )(place, frames, *[visits] * batch, *before)
    return before, token


def next_h_kernel(n_terms, n_slots, place, *refs):
    inverse_ref, w_ref, _, h_ref, factor_ref = refs[n_terms:]
    h_next = high_dot(total(refs[:n_terms]), inverse_ref[...])
    h_ref[...] = h_next
    rank = h_next.shape[0]
    patients = w_ref.shape[0]
    share = patients // n_slots
    h_rows = h_next.T
    w_rows = jnp.concatenate([w_ref[...], jnp.zeros((LANES - patients, rank), F32)], axis=0)
    w_columns = w_rows.T
    for slot in range(n_slots):
        first = (place[0] ^ slot) * share
        columns = pltpu.roll(w_columns, jnp.where(first == 0, 0, LANES - first), 1)
        factor = jnp.concatenate([h_rows * columns[:, p : p + 1] for p in range(share)], axis=1)
        factor_ref[slot] = jnp.concatenate(three_parts(factor), axis=0)


def next_h(place, terms, inverse, w_start, n_slots, after):
    patients, rank = w_start.shape
    share = patients // n_slots
    return pl.pallas_call(
        functools.partial(next_h_kernel, len(terms), n_slots),
        in_specs=[SMEM_SPEC] + [VMEM_SPEC] * (len(terms) + 2) + [ANY_SPEC],
        out_specs=[VMEM_SPEC] * 2,
        out_shape=[
            jax.ShapeDtypeStruct(inverse.shape, F32),
            jax.ShapeDtypeStruct((n_slots, 3 * rank, share * rank), BF16),
        ],
        compiler_params=parameters(SMALL),
        cost_estimate=SHORT,
        name="next_h",
    )(place, *terms, inverse, w_start, after)


def second_inverse_kernel(h_ref, w_gram_ref, gram_ref, inverse_ref):
    gram = high_dot(h_ref[...], h_ref[...], COLS_BY_COLS)
    gram_ref[...] = gram
    inverse_ref[...] = inverse_of(gram * w_gram_ref[...])


def second_inverse(h_next, w_gram):
    out = jax.ShapeDtypeStruct(w_gram.shape, F32)
    return pl.pallas_call(
        second_inverse_kernel,
        out_shape=[out, out],
        compiler_params=parameters(SMALL),
        cost_estimate=SHORT,
        name="second_inverse",
    )(h_next, w_gram)


def v_terms_kernel(core, factor_ref, first_ref, second_ref, keep_ref, send_ref, terms_ref):
    step = pl.program_id(0)
    rank, width = terms_ref.shape
    half = width // 2
    large = low_dot(factor_ref[0], first_ref[0])
    small = low_dot(factor_ref[0, : 2 * rank], second_ref[0])
    terms = large[:rank] + (large[rank : 2 * rank] + small[:rank]) + (large[2 * rank :] + small[rank:])

    @pl.when(step == 0)
    def _():
        terms_ref[...] = terms

    @pl.when(step > 0)
    def _():
        terms_ref[...] += terms

    @pl.when(step == pl.num_programs(0) - 1)
    def _():
        keep_ref[...] = terms_ref[:, pl.ds(pl.multiple_of(core[0] * half, half), half)]
        send_ref[...] = terms_ref[:, pl.ds(pl.multiple_of((1 - core[0]) * half, half), half)]


def all_v_terms(core, factor, first, second):
    n_slots, rows, width = first.shape
    rank = factor.shape[1] // 3
    half = (rank, width // 2)
    return pl.pallas_call(
        v_terms_kernel,
        grid_spec=pltpu.PrefetchScalarGridSpec(
            num_scalar_prefetch=1,
            grid=(n_slots,),
            in_specs=[
                pl.BlockSpec((1, 3 * rank, rows), lambda i, core: (i, 0, 0)),
                pl.BlockSpec((1, rows, width), lambda i, core: (i, 0, 0)),
                pl.BlockSpec((1, rows, width), lambda i, core: (i, 0, 0)),
            ],
            out_specs=[whole(half)] * 2,
            scratch_shapes=[pltpu.VMEM((rank, width), F32)],
        ),
        out_shape=[jax.ShapeDtypeStruct(half, F32)] * 2,
        compiler_params=parameters(STREAM),
        cost_estimate=SHORT,
        name="v_terms",
    )(core, factor, first, second)


def next_v_kernel(share, place, core, own_ref, other_ref, *refs):
    inverse_ref, h_ref, first_ref, second_ref, v_ref, sums_ref, v_parts, weights = refs
    slot = pl.program_id(0)
    rank = inverse_ref.shape[0]

    @pl.when(slot == 0)
    def _():
        upper = core[0] == 1
        left = jnp.where(upper, other_ref[...], own_ref[...])
        right = jnp.where(upper, own_ref[...], other_ref[...])
        v_rows = high_dot(inverse_ref[...], jnp.concatenate([left, right], axis=1))
        v_ref[...] = v_rows
        v_parts[...] = jnp.concatenate(two_parts(v_rows), axis=0)
        weights[...] = jnp.concatenate([h_ref[...]] * 2, axis=1)
        gram = low_dot(v_parts[...], v_parts[...], ROWS_BY_ROWS)
        gram = gram[:rank, :rank] + (gram[:rank, rank:] + gram[rank:, :rank])
        sums_ref[...] = jnp.concatenate([jnp.zeros((rank, rank), F32), gram], axis=1)

    seen = low_dot(first_ref[0], v_parts[...], ROWS_BY_ROWS) + low_dot(second_ref[0], v_parts[...], ROWS_BY_ROWS)
    first = (place[0] ^ slot) * share
    for p in range(share):
        row = jnp.sum(seen[p * rank : (p + 1) * rank] * weights[...], axis=0, keepdims=True)
        sums_ref[pl.ds(first + p, 1), :rank] = row[:, :rank] + row[:, rank:]


def next_v(place, core, own, other, inverse, h_next, first, second):
    n_slots, rows, width = first.shape
    rank = inverse.shape[0]
    return pl.pallas_call(
        functools.partial(next_v_kernel, rows // rank),
        grid_spec=pltpu.PrefetchScalarGridSpec(
            num_scalar_prefetch=2,
            grid=(n_slots,),
            in_specs=[whole(own.shape)] * 2
            + [whole((rank, rank))] * 2
            + [pl.BlockSpec((1, rows, width), lambda i, place, core: (i, 0, 0))] * 2,
            out_specs=[whole((rank, width)), whole((rank, 2 * rank))],
            scratch_shapes=[pltpu.VMEM((2 * rank, width), BF16), pltpu.VMEM((rank, 2 * rank), F32)],
        ),
        out_shape=[
            jax.ShapeDtypeStruct((rank, width), F32),
            jax.ShapeDtypeStruct((rank, 2 * rank), F32),
        ],
        compiler_params=parameters(STREAM),
        cost_estimate=SHORT,
        name="next_v",
    )(place, core, own, other, inverse, h_next, first, second)


def next_w_kernel(n_sums, *refs):
    gram_ref, w_ref = refs[n_sums:]
    patients, rank = w_ref.shape
    sums = total(refs[:n_sums])
    table = jnp.concatenate([sums[:, rank:] * gram_ref[...], sums.T[:rank]], axis=1)
    w_ref[...] = eliminate(table, rank).T[rank : rank + patients]


def next_w(sums, h_gram, patients):
    rank = h_gram.shape[0]
    return pl.pallas_call(
        functools.partial(next_w_kernel, len(sums)),
        out_shape=jax.ShapeDtypeStruct((patients, rank), F32),
        compiler_params=parameters(SMALL),
        cost_estimate=SHORT,
        name="next_w",
    )(*sums, h_gram)


def swap(x, axis, slot):
    pairs = [(i, i ^ slot) for i in range(lax.axis_size(axis))]
    return lax.ppermute(x, axis, pairs)


def all_terms(x, axis):
    n = lax.axis_size(axis)
    if n > 4:
        return [lax.psum(x, axis)]
    return [x] + [swap(x, axis, s) for s in range(1, n)]


def add_kernel(a_ref, b_ref, after_ref, sum_ref):
    sum_ref[...] = a_ref[...] + b_ref[...]


def add(a, b, after):
    return pl.pallas_call(
        add_kernel,
        in_specs=[VMEM_SPEC] * 2 + [ANY_SPEC],
        out_specs=VMEM_SPEC,
        out_shape=jax.ShapeDtypeStruct(a.shape, a.dtype),
        compiler_params=parameters(SMALL),
        cost_estimate=SHORT,
        name="add_terms",
    )(a, b, after)


def patient_halves(keep, send, after):
    own = keep + swap(send, "patient", 1)
    step = 2
    while step < lax.axis_size("patient"):
        own = add(own, swap(own, "patient", step), after)
        step *= 2
    return own, swap(own, "patient", 1)


def on_device(visits, visit_counts, h_start, v_start, w_start):
    n = lax.axis_size("feature")
    patients, slots, width = visits.shape
    share = patients // n
    place = lax.axis_index("feature").astype(jnp.int32).reshape(1)
    core = lax.rem(lax.axis_index("patient").astype(jnp.int32), 2).reshape(1)
    by_owner = visits.reshape(n, share, slots, width)
    v_rows = v_start.T

    coded = [swap(project_for(slot, place, by_owner, v_rows), "feature", slot) for slot in range(n - 1, 0, -1)]
    own, v_local, w_local = project_own(place, by_owner, v_rows, w_start)

    frames, h_local, v_gram = own_frames(place, visit_counts, h_start, w_start, v_local, w_local, own, coded)
    far = list(range(n - 1, 1, -1))
    all_frames = {0: frames} | {slot: swap(frames, "feature", slot) for slot in far + [1]}
    h_sums = all_terms(h_local, "patient")

    projected, token = project_frames(0, place, frames, by_owner, [])
    h_sum, w_gram = sum_h(h_sums, token)
    h_terms = all_terms(h_sum, "feature")
    projected, token = project_frames(1, place, all_frames[1], by_owner, projected)
    first = first_inverse(v_gram, w_gram, token)
    for slot in far:
        projected, token = project_frames(slot, place, all_frames[slot], by_owner, projected)
    h_next, factor = next_h(place, h_terms, first, w_start, n, token)

    keep, send = all_v_terms(core, factor, *projected)
    h_gram, second = second_inverse(h_next, w_gram)
    own_terms, other_terms = patient_halves(keep, send, second)
    v_next, sums = next_v(place, core, own_terms, other_terms, second, h_next, *projected)
    w_next = next_w(all_terms(sums, "feature"), h_gram, patients)
    return (h_next, v_next.T, w_next)


def solution(mesh):
    return jax.shard_map(
        on_device,
        mesh=mesh,
        in_specs=(
            P(("groups", "patient"), None, "feature"),
            P(("groups", "patient")),
            P(),
            P("feature", None),
            P(("groups", "patient"), None),
        ),
        out_specs=(P(None, "groups"), P("feature", "groups"), P("patient", "groups")),
        check_vma=False,
    )
```

```python
import functools

import jax
import jax.numpy as jnp
from jax import lax
from jax.experimental import pallas as pl
from jax.experimental.pallas import tpu as pltpu
from jax.sharding import PartitionSpec as P

NS_STEPS = 12
LANES = 128
LEVELS = 32000.0
COARSE_STEPS = 3
SHORT = pl.CostEstimate(flops=1000, bytes_accessed=1000, transcendentals=0)

epsilon = 1e-06
HIGH = lax.Precision.HIGHEST
F32 = jnp.float32
BF16 = jnp.bfloat16
MIB = 1024 * 1024

ROWS_BY_COLS = (((1,), (0,)), ((), ()))
ROWS_BY_ROWS = (((1,), (1,)), ((), ()))
COLS_BY_COLS = (((0,), (0,)), ((), ()))


def low_dot(a, b, dims=ROWS_BY_COLS):
    return lax.dot_general(a, b, dims, preferred_element_type=F32)


def high_dot(a, b, dims=ROWS_BY_COLS):
    return lax.dot_general(a, b, dims, precision=HIGH, preferred_element_type=F32)


def two_parts(x):
    first = x.astype(BF16)
    return first, (x - first.astype(F32)).astype(BF16)


def three_parts(x):
    first = x.astype(BF16)
    rest = x - first.astype(F32)
    second = rest.astype(BF16)
    return first, second, (rest - second.astype(F32)).astype(BF16)


def lane_numbers(shape):
    return lax.broadcasted_iota(jnp.int32, shape, len(shape) - 1)


ANY_SPEC = pl.BlockSpec(memory_space=pl.ANY)


def parameters(mib):
    return pltpu.CompilerParams(vmem_limit_bytes=mib * MIB)


STREAM = 50
SMALL = 16
VMEM_SPEC = pl.BlockSpec(memory_space=pltpu.VMEM)
SMEM_SPEC = pl.BlockSpec(memory_space=pltpu.SMEM)


def exponent_rows(share):
    return -(-(share + 1) // 16) * 16


def payload_shape(share, rank, slots):
    return (share * rank + rank // 2 + exponent_rows(share), slots)


def row_exponent(x):
    top = jnp.max(jnp.abs(x), axis=1, keepdims=True)
    return jnp.ceil(jnp.log2(jnp.maximum(top, 1e-30)))


def fetch(source, buffers, sems):
    copies = [
        pltpu.make_async_copy(source.at[p], buffers.at[p], sems.at[p]) for p in range(buffers.shape[0])
    ]
    for copy in copies:
        copy.start()
    return copies


def project_patient(v_ref, visits):
    return low_dot(visits, v_ref[...], ROWS_BY_ROWS).T


def encode_rest(share, v_ref, coded_ref, exponents):
    rank = v_ref.shape[0]
    gram = low_dot(v_ref[...], v_ref[...], ROWS_BY_ROWS)
    exponent = row_exponent(gram)
    scaled = gram * (LEVELS / jnp.exp2(exponent))
    first = jnp.floor(scaled + 0.5)
    second = jnp.floor((scaled - first) * (2 * LEVELS) + 0.5)
    digits = jnp.concatenate([first, second], axis=1)
    digits = jnp.concatenate([digits[: rank // 2], digits[rank // 2 :]], axis=1)
    coded_ref[pl.ds(share * rank, rank // 2), :] = digits.astype(jnp.int32).astype(jnp.int16)
    exponents = jnp.where(lane_numbers(exponents.shape) == share, exponent, exponents)
    rows = exponent_rows(share)
    last = exponents.T[:rows]
    last = jnp.concatenate([last, jnp.zeros((rows, coded_ref.shape[1] - rank), F32)], axis=1)
    coded_ref[pl.ds(share * rank + rank // 2, rows), :] = last.astype(jnp.int32).astype(jnp.int16)


def decode(coded_ref, share, rank):
    def rows(first, count):
        return coded_ref[pl.ds(first, count), :].astype(jnp.int32).astype(F32)

    exponents = rows(share * rank + rank // 2, exponent_rows(share))[:, :LANES].T
    steps = jnp.exp2(exponents[:rank]) * (1.0 / LEVELS)
    digits = rows(share * rank, rank // 2)
    digits = jnp.concatenate([digits[:, : 2 * rank], digits[:, 2 * rank :]], axis=0)
    gram = (digits[:, :rank] + digits[:, rank:] * (0.5 / LEVELS)) * steps[:, share : share + 1]
    return [rows(p * rank, rank) * steps[:, p : p + 1] for p in range(share)], gram


def send_projection_kernel(slot, place, v_ref, visits_ref, coded_ref, buffers, sems):
    copies = fetch(visits_ref.at[place[0] ^ slot], buffers, sems)
    share, rank = len(copies), v_ref.shape[0]
    exponents = jnp.zeros((rank, LANES), F32)
    for p, copy in enumerate(copies):
        copy.wait()
        proj = project_patient(v_ref, buffers[p])
        exponent = row_exponent(proj)
        coded = jnp.floor(proj * (LEVELS / jnp.exp2(exponent)) + 0.5)
        coded_ref[pl.ds(p * rank, rank), :] = coded.astype(jnp.int32).astype(jnp.int16)
        exponents = jnp.where(lane_numbers(exponents.shape) == p, exponent, exponents)
    encode_rest(share, v_ref, coded_ref, exponents)


def own_projection_kernel(place, v_ref, w_ref, visits_ref, proj_ref, v_gram_ref, w_gram_ref, buffers, sems):
    copies = fetch(visits_ref.at[place[0]], buffers, sems)
    v_gram_ref[...] = low_dot(v_ref[...], v_ref[...], ROWS_BY_ROWS)
    w_gram_ref[...] = high_dot(w_ref[...], w_ref[...], COLS_BY_COLS)
    for p, copy in enumerate(copies):
        copy.wait()
        proj_ref[p] = project_patient(v_ref, buffers[p])


def visits_buffers(visits):
    share = visits.shape[1]
    return [pltpu.VMEM(visits.shape[1:], BF16), pltpu.SemaphoreType.DMA((share,))]


def project_for(slot, place, visits, v_rows):
    _, share, slots, width = visits.shape
    rank = v_rows.shape[0]
    return pl.pallas_call(
        functools.partial(send_projection_kernel, slot),
        in_specs=[SMEM_SPEC, VMEM_SPEC, ANY_SPEC],
        out_specs=VMEM_SPEC,
        out_shape=jax.ShapeDtypeStruct(payload_shape(share, rank, slots), jnp.int16),
        scratch_shapes=visits_buffers(visits),
        compiler_params=parameters(STREAM),
        cost_estimate=SHORT,
        name="project_send",
    )(place, v_rows, visits)


def project_own(place, visits, v_rows, w_start):
    _, share, slots, width = visits.shape
    rank = v_rows.shape[0]
    gram = (rank, rank)
    return pl.pallas_call(
        own_projection_kernel,
        in_specs=[SMEM_SPEC, VMEM_SPEC, VMEM_SPEC, ANY_SPEC],
        out_specs=[VMEM_SPEC] * 3,
        out_shape=[
            jax.ShapeDtypeStruct((share, rank, slots), F32),
            jax.ShapeDtypeStruct(gram, F32),
            jax.ShapeDtypeStruct(gram, F32),
        ],
        scratch_shapes=visits_buffers(visits),
        compiler_params=parameters(STREAM),
        cost_estimate=SHORT,
        name="project_own",
    )(place, v_rows, w_start, visits)


def pair_inverse(a, b, c, d):
    scale = 1.0 / (a * d - b * c)
    return d * scale, b * scale, c * scale, a * scale


def eliminate(table, rank):
    tiles = [table[8 * t : 8 * t + 8] for t in range(rank // 8)]
    rows = lax.broadcasted_iota(jnp.int32, tiles[0].shape, 0)
    for i in range(0, rank, 4):
        columns = [[jnp.broadcast_to(t[:, i + q : i + q + 1], t.shape) for q in range(4)] for t in tiles]
        home, first = i // 8, i % 8
        r0, r1, r2, r3 = (tiles[home][first + q : first + q + 1] for q in range(4))
        m = [[columns[home][q][first + p : first + p + 1] for q in range(4)] for p in range(4)]
        d, b, c, a = pair_inverse(m[0][0], m[0][1], m[1][0], m[1][1])
        q02, q03 = d * m[0][2] - b * m[1][2], d * m[0][3] - b * m[1][3]
        q12, q13 = a * m[1][2] - c * m[0][2], a * m[1][3] - c * m[0][3]
        y0, y1 = d * r0 - b * r1, a * r1 - c * r0
        z2 = r2 - (m[2][0] * y0 + m[2][1] * y1)
        z3 = r3 - (m[3][0] * y0 + m[3][1] * y1)
        d, b, c, a = pair_inverse(
            m[2][2] - (m[2][0] * q02 + m[2][1] * q12),
            m[2][3] - (m[2][0] * q03 + m[2][1] * q13),
            m[3][2] - (m[3][0] * q02 + m[3][1] * q12),
            m[3][3] - (m[3][0] * q03 + m[3][1] * q13),
        )
        n2, n3 = d * z2 - b * z3, a * z3 - c * z2
        new = [y0 - (q02 * n2 + q03 * n3), y1 - (q12 * n2 + q13 * n3), n2, n3]
        for t, (c0, c1, c2, c3) in enumerate(columns):
            tile = tiles[t] - ((c0 * new[0] + c1 * new[1]) + (c2 * new[2] + c3 * new[3]))
            if t == home:
                for q in range(4):
                    tile = jnp.where(rows == first + q, new[q], tile)
            tiles[t] = tile
    return jnp.concatenate(tiles, axis=0)


def inverse_of(gram):
    rank = gram.shape[0]
    eye = (lax.broadcasted_iota(jnp.int32, gram.shape, 0) == lane_numbers(gram.shape)).astype(F32)
    return eliminate(jnp.concatenate([gram, eye], axis=1), rank)[:, rank:]


def total(refs):
    out = refs[0][...]
    for ref in refs[1:]:
        out = out + ref[...]
    return out


def first_inverse_kernel(v_gram_ref, w_gram_ref, after_ref, inverse_ref):
    inverse_ref[...] = inverse_of(w_gram_ref[...] * v_gram_ref[...])


def first_inverse(v_gram, w_gram, after):
    return pl.pallas_call(
        first_inverse_kernel,
        in_specs=[VMEM_SPEC] * 2 + [ANY_SPEC],
        out_specs=VMEM_SPEC,
        out_shape=jax.ShapeDtypeStruct(w_gram.shape, F32),
        compiler_params=parameters(SMALL),
        cost_estimate=SHORT,
        name="first_inverse",
    )(v_gram, w_gram, after)


def sum_h_kernel(n_terms, *refs):
    h_ref, w_gram_ref = refs[n_terms + 1 :]
    rank = h_ref.shape[0]
    both = total(refs[:n_terms])
    h_ref[...] = both[:, :rank]
    w_gram_ref[...] = both[:, rank:]


def sum_h(terms, after):
    rank = terms[0].shape[0]
    return pl.pallas_call(
        functools.partial(sum_h_kernel, len(terms)),
        in_specs=[VMEM_SPEC] * len(terms) + [ANY_SPEC],
        out_specs=[VMEM_SPEC] * 2,
        out_shape=[jax.ShapeDtypeStruct((rank, rank), F32)] * 2,
        compiler_params=parameters(SMALL),
        cost_estimate=SHORT,
        name="sum_h",
    )(*terms, after)


def sweep_once(frames, p, rank, fine):
    frame = frames[p]
    first, second = two_parts(frame)
    if fine:
        both = low_dot(jnp.concatenate([first, second], axis=0), first, ROWS_BY_ROWS)
        gram = both[:rank] + (both[rank:] + both[rank:].T)
        gram_first, gram_second = two_parts(gram)
        moved = low_dot(
            jnp.concatenate([gram_first, gram_second, gram_first], axis=1),
            jnp.concatenate([first, first, second], axis=0),
        )
    else:
        moved = low_dot(low_dot(first, first, ROWS_BY_ROWS).astype(BF16), first)
    frames[p] = 1.5 * frame - 0.5 * moved


def frames_kernel(share, n_coded, place, counts_ref, h_ref, w_ref, v_gram_ref, w_gram_ref, own_ref, *refs):
    coded = refs[:n_coded]
    frames_ref, terms_ref, v_total_ref, proj, frames = refs[n_coded:]
    first = place[0] * share
    rank, slots = frames.shape[1:]
    pieces = [own_ref[p] for p in range(share)]
    v_gram = v_gram_ref[...]
    for code in coded:
        arrived, gram = decode(code, share, rank)
        pieces = [a + b for a, b in zip(pieces, arrived)]
        v_gram = v_gram + gram
    v_total_ref[...] = v_gram
    for p, piece in enumerate(pieces):
        proj[p] = piece
        mixed = high_dot(h_ref[...] * w_ref[pl.ds(first + p, 1), :], piece)
        mixed = jnp.where(lane_numbers((rank, slots)) < counts_ref[first + p], mixed, 0.0)
        energy = jnp.sum(jnp.sum(mixed * mixed, axis=1, keepdims=True), axis=0, keepdims=True)
        frames[p] = mixed * lax.rsqrt(energy + epsilon)

    def sweep(fine, step, carry):
        for p in range(share):
            sweep_once(frames, p, rank, fine)
        return carry

    lax.fori_loop(0, COARSE_STEPS, functools.partial(sweep, False), 0)
    lax.fori_loop(COARSE_STEPS, NS_STEPS, functools.partial(sweep, True), 0)
    terms = jnp.zeros((rank, rank), F32)
    for p in range(share):
        low = frames[p].astype(BF16)
        frames_ref[p] = low
        parts = three_parts(proj[p])
        product = low_dot(low, parts[0], ROWS_BY_ROWS)
        for part in parts[1:]:
            product = product + low_dot(low, part, ROWS_BY_ROWS)
        terms = terms + product * w_ref[pl.ds(first + p, 1), :]
    terms_ref[...] = jnp.concatenate([terms, w_gram_ref[...]], axis=1)


def own_frames(place, counts, h_start, w_start, v_gram, w_gram, own, coded):
    share, rank, slots = own.shape
    return pl.pallas_call(
        functools.partial(frames_kernel, share, len(coded)),
        in_specs=[SMEM_SPEC] * 2 + [VMEM_SPEC] * (5 + len(coded)),
        out_specs=[VMEM_SPEC] * 3,
        out_shape=[
            jax.ShapeDtypeStruct(own.shape, BF16),
            jax.ShapeDtypeStruct((rank, 2 * rank), F32),
            jax.ShapeDtypeStruct((rank, rank), F32),
        ],
        scratch_shapes=[pltpu.VMEM(own.shape, F32)] * 2,
        compiler_params=parameters(SMALL),
        cost_estimate=SHORT,
        name="own_frames",
    )(place, counts, h_start, w_start, v_gram, w_gram, own, *coded)


def projected_kernel(slot, place, frames_ref, visits_ref, *refs):
    first_ref, second_ref, token_ref, buffers, first, second, sems, out_sems = refs[-8:]
    copies = fetch(visits_ref.at[place[0] ^ slot], buffers, sems)
    rank = frames_ref.shape[1]
    token_ref[...] = jnp.zeros_like(token_ref)
    sent = []
    for p, copy in enumerate(copies):
        copy.wait()
        rows = pl.ds(p * rank, rank)
        first[rows, :], second[rows, :] = two_parts(low_dot(frames_ref[p], buffers[p]))
        for i, (source, target) in enumerate([(first, first_ref), (second, second_ref)]):
            sent.append(pltpu.make_async_copy(source.at[rows], target.at[slot, rows], out_sems.at[i, p]))
            sent[-1].start()
    for copy in sent:
        copy.wait()


def project_frames(slot, place, frames, visits, before):
    n_slots, share, slots, width = visits.shape
    rank = frames.shape[1]
    out = jax.ShapeDtypeStruct((n_slots, share * rank, width), BF16)
    *before, token = pl.pallas_call(
        functools.partial(projected_kernel, slot),
        in_specs=[SMEM_SPEC, VMEM_SPEC, ANY_SPEC] + [ANY_SPEC] * len(before),
        out_specs=[ANY_SPEC, ANY_SPEC, VMEM_SPEC],
        out_shape=[out, out, jax.ShapeDtypeStruct((8, LANES), F32)],
        scratch_shapes=[
            pltpu.VMEM(visits.shape[1:], BF16),
            pltpu.VMEM((share * rank, width), BF16),
            pltpu.VMEM((share * rank, width), BF16),
            pltpu.SemaphoreType.DMA((share,)),
            pltpu.SemaphoreType.DMA((2, share)),
        ],
        input_output_aliases={3: 0, 4: 1} if before else {},
        compiler_params=parameters(STREAM),
        cost_estimate=SHORT,
        name="project_frames",
    )(place, frames, visits, *before)
    return before, token


def next_h_kernel(n_terms, n_slots, place, *refs):
    inverse_ref, w_ref, _, h_ref, factor_ref = refs[n_terms:]
    h_next = high_dot(total(refs[:n_terms]), inverse_ref[...])
    h_ref[...] = h_next
    rank = h_next.shape[0]
    patients = w_ref.shape[0]
    share = patients // n_slots
    h_rows = h_next.T
    w_rows = jnp.concatenate([w_ref[...], jnp.zeros((LANES - patients, rank), F32)], axis=0)
    w_columns = w_rows.T
    for slot in range(n_slots):
        first = (place[0] ^ slot) * share
        columns = pltpu.roll(w_columns, jnp.where(first == 0, 0, LANES - first), 1)
        factor = jnp.concatenate([h_rows * columns[:, p : p + 1] for p in range(share)], axis=1)
        factor_ref[slot] = jnp.concatenate(three_parts(factor), axis=0)


def next_h(place, terms, inverse, w_start, n_slots, after):
    patients, rank = w_start.shape
    share = patients // n_slots
    return pl.pallas_call(
        functools.partial(next_h_kernel, len(terms), n_slots),
        in_specs=[SMEM_SPEC] + [VMEM_SPEC] * (len(terms) + 2) + [ANY_SPEC],
        out_specs=[VMEM_SPEC] * 2,
        out_shape=[
            jax.ShapeDtypeStruct(inverse.shape, F32),
            jax.ShapeDtypeStruct((n_slots, 3 * rank, share * rank), BF16),
        ],
        compiler_params=parameters(SMALL),
        cost_estimate=SHORT,
        name="next_h",
    )(place, *terms, inverse, w_start, after)


def second_inverse_kernel(h_ref, w_gram_ref, gram_ref, inverse_ref):
    gram = high_dot(h_ref[...], h_ref[...], COLS_BY_COLS)
    gram_ref[...] = gram
    inverse_ref[...] = inverse_of(gram * w_gram_ref[...])


def second_inverse(h_next, w_gram):
    out = jax.ShapeDtypeStruct(w_gram.shape, F32)
    return pl.pallas_call(
        second_inverse_kernel,
        out_shape=[out, out],
        compiler_params=parameters(SMALL),
        cost_estimate=SHORT,
        name="second_inverse",
    )(h_next, w_gram)


def v_terms_kernel(core, factor_ref, first_ref, second_ref, keep_ref, send_ref, terms_ref, first, second, sems):
    firsts = fetch(first_ref, first, sems.at[0])
    seconds = fetch(second_ref, second, sems.at[1])
    rank, width = terms_ref.shape
    half = width // 2
    for slot, copies in enumerate(zip(firsts, seconds)):
        for copy in copies:
            copy.wait()
        large = low_dot(factor_ref[slot], first[slot])
        small = low_dot(factor_ref[slot, : 2 * rank], second[slot])
        terms = large[:rank] + (large[rank : 2 * rank] + small[:rank]) + (large[2 * rank :] + small[rank:])
        terms_ref[...] = terms + terms_ref[...] if slot else terms
    keep_ref[...] = terms_ref[:, pl.ds(pl.multiple_of(core[0] * half, half), half)]
    send_ref[...] = terms_ref[:, pl.ds(pl.multiple_of((1 - core[0]) * half, half), half)]


def projected_buffers(projected):
    return [pltpu.VMEM(projected.shape, BF16)] * 2 + [pltpu.SemaphoreType.DMA((2, projected.shape[0]))]


def all_v_terms(core, factor, first, second):
    n_slots, rows, width = first.shape
    rank = factor.shape[1] // 3
    half = (rank, width // 2)
    return pl.pallas_call(
        v_terms_kernel,
        in_specs=[SMEM_SPEC, VMEM_SPEC, ANY_SPEC, ANY_SPEC],
        out_specs=[VMEM_SPEC] * 2,
        out_shape=[jax.ShapeDtypeStruct(half, F32)] * 2,
        scratch_shapes=[pltpu.VMEM((rank, width), F32)] + projected_buffers(first),
        compiler_params=parameters(STREAM),
        cost_estimate=SHORT,
        name="v_terms",
    )(core, factor, first, second)


def next_v_kernel(share, place, core, own_ref, other_ref, inverse_ref, h_ref, first_ref, second_ref, v_ref, sums_ref, *refs):
    v_parts, first, second, sems = refs
    firsts = fetch(first_ref, first, sems.at[0])
    seconds = fetch(second_ref, second, sems.at[1])
    rank = inverse_ref.shape[0]
    upper = core[0] == 1
    left = jnp.where(upper, other_ref[...], own_ref[...])
    right = jnp.where(upper, own_ref[...], other_ref[...])
    v_rows = high_dot(inverse_ref[...], jnp.concatenate([left, right], axis=1))
    v_ref[...] = v_rows
    v_parts[...] = jnp.concatenate(two_parts(v_rows), axis=0)
    weights = jnp.concatenate([h_ref[...]] * 2, axis=1)
    gram = low_dot(v_parts[...], v_parts[...], ROWS_BY_ROWS)
    gram = gram[:rank, :rank] + (gram[:rank, rank:] + gram[rank:, :rank])
    sums_ref[...] = jnp.concatenate([jnp.zeros((rank, rank), F32), gram], axis=1)
    for slot, copies in enumerate(zip(firsts, seconds)):
        for copy in copies:
            copy.wait()
        seen = low_dot(first[slot], v_parts[...], ROWS_BY_ROWS) + low_dot(second[slot], v_parts[...], ROWS_BY_ROWS)
        start = (place[0] ^ slot) * share
        for p in range(share):
            row = jnp.sum(seen[p * rank : (p + 1) * rank] * weights, axis=0, keepdims=True)
            sums_ref[pl.ds(start + p, 1), :rank] = row[:, :rank] + row[:, rank:]


def next_v(place, core, own, other, inverse, h_next, first, second):
    n_slots, rows, width = first.shape
    rank = inverse.shape[0]
    return pl.pallas_call(
        functools.partial(next_v_kernel, rows // rank),
        in_specs=[SMEM_SPEC] * 2 + [VMEM_SPEC] * 4 + [ANY_SPEC] * 2,
        out_specs=[VMEM_SPEC] * 2,
        out_shape=[
            jax.ShapeDtypeStruct((rank, width), F32),
            jax.ShapeDtypeStruct((rank, 2 * rank), F32),
        ],
        scratch_shapes=[pltpu.VMEM((2 * rank, width), BF16)] + projected_buffers(first),
        compiler_params=parameters(STREAM),
        cost_estimate=SHORT,
        name="next_v",
    )(place, core, own, other, inverse, h_next, first, second)


def next_w_kernel(n_sums, *refs):
    gram_ref, w_ref = refs[n_sums:]
    patients, rank = w_ref.shape
    sums = total(refs[:n_sums])
    table = jnp.concatenate([sums[:, rank:] * gram_ref[...], sums.T[:rank]], axis=1)
    w_ref[...] = eliminate(table, rank).T[rank : rank + patients]


def next_w(sums, h_gram, patients):
    rank = h_gram.shape[0]
    return pl.pallas_call(
        functools.partial(next_w_kernel, len(sums)),
        out_shape=jax.ShapeDtypeStruct((patients, rank), F32),
        compiler_params=parameters(SMALL),
        cost_estimate=SHORT,
        name="next_w",
    )(*sums, h_gram)


def swap(x, axis, slot):
    pairs = [(i, i ^ slot) for i in range(lax.axis_size(axis))]
    return lax.ppermute(x, axis, pairs)


def all_terms(x, axis):
    n = lax.axis_size(axis)
    if n > 4:
        return [lax.psum(x, axis)]
    return [x] + [swap(x, axis, s) for s in range(1, n)]


def add_kernel(a_ref, b_ref, after_ref, sum_ref):
    sum_ref[...] = a_ref[...] + b_ref[...]


def add(a, b, after):
    return pl.pallas_call(
        add_kernel,
        in_specs=[VMEM_SPEC] * 2 + [ANY_SPEC],
        out_specs=VMEM_SPEC,
        out_shape=jax.ShapeDtypeStruct(a.shape, a.dtype),
        compiler_params=parameters(SMALL),
        cost_estimate=SHORT,
        name="add_terms",
    )(a, b, after)


def patient_halves(keep, send, after):
    own = keep + swap(send, "patient", 1)
    step = 2
    while step < lax.axis_size("patient"):
        own = add(own, swap(own, "patient", step), after)
        step *= 2
    return own, swap(own, "patient", 1)


def on_device(visits, visit_counts, h_start, v_start, w_start):
    n = lax.axis_size("feature")
    patients, slots, width = visits.shape
    share = patients // n
    place = lax.axis_index("feature").astype(jnp.int32).reshape(1)
    core = lax.rem(lax.axis_index("patient").astype(jnp.int32), 2).reshape(1)
    by_owner = visits.reshape(n, share, slots, width)
    v_rows = v_start.T

    coded = [swap(project_for(slot, place, by_owner, v_rows), "feature", slot) for slot in range(n - 1, 0, -1)]
    own, v_local, w_local = project_own(place, by_owner, v_rows, w_start)

    frames, h_local, v_gram = own_frames(place, visit_counts, h_start, w_start, v_local, w_local, own, coded)
    far = list(range(n - 1, 1, -1))
    all_frames = {0: frames} | {slot: swap(frames, "feature", slot) for slot in far + [1]}
    h_sums = all_terms(h_local, "patient")

    projected, token = project_frames(0, place, frames, by_owner, [])
    h_sum, w_gram = sum_h(h_sums, token)
    h_terms = all_terms(h_sum, "feature")
    projected, token = project_frames(1, place, all_frames[1], by_owner, projected)
    first = first_inverse(v_gram, w_gram, token)
    for slot in far:
        projected, token = project_frames(slot, place, all_frames[slot], by_owner, projected)
    h_next, factor = next_h(place, h_terms, first, w_start, n, token)

    keep, send = all_v_terms(core, factor, *projected)
    h_gram, second = second_inverse(h_next, w_gram)
    own_terms, other_terms = patient_halves(keep, send, second)
    v_next, sums = next_v(place, core, own_terms, other_terms, second, h_next, *projected)
    w_next = next_w(all_terms(sums, "feature"), h_gram, patients)
    return (h_next, v_next.T, w_next)


def solution(mesh):
    return jax.shard_map(
        on_device,
        mesh=mesh,
        in_specs=(
            P(("groups", "patient"), None, "feature"),
            P(("groups", "patient")),
            P(),
            P("feature", None),
            P(("groups", "patient"), None),
        ),
        out_specs=(P(None, "groups"), P("feature", "groups"), P("patient", "groups")),
        check_vma=False,
    )
```

```python
import functools

import jax
import jax.numpy as jnp
from jax import lax
from jax.experimental import pallas as pl
from jax.experimental.pallas import tpu as pltpu
from jax.sharding import PartitionSpec as P

NS_STEPS = 12
LANES = 128
LEVELS = 32000.0
COARSE_STEPS = 3
SHORT = pl.CostEstimate(flops=1000, bytes_accessed=1000, transcendentals=0)

epsilon = 1e-06
HIGH = lax.Precision.HIGHEST
F32 = jnp.float32
BF16 = jnp.bfloat16
MIB = 1024 * 1024

ROWS_BY_COLS = (((1,), (0,)), ((), ()))
ROWS_BY_ROWS = (((1,), (1,)), ((), ()))
COLS_BY_COLS = (((0,), (0,)), ((), ()))


def low_dot(a, b, dims=ROWS_BY_COLS):
    return lax.dot_general(a, b, dims, preferred_element_type=F32)


def high_dot(a, b, dims=ROWS_BY_COLS):
    return lax.dot_general(a, b, dims, precision=HIGH, preferred_element_type=F32)


def two_parts(x):
    first = x.astype(BF16)
    return first, (x - first.astype(F32)).astype(BF16)


def three_parts(x):
    first = x.astype(BF16)
    rest = x - first.astype(F32)
    second = rest.astype(BF16)
    return first, second, (rest - second.astype(F32)).astype(BF16)


def lane_numbers(shape):
    return lax.broadcasted_iota(jnp.int32, shape, len(shape) - 1)


ANY_SPEC = pl.BlockSpec(memory_space=pl.ANY)


def whole(shape):
    return pl.BlockSpec(shape, lambda *place: (0,) * len(shape))


def parameters(mib):
    return pltpu.CompilerParams(vmem_limit_bytes=mib * MIB)


STREAM = 50
SMALL = 16
VMEM_SPEC = pl.BlockSpec(memory_space=pltpu.VMEM)
SMEM_SPEC = pl.BlockSpec(memory_space=pltpu.SMEM)


def exponent_rows(count):
    return -(-(count + 1) // 16) * 16


def payload_shape(count, rank, slots, with_gram):
    return (count * rank + (rank // 2 if with_gram else 0) + exponent_rows(count), slots)


def row_exponent(x):
    top = jnp.max(jnp.abs(x), axis=1, keepdims=True)
    return jnp.ceil(jnp.log2(jnp.maximum(top, 1e-30)))


def fetch(source, buffers, sems):
    copies = [pltpu.make_async_copy(source.at[p], buffers.at[p], sems.at[p]) for p in range(buffers.shape[0])]
    for copy in copies:
        copy.start()
    return copies


def decode(coded_ref, count, rank, with_gram):
    def rows(first, number):
        return coded_ref[pl.ds(first, number), :].astype(jnp.int32).astype(F32)

    gram_rows = rank // 2 if with_gram else 0
    exponents = rows(count * rank + gram_rows, exponent_rows(count))[:, :LANES].T
    steps = jnp.exp2(exponents[:rank]) * (1.0 / LEVELS)
    gram = None
    if with_gram:
        digits = rows(count * rank, gram_rows)
        digits = jnp.concatenate([digits[:, : 2 * rank], digits[:, 2 * rank :]], axis=0)
        gram = (digits[:, :rank] + digits[:, rank:] * (0.5 / LEVELS)) * steps[:, count : count + 1]
    return [rows(p * rank, rank) * steps[:, p : p + 1] for p in range(count)], gram


def send_projection_kernel(slot, first, with_gram, place, v_ref, visits_ref, coded_ref, buffers, sems):
    count, rank = buffers.shape[0], v_ref.shape[0]
    copies = fetch(visits_ref.at[place[0] ^ slot, pl.ds(first, count)], buffers, sems)
    exponents = jnp.zeros((rank, LANES), F32)
    lanes = lane_numbers(exponents.shape)
    end = count * rank
    if with_gram:
        gram = low_dot(v_ref[...], v_ref[...], ROWS_BY_ROWS)
        exponent = row_exponent(gram)
        scaled = gram * (LEVELS / jnp.exp2(exponent))
        whole = jnp.floor(scaled + 0.5)
        rest = jnp.floor((scaled - whole) * (2 * LEVELS) + 0.5)
        digits = jnp.concatenate([whole, rest], axis=1)
        digits = jnp.concatenate([digits[: rank // 2], digits[rank // 2 :]], axis=1)
        coded_ref[pl.ds(end, rank // 2), :] = digits.astype(jnp.int32).astype(jnp.int16)
        exponents = jnp.where(lanes == count, exponent, exponents)
        end += rank // 2
    for p, copy in enumerate(copies):
        copy.wait()
        proj = low_dot(v_ref[...], buffers[p], ROWS_BY_ROWS)
        exponent = row_exponent(proj)
        coded = jnp.floor(proj * (LEVELS / jnp.exp2(exponent)) + 0.5)
        coded_ref[pl.ds(p * rank, rank), :] = coded.astype(jnp.int32).astype(jnp.int16)
        exponents = jnp.where(lanes == p, exponent, exponents)
    rows = exponent_rows(count)
    last = jnp.concatenate([exponents.T[:rows], jnp.zeros((rows, coded_ref.shape[1] - rank), F32)], axis=1)
    coded_ref[pl.ds(end, rows), :] = last.astype(jnp.int32).astype(jnp.int16)


def own_projection_kernel(place, v_ref, w_ref, visits_ref, *refs):
    *proj_refs, v_gram_ref, w_gram_ref, buffers, sems = refs
    copies = fetch(visits_ref.at[place[0]], buffers, sems)
    v_gram_ref[...] = low_dot(v_ref[...], v_ref[...], ROWS_BY_ROWS)
    w_gram_ref[...] = high_dot(w_ref[...], w_ref[...], COLS_BY_COLS)
    count = len(copies) // len(proj_refs)
    for p, copy in enumerate(copies):
        copy.wait()
        proj_refs[p // count][p % count] = low_dot(v_ref[...], buffers[p], ROWS_BY_ROWS)


def project_for(slot, part, n_parts, place, visits, v_rows):
    _, share, slots, width = visits.shape
    rank = v_rows.shape[0]
    count = share // n_parts
    return pl.pallas_call(
        functools.partial(send_projection_kernel, slot, part * count, part == 0),
        in_specs=[SMEM_SPEC, VMEM_SPEC, ANY_SPEC],
        out_specs=VMEM_SPEC,
        out_shape=jax.ShapeDtypeStruct(payload_shape(count, rank, slots, part == 0), jnp.int16),
        scratch_shapes=[pltpu.VMEM((count, slots, width), BF16), pltpu.SemaphoreType.DMA((count,))],
        compiler_params=parameters(STREAM),
        cost_estimate=SHORT,
        name="project_send",
    )(place, v_rows, visits)


def project_own(n_parts, place, visits, v_rows, w_start):
    _, share, slots, width = visits.shape
    rank = v_rows.shape[0]
    gram = jax.ShapeDtypeStruct((rank, rank), F32)
    proj = jax.ShapeDtypeStruct((share // n_parts, rank, slots), F32)
    *own, v_gram, w_gram = pl.pallas_call(
        own_projection_kernel,
        in_specs=[SMEM_SPEC, VMEM_SPEC, VMEM_SPEC, ANY_SPEC],
        out_specs=[VMEM_SPEC] * (n_parts + 2),
        out_shape=[proj] * n_parts + [gram] * 2,
        scratch_shapes=[pltpu.VMEM((share, slots, width), BF16), pltpu.SemaphoreType.DMA((share,))],
        compiler_params=parameters(STREAM),
        cost_estimate=SHORT,
        name="project_own",
    )(place, v_rows, w_start, visits)
    return own, v_gram, w_gram


def pair_inverse(a, b, c, d):
    scale = 1.0 / (a * d - b * c)
    return d * scale, b * scale, c * scale, a * scale


def eliminate(table, rank):
    tiles = [table[8 * t : 8 * t + 8] for t in range(rank // 8)]
    rows = lax.broadcasted_iota(jnp.int32, tiles[0].shape, 0)
    for i in range(0, rank, 4):
        columns = [[jnp.broadcast_to(t[:, i + q : i + q + 1], t.shape) for q in range(4)] for t in tiles]
        home, first = i // 8, i % 8
        r0, r1, r2, r3 = (tiles[home][first + q : first + q + 1] for q in range(4))
        m = [[columns[home][q][first + p : first + p + 1] for q in range(4)] for p in range(4)]
        d, b, c, a = pair_inverse(m[0][0], m[0][1], m[1][0], m[1][1])
        q02, q03 = d * m[0][2] - b * m[1][2], d * m[0][3] - b * m[1][3]
        q12, q13 = a * m[1][2] - c * m[0][2], a * m[1][3] - c * m[0][3]
        y0, y1 = d * r0 - b * r1, a * r1 - c * r0
        z2 = r2 - (m[2][0] * y0 + m[2][1] * y1)
        z3 = r3 - (m[3][0] * y0 + m[3][1] * y1)
        d, b, c, a = pair_inverse(
            m[2][2] - (m[2][0] * q02 + m[2][1] * q12),
            m[2][3] - (m[2][0] * q03 + m[2][1] * q13),
            m[3][2] - (m[3][0] * q02 + m[3][1] * q12),
            m[3][3] - (m[3][0] * q03 + m[3][1] * q13),
        )
        n2, n3 = d * z2 - b * z3, a * z3 - c * z2
        new = [y0 - (q02 * n2 + q03 * n3), y1 - (q12 * n2 + q13 * n3), n2, n3]
        for t, (c0, c1, c2, c3) in enumerate(columns):
            tile = tiles[t] - ((c0 * new[0] + c1 * new[1]) + (c2 * new[2] + c3 * new[3]))
            if t == home:
                for q in range(4):
                    tile = jnp.where(rows == first + q, new[q], tile)
            tiles[t] = tile
    return jnp.concatenate(tiles, axis=0)


def inverse_of(gram):
    rank = gram.shape[0]
    eye = (lax.broadcasted_iota(jnp.int32, gram.shape, 0) == lane_numbers(gram.shape)).astype(F32)
    return eliminate(jnp.concatenate([gram, eye], axis=1), rank)[:, rank:]


def total(refs):
    out = refs[0][...]
    for ref in refs[1:]:
        out = out + ref[...]
    return out


def first_inverse_kernel(v_gram_ref, w_gram_ref, after_ref, inverse_ref):
    inverse_ref[...] = inverse_of(w_gram_ref[...] * v_gram_ref[...])


def first_inverse(v_gram, w_gram, after):
    return pl.pallas_call(
        first_inverse_kernel,
        in_specs=[VMEM_SPEC] * 2 + [ANY_SPEC],
        out_specs=VMEM_SPEC,
        out_shape=jax.ShapeDtypeStruct(w_gram.shape, F32),
        compiler_params=parameters(SMALL),
        cost_estimate=SHORT,
        name="first_inverse",
    )(v_gram, w_gram, after)


def sum_h_kernel(n_terms, *refs):
    h_ref, w_gram_ref = refs[n_terms + 1 :]
    rank = h_ref.shape[0]
    both = total(refs[:n_terms])
    h_ref[...] = both[:, :rank]
    w_gram_ref[...] = both[:, rank:]


def sum_h(terms, after):
    rank = terms[0].shape[0]
    return pl.pallas_call(
        functools.partial(sum_h_kernel, len(terms)),
        in_specs=[VMEM_SPEC] * len(terms) + [ANY_SPEC],
        out_specs=[VMEM_SPEC] * 2,
        out_shape=[jax.ShapeDtypeStruct((rank, rank), F32)] * 2,
        compiler_params=parameters(SMALL),
        cost_estimate=SHORT,
        name="sum_h",
    )(*terms, after)


def sweep_once(frames, p, rank, fine):
    frame = frames[p]
    first, second = two_parts(frame)
    if fine:
        both = low_dot(jnp.concatenate([first, second], axis=0), first, ROWS_BY_ROWS)
        gram = both[:rank] + both[rank:] + low_dot(first, second, ROWS_BY_ROWS)
        gram_first, gram_second = two_parts(gram)
        moved = low_dot(jnp.concatenate([gram_first, gram_second], axis=0), first)
        moved = moved[:rank] + moved[rank:] + low_dot(gram_first, second)
    else:
        moved = low_dot(low_dot(first, first, ROWS_BY_ROWS).astype(BF16), first)
    frames[p] = 1.5 * frame - 0.5 * moved


def frames_kernel(part, share, n_coded, place, counts_ref, h_ref, w_ref, v_gram_ref, w_gram_ref, own_ref, *refs):
    coded, earlier = refs[:n_coded], refs[n_coded:-5]
    frames_ref, terms_ref, v_total_ref, proj, frames = refs[-5:]
    count, rank, slots = frames.shape
    done = part * count
    first = place[0] * share + done
    pieces = [own_ref[p] for p in range(count)]
    v_gram = v_gram_ref[...]
    for code in coded:
        arrived, gram = decode(code, count, rank, part == 0)
        pieces = [a + b for a, b in zip(pieces, arrived)]
        if gram is not None:
            v_gram = v_gram + gram
    v_total_ref[...] = v_gram
    for p, piece in enumerate(pieces):
        proj[p] = piece
        mixed = high_dot(h_ref[...] * w_ref[pl.ds(first + p, 1), :], piece)
        mixed = jnp.where(lane_numbers((rank, slots)) < counts_ref[first + p], mixed, 0.0)
        energy = jnp.sum(jnp.sum(mixed * mixed, axis=1, keepdims=True), axis=0, keepdims=True)
        frames[p] = mixed * lax.rsqrt(energy + epsilon)

    def sweep(fine, step, carry):
        for p in range(count):
            sweep_once(frames, p, rank, fine)
        return carry

    lax.fori_loop(0, COARSE_STEPS, functools.partial(sweep, False), 0)
    lax.fori_loop(COARSE_STEPS, NS_STEPS, functools.partial(sweep, True), 0)
    terms = w_gram_ref[...]
    if earlier:
        frames_ref[:done] = earlier[0][...]
        terms = earlier[1][...]
    terms, w_gram = (terms[:, :rank], terms[:, rank:]) if earlier else (jnp.zeros_like(terms), terms)
    for p in range(count):
        low = frames[p].astype(BF16)
        frames_ref[done + p] = low
        parts = three_parts(proj[p])
        product = low_dot(low, parts[0], ROWS_BY_ROWS)
        for piece in parts[1:]:
            product = product + low_dot(low, piece, ROWS_BY_ROWS)
        terms = terms + product * w_ref[pl.ds(first + p, 1), :]
    terms_ref[...] = jnp.concatenate([terms, w_gram], axis=1)


def own_frames(part, n_parts, place, counts, h_start, w_start, v_gram, w_gram, own, coded, earlier):
    count, rank, slots = own.shape
    return pl.pallas_call(
        functools.partial(frames_kernel, part, count * n_parts, len(coded)),
        in_specs=[SMEM_SPEC] * 2 + [VMEM_SPEC] * (5 + len(coded) + len(earlier)),
        out_specs=[VMEM_SPEC] * 3,
        out_shape=[
            jax.ShapeDtypeStruct(((part + 1) * count, rank, slots), BF16),
            jax.ShapeDtypeStruct((rank, 2 * rank), F32),
            jax.ShapeDtypeStruct((rank, rank), F32),
        ],
        scratch_shapes=[pltpu.VMEM(own.shape, F32)] * 2,
        compiler_params=parameters(SMALL),
        cost_estimate=SHORT,
        name="own_frames",
    )(place, counts, h_start, w_start, v_gram, w_gram, own, *coded, *earlier)


def projected_kernel(slot, place, frames_ref, visits_ref, *refs):
    first_ref, second_ref, token_ref, buffers, first, second, sems, out_sems = refs[-8:]
    copies = fetch(visits_ref.at[place[0] ^ slot], buffers, sems)
    rank = frames_ref.shape[1]
    token_ref[...] = jnp.zeros_like(token_ref)
    sent = []
    for p, copy in enumerate(copies):
        copy.wait()
        rows = pl.ds(p * rank, rank)
        first[rows, :], second[rows, :] = two_parts(low_dot(frames_ref[p], buffers[p]))
        for i, (source, target) in enumerate([(first, first_ref), (second, second_ref)]):
            sent.append(pltpu.make_async_copy(source.at[rows], target.at[slot, rows], out_sems.at[i, p]))
            sent[-1].start()
    for copy in sent:
        copy.wait()


def project_frames(slot, place, frames, visits, before):
    n_slots, share, slots, width = visits.shape
    rank = frames.shape[1]
    out = jax.ShapeDtypeStruct((n_slots, share * rank, width), BF16)
    *before, token = pl.pallas_call(
        functools.partial(projected_kernel, slot),
        in_specs=[SMEM_SPEC, VMEM_SPEC, ANY_SPEC] + [ANY_SPEC] * len(before),
        out_specs=[ANY_SPEC, ANY_SPEC, VMEM_SPEC],
        out_shape=[out, out, jax.ShapeDtypeStruct((8, LANES), F32)],
        scratch_shapes=[
            pltpu.VMEM(visits.shape[1:], BF16),
            pltpu.VMEM((share * rank, width), BF16),
            pltpu.VMEM((share * rank, width), BF16),
            pltpu.SemaphoreType.DMA((share,)),
            pltpu.SemaphoreType.DMA((2, share)),
        ],
        input_output_aliases={3: 0, 4: 1} if before else {},
        compiler_params=parameters(STREAM),
        cost_estimate=SHORT,
        name="project_frames",
    )(place, frames, visits, *before)
    return before, token


def next_h_kernel(n_terms, n_slots, place, *refs):
    inverse_ref, w_ref, _, h_ref, factor_ref = refs[n_terms:]
    h_next = high_dot(total(refs[:n_terms]), inverse_ref[...])
    h_ref[...] = h_next
    rank = h_next.shape[0]
    patients = w_ref.shape[0]
    share = patients // n_slots
    h_rows = h_next.T
    w_rows = jnp.concatenate([w_ref[...], jnp.zeros((LANES - patients, rank), F32)], axis=0)
    w_columns = w_rows.T
    for slot in range(n_slots):
        first = (place[0] ^ slot) * share
        columns = pltpu.roll(w_columns, jnp.where(first == 0, 0, LANES - first), 1)
        factor = jnp.concatenate([h_rows * columns[:, p : p + 1] for p in range(share)], axis=1)
        factor_ref[slot] = jnp.concatenate(three_parts(factor), axis=0)


def next_h(place, terms, inverse, w_start, n_slots, after):
    patients, rank = w_start.shape
    share = patients // n_slots
    return pl.pallas_call(
        functools.partial(next_h_kernel, len(terms), n_slots),
        in_specs=[SMEM_SPEC] + [VMEM_SPEC] * (len(terms) + 2) + [ANY_SPEC],
        out_specs=[VMEM_SPEC] * 2,
        out_shape=[
            jax.ShapeDtypeStruct(inverse.shape, F32),
            jax.ShapeDtypeStruct((n_slots, 3 * rank, share * rank), BF16),
        ],
        compiler_params=parameters(SMALL),
        cost_estimate=SHORT,
        name="next_h",
    )(place, *terms, inverse, w_start, after)


def second_inverse_kernel(h_ref, w_gram_ref, gram_ref, inverse_ref):
    gram = high_dot(h_ref[...], h_ref[...], COLS_BY_COLS)
    gram_ref[...] = gram
    inverse_ref[...] = inverse_of(gram * w_gram_ref[...])


def second_inverse(h_next, w_gram):
    out = jax.ShapeDtypeStruct(w_gram.shape, F32)
    return pl.pallas_call(
        second_inverse_kernel,
        out_shape=[out, out],
        compiler_params=parameters(SMALL),
        cost_estimate=SHORT,
        name="second_inverse",
    )(h_next, w_gram)


def v_terms_kernel(core, factor_ref, first_ref, second_ref, keep_ref, send_ref, terms_ref, first, second, sems):
    firsts = fetch(first_ref, first, sems.at[0])
    seconds = fetch(second_ref, second, sems.at[1])
    rank, width = terms_ref.shape
    half = width // 2
    for slot, copies in enumerate(zip(firsts, seconds)):
        for copy in copies:
            copy.wait()
        large = low_dot(factor_ref[slot], first[slot])
        small = low_dot(factor_ref[slot, : 2 * rank], second[slot])
        terms = large[:rank] + (large[rank : 2 * rank] + small[:rank]) + (large[2 * rank :] + small[rank:])
        terms_ref[...] = terms + terms_ref[...] if slot else terms
    keep_ref[...] = terms_ref[:, pl.ds(pl.multiple_of(core[0] * half, half), half)]
    send_ref[...] = terms_ref[:, pl.ds(pl.multiple_of((1 - core[0]) * half, half), half)]


def projected_buffers(projected):
    return [pltpu.VMEM(projected.shape, BF16)] * 2 + [pltpu.SemaphoreType.DMA((2, projected.shape[0]))]


def all_v_terms(core, factor, first, second):
    n_slots, rows, width = first.shape
    rank = factor.shape[1] // 3
    half = (rank, width // 2)
    return pl.pallas_call(
        v_terms_kernel,
        in_specs=[SMEM_SPEC, VMEM_SPEC, ANY_SPEC, ANY_SPEC],
        out_specs=[VMEM_SPEC] * 2,
        out_shape=[jax.ShapeDtypeStruct(half, F32)] * 2,
        scratch_shapes=[pltpu.VMEM((rank, width), F32)] + projected_buffers(first),
        compiler_params=parameters(STREAM),
        cost_estimate=SHORT,
        name="v_terms",
    )(core, factor, first, second)


def next_v_kernel(share, place, core, own_ref, other_ref, *refs):
    inverse_ref, h_ref, first_ref, second_ref, v_ref, copies_ref, v_parts, weights, sums_ref = refs
    slot = pl.program_id(0)
    rank = inverse_ref.shape[0]

    @pl.when(slot == 0)
    def _():
        upper = core[0] == 1
        left = jnp.where(upper, other_ref[...], own_ref[...])
        right = jnp.where(upper, own_ref[...], other_ref[...])
        v_rows = high_dot(inverse_ref[...], jnp.concatenate([left, right], axis=1))
        v_ref[...] = v_rows
        v_parts[...] = jnp.concatenate(two_parts(v_rows), axis=0)
        weights[...] = jnp.concatenate([h_ref[...]] * 2, axis=1)
        gram = low_dot(v_parts[...], v_parts[...], ROWS_BY_ROWS)
        gram = gram[:rank, :rank] + (gram[:rank, rank:] + gram[rank:, :rank])
        sums_ref[...] = jnp.concatenate([jnp.zeros((rank, rank), F32), gram], axis=1)

    seen = low_dot(first_ref[0], v_parts[...], ROWS_BY_ROWS) + low_dot(second_ref[0], v_parts[...], ROWS_BY_ROWS)
    first = (place[0] ^ slot) * share
    for p in range(share):
        row = jnp.sum(seen[p * rank : (p + 1) * rank] * weights[...], axis=0, keepdims=True)
        sums_ref[pl.ds(first + p, 1), :rank] = row[:, :rank] + row[:, rank:]

    @pl.when(slot == pl.num_programs(0) - 1)
    def _():
        for device in range(copies_ref.shape[0]):
            copies_ref[device] = sums_ref[...]


def next_v(place, core, own, other, inverse, h_next, first, second):
    n_slots, rows, width = first.shape
    rank = inverse.shape[0]
    return pl.pallas_call(
        functools.partial(next_v_kernel, rows // rank),
        grid_spec=pltpu.PrefetchScalarGridSpec(
            num_scalar_prefetch=2,
            grid=(n_slots,),
            in_specs=[whole(own.shape)] * 2
            + [whole((rank, rank))] * 2
            + [pl.BlockSpec((1, rows, width), lambda i, place, core: (i, 0, 0))] * 2,
            out_specs=[whole((rank, width)), whole((n_slots, rank, 2 * rank))],
            scratch_shapes=[pltpu.VMEM((2 * rank, width), BF16)] + [pltpu.VMEM((rank, 2 * rank), F32)] * 2,
        ),
        out_shape=[
            jax.ShapeDtypeStruct((rank, width), F32),
            jax.ShapeDtypeStruct((n_slots, rank, 2 * rank), F32),
        ],
        compiler_params=parameters(STREAM),
        cost_estimate=SHORT,
        name="next_v",
    )(place, core, own, other, inverse, h_next, first, second)


def next_w_kernel(sums_ref, gram_ref, w_ref):
    patients, rank = w_ref.shape
    sums = sums_ref[0]
    for device in range(1, sums_ref.shape[0]):
        sums = sums + sums_ref[device]
    table = jnp.concatenate([sums[:, rank:] * gram_ref[...], sums.T[:rank]], axis=1)
    w_ref[...] = eliminate(table, rank).T[rank : rank + patients]


def next_w(sums, h_gram, patients):
    rank = h_gram.shape[0]
    return pl.pallas_call(
        next_w_kernel,
        in_specs=[VMEM_SPEC] * 2,
        out_specs=VMEM_SPEC,
        out_shape=jax.ShapeDtypeStruct((patients, rank), F32),
        compiler_params=parameters(SMALL),
        cost_estimate=SHORT,
        name="next_w",
    )(sums, h_gram)


def swap(x, axis, slot):
    pairs = [(i, i ^ slot) for i in range(lax.axis_size(axis))]
    return lax.ppermute(x, axis, pairs)


def all_terms(x, axis):
    n = lax.axis_size(axis)
    if n > 4:
        return [lax.psum(x, axis)]
    return [x] + [swap(x, axis, s) for s in range(1, n)]


def add_kernel(a_ref, b_ref, after_ref, sum_ref):
    sum_ref[...] = a_ref[...] + b_ref[...]


def add(a, b, after):
    return pl.pallas_call(
        add_kernel,
        in_specs=[VMEM_SPEC] * 2 + [ANY_SPEC],
        out_specs=VMEM_SPEC,
        out_shape=jax.ShapeDtypeStruct(a.shape, a.dtype),
        compiler_params=parameters(SMALL),
        cost_estimate=SHORT,
        name="add_terms",
    )(a, b, after)


def patient_halves(keep, send, after):
    own = keep + swap(send, "patient", 1)
    step = 2
    while step < lax.axis_size("patient"):
        own = add(own, swap(own, "patient", step), after)
        step *= 2
    return own, swap(own, "patient", 1)


def on_device(visits, visit_counts, h_start, v_start, w_start):
    n = lax.axis_size("feature")
    patients, slots, width = visits.shape
    share = patients // n
    place = lax.axis_index("feature").astype(jnp.int32).reshape(1)
    core = lax.rem(lax.axis_index("patient").astype(jnp.int32), 2).reshape(1)
    by_owner = visits.reshape(n, share, slots, width)
    v_rows = v_start.T

    n_parts = 2 if share % 2 == 0 else 1
    coded = [
        [swap(project_for(slot, part, n_parts, place, by_owner, v_rows), "feature", slot) for slot in range(n - 1, 0, -1)]
        for part in range(n_parts)
    ]
    own, v_gram, w_local = project_own(n_parts, place, by_owner, v_rows, w_start)
    earlier = []
    for part in range(n_parts):
        frames, h_local, v_gram = own_frames(
            part, n_parts, place, visit_counts, h_start, w_start, v_gram, w_local, own[part], coded[part], earlier
        )
        earlier = [frames, h_local]
    far = list(range(n - 1, 1, -1))
    all_frames = {0: frames} | {slot: swap(frames, "feature", slot) for slot in far + [1]}
    h_sums = all_terms(h_local, "patient")

    projected, token = project_frames(0, place, frames, by_owner, [])
    h_sum, w_gram = sum_h(h_sums, token)
    h_terms = all_terms(h_sum, "feature")
    projected, token = project_frames(1, place, all_frames[1], by_owner, projected)
    first = first_inverse(v_gram, w_gram, token)
    for slot in far:
        projected, token = project_frames(slot, place, all_frames[slot], by_owner, projected)
    h_next, factor = next_h(place, h_terms, first, w_start, n, token)

    keep, send = all_v_terms(core, factor, *projected)
    h_gram, second = second_inverse(h_next, w_gram)
    own_terms, other_terms = patient_halves(keep, send, second)
    v_next, sums = next_v(place, core, own_terms, other_terms, second, h_next, *projected)
    w_next = next_w(lax.all_to_all(sums, "feature", 0, 0), h_gram, patients)
    return (h_next, v_next.T, w_next)


def solution(mesh):
    return jax.shard_map(
        on_device,
        mesh=mesh,
        in_specs=(
            P(("groups", "patient"), None, "feature"),
            P(("groups", "patient")),
            P(),
            P("feature", None),
            P(("groups", "patient"), None),
        ),
        out_specs=(P(None, "groups"), P("feature", "groups"), P("patient", "groups")),
        check_vma=False,
    )
```

```python
import functools

import jax
import jax.numpy as jnp
from jax import lax
from jax.experimental import pallas as pl
from jax.experimental.pallas import tpu as pltpu
from jax.sharding import PartitionSpec as P

NS_STEPS = 12
LANES = 128
LEVELS = 32000.0
COARSE_STEPS = 3
SHORT = pl.CostEstimate(flops=1000, bytes_accessed=1000, transcendentals=0)

epsilon = 1e-06
HIGH = lax.Precision.HIGHEST
F32 = jnp.float32
BF16 = jnp.bfloat16
MIB = 1024 * 1024

ROWS_BY_COLS = (((1,), (0,)), ((), ()))
ROWS_BY_ROWS = (((1,), (1,)), ((), ()))
COLS_BY_COLS = (((0,), (0,)), ((), ()))


def low_dot(a, b, dims=ROWS_BY_COLS):
    return lax.dot_general(a, b, dims, preferred_element_type=F32)


def high_dot(a, b, dims=ROWS_BY_COLS):
    return lax.dot_general(a, b, dims, precision=HIGH, preferred_element_type=F32)


def two_parts(x):
    first = x.astype(BF16)
    return first, (x - first.astype(F32)).astype(BF16)


def three_parts(x):
    first = x.astype(BF16)
    rest = x - first.astype(F32)
    second = rest.astype(BF16)
    return first, second, (rest - second.astype(F32)).astype(BF16)


def lane_numbers(shape):
    return lax.broadcasted_iota(jnp.int32, shape, len(shape) - 1)


ANY_SPEC = pl.BlockSpec(memory_space=pl.ANY)
HBM_SPEC = pl.BlockSpec(memory_space=pltpu.HBM)


def parameters(mib):
    return pltpu.CompilerParams(vmem_limit_bytes=mib * MIB)


LIMIT = 16
AHEAD = 2
VMEM_SPEC = pl.BlockSpec(memory_space=pltpu.VMEM)
SMEM_SPEC = pl.BlockSpec(memory_space=pltpu.SMEM)


def exponent_rows(share):
    return -(-(share + 1) // 16) * 16


def payload_shape(share, rank, slots):
    return (share * rank + rank // 2 + exponent_rows(share), slots)


def row_exponent(x):
    top = jnp.max(jnp.abs(x), axis=1, keepdims=True)
    return jnp.ceil(jnp.log2(jnp.maximum(top, 1e-30)))


def patients_of(source, buffers, sems):
    count = buffers.shape[0]
    copies = [pltpu.make_async_copy(source.at[p], buffers.at[p], sems.at[p]) for p in range(count)]
    for copy in copies[:AHEAD]:
        copy.start()
    for p, copy in enumerate(copies):
        copy.wait()
        if p + AHEAD < count:
            copies[p + AHEAD].start()
        yield buffers[p]


def encode_rest(share, v_ref, coded_ref, exponents):
    rank = v_ref.shape[0]
    gram = low_dot(v_ref[...], v_ref[...], ROWS_BY_ROWS)
    exponent = row_exponent(gram)
    scaled = gram * (LEVELS / jnp.exp2(exponent))
    first = jnp.floor(scaled + 0.5)
    second = jnp.floor((scaled - first) * (2 * LEVELS) + 0.5)
    digits = jnp.concatenate([first, second], axis=1)
    digits = jnp.concatenate([digits[: rank // 2], digits[rank // 2 :]], axis=1)
    coded_ref[pl.ds(share * rank, rank // 2), :] = digits.astype(jnp.int32).astype(jnp.int16)
    exponents = jnp.where(lane_numbers(exponents.shape) == share, exponent, exponents)
    rows = exponent_rows(share)
    last = exponents.T[:rows]
    last = jnp.concatenate([last, jnp.zeros((rows, coded_ref.shape[1] - rank), F32)], axis=1)
    coded_ref[pl.ds(share * rank + rank // 2, rows), :] = last.astype(jnp.int32).astype(jnp.int16)


def decode(coded_ref, share, rank):
    def rows(first, count):
        return coded_ref[pl.ds(first, count), :].astype(jnp.int32).astype(F32)

    exponents = rows(share * rank + rank // 2, exponent_rows(share))[:, :LANES].T
    steps = jnp.exp2(exponents[:rank]) * (1.0 / LEVELS)
    digits = rows(share * rank, rank // 2)
    digits = jnp.concatenate([digits[:, : 2 * rank], digits[:, 2 * rank :]], axis=0)
    gram = (digits[:, :rank] + digits[:, rank:] * (0.5 / LEVELS)) * steps[:, share : share + 1]
    return [rows(p * rank, rank) * steps[:, p : p + 1] for p in range(share)], gram


def send_projection_kernel(slot, place, v_hbm, visits_ref, coded_ref, v_ref, buffers, sems, v_sem):
    v_copy = pltpu.make_async_copy(v_hbm, v_ref, v_sem)
    v_copy.start()
    share, rank = buffers.shape[0], v_ref.shape[0]
    exponents = jnp.zeros((rank, LANES), F32)
    for p, visits in enumerate(patients_of(visits_ref.at[place[0] ^ slot], buffers, sems)):
        if p == 0:
            v_copy.wait()
        proj = low_dot(v_ref[...], visits, ROWS_BY_ROWS)
        exponent = row_exponent(proj)
        coded = jnp.floor(proj * (LEVELS / jnp.exp2(exponent)) + 0.5)
        coded_ref[pl.ds(p * rank, rank), :] = coded.astype(jnp.int32).astype(jnp.int16)
        exponents = jnp.where(lane_numbers(exponents.shape) == p, exponent, exponents)
    encode_rest(share, v_ref, coded_ref, exponents)


def own_projection_kernel(place, v_hbm, w_ref, visits_ref, proj_ref, v_gram_ref, w_gram_ref, v_ref, buffers, sems, v_sem):
    v_copy = pltpu.make_async_copy(v_hbm, v_ref, v_sem)
    v_copy.start()
    for p, visits in enumerate(patients_of(visits_ref.at[place[0]], buffers, sems)):
        if p == 0:
            v_copy.wait()
        proj_ref[p] = low_dot(v_ref[...], visits, ROWS_BY_ROWS)
    v_gram_ref[...] = low_dot(v_ref[...], v_ref[...], ROWS_BY_ROWS)
    w_gram_ref[...] = high_dot(w_ref[...], w_ref[...], COLS_BY_COLS)


def projection_buffers(visits, v_rows):
    return [
        pltpu.VMEM(v_rows.shape, BF16),
        pltpu.VMEM(visits.shape[1:], BF16),
        pltpu.SemaphoreType.DMA((visits.shape[1],)),
        pltpu.SemaphoreType.DMA,
    ]


def project_for(slot, place, visits, v_rows):
    _, share, slots, width = visits.shape
    rank = v_rows.shape[0]
    return pl.pallas_call(
        functools.partial(send_projection_kernel, slot),
        in_specs=[SMEM_SPEC, HBM_SPEC, HBM_SPEC],
        out_specs=VMEM_SPEC,
        out_shape=jax.ShapeDtypeStruct(payload_shape(share, rank, slots), jnp.int16),
        scratch_shapes=projection_buffers(visits, v_rows),
        compiler_params=parameters(LIMIT),
        cost_estimate=SHORT,
        name="project_send",
    )(place, v_rows, visits)


def project_own(place, visits, v_rows, w_start):
    _, share, slots, width = visits.shape
    rank = v_rows.shape[0]
    gram = (rank, rank)
    return pl.pallas_call(
        own_projection_kernel,
        in_specs=[SMEM_SPEC, HBM_SPEC, VMEM_SPEC, HBM_SPEC],
        out_specs=[VMEM_SPEC] * 3,
        out_shape=[
            jax.ShapeDtypeStruct((share, rank, slots), F32),
            jax.ShapeDtypeStruct(gram, F32),
            jax.ShapeDtypeStruct(gram, F32),
        ],
        scratch_shapes=projection_buffers(visits, v_rows),
        compiler_params=parameters(LIMIT),
        cost_estimate=SHORT,
        name="project_own",
    )(place, v_rows, w_start, visits)


def pair_inverse(a, b, c, d):
    scale = 1.0 / (a * d - b * c)
    return d * scale, b * scale, c * scale, a * scale


def eliminate(table, rank):
    tiles = [table[8 * t : 8 * t + 8] for t in range(rank // 8)]
    rows = lax.broadcasted_iota(jnp.int32, tiles[0].shape, 0)
    for i in range(0, rank, 4):
        columns = [[jnp.broadcast_to(t[:, i + q : i + q + 1], t.shape) for q in range(4)] for t in tiles]
        home, first = i // 8, i % 8
        r0, r1, r2, r3 = (tiles[home][first + q : first + q + 1] for q in range(4))
        m = [[columns[home][q][first + p : first + p + 1] for q in range(4)] for p in range(4)]
        d, b, c, a = pair_inverse(m[0][0], m[0][1], m[1][0], m[1][1])
        q02, q03 = d * m[0][2] - b * m[1][2], d * m[0][3] - b * m[1][3]
        q12, q13 = a * m[1][2] - c * m[0][2], a * m[1][3] - c * m[0][3]
        y0, y1 = d * r0 - b * r1, a * r1 - c * r0
        z2 = r2 - (m[2][0] * y0 + m[2][1] * y1)
        z3 = r3 - (m[3][0] * y0 + m[3][1] * y1)
        d, b, c, a = pair_inverse(
            m[2][2] - (m[2][0] * q02 + m[2][1] * q12),
            m[2][3] - (m[2][0] * q03 + m[2][1] * q13),
            m[3][2] - (m[3][0] * q02 + m[3][1] * q12),
            m[3][3] - (m[3][0] * q03 + m[3][1] * q13),
        )
        n2, n3 = d * z2 - b * z3, a * z3 - c * z2
        new = [y0 - (q02 * n2 + q03 * n3), y1 - (q12 * n2 + q13 * n3), n2, n3]
        for t, (c0, c1, c2, c3) in enumerate(columns):
            tile = tiles[t] - ((c0 * new[0] + c1 * new[1]) + (c2 * new[2] + c3 * new[3]))
            if t == home:
                for q in range(4):
                    tile = jnp.where(rows == first + q, new[q], tile)
            tiles[t] = tile
    return jnp.concatenate(tiles, axis=0)


def inverse_of(gram):
    rank = gram.shape[0]
    eye = (lax.broadcasted_iota(jnp.int32, gram.shape, 0) == lane_numbers(gram.shape)).astype(F32)
    return eliminate(jnp.concatenate([gram, eye], axis=1), rank)[:, rank:]


def total(refs):
    out = refs[0][...]
    for ref in refs[1:]:
        out = out + ref[...]
    return out


def first_inverse_kernel(v_gram_ref, w_gram_ref, after_ref, inverse_ref):
    inverse_ref[...] = inverse_of(w_gram_ref[...] * v_gram_ref[...])


def first_inverse(v_gram, w_gram, after):
    return pl.pallas_call(
        first_inverse_kernel,
        in_specs=[VMEM_SPEC] * 2 + [ANY_SPEC],
        out_specs=VMEM_SPEC,
        out_shape=jax.ShapeDtypeStruct(w_gram.shape, F32),
        compiler_params=parameters(LIMIT),
        cost_estimate=SHORT,
        name="first_inverse",
    )(v_gram, w_gram, after)


def sum_h_kernel(n_terms, *refs):
    h_ref, w_gram_ref = refs[n_terms + 1 :]
    rank = h_ref.shape[0]
    both = total(refs[:n_terms])
    h_ref[...] = both[:, :rank]
    w_gram_ref[...] = both[:, rank:]


def sum_h(terms, after):
    rank = terms[0].shape[0]
    return pl.pallas_call(
        functools.partial(sum_h_kernel, len(terms)),
        in_specs=[VMEM_SPEC] * len(terms) + [ANY_SPEC],
        out_specs=[VMEM_SPEC] * 2,
        out_shape=[jax.ShapeDtypeStruct((rank, rank), F32)] * 2,
        compiler_params=parameters(LIMIT),
        cost_estimate=SHORT,
        name="sum_h",
    )(*terms, after)


def sweep_once(frames, p, rank, fine):
    frame = frames[p]
    if fine:
        both = jnp.concatenate(two_parts(frame), axis=0)
        blocks = low_dot(both, both, ROWS_BY_ROWS)
        blocks = blocks[:rank] + blocks[rank:]
        gram = blocks + pltpu.roll(blocks, rank, 1)
        moved = low_dot(jnp.concatenate(two_parts(gram), axis=0), both)
        moved = moved[:rank] + moved[rank:]
    else:
        first = frame.astype(BF16)
        moved = low_dot(low_dot(first, first, ROWS_BY_ROWS).astype(BF16), first)
    frames[p] = 1.5 * frame - 0.5 * moved


def frames_kernel(share, n_coded, place, counts_ref, h_ref, w_ref, v_gram_ref, w_gram_ref, own_ref, *refs):
    coded = refs[:n_coded]
    frames_ref, terms_ref, v_total_ref, proj, frames = refs[n_coded:]
    first = place[0] * share
    rank, slots = frames.shape[1:]
    pieces = [own_ref[p] for p in range(share)]
    v_gram = v_gram_ref[...]
    for code in coded:
        arrived, gram = decode(code, share, rank)
        pieces = [a + b for a, b in zip(pieces, arrived)]
        v_gram = v_gram + gram
    v_total_ref[...] = v_gram
    for p, piece in enumerate(pieces):
        proj[p] = piece
        mixed = high_dot(h_ref[...] * w_ref[pl.ds(first + p, 1), :], piece)
        mixed = jnp.where(lane_numbers((rank, slots)) < counts_ref[first + p], mixed, 0.0)
        energy = jnp.sum(jnp.sum(mixed * mixed, axis=1, keepdims=True), axis=0, keepdims=True)
        frames[p] = mixed * lax.rsqrt(energy + epsilon)

    def sweep(fine, step, carry):
        for p in range(share):
            sweep_once(frames, p, rank, fine)
        return carry

    lax.fori_loop(0, COARSE_STEPS, functools.partial(sweep, False), 0)
    lax.fori_loop(COARSE_STEPS, NS_STEPS, functools.partial(sweep, True), 0)
    terms = jnp.zeros((rank, rank), F32)
    for p in range(share):
        low = frames[p].astype(BF16)
        frames_ref[p] = low
        parts = three_parts(proj[p])
        product = low_dot(low, parts[0], ROWS_BY_ROWS)
        for part in parts[1:]:
            product = product + low_dot(low, part, ROWS_BY_ROWS)
        terms = terms + product * w_ref[pl.ds(first + p, 1), :]
    terms_ref[...] = jnp.concatenate([terms, w_gram_ref[...]], axis=1)


def own_frames(place, counts, h_start, w_start, v_gram, w_gram, own, coded):
    share, rank, slots = own.shape
    return pl.pallas_call(
        functools.partial(frames_kernel, share, len(coded)),
        in_specs=[SMEM_SPEC] * 2 + [VMEM_SPEC] * (5 + len(coded)),
        out_specs=[VMEM_SPEC] * 3,
        out_shape=[
            jax.ShapeDtypeStruct(own.shape, BF16),
            jax.ShapeDtypeStruct((rank, 2 * rank), F32),
            jax.ShapeDtypeStruct((rank, rank), F32),
        ],
        scratch_shapes=[pltpu.VMEM(own.shape, F32)] * 2,
        compiler_params=parameters(LIMIT),
        cost_estimate=SHORT,
        name="own_frames",
    )(place, counts, h_start, w_start, v_gram, w_gram, own, *coded)


def projected_kernel(slot, place, frames_ref, visits_ref, first_ref, second_ref, token_ref):
    owner = place[0] ^ slot
    share, rank, _ = frames_ref.shape
    token_ref[...] = jnp.zeros_like(token_ref)
    for p in range(share):
        rows = pl.ds(p * rank, rank)
        first_ref[rows, :], second_ref[rows, :] = two_parts(low_dot(frames_ref[p], visits_ref[owner, p]))


def project_frames(slot, place, frames, visits):
    _, share, slots, width = visits.shape
    rank = frames.shape[1]
    out = jax.ShapeDtypeStruct((share * rank, width), BF16)
    *parts, token = pl.pallas_call(
        functools.partial(projected_kernel, slot),
        in_specs=[SMEM_SPEC, VMEM_SPEC, VMEM_SPEC],
        out_specs=[VMEM_SPEC] * 3,
        out_shape=[out, out, jax.ShapeDtypeStruct((8, LANES), F32)],
        compiler_params=parameters(LIMIT),
        cost_estimate=SHORT,
        name="project_frames",
    )(place, frames, visits)
    return parts, token


def next_h_kernel(n_terms, n_slots, place, *refs):
    inverse_ref, w_ref, _, h_ref, factor_ref = refs[n_terms:]
    h_next = high_dot(total(refs[:n_terms]), inverse_ref[...])
    h_ref[...] = h_next
    rank = h_next.shape[0]
    patients = w_ref.shape[0]
    share = patients // n_slots
    h_rows = h_next.T
    w_rows = jnp.concatenate([w_ref[...], jnp.zeros((LANES - patients, rank), F32)], axis=0)
    w_columns = w_rows.T
    for slot in range(n_slots):
        first = (place[0] ^ slot) * share
        columns = pltpu.roll(w_columns, jnp.where(first == 0, 0, LANES - first), 1)
        factor = jnp.concatenate([h_rows * columns[:, p : p + 1] for p in range(share)], axis=1)
        factor_ref[slot] = jnp.concatenate(three_parts(factor), axis=0)


def next_h(place, terms, inverse, w_start, n_slots, after):
    patients, rank = w_start.shape
    share = patients // n_slots
    return pl.pallas_call(
        functools.partial(next_h_kernel, len(terms), n_slots),
        in_specs=[SMEM_SPEC] + [VMEM_SPEC] * (len(terms) + 2) + [ANY_SPEC],
        out_specs=[VMEM_SPEC] * 2,
        out_shape=[
            jax.ShapeDtypeStruct(inverse.shape, F32),
            jax.ShapeDtypeStruct((n_slots, 3 * rank, share * rank), BF16),
        ],
        compiler_params=parameters(LIMIT),
        cost_estimate=SHORT,
        name="next_h",
    )(place, *terms, inverse, w_start, after)


def second_inverse_kernel(h_ref, w_gram_ref, gram_ref, inverse_ref):
    gram = high_dot(h_ref[...], h_ref[...], COLS_BY_COLS)
    gram_ref[...] = gram
    inverse_ref[...] = inverse_of(gram * w_gram_ref[...])


def second_inverse(h_next, w_gram):
    out = jax.ShapeDtypeStruct(w_gram.shape, F32)
    return pl.pallas_call(
        second_inverse_kernel,
        out_shape=[out, out],
        compiler_params=parameters(LIMIT),
        cost_estimate=SHORT,
        name="second_inverse",
    )(h_next, w_gram)


def v_terms_kernel(core, factor_ref, *refs):
    *parts, keep_ref, send_ref, terms_ref = refs
    rank, width = terms_ref.shape
    half = width // 2
    for slot in range(len(parts) // 2):
        large = low_dot(factor_ref[slot], parts[2 * slot][...])
        small = low_dot(factor_ref[slot, : 2 * rank], parts[2 * slot + 1][...])
        terms = large[:rank] + (large[rank : 2 * rank] + small[:rank]) + (large[2 * rank :] + small[rank:])
        terms_ref[...] = terms + terms_ref[...] if slot else terms
    keep_ref[...] = terms_ref[:, pl.ds(pl.multiple_of(core[0] * half, half), half)]
    send_ref[...] = terms_ref[:, pl.ds(pl.multiple_of((1 - core[0]) * half, half), half)]


def all_v_terms(core, factor, projected):
    width = projected[0].shape[1]
    rank = factor.shape[1] // 3
    half = (rank, width // 2)
    return pl.pallas_call(
        v_terms_kernel,
        in_specs=[SMEM_SPEC] + [VMEM_SPEC] * (1 + len(projected)),
        out_specs=[VMEM_SPEC] * 2,
        out_shape=[jax.ShapeDtypeStruct(half, F32)] * 2,
        scratch_shapes=[pltpu.VMEM((rank, width), F32)],
        compiler_params=parameters(LIMIT),
        cost_estimate=SHORT,
        name="v_terms",
    )(core, factor, *projected)


def next_v_kernel(n_parts, place, core, own_ref, other_ref, inverse_ref, h_ref, *refs):
    parts, (v_ref, sums_ref, v_parts) = refs[:n_parts], refs[n_parts:]
    rank = inverse_ref.shape[0]
    share = parts[0].shape[0] // rank
    upper = core[0] == 1
    left = jnp.where(upper, other_ref[...], own_ref[...])
    right = jnp.where(upper, own_ref[...], other_ref[...])
    v_rows = high_dot(inverse_ref[...], jnp.concatenate([left, right], axis=1))
    v_ref[...] = v_rows
    v_parts[...] = jnp.concatenate(two_parts(v_rows), axis=0)
    weights = jnp.concatenate([h_ref[...]] * 2, axis=1)
    gram = low_dot(v_parts[...], v_parts[...], ROWS_BY_ROWS)
    gram = gram[:rank, :rank] + (gram[:rank, rank:] + gram[rank:, :rank])
    sums_ref[...] = jnp.concatenate([jnp.zeros((rank, rank), F32), gram], axis=1)
    for slot in range(n_parts // 2):
        seen = low_dot(parts[2 * slot][...], v_parts[...], ROWS_BY_ROWS)
        seen = seen + low_dot(parts[2 * slot + 1][...], v_parts[...], ROWS_BY_ROWS)
        first = (place[0] ^ slot) * share
        for p in range(share):
            row = jnp.sum(seen[p * rank : (p + 1) * rank] * weights, axis=0, keepdims=True)
            sums_ref[pl.ds(first + p, 1), :rank] = row[:, :rank] + row[:, rank:]


def next_v(place, core, own, other, inverse, h_next, projected):
    width = projected[0].shape[1]
    rank = inverse.shape[0]
    return pl.pallas_call(
        functools.partial(next_v_kernel, len(projected)),
        in_specs=[SMEM_SPEC] * 2 + [VMEM_SPEC] * (4 + len(projected)),
        out_specs=[VMEM_SPEC] * 2,
        out_shape=[
            jax.ShapeDtypeStruct((rank, width), F32),
            jax.ShapeDtypeStruct((rank, 2 * rank), F32),
        ],
        scratch_shapes=[pltpu.VMEM((2 * rank, width), BF16)],
        compiler_params=parameters(LIMIT),
        cost_estimate=SHORT,
        name="next_v",
    )(place, core, own, other, inverse, h_next, *projected)


def next_w_kernel(n_sums, *refs):
    gram_ref, w_ref = refs[n_sums:]
    patients, rank = w_ref.shape
    sums = total(refs[:n_sums])
    table = jnp.concatenate([sums[:, rank:] * gram_ref[...], sums.T[:rank]], axis=1)
    w_ref[...] = eliminate(table, rank).T[rank : rank + patients]


def next_w(sums, h_gram, patients):
    rank = h_gram.shape[0]
    return pl.pallas_call(
        functools.partial(next_w_kernel, len(sums)),
        out_shape=jax.ShapeDtypeStruct((patients, rank), F32),
        compiler_params=parameters(LIMIT),
        cost_estimate=SHORT,
        name="next_w",
    )(*sums, h_gram)


def swap(x, axis, slot):
    pairs = [(i, i ^ slot) for i in range(lax.axis_size(axis))]
    return lax.ppermute(x, axis, pairs)


def all_terms(x, axis):
    n = lax.axis_size(axis)
    if n > 4:
        return [lax.psum(x, axis)]
    return [x] + [swap(x, axis, s) for s in range(1, n)]


def staged_terms(x, axis):
    n = lax.axis_size(axis)
    step = 1
    while 2 * step < n:
        x = x + swap(x, axis, step)
        step *= 2
    return [x, swap(x, axis, step)]


def add_kernel(a_ref, b_ref, after_ref, sum_ref):
    sum_ref[...] = a_ref[...] + b_ref[...]


def add(a, b, after):
    return pl.pallas_call(
        add_kernel,
        in_specs=[VMEM_SPEC] * 2 + [ANY_SPEC],
        out_specs=VMEM_SPEC,
        out_shape=jax.ShapeDtypeStruct(a.shape, a.dtype),
        compiler_params=parameters(LIMIT),
        cost_estimate=SHORT,
        name="add_terms",
    )(a, b, after)


def patient_halves(keep, send, after):
    own = keep + swap(send, "patient", 1)
    step = 2
    while step < lax.axis_size("patient"):
        own = add(own, swap(own, "patient", step), after)
        step *= 2
    return own, swap(own, "patient", 1)


def on_device(visits, visit_counts, h_start, v_start, w_start):
    n = lax.axis_size("feature")
    patients, slots, width = visits.shape
    share = patients // n
    place = lax.axis_index("feature").astype(jnp.int32).reshape(1)
    core = lax.rem(lax.axis_index("patient").astype(jnp.int32), 2).reshape(1)
    by_owner = visits.reshape(n, share, slots, width)
    in_hbm = pltpu.with_memory_space_constraint(by_owner, pltpu.HBM)
    v_rows = pltpu.with_memory_space_constraint(v_start.T, pltpu.HBM)

    coded = [swap(project_for(slot, place, in_hbm, v_rows), "feature", slot) for slot in range(n - 1, 0, -1)]
    own, v_local, w_local = project_own(place, in_hbm, v_rows, w_start)

    frames, h_local, v_gram = own_frames(place, visit_counts, h_start, w_start, v_local, w_local, own, coded)
    far = list(range(n - 1, 1, -1))
    all_frames = {0: frames} | {slot: swap(frames, "feature", slot) for slot in far + [1]}
    h_sums = all_terms(h_local, "patient")

    parts, token = project_frames(0, place, frames, by_owner)
    projected = {0: parts}
    h_sum, w_gram = sum_h(h_sums, token)
    h_terms = all_terms(h_sum, "feature")
    projected[1], token = project_frames(1, place, all_frames[1], by_owner)
    first = first_inverse(v_gram, w_gram, token)
    for slot in far:
        projected[slot], token = project_frames(slot, place, all_frames[slot], by_owner)
    h_next, factor = next_h(place, h_terms, first, w_start, n, token)

    flat = [part for slot in range(n) for part in projected[slot]]
    keep, send = all_v_terms(core, factor, flat)
    h_gram, second = second_inverse(h_next, w_gram)
    own_terms, other_terms = patient_halves(keep, send, second)
    v_next, sums = next_v(place, core, own_terms, other_terms, second, h_next, flat)
    w_next = next_w(staged_terms(sums, "feature"), h_gram, patients)
    return (h_next, v_next.T, w_next)


def solution(mesh):
    return jax.shard_map(
        on_device,
        mesh=mesh,
        in_specs=(
            P(("groups", "patient"), None, "feature"),
            P(("groups", "patient")),
            P(),
            P("feature", None),
            P(("groups", "patient"), None),
        ),
        out_specs=(P(None, "groups"), P("feature", "groups"), P("patient", "groups")),
        check_vma=False,
    )
```

```python
import functools

import jax
import jax.numpy as jnp
from jax import lax
from jax.experimental import pallas as pl
from jax.experimental.pallas import tpu as pltpu
from jax.sharding import PartitionSpec as P

NS_STEPS = 12
LANES = 128
LEVELS = 32000.0
COARSE_STEPS = 3
SHORT = pl.CostEstimate(flops=1000, bytes_accessed=1000, transcendentals=0)

epsilon = 1e-06
HIGH = lax.Precision.HIGHEST
F32 = jnp.float32
BF16 = jnp.bfloat16
MIB = 1024 * 1024

ROWS_BY_COLS = (((1,), (0,)), ((), ()))
ROWS_BY_ROWS = (((1,), (1,)), ((), ()))
COLS_BY_COLS = (((0,), (0,)), ((), ()))


def low_dot(a, b, dims=ROWS_BY_COLS):
    return lax.dot_general(a, b, dims, preferred_element_type=F32)


def high_dot(a, b, dims=ROWS_BY_COLS):
    return lax.dot_general(a, b, dims, precision=HIGH, preferred_element_type=F32)


def two_parts(x):
    first = x.astype(BF16)
    return first, (x - first.astype(F32)).astype(BF16)


def three_parts(x):
    first = x.astype(BF16)
    rest = x - first.astype(F32)
    second = rest.astype(BF16)
    return first, second, (rest - second.astype(F32)).astype(BF16)


def feature_of(place):
    return place[0] >> 1


def core_of(place):
    return place[0] & 1


def lane_numbers(shape):
    return lax.broadcasted_iota(jnp.int32, shape, len(shape) - 1)


ANY_SPEC = pl.BlockSpec(memory_space=pl.ANY)
HBM_SPEC = pl.BlockSpec(memory_space=pltpu.HBM)


def parameters(mib):
    return pltpu.CompilerParams(vmem_limit_bytes=mib * MIB)


LIMIT = 8
VMEM_SPEC = pl.BlockSpec(memory_space=pltpu.VMEM)
SMEM_SPEC = pl.BlockSpec(memory_space=pltpu.SMEM)


def exponent_rows(share):
    return -(-(share + 1) // 16) * 16


def payload_shape(share, rank, slots):
    return (share * rank + rank // 2 + exponent_rows(share), slots)


def row_exponent(x):
    top = jnp.max(jnp.abs(x), axis=1, keepdims=True)
    return jnp.ceil(jnp.log2(jnp.maximum(top, 1e-30)))


def patients_of(source, buffers, sems):
    count = buffers.shape[0]
    group = count // sems.shape[0]
    rows = [pl.ds(first, group) for first in range(0, count, group)]
    copies = [pltpu.make_async_copy(source.at[r], buffers.at[r], sems.at[i]) for i, r in enumerate(rows)]
    for copy in copies:
        copy.start()
    for p in range(count):
        if p % group == 0:
            copies[p // group].wait()
        yield buffers[p]


def encode_rest(share, v_ref, coded_ref, exponents):
    rank = v_ref.shape[0]
    gram = low_dot(v_ref[...], v_ref[...], ROWS_BY_ROWS)
    exponent = row_exponent(gram)
    scaled = gram * (LEVELS / jnp.exp2(exponent))
    first = jnp.floor(scaled + 0.5)
    second = jnp.floor((scaled - first) * (2 * LEVELS) + 0.5)
    digits = jnp.concatenate([first, second], axis=1)
    digits = jnp.concatenate([digits[: rank // 2], digits[rank // 2 :]], axis=1)
    coded_ref[pl.ds(share * rank, rank // 2), :] = digits.astype(jnp.int32).astype(jnp.int16)
    exponents = jnp.where(lane_numbers(exponents.shape) == share, exponent, exponents)
    rows = exponent_rows(share)
    last = exponents.T[:rows]
    last = jnp.concatenate([last, jnp.zeros((rows, coded_ref.shape[1] - rank), F32)], axis=1)
    coded_ref[pl.ds(share * rank + rank // 2, rows), :] = last.astype(jnp.int32).astype(jnp.int16)


def decode(coded_ref, share, rank):
    def rows(first, count):
        return coded_ref[pl.ds(first, count), :].astype(jnp.int32).astype(F32)

    exponents = rows(share * rank + rank // 2, exponent_rows(share))[:, :LANES].T
    steps = jnp.exp2(exponents[:rank]) * (1.0 / LEVELS)
    digits = rows(share * rank, rank // 2)
    digits = jnp.concatenate([digits[:, : 2 * rank], digits[:, 2 * rank :]], axis=0)
    gram = (digits[:, :rank] + digits[:, rank:] * (0.5 / LEVELS)) * steps[:, share : share + 1]
    return [rows(p * rank, rank) * steps[:, p : p + 1] for p in range(share)], gram


def send_projection_kernel(slot, place, v_hbm, visits_ref, coded_ref, v_ref, buffers, sems, v_sem):
    v_copy = pltpu.make_async_copy(v_hbm, v_ref, v_sem)
    v_copy.start()
    share, rank = buffers.shape[0], v_ref.shape[0]
    exponents = jnp.zeros((rank, LANES), F32)
    for p, visits in enumerate(patients_of(visits_ref.at[feature_of(place) ^ slot], buffers, sems)):
        if p == 0:
            v_copy.wait()
        proj = low_dot(v_ref[...], visits, ROWS_BY_ROWS)
        exponent = row_exponent(proj)
        coded = jnp.floor(proj * (LEVELS / jnp.exp2(exponent)) + 0.5)
        coded_ref[pl.ds(p * rank, rank), :] = coded.astype(jnp.int32).astype(jnp.int16)
        exponents = jnp.where(lane_numbers(exponents.shape) == p, exponent, exponents)
    encode_rest(share, v_ref, coded_ref, exponents)


def own_projection_kernel(place, v_hbm, w_ref, visits_ref, proj_ref, v_gram_ref, w_gram_ref, v_ref, buffers, sems, v_sem):
    v_copy = pltpu.make_async_copy(v_hbm, v_ref, v_sem)
    v_copy.start()
    for p, visits in enumerate(patients_of(visits_ref.at[feature_of(place)], buffers, sems)):
        if p == 0:
            v_copy.wait()
        proj_ref[p] = low_dot(v_ref[...], visits, ROWS_BY_ROWS)
    v_gram_ref[...] = low_dot(v_ref[...], v_ref[...], ROWS_BY_ROWS)
    w_gram_ref[...] = high_dot(w_ref[...], w_ref[...], COLS_BY_COLS)


def projection_buffers(visits, v_rows):
    return [
        pltpu.VMEM(v_rows.shape, BF16),
        pltpu.VMEM(visits.shape[1:], BF16),
        pltpu.SemaphoreType.DMA((2 if visits.shape[1] % 2 == 0 else 1,)),
        pltpu.SemaphoreType.DMA,
    ]


def project_for(slot, place, visits, v_rows):
    _, share, slots, width = visits.shape
    rank = v_rows.shape[0]
    return pl.pallas_call(
        functools.partial(send_projection_kernel, slot),
        in_specs=[SMEM_SPEC, HBM_SPEC, HBM_SPEC],
        out_specs=VMEM_SPEC,
        out_shape=jax.ShapeDtypeStruct(payload_shape(share, rank, slots), jnp.int16),
        scratch_shapes=projection_buffers(visits, v_rows),
        compiler_params=parameters(LIMIT),
        cost_estimate=SHORT,
        name="project_send",
    )(place, v_rows, visits)


def project_own(place, visits, v_rows, w_start):
    _, share, slots, width = visits.shape
    rank = v_rows.shape[0]
    gram = (rank, rank)
    return pl.pallas_call(
        own_projection_kernel,
        in_specs=[SMEM_SPEC, HBM_SPEC, VMEM_SPEC, HBM_SPEC],
        out_specs=[VMEM_SPEC] * 3,
        out_shape=[
            jax.ShapeDtypeStruct((share, rank, slots), F32),
            jax.ShapeDtypeStruct(gram, F32),
            jax.ShapeDtypeStruct(gram, F32),
        ],
        scratch_shapes=projection_buffers(visits, v_rows),
        compiler_params=parameters(LIMIT),
        cost_estimate=SHORT,
        name="project_own",
    )(place, v_rows, w_start, visits)


def pair_inverse(a, b, c, d):
    scale = 1.0 / (a * d - b * c)
    return d * scale, b * scale, c * scale, a * scale


def eliminate(table, rank):
    tiles = [table[8 * t : 8 * t + 8] for t in range(rank // 8)]
    rows = lax.broadcasted_iota(jnp.int32, tiles[0].shape, 0)
    for i in range(0, rank, 4):
        columns = [[jnp.broadcast_to(t[:, i + q : i + q + 1], t.shape) for q in range(4)] for t in tiles]
        home, first = i // 8, i % 8
        r0, r1, r2, r3 = (tiles[home][first + q : first + q + 1] for q in range(4))
        m = [[columns[home][q][first + p : first + p + 1] for q in range(4)] for p in range(4)]
        d, b, c, a = pair_inverse(m[0][0], m[0][1], m[1][0], m[1][1])
        q02, q03 = d * m[0][2] - b * m[1][2], d * m[0][3] - b * m[1][3]
        q12, q13 = a * m[1][2] - c * m[0][2], a * m[1][3] - c * m[0][3]
        y0, y1 = d * r0 - b * r1, a * r1 - c * r0
        z2 = r2 - (m[2][0] * y0 + m[2][1] * y1)
        z3 = r3 - (m[3][0] * y0 + m[3][1] * y1)
        d, b, c, a = pair_inverse(
            m[2][2] - (m[2][0] * q02 + m[2][1] * q12),
            m[2][3] - (m[2][0] * q03 + m[2][1] * q13),
            m[3][2] - (m[3][0] * q02 + m[3][1] * q12),
            m[3][3] - (m[3][0] * q03 + m[3][1] * q13),
        )
        n2, n3 = d * z2 - b * z3, a * z3 - c * z2
        new = [y0 - (q02 * n2 + q03 * n3), y1 - (q12 * n2 + q13 * n3), n2, n3]
        for t, (c0, c1, c2, c3) in enumerate(columns):
            tile = tiles[t] - ((c0 * new[0] + c1 * new[1]) + (c2 * new[2] + c3 * new[3]))
            if t == home:
                for q in range(4):
                    tile = jnp.where(rows == first + q, new[q], tile)
            tiles[t] = tile
    return jnp.concatenate(tiles, axis=0)


def inverse_of(gram):
    rank = gram.shape[0]
    eye = (lax.broadcasted_iota(jnp.int32, gram.shape, 0) == lane_numbers(gram.shape)).astype(F32)
    return eliminate(jnp.concatenate([gram, eye], axis=1), rank)[:, rank:]


def total(refs):
    out = refs[0][...]
    for ref in refs[1:]:
        out = out + ref[...]
    return out


def first_inverse_kernel(v_gram_ref, w_gram_ref, after_ref, inverse_ref):
    inverse_ref[...] = inverse_of(w_gram_ref[...] * v_gram_ref[...])


def first_inverse(v_gram, w_gram, after):
    return pl.pallas_call(
        first_inverse_kernel,
        in_specs=[VMEM_SPEC] * 2 + [ANY_SPEC],
        out_specs=VMEM_SPEC,
        out_shape=jax.ShapeDtypeStruct(w_gram.shape, F32),
        compiler_params=parameters(LIMIT),
        cost_estimate=SHORT,
        name="first_inverse",
    )(v_gram, w_gram, after)


def sum_h_kernel(n_terms, *refs):
    h_ref, w_gram_ref = refs[n_terms + 1 :]
    rank = h_ref.shape[0]
    both = total(refs[:n_terms])
    h_ref[...] = both[:, :rank]
    w_gram_ref[...] = both[:, rank:]


def sum_h(terms, after):
    rank = terms[0].shape[0]
    return pl.pallas_call(
        functools.partial(sum_h_kernel, len(terms)),
        in_specs=[VMEM_SPEC] * len(terms) + [ANY_SPEC],
        out_specs=[VMEM_SPEC] * 2,
        out_shape=[jax.ShapeDtypeStruct((rank, rank), F32)] * 2,
        compiler_params=parameters(LIMIT),
        cost_estimate=SHORT,
        name="sum_h",
    )(*terms, after)


def sweep_all(frames, rank, fine):
    patients = range(frames.shape[0])
    if fine:
        both = [jnp.concatenate(two_parts(frames[p]), axis=0) for p in patients]
        blocks = [low_dot(x, x, ROWS_BY_ROWS) for x in both]
        blocks = [x[:rank] + x[rank:] for x in blocks]
        grams = [x + pltpu.roll(x, rank, 1) for x in blocks]
        moved = [low_dot(jnp.concatenate(two_parts(g), axis=0), x) for g, x in zip(grams, both)]
        moved = [x[:rank] + x[rank:] for x in moved]
    else:
        first = [frames[p].astype(BF16) for p in patients]
        grams = [low_dot(x, x, ROWS_BY_ROWS).astype(BF16) for x in first]
        moved = [low_dot(g, x) for g, x in zip(grams, first)]
    for p in patients:
        frames[p] = 1.5 * frames[p] - 0.5 * moved[p]


def frames_kernel(share, n_coded, place, counts_ref, h_ref, w_ref, v_gram_ref, w_gram_ref, own_ref, *refs):
    coded = refs[:n_coded]
    frames_ref, terms_ref, v_total_ref, proj, frames = refs[n_coded:]
    first = feature_of(place) * share
    rank, slots = frames.shape[1:]
    pieces = [own_ref[p] for p in range(share)]
    v_gram = v_gram_ref[...]
    for code in coded:
        arrived, gram = decode(code, share, rank)
        pieces = [a + b for a, b in zip(pieces, arrived)]
        v_gram = v_gram + gram
    v_total_ref[...] = v_gram
    for p, piece in enumerate(pieces):
        proj[p] = piece
        mixed = high_dot(h_ref[...] * w_ref[pl.ds(first + p, 1), :], piece)
        mixed = jnp.where(lane_numbers((rank, slots)) < counts_ref[first + p], mixed, 0.0)
        energy = jnp.sum(jnp.sum(mixed * mixed, axis=1, keepdims=True), axis=0, keepdims=True)
        frames[p] = mixed * lax.rsqrt(energy + epsilon)

    def sweep(fine, step, carry):
        sweep_all(frames, rank, fine)
        return carry

    lax.fori_loop(0, COARSE_STEPS, functools.partial(sweep, False), 0)
    lax.fori_loop(COARSE_STEPS, NS_STEPS, functools.partial(sweep, True), 0)
    terms = jnp.zeros((rank, rank), F32)
    for p in range(share):
        low = frames[p].astype(BF16)
        frames_ref[p] = low
        parts = three_parts(proj[p])
        product = low_dot(low, parts[0], ROWS_BY_ROWS)
        for part in parts[1:]:
            product = product + low_dot(low, part, ROWS_BY_ROWS)
        terms = terms + product * w_ref[pl.ds(first + p, 1), :]
    terms_ref[...] = jnp.concatenate([terms, w_gram_ref[...]], axis=1)


def own_frames(place, counts, h_start, w_start, v_gram, w_gram, own, coded):
    share, rank, slots = own.shape
    return pl.pallas_call(
        functools.partial(frames_kernel, share, len(coded)),
        in_specs=[SMEM_SPEC] * 2 + [VMEM_SPEC] * (5 + len(coded)),
        out_specs=[VMEM_SPEC] * 3,
        out_shape=[
            jax.ShapeDtypeStruct(own.shape, BF16),
            jax.ShapeDtypeStruct((rank, 2 * rank), F32),
            jax.ShapeDtypeStruct((rank, rank), F32),
        ],
        scratch_shapes=[pltpu.VMEM(own.shape, F32)] * 2,
        compiler_params=parameters(LIMIT),
        cost_estimate=SHORT,
        name="own_frames",
    )(place, counts, h_start, w_start, v_gram, w_gram, own, *coded)


def projected_kernel(slot, place, frames_ref, visits_ref, first_ref, second_ref, token_ref):
    owner = feature_of(place) ^ slot
    share, rank, _ = frames_ref.shape
    token_ref[...] = jnp.zeros_like(token_ref)
    for p in range(share):
        rows = pl.ds(p * rank, rank)
        first_ref[rows, :], second_ref[rows, :] = two_parts(low_dot(frames_ref[p], visits_ref[owner, p]))


def project_frames(slot, place, frames, visits):
    _, share, slots, width = visits.shape
    rank = frames.shape[1]
    out = jax.ShapeDtypeStruct((share * rank, width), BF16)
    *parts, token = pl.pallas_call(
        functools.partial(projected_kernel, slot),
        in_specs=[SMEM_SPEC, VMEM_SPEC, VMEM_SPEC],
        out_specs=[VMEM_SPEC] * 3,
        out_shape=[out, out, jax.ShapeDtypeStruct((8, LANES), F32)],
        compiler_params=parameters(LIMIT),
        cost_estimate=SHORT,
        name="project_frames",
    )(place, frames, visits)
    return parts, token


def next_h_kernel(n_terms, n_slots, place, *refs):
    inverse_ref, w_ref, _, result_ref, h_ref, factor_ref = refs[n_terms:]
    h_next = high_dot(total(refs[:n_terms]), inverse_ref[...])
    result_ref[...] = h_next
    h_ref[...] = h_next
    rank = h_next.shape[0]
    patients = w_ref.shape[0]
    share = patients // n_slots
    h_rows = h_next.T
    w_rows = jnp.concatenate([w_ref[...], jnp.zeros((LANES - patients, rank), F32)], axis=0)
    w_columns = w_rows.T
    for slot in range(n_slots):
        first = (feature_of(place) ^ slot) * share
        columns = pltpu.roll(w_columns, jnp.where(first == 0, 0, LANES - first), 1)
        factor = jnp.concatenate([h_rows * columns[:, p : p + 1] for p in range(share)], axis=1)
        factor_ref[slot] = jnp.concatenate(three_parts(factor), axis=0)


def next_h(place, terms, inverse, w_start, n_slots, after):
    patients, rank = w_start.shape
    share = patients // n_slots
    return pl.pallas_call(
        functools.partial(next_h_kernel, len(terms), n_slots),
        in_specs=[SMEM_SPEC] + [VMEM_SPEC] * (len(terms) + 2) + [ANY_SPEC],
        out_specs=[VMEM_SPEC] * 3,
        out_shape=[
            jax.ShapeDtypeStruct(inverse.shape, F32),
            jax.ShapeDtypeStruct(inverse.shape, F32),
            jax.ShapeDtypeStruct((n_slots, 3 * rank, share * rank), BF16),
        ],
        compiler_params=parameters(LIMIT),
        cost_estimate=SHORT,
        name="next_h",
    )(place, *terms, inverse, w_start, after)


def second_inverse_kernel(h_ref, w_gram_ref, gram_ref, inverse_ref):
    gram = high_dot(h_ref[...], h_ref[...], COLS_BY_COLS)
    gram_ref[...] = gram
    inverse_ref[...] = inverse_of(gram * w_gram_ref[...])


def second_inverse(h_next, w_gram):
    out = jax.ShapeDtypeStruct(w_gram.shape, F32)
    return pl.pallas_call(
        second_inverse_kernel,
        out_shape=[out, out],
        compiler_params=parameters(LIMIT),
        cost_estimate=SHORT,
        name="second_inverse",
    )(h_next, w_gram)


def v_terms_kernel(place, factor_ref, *refs):
    *parts, keep_ref, send_ref, terms_ref = refs
    rank, width = terms_ref.shape
    half = width // 2
    for slot in range(len(parts) // 2):
        large = low_dot(factor_ref[slot], parts[2 * slot][...])
        small = low_dot(factor_ref[slot, : 2 * rank], parts[2 * slot + 1][...])
        terms = large[:rank] + (large[rank : 2 * rank] + small[:rank]) + (large[2 * rank :] + small[rank:])
        terms_ref[...] = terms + terms_ref[...] if slot else terms
    keep_ref[...] = terms_ref[:, pl.ds(pl.multiple_of(core_of(place) * half, half), half)]
    send_ref[...] = terms_ref[:, pl.ds(pl.multiple_of((1 - core_of(place)) * half, half), half)]


def all_v_terms(place, factor, projected):
    width = projected[0].shape[1]
    rank = factor.shape[1] // 3
    half = (rank, width // 2)
    return pl.pallas_call(
        v_terms_kernel,
        in_specs=[SMEM_SPEC] + [VMEM_SPEC] * (1 + len(projected)),
        out_specs=[VMEM_SPEC] * 2,
        out_shape=[jax.ShapeDtypeStruct(half, F32)] * 2,
        scratch_shapes=[pltpu.VMEM((rank, width), F32)],
        compiler_params=parameters(LIMIT),
        cost_estimate=SHORT,
        name="v_terms",
    )(place, factor, *projected)


def next_v_kernel(n_parts, place, own_ref, other_ref, inverse_ref, h_ref, *refs):
    parts, (v_ref, sums_ref, v_parts) = refs[:n_parts], refs[n_parts:]
    rank = inverse_ref.shape[0]
    share = parts[0].shape[0] // rank
    upper = core_of(place) == 1
    left = jnp.where(upper, other_ref[...], own_ref[...])
    right = jnp.where(upper, own_ref[...], other_ref[...])
    v_rows = high_dot(inverse_ref[...], jnp.concatenate([left, right], axis=1))
    v_ref[...] = v_rows
    v_parts[...] = jnp.concatenate(two_parts(v_rows), axis=0)
    weights = jnp.concatenate([h_ref[...]] * 2, axis=1)
    gram = low_dot(v_parts[...], v_parts[...], ROWS_BY_ROWS)
    gram = gram[:rank, :rank] + (gram[:rank, rank:] + gram[rank:, :rank])
    sums_ref[...] = jnp.concatenate([jnp.zeros((rank, rank), F32), gram], axis=1)
    for slot in range(n_parts // 2):
        seen = low_dot(parts[2 * slot][...], v_parts[...], ROWS_BY_ROWS)
        seen = seen + low_dot(parts[2 * slot + 1][...], v_parts[...], ROWS_BY_ROWS)
        first = (feature_of(place) ^ slot) * share
        for p in range(share):
            row = jnp.sum(seen[p * rank : (p + 1) * rank] * weights, axis=0, keepdims=True)
            sums_ref[pl.ds(first + p, 1), :rank] = row[:, :rank] + row[:, rank:]


def next_v(place, own, other, inverse, h_next, projected):
    width = projected[0].shape[1]
    rank = inverse.shape[0]
    return pl.pallas_call(
        functools.partial(next_v_kernel, len(projected)),
        in_specs=[SMEM_SPEC] + [VMEM_SPEC] * (4 + len(projected)),
        out_specs=[VMEM_SPEC] * 2,
        out_shape=[
            jax.ShapeDtypeStruct((rank, width), F32),
            jax.ShapeDtypeStruct((rank, 2 * rank), F32),
        ],
        scratch_shapes=[pltpu.VMEM((2 * rank, width), BF16)],
        compiler_params=parameters(LIMIT),
        cost_estimate=SHORT,
        name="next_v",
    )(place, own, other, inverse, h_next, *projected)


def next_w_kernel(n_sums, *refs):
    gram_ref, w_ref = refs[n_sums:]
    patients, rank = w_ref.shape
    sums = total(refs[:n_sums])
    table = jnp.concatenate([sums[:, rank:] * gram_ref[...], sums.T[:rank]], axis=1)
    w_ref[...] = eliminate(table, rank).T[rank : rank + patients]


def next_w(sums, h_gram, patients):
    rank = h_gram.shape[0]
    return pl.pallas_call(
        functools.partial(next_w_kernel, len(sums)),
        out_shape=jax.ShapeDtypeStruct((patients, rank), F32),
        compiler_params=parameters(LIMIT),
        cost_estimate=SHORT,
        name="next_w",
    )(*sums, h_gram)


def swap(x, axis, slot):
    pairs = [(i, i ^ slot) for i in range(lax.axis_size(axis))]
    return lax.ppermute(x, axis, pairs)


def all_terms(x, axis):
    n = lax.axis_size(axis)
    if n > 4:
        return [lax.psum(x, axis)]
    return [x] + [swap(x, axis, s) for s in range(1, n)]


def staged_terms(x, axis):
    n = lax.axis_size(axis)
    step = 1
    while 2 * step < n:
        x = add(x, swap(x, axis, step), [])
        step *= 2
    return [x, swap(x, axis, step)]


def add_kernel(a_ref, b_ref, *refs):
    refs[-1][...] = a_ref[...] + b_ref[...]


def add(a, b, after):
    return pl.pallas_call(
        add_kernel,
        in_specs=[VMEM_SPEC] * 2 + [ANY_SPEC] * len(after),
        out_specs=VMEM_SPEC,
        out_shape=jax.ShapeDtypeStruct(a.shape, a.dtype),
        compiler_params=parameters(LIMIT),
        cost_estimate=SHORT,
        name="add_terms",
    )(a, b, *after)


def patient_halves(keep, send, after):
    own = add(keep, swap(send, "patient", 1), [])
    step = 2
    while step < lax.axis_size("patient"):
        own = add(own, swap(own, "patient", step), [after])
        step *= 2
    return own, swap(own, "patient", 1)


def on_device(visits, visit_counts, h_start, v_start, w_start):
    n = lax.axis_size("feature")
    patients, slots, width = visits.shape
    share = patients // n
    place = (2 * lax.axis_index("feature") + (lax.axis_index("patient") & 1)).astype(jnp.int32).reshape(1)
    by_owner = visits.reshape(n, share, slots, width)
    in_hbm = pltpu.with_memory_space_constraint(by_owner, pltpu.HBM)
    v_rows = pltpu.with_memory_space_constraint(v_start.T, pltpu.HBM)

    coded = [swap(project_for(slot, place, in_hbm, v_rows), "feature", slot) for slot in range(n - 1, 0, -1)]
    own, v_local, w_local = project_own(place, in_hbm, v_rows, w_start)

    frames, h_local, v_gram = own_frames(place, visit_counts, h_start, w_start, v_local, w_local, own, coded)
    far = list(range(n - 1, 1, -1))
    all_frames = {0: frames} | {slot: swap(frames, "feature", slot) for slot in far + [1]}
    h_sums = all_terms(h_local, "patient")

    parts, token = project_frames(0, place, frames, by_owner)
    projected = {0: parts}
    h_sum, w_gram = sum_h(h_sums, token)
    h_terms = all_terms(h_sum, "feature")
    projected[1], token = project_frames(1, place, all_frames[1], by_owner)
    first = first_inverse(v_gram, w_gram, token)
    for slot in far:
        projected[slot], token = project_frames(slot, place, all_frames[slot], by_owner)
    h_result, h_next, factor = next_h(place, h_terms, first, w_start, n, token)

    flat = [part for slot in range(n) for part in projected[slot]]
    keep, send = all_v_terms(place, factor, flat)
    h_gram, second = second_inverse(h_next, w_gram)
    own_terms, other_terms = patient_halves(keep, send, second)
    v_next, sums = next_v(place, own_terms, other_terms, second, h_next, flat)
    w_next = next_w(staged_terms(sums, "feature"), h_gram, patients)
    return (h_result, v_next.T, w_next)


def solution(mesh):
    return jax.shard_map(
        on_device,
        mesh=mesh,
        in_specs=(
            P(("groups", "patient"), None, "feature"),
            P(("groups", "patient")),
            P(),
            P("feature", None),
            P(("groups", "patient"), None),
        ),
        out_specs=(P(None, "groups"), P("feature", "groups"), P("patient", "groups")),
        check_vma=False,
    )
```

```python
import functools

import jax
import jax.numpy as jnp
from jax import lax
from jax.experimental import pallas as pl
from jax.experimental.pallas import tpu as pltpu
from jax.sharding import PartitionSpec as P

NS_STEPS = 12
LANES = 128
LEVELS = 32000.0
COARSE_STEPS = 3
SHORT = pl.CostEstimate(flops=1000, bytes_accessed=1000, transcendentals=0)

epsilon = 1e-06
HIGH = lax.Precision.HIGHEST
F32 = jnp.float32
BF16 = jnp.bfloat16
MIB = 1024 * 1024

ROWS_BY_COLS = (((1,), (0,)), ((), ()))
ROWS_BY_ROWS = (((1,), (1,)), ((), ()))
COLS_BY_COLS = (((0,), (0,)), ((), ()))


def low_dot(a, b, dims=ROWS_BY_COLS):
    return lax.dot_general(a, b, dims, preferred_element_type=F32)


def high_dot(a, b, dims=ROWS_BY_COLS):
    return lax.dot_general(a, b, dims, precision=HIGH, preferred_element_type=F32)


def two_parts(x):
    first = x.astype(BF16)
    return first, (x - first.astype(F32)).astype(BF16)


def three_parts(x):
    first = x.astype(BF16)
    rest = x - first.astype(F32)
    second = rest.astype(BF16)
    return first, second, (rest - second.astype(F32)).astype(BF16)


def feature_of(place):
    return place[0] >> 1


def core_of(place):
    return place[0] & 1


def lane_numbers(shape):
    return lax.broadcasted_iota(jnp.int32, shape, len(shape) - 1)


ANY_SPEC = pl.BlockSpec(memory_space=pl.ANY)
HBM_SPEC = pl.BlockSpec(memory_space=pltpu.HBM)


def parameters(mib):
    return pltpu.CompilerParams(vmem_limit_bytes=mib * MIB)


LIMIT = 8
VMEM_SPEC = pl.BlockSpec(memory_space=pltpu.VMEM)
SMEM_SPEC = pl.BlockSpec(memory_space=pltpu.SMEM)


def exponent_rows(count):
    return -(-(count + 1) // 16) * 16


def payload_shape(count, rank, slots, with_gram):
    return (count * rank + (rank // 2 if with_gram else 0) + exponent_rows(count), slots)


def row_exponent(x):
    top = jnp.max(jnp.abs(x), axis=1, keepdims=True)
    return jnp.ceil(jnp.log2(jnp.maximum(top, 1e-30)))


def patients_of(source, buffers, sems):
    count = buffers.shape[0]
    group = count // sems.shape[0]
    rows = [pl.ds(first, group) for first in range(0, count, group)]
    copies = [pltpu.make_async_copy(source.at[r], buffers.at[r], sems.at[i]) for i, r in enumerate(rows)]
    for copy in copies:
        copy.start()
    for p in range(count):
        if p % group == 0:
            copies[p // group].wait()
        yield buffers[p]


def decode(coded_ref, count, rank, with_gram):
    def rows(first, number):
        return coded_ref[pl.ds(first, number), :].astype(jnp.int32).astype(F32)

    gram_rows = rank // 2 if with_gram else 0
    exponents = rows(count * rank + gram_rows, exponent_rows(count))[:, :LANES].T
    steps = jnp.exp2(exponents[:rank]) * (1.0 / LEVELS)
    gram = None
    if with_gram:
        digits = rows(count * rank, gram_rows)
        digits = jnp.concatenate([digits[:, : 2 * rank], digits[:, 2 * rank :]], axis=0)
        gram = (digits[:, :rank] + digits[:, rank:] * (0.5 / LEVELS)) * steps[:, count : count + 1]
    return [rows(p * rank, rank) * steps[:, p : p + 1] for p in range(count)], gram


def encode_gram(v_ref, coded_ref, first_row):
    rank = v_ref.shape[0]
    gram = low_dot(v_ref[...], v_ref[...], ROWS_BY_ROWS)
    exponent = row_exponent(gram)
    scaled = gram * (LEVELS / jnp.exp2(exponent))
    whole = jnp.floor(scaled + 0.5)
    rest = jnp.floor((scaled - whole) * (2 * LEVELS) + 0.5)
    digits = jnp.concatenate([whole, rest], axis=1)
    digits = jnp.concatenate([digits[: rank // 2], digits[rank // 2 :]], axis=1)
    coded_ref[pl.ds(first_row, rank // 2), :] = digits.astype(jnp.int32).astype(jnp.int16)
    return exponent


def send_projection_kernel(slot, place, v_hbm, visits_ref, *refs):
    *coded_refs, v_ref, buffers, sems, v_sem = refs
    v_copy = pltpu.make_async_copy(v_hbm, v_ref, v_sem)
    v_copy.start()
    rank = v_ref.shape[0]
    count = buffers.shape[0] // len(coded_refs)
    lanes = lane_numbers((rank, LANES))
    exponents = [jnp.zeros((rank, LANES), F32) for _ in coded_refs]
    for p, visits in enumerate(patients_of(visits_ref.at[feature_of(place) ^ slot], buffers, sems)):
        part, i = divmod(p, count)
        if p == 0:
            v_copy.wait()
        proj = low_dot(v_ref[...], visits, ROWS_BY_ROWS)
        exponent = row_exponent(proj)
        coded = jnp.floor(proj * (LEVELS / jnp.exp2(exponent)) + 0.5)
        coded_refs[part][pl.ds(i * rank, rank), :] = coded.astype(jnp.int32).astype(jnp.int16)
        exponents[part] = jnp.where(lanes == i, exponent, exponents[part])
    for part, coded_ref in enumerate(coded_refs):
        end = count * rank
        if part == 0:
            exponents[0] = jnp.where(lanes == count, encode_gram(v_ref, coded_ref, end), exponents[0])
            end += rank // 2
        rows = exponent_rows(count)
        last = exponents[part].T[:rows]
        last = jnp.concatenate([last, jnp.zeros((rows, coded_ref.shape[1] - rank), F32)], axis=1)
        coded_ref[pl.ds(end, rows), :] = last.astype(jnp.int32).astype(jnp.int16)


def own_projection_kernel(place, v_hbm, w_ref, visits_ref, *refs):
    *proj_refs, v_gram_ref, w_gram_ref, v_ref, buffers, sems, v_sem = refs
    v_copy = pltpu.make_async_copy(v_hbm, v_ref, v_sem)
    v_copy.start()
    count = buffers.shape[0] // len(proj_refs)
    for p, visits in enumerate(patients_of(visits_ref.at[feature_of(place)], buffers, sems)):
        if p == 0:
            v_copy.wait()
        proj_refs[p // count][p % count] = low_dot(v_ref[...], visits, ROWS_BY_ROWS)
    v_gram_ref[...] = low_dot(v_ref[...], v_ref[...], ROWS_BY_ROWS)
    w_gram = high_dot(w_ref[...], w_ref[...], COLS_BY_COLS)
    w_gram_ref[...] = jnp.concatenate([jnp.zeros_like(w_gram), w_gram], axis=1)


def projection_buffers(visits, v_rows):
    return [
        pltpu.VMEM(v_rows.shape, BF16),
        pltpu.VMEM(visits.shape[1:], BF16),
        pltpu.SemaphoreType.DMA((2 if visits.shape[1] % 2 == 0 else 1,)),
        pltpu.SemaphoreType.DMA,
    ]


def project_for(slot, n_parts, place, visits, v_rows):
    _, share, slots, width = visits.shape
    rank = v_rows.shape[0]
    shapes = [payload_shape(share // n_parts, rank, slots, part == 0) for part in range(n_parts)]
    return pl.pallas_call(
        functools.partial(send_projection_kernel, slot),
        in_specs=[SMEM_SPEC, HBM_SPEC, HBM_SPEC],
        out_specs=[VMEM_SPEC] * n_parts,
        out_shape=[jax.ShapeDtypeStruct(shape, jnp.int16) for shape in shapes],
        scratch_shapes=projection_buffers(visits, v_rows),
        compiler_params=parameters(LIMIT),
        cost_estimate=SHORT,
        name="project_send",
    )(place, v_rows, visits)


def project_own(n_parts, place, visits, v_rows, w_start):
    _, share, slots, width = visits.shape
    rank = v_rows.shape[0]
    gram = jax.ShapeDtypeStruct((rank, rank), F32)
    proj = jax.ShapeDtypeStruct((share // n_parts, rank, slots), F32)
    *own, v_gram, w_gram = pl.pallas_call(
        own_projection_kernel,
        in_specs=[SMEM_SPEC, HBM_SPEC, VMEM_SPEC, HBM_SPEC],
        out_specs=[VMEM_SPEC] * (n_parts + 2),
        out_shape=[proj] * n_parts + [gram, jax.ShapeDtypeStruct((rank, 2 * rank), F32)],
        scratch_shapes=projection_buffers(visits, v_rows),
        compiler_params=parameters(LIMIT),
        cost_estimate=SHORT,
        name="project_own",
    )(place, v_rows, w_start, visits)
    return own, v_gram, w_gram


def pair_inverse(a, b, c, d):
    scale = 1.0 / (a * d - b * c)
    return d * scale, b * scale, c * scale, a * scale


def eliminate(table, rank):
    tiles = [table[8 * t : 8 * t + 8] for t in range(rank // 8)]
    rows = lax.broadcasted_iota(jnp.int32, tiles[0].shape, 0)
    for i in range(0, rank, 4):
        columns = [[jnp.broadcast_to(t[:, i + q : i + q + 1], t.shape) for q in range(4)] for t in tiles]
        home, first = i // 8, i % 8
        r0, r1, r2, r3 = (tiles[home][first + q : first + q + 1] for q in range(4))
        m = [[columns[home][q][first + p : first + p + 1] for q in range(4)] for p in range(4)]
        d, b, c, a = pair_inverse(m[0][0], m[0][1], m[1][0], m[1][1])
        q02, q03 = d * m[0][2] - b * m[1][2], d * m[0][3] - b * m[1][3]
        q12, q13 = a * m[1][2] - c * m[0][2], a * m[1][3] - c * m[0][3]
        y0, y1 = d * r0 - b * r1, a * r1 - c * r0
        z2 = r2 - (m[2][0] * y0 + m[2][1] * y1)
        z3 = r3 - (m[3][0] * y0 + m[3][1] * y1)
        d, b, c, a = pair_inverse(
            m[2][2] - (m[2][0] * q02 + m[2][1] * q12),
            m[2][3] - (m[2][0] * q03 + m[2][1] * q13),
            m[3][2] - (m[3][0] * q02 + m[3][1] * q12),
            m[3][3] - (m[3][0] * q03 + m[3][1] * q13),
        )
        n2, n3 = d * z2 - b * z3, a * z3 - c * z2
        new = [y0 - (q02 * n2 + q03 * n3), y1 - (q12 * n2 + q13 * n3), n2, n3]
        for t, (c0, c1, c2, c3) in enumerate(columns):
            tile = tiles[t] - ((c0 * new[0] + c1 * new[1]) + (c2 * new[2] + c3 * new[3]))
            if t == home:
                for q in range(4):
                    tile = jnp.where(rows == first + q, new[q], tile)
            tiles[t] = tile
    return jnp.concatenate(tiles, axis=0)


def inverse_of(gram):
    rank = gram.shape[0]
    eye = (lax.broadcasted_iota(jnp.int32, gram.shape, 0) == lane_numbers(gram.shape)).astype(F32)
    return eliminate(jnp.concatenate([gram, eye], axis=1), rank)[:, rank:]


def total(refs):
    out = refs[0][...]
    for ref in refs[1:]:
        out = out + ref[...]
    return out


def first_inverse_kernel(v_gram_ref, w_gram_ref, after_ref, inverse_ref):
    inverse_ref[...] = inverse_of(w_gram_ref[...] * v_gram_ref[...])


def first_inverse(v_gram, w_gram, after):
    return pl.pallas_call(
        first_inverse_kernel,
        in_specs=[VMEM_SPEC] * 2 + [ANY_SPEC],
        out_specs=VMEM_SPEC,
        out_shape=jax.ShapeDtypeStruct(w_gram.shape, F32),
        compiler_params=parameters(LIMIT),
        cost_estimate=SHORT,
        name="first_inverse",
    )(v_gram, w_gram, after)


def sum_h_kernel(n_terms, *refs):
    h_ref, w_gram_ref = refs[n_terms + 1 :]
    rank = h_ref.shape[0]
    both = total(refs[:n_terms])
    h_ref[...] = both[:, :rank]
    w_gram_ref[...] = both[:, rank:]


def sum_h(terms, after):
    rank = terms[0].shape[0]
    return pl.pallas_call(
        functools.partial(sum_h_kernel, len(terms)),
        in_specs=[VMEM_SPEC] * len(terms) + [ANY_SPEC],
        out_specs=[VMEM_SPEC] * 2,
        out_shape=[jax.ShapeDtypeStruct((rank, rank), F32)] * 2,
        compiler_params=parameters(LIMIT),
        cost_estimate=SHORT,
        name="sum_h",
    )(*terms, after)


def sweep_all(frames, rank, fine):
    patients = range(frames.shape[0])
    if fine:
        both = [jnp.concatenate(two_parts(frames[p]), axis=0) for p in patients]
        blocks = [low_dot(x, x, ROWS_BY_ROWS) for x in both]
        blocks = [x[:rank] + x[rank:] for x in blocks]
        grams = [x + pltpu.roll(x, rank, 1) for x in blocks]
        moved = [low_dot(jnp.concatenate(two_parts(g), axis=0), x) for g, x in zip(grams, both)]
        moved = [x[:rank] + x[rank:] for x in moved]
    else:
        first = [frames[p].astype(BF16) for p in patients]
        grams = [low_dot(x, x, ROWS_BY_ROWS).astype(BF16) for x in first]
        moved = [low_dot(g, x) for g, x in zip(grams, first)]
    for p in patients:
        frames[p] = 1.5 * frames[p] - 0.5 * moved[p]


def frames_kernel(part, share, n_coded, place, counts_ref, h_ref, w_ref, v_gram_ref, before_ref, own_ref, *refs):
    coded = refs[:n_coded]
    frames_ref, terms_ref, v_total_ref, proj, frames = refs[n_coded:]
    count, rank, slots = frames.shape
    first = feature_of(place) * share + part * count
    pieces = [own_ref[p] for p in range(count)]
    v_gram = v_gram_ref[...]
    for code in coded:
        arrived, gram = decode(code, count, rank, part == 0)
        pieces = [a + b for a, b in zip(pieces, arrived)]
        if gram is not None:
            v_gram = v_gram + gram
    v_total_ref[...] = v_gram
    for p, piece in enumerate(pieces):
        proj[p] = piece
        mixed = high_dot(h_ref[...] * w_ref[pl.ds(first + p, 1), :], piece)
        mixed = jnp.where(lane_numbers((rank, slots)) < counts_ref[first + p], mixed, 0.0)
        energy = jnp.sum(jnp.sum(mixed * mixed, axis=1, keepdims=True), axis=0, keepdims=True)
        frames[p] = mixed * lax.rsqrt(energy + epsilon)

    def sweep(fine, step, carry):
        sweep_all(frames, rank, fine)
        return carry

    lax.fori_loop(0, COARSE_STEPS, functools.partial(sweep, False), 0)
    lax.fori_loop(COARSE_STEPS, NS_STEPS, functools.partial(sweep, True), 0)
    before = before_ref[...]
    terms = before[:, :rank]
    for p in range(count):
        low = frames[p].astype(BF16)
        frames_ref[p] = low
        parts = three_parts(proj[p])
        product = low_dot(low, parts[0], ROWS_BY_ROWS)
        for piece in parts[1:]:
            product = product + low_dot(low, piece, ROWS_BY_ROWS)
        terms = terms + product * w_ref[pl.ds(first + p, 1), :]
    terms_ref[...] = jnp.concatenate([terms, before[:, rank:]], axis=1)


def own_frames(part, n_parts, place, counts, h_start, w_start, v_gram, before, own, coded):
    count, rank, slots = own.shape
    return pl.pallas_call(
        functools.partial(frames_kernel, part, count * n_parts, len(coded)),
        in_specs=[SMEM_SPEC] * 2 + [VMEM_SPEC] * (5 + len(coded)),
        out_specs=[VMEM_SPEC] * 3,
        out_shape=[
            jax.ShapeDtypeStruct(own.shape, BF16),
            jax.ShapeDtypeStruct((rank, 2 * rank), F32),
            jax.ShapeDtypeStruct((rank, rank), F32),
        ],
        scratch_shapes=[pltpu.VMEM(own.shape, F32)] * 2,
        compiler_params=parameters(LIMIT),
        cost_estimate=SHORT,
        name="own_frames",
    )(place, counts, h_start, w_start, v_gram, before, own, *coded)


def projected_kernel(items, place, visits_ref, *refs):
    frames_refs, outs, token_ref = refs[: len(items)], refs[-2 * len(items) - 1 : -1], refs[-1]
    token_ref[...] = jnp.zeros_like(token_ref)
    for i, (slot, part) in enumerate(items):
        owner = feature_of(place) ^ slot
        count, rank, _ = frames_refs[i].shape
        for p in range(count):
            rows = pl.ds(p * rank, rank)
            product = low_dot(frames_refs[i][p], visits_ref[owner, part * count + p])
            outs[2 * i][rows, :], outs[2 * i + 1][rows, :] = two_parts(product)


def project_frames(items, place, frames, visits, after):
    width = visits.shape[-1]
    count, rank, _ = frames[0, 0].shape
    out = jax.ShapeDtypeStruct((count * rank, width), BF16)
    *parts, token = pl.pallas_call(
        functools.partial(projected_kernel, items),
        in_specs=[SMEM_SPEC] + [VMEM_SPEC] * (1 + len(items)) + [ANY_SPEC] * len(after),
        out_specs=[VMEM_SPEC] * (2 * len(items) + 1),
        out_shape=[out] * (2 * len(items)) + [jax.ShapeDtypeStruct((8, LANES), F32)],
        compiler_params=parameters(LIMIT),
        cost_estimate=SHORT,
        name="project_frames",
    )(place, visits, *[frames[item] for item in items], *after)
    return {item: parts[2 * i : 2 * i + 2] for i, item in enumerate(items)}, token


def next_h_kernel(n_terms, n_slots, place, *refs):
    inverse_ref, w_ref, _, result_ref, h_ref, factor_ref = refs[n_terms:]
    h_next = high_dot(total(refs[:n_terms]), inverse_ref[...])
    result_ref[...] = h_next
    h_ref[...] = h_next
    rank = h_next.shape[0]
    patients = w_ref.shape[0]
    share = patients // n_slots
    h_rows = h_next.T
    w_rows = jnp.concatenate([w_ref[...], jnp.zeros((LANES - patients, rank), F32)], axis=0)
    w_columns = w_rows.T
    for slot in range(n_slots):
        first = (feature_of(place) ^ slot) * share
        columns = pltpu.roll(w_columns, jnp.where(first == 0, 0, LANES - first), 1)
        factor = jnp.concatenate([h_rows * columns[:, p : p + 1] for p in range(share)], axis=1)
        factor_ref[slot] = jnp.concatenate(three_parts(factor), axis=0)


def next_h(place, terms, inverse, w_start, n_slots, after):
    patients, rank = w_start.shape
    share = patients // n_slots
    return pl.pallas_call(
        functools.partial(next_h_kernel, len(terms), n_slots),
        in_specs=[SMEM_SPEC] + [VMEM_SPEC] * (len(terms) + 2) + [ANY_SPEC],
        out_specs=[VMEM_SPEC] * 3,
        out_shape=[
            jax.ShapeDtypeStruct(inverse.shape, F32),
            jax.ShapeDtypeStruct(inverse.shape, F32),
            jax.ShapeDtypeStruct((n_slots, 3 * rank, share * rank), BF16),
        ],
        compiler_params=parameters(LIMIT),
        cost_estimate=SHORT,
        name="next_h",
    )(place, *terms, inverse, w_start, after)


def second_inverse_kernel(h_ref, w_gram_ref, gram_ref, inverse_ref):
    gram = high_dot(h_ref[...], h_ref[...], COLS_BY_COLS)
    gram_ref[...] = gram
    inverse_ref[...] = inverse_of(gram * w_gram_ref[...])


def second_inverse(h_next, w_gram):
    out = jax.ShapeDtypeStruct(w_gram.shape, F32)
    return pl.pallas_call(
        second_inverse_kernel,
        out_shape=[out, out],
        compiler_params=parameters(LIMIT),
        cost_estimate=SHORT,
        name="second_inverse",
    )(h_next, w_gram)


def v_terms_kernel(place, factor_ref, *refs):
    *parts, keep_ref, send_ref, terms_ref = refs
    rank, width = terms_ref.shape
    half = width // 2
    n_slots, _, rows = factor_ref.shape
    count = parts[0].shape[0]
    for i in range(len(parts) // 2):
        slot, first = divmod(i * count, rows)
        columns = pl.ds(first, count)
        large = low_dot(factor_ref[slot, :, columns], parts[2 * i][...])
        small = low_dot(factor_ref[slot, : 2 * rank, columns], parts[2 * i + 1][...])
        terms = large[:rank] + (large[rank : 2 * rank] + small[:rank]) + (large[2 * rank :] + small[rank:])
        terms_ref[...] = terms + terms_ref[...] if i else terms
    keep_ref[...] = terms_ref[:, pl.ds(pl.multiple_of(core_of(place) * half, half), half)]
    send_ref[...] = terms_ref[:, pl.ds(pl.multiple_of((1 - core_of(place)) * half, half), half)]


def all_v_terms(place, factor, projected):
    width = projected[0].shape[1]
    rank = factor.shape[1] // 3
    half = (rank, width // 2)
    return pl.pallas_call(
        v_terms_kernel,
        in_specs=[SMEM_SPEC] + [VMEM_SPEC] * (1 + len(projected)),
        out_specs=[VMEM_SPEC] * 2,
        out_shape=[jax.ShapeDtypeStruct(half, F32)] * 2,
        scratch_shapes=[pltpu.VMEM((rank, width), F32)],
        compiler_params=parameters(LIMIT),
        cost_estimate=SHORT,
        name="v_terms",
    )(place, factor, *projected)


def next_v_kernel(n_parts, share, place, own_ref, other_ref, inverse_ref, h_ref, *refs):
    parts, (v_ref, sums_ref, v_parts) = refs[:n_parts], refs[n_parts:]
    rank = inverse_ref.shape[0]
    count = parts[0].shape[0] // rank
    upper = core_of(place) == 1
    left = jnp.where(upper, other_ref[...], own_ref[...])
    right = jnp.where(upper, own_ref[...], other_ref[...])
    v_rows = high_dot(inverse_ref[...], jnp.concatenate([left, right], axis=1))
    v_ref[...] = v_rows
    v_parts[...] = jnp.concatenate(two_parts(v_rows), axis=0)
    weights = jnp.concatenate([h_ref[...]] * 2, axis=1)
    gram = low_dot(v_parts[...], v_parts[...], ROWS_BY_ROWS)
    gram = gram[:rank, :rank] + (gram[:rank, rank:] + gram[rank:, :rank])
    sums_ref[...] = jnp.concatenate([jnp.zeros((rank, rank), F32), gram], axis=1)
    for i in range(n_parts // 2):
        seen = low_dot(parts[2 * i][...], v_parts[...], ROWS_BY_ROWS)
        seen = seen + low_dot(parts[2 * i + 1][...], v_parts[...], ROWS_BY_ROWS)
        slot, done = divmod(i * count, share)
        first = (feature_of(place) ^ slot) * share + done
        for p in range(count):
            row = jnp.sum(seen[p * rank : (p + 1) * rank] * weights, axis=0, keepdims=True)
            sums_ref[pl.ds(first + p, 1), :rank] = row[:, :rank] + row[:, rank:]


def next_v(share, place, own, other, inverse, h_next, projected):
    width = projected[0].shape[1]
    rank = inverse.shape[0]
    return pl.pallas_call(
        functools.partial(next_v_kernel, len(projected), share),
        in_specs=[SMEM_SPEC] + [VMEM_SPEC] * (4 + len(projected)),
        out_specs=[VMEM_SPEC] * 2,
        out_shape=[
            jax.ShapeDtypeStruct((rank, width), F32),
            jax.ShapeDtypeStruct((rank, 2 * rank), F32),
        ],
        scratch_shapes=[pltpu.VMEM((2 * rank, width), BF16)],
        compiler_params=parameters(LIMIT),
        cost_estimate=SHORT,
        name="next_v",
    )(place, own, other, inverse, h_next, *projected)


def next_w_kernel(n_sums, *refs):
    gram_ref, w_ref = refs[n_sums:]
    patients, rank = w_ref.shape
    sums = total(refs[:n_sums])
    table = jnp.concatenate([sums[:, rank:] * gram_ref[...], sums.T[:rank]], axis=1)
    w_ref[...] = eliminate(table, rank).T[rank : rank + patients]


def next_w(sums, h_gram, patients):
    rank = h_gram.shape[0]
    return pl.pallas_call(
        functools.partial(next_w_kernel, len(sums)),
        out_shape=jax.ShapeDtypeStruct((patients, rank), F32),
        compiler_params=parameters(LIMIT),
        cost_estimate=SHORT,
        name="next_w",
    )(*sums, h_gram)


def swap(x, axis, slot):
    pairs = [(i, i ^ slot) for i in range(lax.axis_size(axis))]
    return lax.ppermute(x, axis, pairs)


def all_terms(x, axis):
    n = lax.axis_size(axis)
    if n > 4:
        return [lax.psum(x, axis)]
    return [x] + [swap(x, axis, s) for s in range(1, n)]


def staged_terms(x, axis, after):
    n = lax.axis_size(axis)
    step = 1
    while 2 * step < n:
        x = add(x, swap(x, axis, step), after)
        step *= 2
    return [x, swap(x, axis, step)]


def add_kernel(a_ref, b_ref, *refs):
    refs[-1][...] = a_ref[...] + b_ref[...]


def add(a, b, after):
    return pl.pallas_call(
        add_kernel,
        in_specs=[VMEM_SPEC] * 2 + [ANY_SPEC] * len(after),
        out_specs=VMEM_SPEC,
        out_shape=jax.ShapeDtypeStruct(a.shape, a.dtype),
        compiler_params=parameters(LIMIT),
        cost_estimate=SHORT,
        name="add_terms",
    )(a, b, *after)


def patient_halves(keep, send, after):
    own = add(keep, swap(send, "patient", 1), [])
    step = 2
    while step < lax.axis_size("patient"):
        own = add(own, swap(own, "patient", step), [after])
        step *= 2
    return own, swap(own, "patient", 1)


def on_device(visits, visit_counts, h_start, v_start, w_start):
    n = lax.axis_size("feature")
    patients, slots, width = visits.shape
    share = patients // n
    place = (2 * lax.axis_index("feature") + (lax.axis_index("patient") & 1)).astype(jnp.int32).reshape(1)
    by_owner = visits.reshape(n, share, slots, width)
    in_hbm = pltpu.with_memory_space_constraint(by_owner, pltpu.HBM)
    v_rows = pltpu.with_memory_space_constraint(v_start.T, pltpu.HBM)

    n_parts = 2 if share % 2 == 0 else 1
    halves = range(n_parts)
    far = list(range(n - 1, 1, -1))
    sent = {slot: project_for(slot, n_parts, place, in_hbm, v_rows) for slot in far + [1]}
    coded = [[swap(sent[slot][part], "feature", slot) for slot in far + [1]] for part in halves]
    own, v_gram, h_local = project_own(n_parts, place, in_hbm, v_rows, w_start)
    frames = {}
    for part in halves:
        frames[0, part], h_local, v_gram = own_frames(
            part, n_parts, place, visit_counts, h_start, w_start, v_gram, h_local, own[part], coded[part]
        )
        for slot in far + [1]:
            frames[slot, part] = swap(frames[0, part], "feature", slot)

    projected, token = project_frames([(0, part) for part in halves], place, frames, by_owner, [])
    for part in halves[:-1]:
        more, token = project_frames([(slot, part) for slot in [1] + far], place, frames, by_owner, [token])
        projected |= more
    h_sum, w_gram = sum_h(staged_terms(h_local, "patient", [token]), token)
    h_terms = all_terms(h_sum, "feature")
    last = halves[-1]
    after = h_sum
    for slot in [1] + far:
        more, token = project_frames([(slot, last)], place, frames, by_owner, [after])
        projected |= more
        if slot == 1:
            first = first_inverse(v_gram, w_gram, token)
        after = token
    h_result, h_next, factor = next_h(place, h_terms, first, w_start, n, token)

    flat = [x for slot in range(n) for part in halves for x in projected[slot, part]]
    keep, send = all_v_terms(place, factor, flat)
    h_gram, second = second_inverse(h_next, w_gram)
    own_terms, other_terms = patient_halves(keep, send, second)
    v_next, sums = next_v(share, place, own_terms, other_terms, second, h_next, flat)
    w_next = next_w(all_terms(sums, "feature"), h_gram, patients)
    return (h_result, v_next.T, w_next)


def solution(mesh):
    return jax.shard_map(
        on_device,
        mesh=mesh,
        in_specs=(
            P(("groups", "patient"), None, "feature"),
            P(("groups", "patient")),
            P(),
            P("feature", None),
            P(("groups", "patient"), None),
        ),
        out_specs=(P(None, "groups"), P("feature", "groups"), P("patient", "groups")),
        check_vma=False,
    )
```

```python
import functools

import jax
import jax.numpy as jnp
from jax import lax
from jax.experimental import pallas as pl
from jax.experimental.pallas import tpu as pltpu
from jax.sharding import PartitionSpec as P

NS_STEPS = 12
LANES = 128
LEVELS = 32000.0
COARSE_STEPS = 3
SHORT = pl.CostEstimate(flops=1000, bytes_accessed=1000, transcendentals=0)

epsilon = 1e-06
HIGH = lax.Precision.HIGHEST
F32 = jnp.float32
BF16 = jnp.bfloat16
MIB = 1024 * 1024

ROWS_BY_COLS = (((1,), (0,)), ((), ()))
ROWS_BY_ROWS = (((1,), (1,)), ((), ()))
COLS_BY_COLS = (((0,), (0,)), ((), ()))


def low_dot(a, b, dims=ROWS_BY_COLS):
    return lax.dot_general(a, b, dims, preferred_element_type=F32)


def high_dot(a, b, dims=ROWS_BY_COLS):
    return lax.dot_general(a, b, dims, precision=HIGH, preferred_element_type=F32)


def two_parts(x):
    first = x.astype(BF16)
    return first, (x - first.astype(F32)).astype(BF16)


def three_parts(x):
    first = x.astype(BF16)
    rest = x - first.astype(F32)
    second = rest.astype(BF16)
    return first, second, (rest - second.astype(F32)).astype(BF16)


def feature_of(place):
    return place[0] >> 1


def core_of(place):
    return place[0] & 1


def lane_numbers(shape):
    return lax.broadcasted_iota(jnp.int32, shape, len(shape) - 1)


ANY_SPEC = pl.BlockSpec(memory_space=pl.ANY)
HBM_SPEC = pl.BlockSpec(memory_space=pltpu.HBM)


def parameters(mib):
    return pltpu.CompilerParams(vmem_limit_bytes=mib * MIB)


LIMIT = 8
VMEM_SPEC = pl.BlockSpec(memory_space=pltpu.VMEM)
SMEM_SPEC = pl.BlockSpec(memory_space=pltpu.SMEM)


def exponent_rows(count):
    return -(-(count + 1) // 16) * 16


def payload_shape(count, rank, slots, with_gram):
    return (count * rank + (rank // 2 if with_gram else 0) + exponent_rows(count), slots)


def row_exponent(x):
    top = jnp.max(jnp.abs(x), axis=1, keepdims=True)
    return jnp.ceil(jnp.log2(jnp.maximum(top, 1e-30)))


def decode(coded_ref, total_count, first, count, rank, with_gram):
    def rows(start, number):
        return coded_ref[pl.ds(start, number), :].astype(jnp.int32).astype(F32)

    gram_rows = rank // 2 if with_gram else 0
    exponents = rows(total_count * rank + gram_rows, exponent_rows(total_count))[:, :LANES].T
    steps = jnp.exp2(exponents[:rank]) * (1.0 / LEVELS)
    gram = None
    if with_gram and first == 0:
        digits = rows(total_count * rank, gram_rows)
        digits = jnp.concatenate([digits[:, : 2 * rank], digits[:, 2 * rank :]], axis=0)
        gram = (digits[:, :rank] + digits[:, rank:] * (0.5 / LEVELS)) * steps[:, total_count : total_count + 1]
    return [rows(p * rank, rank) * steps[:, p : p + 1] for p in range(first, first + count)], gram


def encode_gram(v_ref, coded_ref, first_row):
    rank = v_ref.shape[0]
    gram = low_dot(v_ref[...], v_ref[...], ROWS_BY_ROWS)
    exponent = row_exponent(gram)
    scaled = gram * (LEVELS / jnp.exp2(exponent))
    whole = jnp.floor(scaled + 0.5)
    rest = jnp.floor((scaled - whole) * (2 * LEVELS) + 0.5)
    digits = jnp.concatenate([whole, rest], axis=1)
    digits = jnp.concatenate([digits[: rank // 2], digits[rank // 2 :]], axis=1)
    coded_ref[pl.ds(first_row, rank // 2), :] = digits.astype(jnp.int32).astype(jnp.int16)
    return exponent


def encode(patients, with_gram, v_ref, coded_ref):
    count, rank = len(patients), v_ref.shape[0]
    lanes = lane_numbers((rank, LANES))
    exponents = jnp.zeros((rank, LANES), F32)
    for p, visits in enumerate(patients):
        proj = low_dot(v_ref[...], visits(), ROWS_BY_ROWS)
        exponent = row_exponent(proj)
        coded = jnp.floor(proj * (LEVELS / jnp.exp2(exponent)) + 0.5)
        coded_ref[pl.ds(p * rank, rank), :] = coded.astype(jnp.int32).astype(jnp.int16)
        exponents = jnp.where(lanes == p, exponent, exponents)
    end = count * rank
    if with_gram:
        exponents = jnp.where(lanes == count, encode_gram(v_ref, coded_ref, end), exponents)
        end += rank // 2
    rows = exponent_rows(count)
    last = jnp.concatenate([exponents.T[:rows], jnp.zeros((rows, coded_ref.shape[1] - rank), F32)], axis=1)
    coded_ref[pl.ds(end, rows), :] = last.astype(jnp.int32).astype(jnp.int16)


def first_projection_kernel(slot, place, v_hbm, visits_ref, coded_ref, v_ref, buffers, sem, v_sem):
    count = buffers.shape[0]
    v_copy = pltpu.make_async_copy(v_hbm, v_ref, v_sem)
    visits_copy = pltpu.make_async_copy(visits_ref.at[feature_of(place) ^ slot, pl.ds(0, count)], buffers, sem)
    v_copy.start()
    visits_copy.start()
    v_copy.wait()
    visits_copy.wait()
    encode([lambda p=p: buffers[p] for p in range(count)], True, v_ref, coded_ref)


def first_projection(slot, count, place, visits, v_rows):
    _, share, slots, width = visits.shape
    rank = v_rows.shape[0]
    return pl.pallas_call(
        functools.partial(first_projection_kernel, slot),
        in_specs=[SMEM_SPEC, HBM_SPEC, HBM_SPEC],
        out_specs=VMEM_SPEC,
        out_shape=jax.ShapeDtypeStruct(payload_shape(count, rank, slots, True), jnp.int16),
        scratch_shapes=[
            pltpu.VMEM(v_rows.shape, BF16),
            pltpu.VMEM((count, slots, width), BF16),
            pltpu.SemaphoreType.DMA,
            pltpu.SemaphoreType.DMA,
        ],
        compiler_params=parameters(LIMIT),
        cost_estimate=SHORT,
        name="project_first",
    )(place, v_rows, visits)


def send_projection_kernel(slot, pieces, place, v_ref, visits_ref, *coded_refs):
    owner = feature_of(place) ^ slot
    for (first, count, with_gram), coded_ref in zip(pieces, coded_refs):
        patients = [lambda p=p: visits_ref[owner, p] for p in range(first, first + count)]
        encode(patients, with_gram, v_ref, coded_ref)


def project_for(slot, pieces, place, visits, v_rows):
    rank, slots = v_rows.shape[0], visits.shape[2]
    shapes = [payload_shape(count, rank, slots, with_gram) for _, count, with_gram in pieces]
    return pl.pallas_call(
        functools.partial(send_projection_kernel, slot, pieces),
        in_specs=[SMEM_SPEC, VMEM_SPEC, VMEM_SPEC],
        out_specs=[VMEM_SPEC] * len(pieces),
        out_shape=[jax.ShapeDtypeStruct(shape, jnp.int16) for shape in shapes],
        compiler_params=parameters(LIMIT),
        cost_estimate=SHORT,
        name="project_send",
    )(place, v_rows, visits)


def own_projection_kernel(place, v_ref, w_ref, visits_ref, *refs):
    *proj_refs, v_gram_ref, w_gram_ref = refs
    count = visits_ref.shape[1] // len(proj_refs)
    for p in range(visits_ref.shape[1]):
        proj_refs[p // count][p % count] = low_dot(v_ref[...], visits_ref[feature_of(place), p], ROWS_BY_ROWS)
    v_gram_ref[...] = low_dot(v_ref[...], v_ref[...], ROWS_BY_ROWS)
    w_gram = high_dot(w_ref[...], w_ref[...], COLS_BY_COLS)
    w_gram_ref[...] = jnp.concatenate([jnp.zeros_like(w_gram), w_gram], axis=1)


def project_own(n_parts, place, visits, v_rows, w_start):
    _, share, slots, width = visits.shape
    rank = v_rows.shape[0]
    gram = jax.ShapeDtypeStruct((rank, rank), F32)
    proj = jax.ShapeDtypeStruct((share // n_parts, rank, slots), F32)
    *own, v_gram, w_gram = pl.pallas_call(
        own_projection_kernel,
        in_specs=[SMEM_SPEC] + [VMEM_SPEC] * 3,
        out_specs=[VMEM_SPEC] * (n_parts + 2),
        out_shape=[proj] * n_parts + [gram, jax.ShapeDtypeStruct((rank, 2 * rank), F32)],
        compiler_params=parameters(LIMIT),
        cost_estimate=SHORT,
        name="project_own",
    )(place, v_rows, w_start, visits)
    return own, v_gram, w_gram


def pair_inverse(a, b, c, d):
    scale = 1.0 / (a * d - b * c)
    return d * scale, b * scale, c * scale, a * scale


def eliminate(table, rank):
    tiles = [table[8 * t : 8 * t + 8] for t in range(rank // 8)]
    rows = lax.broadcasted_iota(jnp.int32, tiles[0].shape, 0)
    for i in range(0, rank, 4):
        columns = [[jnp.broadcast_to(t[:, i + q : i + q + 1], t.shape) for q in range(4)] for t in tiles]
        home, first = i // 8, i % 8
        r0, r1, r2, r3 = (tiles[home][first + q : first + q + 1] for q in range(4))
        m = [[columns[home][q][first + p : first + p + 1] for q in range(4)] for p in range(4)]
        d, b, c, a = pair_inverse(m[0][0], m[0][1], m[1][0], m[1][1])
        q02, q03 = d * m[0][2] - b * m[1][2], d * m[0][3] - b * m[1][3]
        q12, q13 = a * m[1][2] - c * m[0][2], a * m[1][3] - c * m[0][3]
        y0, y1 = d * r0 - b * r1, a * r1 - c * r0
        z2 = r2 - (m[2][0] * y0 + m[2][1] * y1)
        z3 = r3 - (m[3][0] * y0 + m[3][1] * y1)
        d, b, c, a = pair_inverse(
            m[2][2] - (m[2][0] * q02 + m[2][1] * q12),
            m[2][3] - (m[2][0] * q03 + m[2][1] * q13),
            m[3][2] - (m[3][0] * q02 + m[3][1] * q12),
            m[3][3] - (m[3][0] * q03 + m[3][1] * q13),
        )
        n2, n3 = d * z2 - b * z3, a * z3 - c * z2
        new = [y0 - (q02 * n2 + q03 * n3), y1 - (q12 * n2 + q13 * n3), n2, n3]
        for t, (c0, c1, c2, c3) in enumerate(columns):
            tile = tiles[t] - ((c0 * new[0] + c1 * new[1]) + (c2 * new[2] + c3 * new[3]))
            if t == home:
                for q in range(4):
                    tile = jnp.where(rows == first + q, new[q], tile)
            tiles[t] = tile
    return jnp.concatenate(tiles, axis=0)


def inverse_of(gram):
    rank = gram.shape[0]
    eye = (lax.broadcasted_iota(jnp.int32, gram.shape, 0) == lane_numbers(gram.shape)).astype(F32)
    return eliminate(jnp.concatenate([gram, eye], axis=1), rank)[:, rank:]


def total(refs):
    out = refs[0][...]
    for ref in refs[1:]:
        out = out + ref[...]
    return out


def first_inverse_kernel(v_gram_ref, w_gram_ref, after_ref, inverse_ref):
    inverse_ref[...] = inverse_of(w_gram_ref[...] * v_gram_ref[...])


def first_inverse(v_gram, w_gram, after):
    return pl.pallas_call(
        first_inverse_kernel,
        in_specs=[VMEM_SPEC] * 2 + [ANY_SPEC],
        out_specs=VMEM_SPEC,
        out_shape=jax.ShapeDtypeStruct(w_gram.shape, F32),
        compiler_params=parameters(LIMIT),
        cost_estimate=SHORT,
        name="first_inverse",
    )(v_gram, w_gram, after)


def sum_h_kernel(n_terms, *refs):
    h_ref, w_gram_ref = refs[n_terms + 1 :]
    rank = h_ref.shape[0]
    both = total(refs[:n_terms])
    h_ref[...] = both[:, :rank]
    w_gram_ref[...] = both[:, rank:]


def sum_h(terms, after):
    rank = terms[0].shape[0]
    return pl.pallas_call(
        functools.partial(sum_h_kernel, len(terms)),
        in_specs=[VMEM_SPEC] * len(terms) + [ANY_SPEC],
        out_specs=[VMEM_SPEC] * 2,
        out_shape=[jax.ShapeDtypeStruct((rank, rank), F32)] * 2,
        compiler_params=parameters(LIMIT),
        cost_estimate=SHORT,
        name="sum_h",
    )(*terms, after)


def sweep_all(frames, rank, fine):
    patients = range(frames.shape[0])
    if fine:
        both = [jnp.concatenate(two_parts(frames[p]), axis=0) for p in patients]
        blocks = [low_dot(x, x, ROWS_BY_ROWS) for x in both]
        blocks = [x[:rank] + x[rank:] for x in blocks]
        grams = [x + pltpu.roll(x, rank, 1) for x in blocks]
        moved = [low_dot(jnp.concatenate(two_parts(g), axis=0), x) for g, x in zip(grams, both)]
        moved = [x[:rank] + x[rank:] for x in moved]
    else:
        first = [frames[p].astype(BF16) for p in patients]
        grams = [low_dot(x, x, ROWS_BY_ROWS).astype(BF16) for x in first]
        moved = [low_dot(g, x) for g, x in zip(grams, first)]
    for p in patients:
        frames[p] = 1.5 * frames[p] - 0.5 * moved[p]


def frames_kernel(layouts, part, share, place, counts_ref, h_ref, w_ref, v_gram_ref, before_ref, own_ref, *refs):
    coded, refs = refs[: len(layouts)], refs[len(layouts) :]
    frames_ref, terms_ref, v_total_ref, proj, frames = refs
    count, rank, slots = frames.shape
    patients = range(count)
    first = feature_of(place) * share + part * count
    pieces = [own_ref[p] for p in patients]
    v_gram = v_gram_ref[...]
    for code, (total_count, start, with_gram) in zip(coded, layouts):
        arrived, gram = decode(code, total_count, start, count, rank, with_gram)
        pieces = [a + b for a, b in zip(pieces, arrived)]
        if gram is not None:
            v_gram = v_gram + gram
    v_total_ref[...] = v_gram
    for p in patients:
        proj[p] = pieces[p]
    weights = [w_ref[pl.ds(first + p, 1), :] for p in patients]
    mixed = [high_dot(h_ref[...] * weights[p], pieces[p]) for p in patients]
    lanes = lane_numbers((rank, slots))
    mixed = [jnp.where(lanes < counts_ref[first + p], mixed[p], 0.0) for p in patients]
    energy = [jnp.sum(jnp.sum(x * x, axis=1, keepdims=True), axis=0, keepdims=True) for x in mixed]
    for p in patients:
        frames[p] = mixed[p] * lax.rsqrt(energy[p] + epsilon)

    def sweep(fine, step, carry):
        sweep_all(frames, rank, fine)
        return carry

    lax.fori_loop(0, COARSE_STEPS, functools.partial(sweep, False), 0, unroll=True)
    lax.fori_loop(COARSE_STEPS, NS_STEPS, functools.partial(sweep, True), 0, unroll=3)
    low = [frames[p].astype(BF16) for p in patients]
    for p in patients:
        frames_ref[p] = low[p]
    products = [jnp.concatenate(three_parts(proj[p]), axis=0) for p in patients]
    products = [low_dot(low[p], products[p], ROWS_BY_ROWS) for p in patients]
    before = before_ref[...]
    terms = before[:, :rank]
    for p in patients:
        product = products[p][:, :rank] + (products[p][:, rank : 2 * rank] + products[p][:, 2 * rank :])
        terms = terms + product * weights[p]
    terms_ref[...] = jnp.concatenate([terms, before[:, rank:]], axis=1)


def own_frames(layouts, part, n_parts, place, counts, h_start, w_start, v_gram, before, own, coded):
    count, rank, slots = own.shape
    share = count * n_parts
    return pl.pallas_call(
        functools.partial(frames_kernel, layouts, part, share),
        in_specs=[SMEM_SPEC] * 2 + [VMEM_SPEC] * (5 + len(coded)),
        out_specs=[VMEM_SPEC] * 3,
        out_shape=[
            jax.ShapeDtypeStruct(own.shape, BF16),
            jax.ShapeDtypeStruct((rank, 2 * rank), F32),
            jax.ShapeDtypeStruct((rank, rank), F32),
        ],
        scratch_shapes=[pltpu.VMEM(own.shape, F32)] * 2,
        compiler_params=parameters(LIMIT),
        cost_estimate=SHORT,
        name="own_frames",
    )(place, counts, h_start, w_start, v_gram, before, own, *coded)


def projected_kernel(items, place, visits_ref, *refs):
    frames_refs, outs, token_ref = refs[: len(items)], refs[-2 * len(items) - 1 : -1], refs[-1]
    token_ref[...] = jnp.zeros_like(token_ref)
    for i, (slot, first) in enumerate(items):
        owner = feature_of(place) ^ slot
        count, rank, _ = frames_refs[i].shape
        for p in range(count):
            rows = pl.ds(p * rank, rank)
            product = low_dot(frames_refs[i][p], visits_ref[owner, first + p])
            outs[2 * i][rows, :], outs[2 * i + 1][rows, :] = two_parts(product)


def project_frames(items, place, frames, visits, after):
    width = visits.shape[-1]
    outs = []
    for item in items:
        count, rank, _ = frames[item].shape
        outs += [jax.ShapeDtypeStruct((count * rank, width), BF16)] * 2
    *parts, token = pl.pallas_call(
        functools.partial(projected_kernel, items),
        in_specs=[SMEM_SPEC] + [VMEM_SPEC] * (1 + len(items)) + [ANY_SPEC] * len(after),
        out_specs=[VMEM_SPEC] * (len(outs) + 1),
        out_shape=outs + [jax.ShapeDtypeStruct((8, LANES), F32)],
        compiler_params=parameters(LIMIT),
        cost_estimate=SHORT,
        name="project_frames",
    )(place, visits, *[frames[item] for item in items], *after)
    return {item: parts[2 * i : 2 * i + 2] for i, item in enumerate(items)}, token


def next_h_kernel(n_terms, n_slots, place, *refs):
    inverse_ref, w_ref, _, result_ref, h_ref, factor_ref = refs[n_terms:]
    h_next = high_dot(total(refs[:n_terms]), inverse_ref[...])
    result_ref[...] = h_next
    h_ref[...] = h_next
    rank = h_next.shape[0]
    patients = w_ref.shape[0]
    share = patients // n_slots
    h_rows = h_next.T
    w_rows = jnp.concatenate([w_ref[...], jnp.zeros((LANES - patients, rank), F32)], axis=0)
    w_columns = w_rows.T
    for slot in range(n_slots):
        first = (feature_of(place) ^ slot) * share
        columns = pltpu.roll(w_columns, jnp.where(first == 0, 0, LANES - first), 1)
        factor = jnp.concatenate([h_rows * columns[:, p : p + 1] for p in range(share)], axis=1)
        factor_ref[slot] = jnp.concatenate(three_parts(factor), axis=0)


def next_h(place, terms, inverse, w_start, n_slots, after):
    patients, rank = w_start.shape
    share = patients // n_slots
    return pl.pallas_call(
        functools.partial(next_h_kernel, len(terms), n_slots),
        in_specs=[SMEM_SPEC] + [VMEM_SPEC] * (len(terms) + 2) + [ANY_SPEC],
        out_specs=[VMEM_SPEC] * 3,
        out_shape=[
            jax.ShapeDtypeStruct(inverse.shape, F32),
            jax.ShapeDtypeStruct(inverse.shape, F32),
            jax.ShapeDtypeStruct((n_slots, 3 * rank, share * rank), BF16),
        ],
        compiler_params=parameters(LIMIT),
        cost_estimate=SHORT,
        name="next_h",
    )(place, *terms, inverse, w_start, after)


def second_inverse_kernel(h_ref, w_gram_ref, gram_ref, inverse_ref):
    gram = high_dot(h_ref[...], h_ref[...], COLS_BY_COLS)
    gram_ref[...] = gram
    inverse_ref[...] = inverse_of(gram * w_gram_ref[...])


def second_inverse(h_next, w_gram):
    out = jax.ShapeDtypeStruct(w_gram.shape, F32)
    return pl.pallas_call(
        second_inverse_kernel,
        out_shape=[out, out],
        compiler_params=parameters(LIMIT),
        cost_estimate=SHORT,
        name="second_inverse",
    )(h_next, w_gram)


def v_terms_kernel(items, place, factor_ref, *refs):
    *parts, keep_ref, send_ref, terms_ref = refs
    rank, width = terms_ref.shape
    half = width // 2
    for i, (slot, first) in enumerate(items):
        columns = pl.ds(first * rank, parts[2 * i].shape[0])
        large = low_dot(factor_ref[slot, :, columns], parts[2 * i][...])
        small = low_dot(factor_ref[slot, : 2 * rank, columns], parts[2 * i + 1][...])
        terms = large[:rank] + (large[rank : 2 * rank] + small[:rank]) + (large[2 * rank :] + small[rank:])
        terms_ref[...] = terms + terms_ref[...] if i else terms
    keep_ref[...] = terms_ref[:, pl.ds(pl.multiple_of(core_of(place) * half, half), half)]
    send_ref[...] = terms_ref[:, pl.ds(pl.multiple_of((1 - core_of(place)) * half, half), half)]


def all_v_terms(items, place, factor, projected):
    width = projected[0].shape[1]
    rank = factor.shape[1] // 3
    half = (rank, width // 2)
    return pl.pallas_call(
        functools.partial(v_terms_kernel, items),
        in_specs=[SMEM_SPEC] + [VMEM_SPEC] * (1 + len(projected)),
        out_specs=[VMEM_SPEC] * 2,
        out_shape=[jax.ShapeDtypeStruct(half, F32)] * 2,
        scratch_shapes=[pltpu.VMEM((rank, width), F32)],
        compiler_params=parameters(LIMIT),
        cost_estimate=SHORT,
        name="v_terms",
    )(place, factor, *projected)


def next_v_kernel(items, share, place, own_ref, other_ref, inverse_ref, h_ref, *refs):
    *parts, v_ref, sums_ref, v_parts = refs
    rank = inverse_ref.shape[0]
    upper = core_of(place) == 1
    left = jnp.where(upper, other_ref[...], own_ref[...])
    right = jnp.where(upper, own_ref[...], other_ref[...])
    v_rows = high_dot(inverse_ref[...], jnp.concatenate([left, right], axis=1))
    v_ref[...] = v_rows
    v_parts[...] = jnp.concatenate(two_parts(v_rows), axis=0)
    weights = jnp.concatenate([h_ref[...]] * 2, axis=1)
    gram = low_dot(v_parts[...], v_parts[...], ROWS_BY_ROWS)
    gram = gram[:rank, :rank] + (gram[:rank, rank:] + gram[rank:, :rank])
    sums_ref[...] = jnp.concatenate([jnp.zeros((rank, rank), F32), gram], axis=1)
    for i, (slot, done) in enumerate(items):
        seen = low_dot(parts[2 * i][...], v_parts[...], ROWS_BY_ROWS)
        seen = seen + low_dot(parts[2 * i + 1][...], v_parts[...], ROWS_BY_ROWS)
        first = (feature_of(place) ^ slot) * share + done
        for p in range(seen.shape[0] // rank):
            row = jnp.sum(seen[p * rank : (p + 1) * rank] * weights, axis=0, keepdims=True)
            sums_ref[pl.ds(first + p, 1), :rank] = row[:, :rank] + row[:, rank:]


def next_v(items, share, place, own, other, inverse, h_next, projected):
    width = projected[0].shape[1]
    rank = inverse.shape[0]
    return pl.pallas_call(
        functools.partial(next_v_kernel, items, share),
        in_specs=[SMEM_SPEC] + [VMEM_SPEC] * (4 + len(projected)),
        out_specs=[VMEM_SPEC] * 2,
        out_shape=[
            jax.ShapeDtypeStruct((rank, width), F32),
            jax.ShapeDtypeStruct((rank, 2 * rank), F32),
        ],
        scratch_shapes=[pltpu.VMEM((2 * rank, width), BF16)],
        compiler_params=parameters(LIMIT),
        cost_estimate=SHORT,
        name="next_v",
    )(place, own, other, inverse, h_next, *projected)


def next_w_kernel(n_sums, *refs):
    gram_ref, w_ref = refs[n_sums:]
    patients, rank = w_ref.shape
    sums = total(refs[:n_sums])
    table = jnp.concatenate([sums[:, rank:] * gram_ref[...], sums.T[:rank]], axis=1)
    w_ref[...] = eliminate(table, rank).T[rank : rank + patients]


def next_w(sums, h_gram, patients):
    rank = h_gram.shape[0]
    return pl.pallas_call(
        functools.partial(next_w_kernel, len(sums)),
        out_shape=jax.ShapeDtypeStruct((patients, rank), F32),
        compiler_params=parameters(LIMIT),
        cost_estimate=SHORT,
        name="next_w",
    )(*sums, h_gram)


def swap(x, axis, slot):
    pairs = [(i, i ^ slot) for i in range(lax.axis_size(axis))]
    return lax.ppermute(x, axis, pairs)


def all_terms(x, axis):
    n = lax.axis_size(axis)
    if n > 4:
        return [lax.psum(x, axis)]
    return [x] + [swap(x, axis, s) for s in range(1, n)]


def staged_terms(x, axis, after):
    n = lax.axis_size(axis)
    step = 1
    while 2 * step < n:
        x = add(x, swap(x, axis, step), after)
        step *= 2
    return [x, swap(x, axis, step)]


def add_kernel(a_ref, b_ref, *refs):
    refs[-1][...] = a_ref[...] + b_ref[...]


def add(a, b, after):
    return pl.pallas_call(
        add_kernel,
        in_specs=[VMEM_SPEC] * 2 + [ANY_SPEC] * len(after),
        out_specs=VMEM_SPEC,
        out_shape=jax.ShapeDtypeStruct(a.shape, a.dtype),
        compiler_params=parameters(LIMIT),
        cost_estimate=SHORT,
        name="add_terms",
    )(a, b, *after)


def patient_halves(keep, send, after):
    own = add(keep, swap(send, "patient", 1), [])
    step = 2
    while step < lax.axis_size("patient"):
        own = add(own, swap(own, "patient", step), [after])
        step *= 2
    return own, swap(own, "patient", 1)


def on_device(visits, visit_counts, h_start, v_start, w_start):
    n = lax.axis_size("feature")
    patients, slots, width = visits.shape
    share = patients // n
    place = (2 * lax.axis_index("feature") + (lax.axis_index("patient") & 1)).astype(jnp.int32).reshape(1)
    by_owner = visits.reshape(n, share, slots, width)
    in_hbm = pltpu.with_memory_space_constraint(by_owner, pltpu.HBM)
    v_rows = pltpu.with_memory_space_constraint(v_start.T, pltpu.HBM)

    n_parts = 2 if share % 2 == 0 else 1
    count = share // n_parts
    firsts = [part * count for part in range(n_parts)]
    far = list(range(n - 1, 1, -1))
    v_near = v_start.T

    sent = {(far[0], 0): first_projection(far[0], count, place, in_hbm, v_rows)}
    for slot in far[1:] + [1]:
        pieces = [(first, count, first == 0) for first in firsts]
        codes = project_for(slot, pieces, place, by_owner, v_near)
        sent |= {(slot, first): code for first, code in zip(firsts, codes)}
    for first in firsts[1:]:
        sent[far[0], first] = project_for(far[0], [(first, count, False)], place, by_owner, v_near)[0]
    sent = {(slot, first): sent[slot, first] for first in firsts for slot in far + [1]}
    arrived = {item: swap(code, "feature", item[0]) for item, code in sent.items()}
    own, v_gram, h_local = project_own(n_parts, place, by_owner, v_near, w_start)

    frames = {}
    for part, first in enumerate(firsts):
        layouts = [(count, 0, first == 0)] * (n - 1)
        coded = [arrived[slot, first] for slot in far + [1]]
        frames[0, first], h_local, v_total = own_frames(
            layouts, part, n_parts, place, visit_counts, h_start, w_start, v_gram, h_local, own[part], coded
        )
        v_gram = v_total if first == 0 else v_gram
        for slot in far + [1]:
            frames[slot, first] = swap(frames[0, first], "feature", slot)

    projected, token = project_frames([(0, first) for first in firsts], place, frames, by_owner, [])
    for first in firsts[:-1]:
        more, token = project_frames([(slot, first) for slot in [1] + far], place, frames, by_owner, [token])
        projected |= more
    h_sum, w_gram = sum_h(staged_terms(h_local, "patient", [token]), token)
    h_terms = all_terms(h_sum, "feature")
    after = h_sum
    for slot in [1] + far:
        more, token = project_frames([(slot, firsts[-1])], place, frames, by_owner, [after])
        projected |= more
        if slot == 1:
            inverse = first_inverse(v_gram, w_gram, token)
        after = token
    h_result, h_next, factor = next_h(place, h_terms, inverse, w_start, n, token)

    items = list(projected)
    flat = [x for item in items for x in projected[item]]
    keep, send = all_v_terms(items, place, factor, flat)
    h_gram, second = second_inverse(h_next, w_gram)
    own_terms, other_terms = patient_halves(keep, send, second)
    v_next, sums = next_v(items, share, place, own_terms, other_terms, second, h_next, flat)
    w_next = next_w(all_terms(sums, "feature"), h_gram, patients)
    return (h_result, v_next.T, w_next)


def solution(mesh):
    return jax.shard_map(
        on_device,
        mesh=mesh,
        in_specs=(
            P(("groups", "patient"), None, "feature"),
            P(("groups", "patient")),
            P(),
            P("feature", None),
            P(("groups", "patient"), None),
        ),
        out_specs=(P(None, "groups"), P("feature", "groups"), P("patient", "groups")),
        check_vma=False,
    )
```

```python
import functools

import jax
import jax.numpy as jnp
from jax import lax
from jax.experimental import pallas as pl
from jax.experimental.pallas import tpu as pltpu
from jax.sharding import PartitionSpec as P

NS_STEPS = 12
LANES = 128
LEVELS = 32000.0
COARSE_STEPS = 3
SHORT = pl.CostEstimate(flops=1000, bytes_accessed=1000, transcendentals=0)

epsilon = 1e-06
HIGH = lax.Precision.HIGHEST
F32 = jnp.float32
BF16 = jnp.bfloat16
MIB = 1024 * 1024

ROWS_BY_COLS = (((1,), (0,)), ((), ()))
ROWS_BY_ROWS = (((1,), (1,)), ((), ()))
COLS_BY_COLS = (((0,), (0,)), ((), ()))


def low_dot(a, b, dims=ROWS_BY_COLS):
    return lax.dot_general(a, b, dims, preferred_element_type=F32)


def high_dot(a, b, dims=ROWS_BY_COLS):
    return lax.dot_general(a, b, dims, precision=HIGH, preferred_element_type=F32)


def two_parts(x):
    first = x.astype(BF16)
    return first, (x - first.astype(F32)).astype(BF16)


def three_parts(x):
    first = x.astype(BF16)
    rest = x - first.astype(F32)
    second = rest.astype(BF16)
    return first, second, (rest - second.astype(F32)).astype(BF16)


def feature_of(place):
    return place[0] >> 1


def core_of(place):
    return place[0] & 1


def lane_numbers(shape):
    return lax.broadcasted_iota(jnp.int32, shape, len(shape) - 1)


ANY_SPEC = pl.BlockSpec(memory_space=pl.ANY)
HBM_SPEC = pl.BlockSpec(memory_space=pltpu.HBM)


def parameters(mib):
    return pltpu.CompilerParams(vmem_limit_bytes=mib * MIB)


LIMIT = 8
VMEM_SPEC = pl.BlockSpec(memory_space=pltpu.VMEM)
SMEM_SPEC = pl.BlockSpec(memory_space=pltpu.SMEM)


def exponent_rows(total_count):
    return -(-(total_count + 1) // 16) * 16


def payload_shape(total_count, rank, slots, with_gram):
    return (total_count * rank + (rank // 2 if with_gram else 0) + exponent_rows(total_count), slots)


def row_exponent(x):
    top = jnp.max(jnp.abs(x), axis=1, keepdims=True)
    return jnp.ceil(jnp.log2(jnp.maximum(top, 1e-30)))


class Payload:
    def __init__(self, ref, slots, count, rank, with_gram):
        self.ref, self.slots, self.count, self.rank, self.with_gram = ref, slots, count, rank, with_gram
        self.entries = len(slots) * count
        gram_rows = rank // 2 if with_gram else 0
        exponents = self.rows(self.entries * rank + gram_rows, exponent_rows(self.entries))
        self.steps = jnp.exp2(exponents[:, :LANES].T[:rank]) * (1.0 / LEVELS)

    def rows(self, first, number):
        return self.ref[pl.ds(first, number), :].astype(jnp.int32).astype(F32)

    def proj(self, slot, p):
        entry = self.slots.index(slot) * self.count + p
        return self.rows(entry * self.rank, self.rank) * self.steps[:, entry : entry + 1]

    def gram(self):
        rank = self.rank
        digits = self.rows(self.entries * rank, rank // 2)
        digits = jnp.concatenate([digits[:, : 2 * rank], digits[:, 2 * rank :]], axis=0)
        return (digits[:, :rank] + digits[:, rank:] * (0.5 / LEVELS)) * self.steps[:, self.entries : self.entries + 1]


def encode(values, gram, coded_ref, rank):
    count = len(values)
    lanes = lane_numbers((rank, LANES))
    exponents = jnp.zeros((rank, LANES), F32)
    for p, value in enumerate(values):
        proj = value()
        exponent = row_exponent(proj)
        coded = jnp.floor(proj * (LEVELS / jnp.exp2(exponent)) + 0.5)
        coded_ref[pl.ds(p * rank, rank), :] = coded.astype(jnp.int32).astype(jnp.int16)
        exponents = jnp.where(lanes == p, exponent, exponents)
    end = count * rank
    if gram is not None:
        exponent = row_exponent(gram)
        scaled = gram * (LEVELS / jnp.exp2(exponent))
        whole = jnp.floor(scaled + 0.5)
        rest = jnp.floor((scaled - whole) * (2 * LEVELS) + 0.5)
        digits = jnp.concatenate([whole, rest], axis=1)
        digits = jnp.concatenate([digits[: rank // 2], digits[rank // 2 :]], axis=1)
        coded_ref[pl.ds(end, rank // 2), :] = digits.astype(jnp.int32).astype(jnp.int16)
        exponents = jnp.where(lanes == count, exponent, exponents)
        end += rank // 2
    rows = exponent_rows(count)
    last = jnp.concatenate([exponents.T[:rows], jnp.zeros((rows, coded_ref.shape[1] - rank), F32)], axis=1)
    coded_ref[pl.ds(end, rows), :] = last.astype(jnp.int32).astype(jnp.int16)


def first_projection_kernel(slots, place, v_hbm, visits_ref, coded_ref, v_ref, buffers, sems, v_sem):
    count = buffers.shape[1]
    v_copy = pltpu.make_async_copy(v_hbm, v_ref, v_sem)
    v_copy.start()
    copies = [
        pltpu.make_async_copy(visits_ref.at[feature_of(place) ^ slot, pl.ds(0, count)], buffers.at[i], sems.at[i])
        for i, slot in enumerate(slots)
    ]
    for copy in copies:
        copy.start()
    v_copy.wait()
    gram = low_dot(v_ref[...], v_ref[...], ROWS_BY_ROWS)

    def value(i, p):
        if p == 0:
            copies[i].wait()
        return low_dot(v_ref[...], buffers[i, p], ROWS_BY_ROWS)

    values = [functools.partial(value, i, p) for i in range(len(slots)) for p in range(count)]
    encode(values, gram, coded_ref, v_ref.shape[0])


def first_projection(slots, count, place, visits, v_rows):
    width = visits.shape[3]
    rank = v_rows.shape[0]
    return pl.pallas_call(
        functools.partial(first_projection_kernel, slots),
        in_specs=[SMEM_SPEC, HBM_SPEC, HBM_SPEC],
        out_specs=VMEM_SPEC,
        out_shape=jax.ShapeDtypeStruct(payload_shape(len(slots) * count, rank, visits.shape[2], True), jnp.int16),
        scratch_shapes=[
            pltpu.VMEM(v_rows.shape, BF16),
            pltpu.VMEM((len(slots), count) + visits.shape[2:], BF16),
            pltpu.SemaphoreType.DMA((len(slots),)),
            pltpu.SemaphoreType.DMA,
        ],
        compiler_params=parameters(LIMIT),
        cost_estimate=SHORT,
        name="project_first",
    )(place, v_rows, visits)


def next_projection_kernel(slots, first, count, layouts, place, v_ref, visits_ref, *refs):
    *arrived, coded_ref = refs
    rank = v_ref.shape[0]
    arrived = [Payload(ref, layout, count, rank, first == 0) for ref, layout in zip(arrived, layouts)]

    def value(slot, p):
        proj = low_dot(v_ref[...], visits_ref[feature_of(place) ^ slot, first + p], ROWS_BY_ROWS)
        for payload in arrived:
            proj = proj + payload.proj(slot, p)
        return proj

    gram = None
    if first == 0:
        gram = low_dot(v_ref[...], v_ref[...], ROWS_BY_ROWS)
        for payload in arrived:
            gram = gram + payload.gram()
    encode([functools.partial(value, slot, p) for slot in slots for p in range(count)], gram, coded_ref, rank)


def next_projection(slots, first, count, layouts, place, visits, v_rows, arrived):
    rank = v_rows.shape[0]
    return pl.pallas_call(
        functools.partial(next_projection_kernel, slots, first, count, layouts),
        in_specs=[SMEM_SPEC] + [VMEM_SPEC] * (2 + len(arrived)),
        out_specs=VMEM_SPEC,
        out_shape=jax.ShapeDtypeStruct(payload_shape(len(slots) * count, rank, visits.shape[2], first == 0), jnp.int16),
        compiler_params=parameters(LIMIT),
        cost_estimate=SHORT,
        name="project_next",
    )(place, v_rows, visits, *arrived)


def own_projection_kernel(place, v_ref, w_ref, visits_ref, *refs):
    *proj_refs, v_gram_ref, w_gram_ref = refs
    count = visits_ref.shape[1] // len(proj_refs)
    for p in range(visits_ref.shape[1]):
        proj_refs[p // count][p % count] = low_dot(v_ref[...], visits_ref[feature_of(place), p], ROWS_BY_ROWS)
    v_gram_ref[...] = low_dot(v_ref[...], v_ref[...], ROWS_BY_ROWS)
    w_gram = high_dot(w_ref[...], w_ref[...], COLS_BY_COLS)
    w_gram_ref[...] = jnp.concatenate([jnp.zeros_like(w_gram), w_gram], axis=1)


def project_own(n_parts, place, visits, v_rows, w_start):
    _, share, slots, width = visits.shape
    rank = v_rows.shape[0]
    gram = jax.ShapeDtypeStruct((rank, rank), F32)
    proj = jax.ShapeDtypeStruct((share // n_parts, rank, slots), F32)
    *own, v_gram, w_gram = pl.pallas_call(
        own_projection_kernel,
        in_specs=[SMEM_SPEC] + [VMEM_SPEC] * 3,
        out_specs=[VMEM_SPEC] * (n_parts + 2),
        out_shape=[proj] * n_parts + [gram, jax.ShapeDtypeStruct((rank, 2 * rank), F32)],
        compiler_params=parameters(LIMIT),
        cost_estimate=SHORT,
        name="project_own",
    )(place, v_rows, w_start, visits)
    return own, v_gram, w_gram


def pair_inverse(a, b, c, d):
    scale = 1.0 / (a * d - b * c)
    return d * scale, b * scale, c * scale, a * scale


def eliminate(table, rank):
    tiles = [table[8 * t : 8 * t + 8] for t in range(rank // 8)]
    rows = lax.broadcasted_iota(jnp.int32, tiles[0].shape, 0)
    for i in range(0, rank, 4):
        columns = [[jnp.broadcast_to(t[:, i + q : i + q + 1], t.shape) for q in range(4)] for t in tiles]
        home, first = i // 8, i % 8
        r0, r1, r2, r3 = (tiles[home][first + q : first + q + 1] for q in range(4))
        m = [[columns[home][q][first + p : first + p + 1] for q in range(4)] for p in range(4)]
        d, b, c, a = pair_inverse(m[0][0], m[0][1], m[1][0], m[1][1])
        q02, q03 = d * m[0][2] - b * m[1][2], d * m[0][3] - b * m[1][3]
        q12, q13 = a * m[1][2] - c * m[0][2], a * m[1][3] - c * m[0][3]
        y0, y1 = d * r0 - b * r1, a * r1 - c * r0
        z2 = r2 - (m[2][0] * y0 + m[2][1] * y1)
        z3 = r3 - (m[3][0] * y0 + m[3][1] * y1)
        d, b, c, a = pair_inverse(
            m[2][2] - (m[2][0] * q02 + m[2][1] * q12),
            m[2][3] - (m[2][0] * q03 + m[2][1] * q13),
            m[3][2] - (m[3][0] * q02 + m[3][1] * q12),
            m[3][3] - (m[3][0] * q03 + m[3][1] * q13),
        )
        n2, n3 = d * z2 - b * z3, a * z3 - c * z2
        new = [y0 - (q02 * n2 + q03 * n3), y1 - (q12 * n2 + q13 * n3), n2, n3]
        for t, (c0, c1, c2, c3) in enumerate(columns):
            tile = tiles[t] - ((c0 * new[0] + c1 * new[1]) + (c2 * new[2] + c3 * new[3]))
            if t == home:
                for q in range(4):
                    tile = jnp.where(rows == first + q, new[q], tile)
            tiles[t] = tile
    return jnp.concatenate(tiles, axis=0)


def inverse_of(gram):
    rank = gram.shape[0]
    eye = (lax.broadcasted_iota(jnp.int32, gram.shape, 0) == lane_numbers(gram.shape)).astype(F32)
    return eliminate(jnp.concatenate([gram, eye], axis=1), rank)[:, rank:]


def total(refs):
    out = refs[0][...]
    for ref in refs[1:]:
        out = out + ref[...]
    return out


def first_inverse_kernel(v_gram_ref, w_gram_ref, after_ref, inverse_ref):
    inverse_ref[...] = inverse_of(w_gram_ref[...] * v_gram_ref[...])


def first_inverse(v_gram, w_gram, after):
    return pl.pallas_call(
        first_inverse_kernel,
        in_specs=[VMEM_SPEC] * 2 + [ANY_SPEC],
        out_specs=VMEM_SPEC,
        out_shape=jax.ShapeDtypeStruct(w_gram.shape, F32),
        compiler_params=parameters(LIMIT),
        cost_estimate=SHORT,
        name="first_inverse",
    )(v_gram, w_gram, after)


def sum_h_kernel(n_terms, *refs):
    h_ref, w_gram_ref = refs[n_terms + 1 :]
    rank = h_ref.shape[0]
    both = total(refs[:n_terms])
    h_ref[...] = both[:, :rank]
    w_gram_ref[...] = both[:, rank:]


def sum_h(terms, after):
    rank = terms[0].shape[0]
    return pl.pallas_call(
        functools.partial(sum_h_kernel, len(terms)),
        in_specs=[VMEM_SPEC] * len(terms) + [ANY_SPEC],
        out_specs=[VMEM_SPEC] * 2,
        out_shape=[jax.ShapeDtypeStruct((rank, rank), F32)] * 2,
        compiler_params=parameters(LIMIT),
        cost_estimate=SHORT,
        name="sum_h",
    )(*terms, after)


def sweep_all(frames, rank, fine):
    patients = range(frames.shape[0])
    if fine:
        both = [jnp.concatenate(two_parts(frames[p]), axis=0) for p in patients]
        blocks = [low_dot(x, x, ROWS_BY_ROWS) for x in both]
        blocks = [x[:rank] + x[rank:] for x in blocks]
        grams = [x + pltpu.roll(x, rank, 1) for x in blocks]
        moved = [low_dot(jnp.concatenate(two_parts(g), axis=0), x) for g, x in zip(grams, both)]
        moved = [x[:rank] + x[rank:] for x in moved]
    else:
        first = [frames[p].astype(BF16) for p in patients]
        grams = [low_dot(x, x, ROWS_BY_ROWS).astype(BF16) for x in first]
        moved = [low_dot(g, x) for g, x in zip(grams, first)]
    for p in patients:
        frames[p] = 1.5 * frames[p] - 0.5 * moved[p]


def frames_kernel(layouts, part, share, place, counts_ref, h_ref, w_ref, v_gram_ref, before_ref, own_ref, *refs):
    coded, refs = refs[: len(layouts)], refs[len(layouts) :]
    frames_ref, terms_ref, v_total_ref, proj, frames = refs
    count, rank, slots = frames.shape
    patients = range(count)
    first = feature_of(place) * share + part * count
    pieces = [own_ref[p] for p in patients]
    v_gram = v_gram_ref[...]
    for code, layout in zip(coded, layouts):
        payload = Payload(code, layout, count, rank, part == 0)
        pieces = [pieces[p] + payload.proj(0, p) for p in patients]
        if part == 0:
            v_gram = v_gram + payload.gram()
    v_total_ref[...] = v_gram
    for p in patients:
        proj[p] = pieces[p]
    weights = [w_ref[pl.ds(first + p, 1), :] for p in patients]
    mixed = [high_dot(h_ref[...] * weights[p], pieces[p]) for p in patients]
    lanes = lane_numbers((rank, slots))
    mixed = [jnp.where(lanes < counts_ref[first + p], mixed[p], 0.0) for p in patients]
    energy = [jnp.sum(jnp.sum(x * x, axis=1, keepdims=True), axis=0, keepdims=True) for x in mixed]
    for p in patients:
        frames[p] = mixed[p] * lax.rsqrt(energy[p] + epsilon)

    def sweep(fine, step, carry):
        sweep_all(frames, rank, fine)
        return carry

    lax.fori_loop(0, COARSE_STEPS, functools.partial(sweep, False), 0, unroll=True)
    lax.fori_loop(COARSE_STEPS, NS_STEPS, functools.partial(sweep, True), 0, unroll=3)
    low = [frames[p].astype(BF16) for p in patients]
    for p in patients:
        frames_ref[p] = low[p]
    products = [jnp.concatenate(three_parts(proj[p]), axis=0) for p in patients]
    products = [low_dot(low[p], products[p], ROWS_BY_ROWS) for p in patients]
    before = before_ref[...]
    terms = before[:, :rank]
    for p in patients:
        product = products[p][:, :rank] + (products[p][:, rank : 2 * rank] + products[p][:, 2 * rank :])
        terms = terms + product * weights[p]
    terms_ref[...] = jnp.concatenate([terms, before[:, rank:]], axis=1)


def own_frames(layouts, part, n_parts, place, counts, h_start, w_start, v_gram, before, own, coded):
    count, rank, slots = own.shape
    share = count * n_parts
    return pl.pallas_call(
        functools.partial(frames_kernel, layouts, part, share),
        in_specs=[SMEM_SPEC] * 2 + [VMEM_SPEC] * (5 + len(coded)),
        out_specs=[VMEM_SPEC] * 3,
        out_shape=[
            jax.ShapeDtypeStruct(own.shape, BF16),
            jax.ShapeDtypeStruct((rank, 2 * rank), F32),
            jax.ShapeDtypeStruct((rank, rank), F32),
        ],
        scratch_shapes=[pltpu.VMEM(own.shape, F32)] * 2,
        compiler_params=parameters(LIMIT),
        cost_estimate=SHORT,
        name="own_frames",
    )(place, counts, h_start, w_start, v_gram, before, own, *coded)


def projected_kernel(items, place, visits_ref, *refs):
    frames_refs, outs, token_ref = refs[: len(items)], refs[-2 * len(items) - 1 : -1], refs[-1]
    token_ref[...] = jnp.zeros_like(token_ref)
    for i, (slots, first) in enumerate(items):
        total_count, rank, _ = frames_refs[i].shape
        count = total_count // len(slots)
        for p in range(total_count):
            rows = pl.ds(p * rank, rank)
            owner = feature_of(place) ^ slots[p // count]
            product = low_dot(frames_refs[i][p], visits_ref[owner, first + p % count])
            outs[2 * i][rows, :], outs[2 * i + 1][rows, :] = two_parts(product)


def join_kernel(count, *refs):
    out_ref = refs[-1]
    first = 0
    for part in refs[:count]:
        out_ref[first : first + part.shape[0]] = part[...]
        first += part.shape[0]


def join(parts, after):
    if len(parts) == 1:
        return parts[0]
    return pl.pallas_call(
        functools.partial(join_kernel, len(parts)),
        in_specs=[VMEM_SPEC] * len(parts) + [ANY_SPEC] * len(after),
        out_specs=VMEM_SPEC,
        out_shape=jax.ShapeDtypeStruct((sum(x.shape[0] for x in parts),) + parts[0].shape[1:], parts[0].dtype),
        compiler_params=parameters(LIMIT),
        cost_estimate=SHORT,
        name="join_frames",
    )(*parts, *after)


def project_frames(items, place, frames, visits, after):
    width = visits.shape[-1]
    outs = []
    for item in items:
        count, rank, _ = frames[item].shape
        outs += [jax.ShapeDtypeStruct((count * rank, width), BF16)] * 2
    *parts, token = pl.pallas_call(
        functools.partial(projected_kernel, items),
        in_specs=[SMEM_SPEC] + [VMEM_SPEC] * (1 + len(items)) + [ANY_SPEC] * len(after),
        out_specs=[VMEM_SPEC] * (len(outs) + 1),
        out_shape=outs + [jax.ShapeDtypeStruct((8, LANES), F32)],
        compiler_params=parameters(LIMIT),
        cost_estimate=SHORT,
        name="project_frames",
    )(place, visits, *[frames[item] for item in items], *after)
    return {item: parts[2 * i : 2 * i + 2] for i, item in enumerate(items)}, token


def next_h_kernel(n_terms, n_slots, place, *refs):
    inverse_ref, w_ref, _, result_ref, h_ref, factor_ref = refs[n_terms:]
    h_next = high_dot(total(refs[:n_terms]), inverse_ref[...])
    result_ref[...] = h_next
    h_ref[...] = h_next
    rank = h_next.shape[0]
    patients = w_ref.shape[0]
    share = patients // n_slots
    h_rows = h_next.T
    w_rows = jnp.concatenate([w_ref[...], jnp.zeros((LANES - patients, rank), F32)], axis=0)
    w_columns = w_rows.T
    for slot in range(n_slots):
        first = (feature_of(place) ^ slot) * share
        columns = pltpu.roll(w_columns, jnp.where(first == 0, 0, LANES - first), 1)
        factor = jnp.concatenate([h_rows * columns[:, p : p + 1] for p in range(share)], axis=1)
        factor_ref[slot] = jnp.concatenate(three_parts(factor), axis=0)


def next_h(place, terms, inverse, w_start, n_slots, after):
    patients, rank = w_start.shape
    share = patients // n_slots
    return pl.pallas_call(
        functools.partial(next_h_kernel, len(terms), n_slots),
        in_specs=[SMEM_SPEC] + [VMEM_SPEC] * (len(terms) + 2) + [ANY_SPEC],
        out_specs=[VMEM_SPEC] * 3,
        out_shape=[
            jax.ShapeDtypeStruct(inverse.shape, F32),
            jax.ShapeDtypeStruct(inverse.shape, F32),
            jax.ShapeDtypeStruct((n_slots, 3 * rank, share * rank), BF16),
        ],
        compiler_params=parameters(LIMIT),
        cost_estimate=SHORT,
        name="next_h",
    )(place, *terms, inverse, w_start, after)


def second_inverse_kernel(h_ref, w_gram_ref, gram_ref, inverse_ref):
    gram = high_dot(h_ref[...], h_ref[...], COLS_BY_COLS)
    gram_ref[...] = gram
    inverse_ref[...] = inverse_of(gram * w_gram_ref[...])


def second_inverse(h_next, w_gram):
    out = jax.ShapeDtypeStruct(w_gram.shape, F32)
    return pl.pallas_call(
        second_inverse_kernel,
        out_shape=[out, out],
        compiler_params=parameters(LIMIT),
        cost_estimate=SHORT,
        name="second_inverse",
    )(h_next, w_gram)


def v_terms_kernel(items, place, factor_ref, *refs):
    *parts, keep_ref, send_ref, terms_ref = refs
    rank, width = terms_ref.shape
    half = width // 2
    total = None
    for i, (slots, first) in enumerate(items):
        count = parts[2 * i].shape[0] // len(slots)
        columns = pl.ds(first * rank, count)
        for k, slot in enumerate(slots):
            rows = pl.ds(k * count, count)
            large = low_dot(factor_ref[slot, :, columns], parts[2 * i][rows, :])
            small = low_dot(factor_ref[slot, : 2 * rank, columns], parts[2 * i + 1][rows, :])
            terms = large[:rank] + (large[rank : 2 * rank] + small[:rank]) + (large[2 * rank :] + small[rank:])
            total = terms if total is None else total + terms
    terms_ref[...] = total
    keep_ref[...] = terms_ref[:, pl.ds(pl.multiple_of(core_of(place) * half, half), half)]
    send_ref[...] = terms_ref[:, pl.ds(pl.multiple_of((1 - core_of(place)) * half, half), half)]


def all_v_terms(items, place, factor, projected):
    width = projected[0].shape[1]
    rank = factor.shape[1] // 3
    half = (rank, width // 2)
    return pl.pallas_call(
        functools.partial(v_terms_kernel, items),
        in_specs=[SMEM_SPEC] + [VMEM_SPEC] * (1 + len(projected)),
        out_specs=[VMEM_SPEC] * 2,
        out_shape=[jax.ShapeDtypeStruct(half, F32)] * 2,
        scratch_shapes=[pltpu.VMEM((rank, width), F32)],
        compiler_params=parameters(LIMIT),
        cost_estimate=SHORT,
        name="v_terms",
    )(place, factor, *projected)


def next_v_kernel(items, share, place, own_ref, other_ref, inverse_ref, h_ref, *refs):
    *parts, v_ref, sums_ref, v_parts = refs
    rank = inverse_ref.shape[0]
    upper = core_of(place) == 1
    left = jnp.where(upper, other_ref[...], own_ref[...])
    right = jnp.where(upper, own_ref[...], other_ref[...])
    v_rows = high_dot(inverse_ref[...], jnp.concatenate([left, right], axis=1))
    v_ref[...] = v_rows
    v_parts[...] = jnp.concatenate(two_parts(v_rows), axis=0)
    weights = jnp.concatenate([h_ref[...]] * 2, axis=1)
    gram = low_dot(v_parts[...], v_parts[...], ROWS_BY_ROWS)
    gram = gram[:rank, :rank] + (gram[:rank, rank:] + gram[rank:, :rank])
    sums_ref[...] = jnp.concatenate([jnp.zeros((rank, rank), F32), gram], axis=1)
    for i, (slots, done) in enumerate(items):
        seen = low_dot(parts[2 * i][...], v_parts[...], ROWS_BY_ROWS)
        seen = seen + low_dot(parts[2 * i + 1][...], v_parts[...], ROWS_BY_ROWS)
        count = seen.shape[0] // rank // len(slots)
        for p in range(seen.shape[0] // rank):
            patient = (feature_of(place) ^ slots[p // count]) * share + done + p % count
            row = jnp.sum(seen[p * rank : (p + 1) * rank] * weights, axis=0, keepdims=True)
            sums_ref[pl.ds(patient, 1), :rank] = row[:, :rank] + row[:, rank:]


def next_v(items, share, place, own, other, inverse, h_next, projected):
    width = projected[0].shape[1]
    rank = inverse.shape[0]
    return pl.pallas_call(
        functools.partial(next_v_kernel, items, share),
        in_specs=[SMEM_SPEC] + [VMEM_SPEC] * (4 + len(projected)),
        out_specs=[VMEM_SPEC] * 2,
        out_shape=[
            jax.ShapeDtypeStruct((rank, width), F32),
            jax.ShapeDtypeStruct((rank, 2 * rank), F32),
        ],
        scratch_shapes=[pltpu.VMEM((2 * rank, width), BF16)],
        compiler_params=parameters(LIMIT),
        cost_estimate=SHORT,
        name="next_v",
    )(place, own, other, inverse, h_next, *projected)


def next_w_kernel(n_sums, *refs):
    gram_ref, w_ref = refs[n_sums:]
    patients, rank = w_ref.shape
    sums = total(refs[:n_sums])
    table = jnp.concatenate([sums[:, rank:] * gram_ref[...], sums.T[:rank]], axis=1)
    w_ref[...] = eliminate(table, rank).T[rank : rank + patients]


def next_w(sums, h_gram, patients):
    rank = h_gram.shape[0]
    return pl.pallas_call(
        functools.partial(next_w_kernel, len(sums)),
        out_shape=jax.ShapeDtypeStruct((patients, rank), F32),
        compiler_params=parameters(LIMIT),
        cost_estimate=SHORT,
        name="next_w",
    )(*sums, h_gram)


def swap(x, axis, slot):
    pairs = [(i, i ^ slot) for i in range(lax.axis_size(axis))]
    return lax.ppermute(x, axis, pairs)


def all_terms(x, axis):
    n = lax.axis_size(axis)
    if n > 4:
        return [lax.psum(x, axis)]
    return [x] + [swap(x, axis, s) for s in range(1, n)]


def staged_terms(x, axis, after):
    n = lax.axis_size(axis)
    step = 1
    while 2 * step < n:
        x = add(x, swap(x, axis, step), after)
        step *= 2
    return [x, swap(x, axis, step)]


def add_kernel(a_ref, b_ref, *refs):
    refs[-1][...] = a_ref[...] + b_ref[...]


def add(a, b, after):
    return pl.pallas_call(
        add_kernel,
        in_specs=[VMEM_SPEC] * 2 + [ANY_SPEC] * len(after),
        out_specs=VMEM_SPEC,
        out_shape=jax.ShapeDtypeStruct(a.shape, a.dtype),
        compiler_params=parameters(LIMIT),
        cost_estimate=SHORT,
        name="add_terms",
    )(a, b, *after)


def patient_halves(keep, send, after):
    own = add(keep, swap(send, "patient", 1), [])
    step = 2
    while step < lax.axis_size("patient"):
        own = add(own, swap(own, "patient", step), [after])
        step *= 2
    return own, swap(own, "patient", 1)


def on_device(visits, visit_counts, h_start, v_start, w_start):
    n = lax.axis_size("feature")
    patients, slots, width = visits.shape
    share = patients // n
    place = (2 * lax.axis_index("feature") + (lax.axis_index("patient") & 1)).astype(jnp.int32).reshape(1)
    by_owner = visits.reshape(n, share, slots, width)
    in_hbm = pltpu.with_memory_space_constraint(by_owner, pltpu.HBM)
    v_rows = pltpu.with_memory_space_constraint(v_start.T, pltpu.HBM)

    n_parts = 2 if share % 2 == 0 else 1
    count = share // n_parts
    firsts = [part * count for part in range(n_parts)]
    bits = [1 << i for i in range(n.bit_length() - 1)]
    v_near = v_start.T

    def send(bit):
        return [slot for slot in range(n) if slot & bit and not slot & (bit - 1)]

    def receive(bit):
        return [slot ^ bit for slot in send(bit)]

    arrived = [[] for _ in firsts]
    for i, bit in enumerate(bits):
        layouts = [receive(before) for before in bits[:i]]
        for part, first in enumerate(firsts):
            if i == 0 and part == 0:
                code = first_projection(send(bit), count, place, in_hbm, v_rows)
            else:
                code = next_projection(send(bit), first, count, layouts, place, by_owner, v_near, arrived[part])
            arrived[part] = arrived[part] + [swap(code, "feature", bit)]
    own, v_gram, h_local = project_own(n_parts, place, by_owner, v_near, w_start)

    layouts = [receive(bit) for bit in bits]
    frames = [[] for _ in firsts]

    def double(part, after):
        for bit in bits[::-1]:
            slots = tuple(slot ^ bit for group, _ in frames[part] for slot in group)
            frames[part].append((slots, swap(join([x for _, x in frames[part]], after), "feature", bit)))

    def project_groups(groups, after):
        arrays = {(frames[part][k][0], firsts[part]): frames[part][k][1] for part, k in groups}
        return project_frames(list(arrays), place, arrays, by_owner, after)

    for part, first in enumerate(firsts):
        low, h_local, v_total = own_frames(
            layouts, part, n_parts, place, visit_counts, h_start, w_start, v_gram, h_local, own[part], arrived[part]
        )
        v_gram = v_total if first == 0 else v_gram
        frames[part].append(((0,), low))
        if part < n_parts - 1:
            double(part, [])

    last = len(bits)
    projected, token = project_groups([(part, 0) for part in range(n_parts)], [])
    h_sums = staged_terms(h_local, "patient", [token])
    double(n_parts - 1, h_sums[:1])
    h_sum, w_gram = sum_h(h_sums, token)
    h_terms = all_terms(h_sum, "feature")
    order = [(part, k) for part in range(n_parts) for k in range(1, last + 1)]
    for group in order:
        more, token = project_groups([group], [token])
        projected |= more
        if group == order[-2]:
            inverse = first_inverse(v_gram, w_gram, token)
    h_result, h_next, factor = next_h(place, h_terms, inverse, w_start, n, token)

    items = list(projected)
    flat = [x for item in items for x in projected[item]]
    keep, send = all_v_terms(items, place, factor, flat)
    h_gram, second = second_inverse(h_next, w_gram)
    own_terms, other_terms = patient_halves(keep, send, second)
    v_next, sums = next_v(items, share, place, own_terms, other_terms, second, h_next, flat)
    w_next = next_w(all_terms(sums, "feature"), h_gram, patients)
    return (h_result, v_next.T, w_next)


def solution(mesh):
    return jax.shard_map(
        on_device,
        mesh=mesh,
        in_specs=(
            P(("groups", "patient"), None, "feature"),
            P(("groups", "patient")),
            P(),
            P("feature", None),
            P(("groups", "patient"), None),
        ),
        out_specs=(P(None, "groups"), P("feature", "groups"), P("patient", "groups")),
        check_vma=False,
    )
```

```python
import functools

import jax
import jax.numpy as jnp
from jax import lax
from jax.experimental import pallas as pl
from jax.experimental.pallas import tpu as pltpu
from jax.sharding import PartitionSpec as P

NS_STEPS = 12
LANES = 128
LEVELS = 32000.0
COARSE_STEPS = 3
SHORT = pl.CostEstimate(flops=1000, bytes_accessed=1000, transcendentals=0)

epsilon = 1e-06
HIGH = lax.Precision.HIGHEST
F32 = jnp.float32
BF16 = jnp.bfloat16
MIB = 1024 * 1024

ROWS_BY_COLS = (((1,), (0,)), ((), ()))
ROWS_BY_ROWS = (((1,), (1,)), ((), ()))
COLS_BY_COLS = (((0,), (0,)), ((), ()))


def low_dot(a, b, dims=ROWS_BY_COLS):
    return lax.dot_general(a, b, dims, preferred_element_type=F32)


def high_dot(a, b, dims=ROWS_BY_COLS):
    return lax.dot_general(a, b, dims, precision=HIGH, preferred_element_type=F32)


def two_parts(x):
    first = x.astype(BF16)
    return first, (x - first.astype(F32)).astype(BF16)


def three_parts(x):
    first = x.astype(BF16)
    rest = x - first.astype(F32)
    second = rest.astype(BF16)
    return first, second, (rest - second.astype(F32)).astype(BF16)


def feature_of(place):
    return place[0] >> 1


def core_of(place):
    return place[0] & 1


def lane_numbers(shape):
    return lax.broadcasted_iota(jnp.int32, shape, len(shape) - 1)


ANY_SPEC = pl.BlockSpec(memory_space=pl.ANY)
HBM_SPEC = pl.BlockSpec(memory_space=pltpu.HBM)


def parameters(mib):
    return pltpu.CompilerParams(vmem_limit_bytes=mib * MIB)


LIMIT = 8
VMEM_SPEC = pl.BlockSpec(memory_space=pltpu.VMEM)
SMEM_SPEC = pl.BlockSpec(memory_space=pltpu.SMEM)


def exponent_rows(total_count):
    return -(-(total_count + 1) // 16) * 16


def payload_shape(total_count, rank, slots, with_gram):
    return (total_count * rank + (rank // 2 if with_gram else 0) + exponent_rows(total_count), slots)


def row_exponent(x):
    top = jnp.max(jnp.abs(x), axis=1, keepdims=True)
    return jnp.ceil(jnp.log2(jnp.maximum(top, 1e-30)))


class Payload:
    def __init__(self, ref, slots, count, rank, with_gram):
        self.ref, self.slots, self.count, self.rank, self.with_gram = ref, slots, count, rank, with_gram
        self.entries = len(slots) * count
        gram_rows = rank // 2 if with_gram else 0
        exponents = self.rows(self.entries * rank + gram_rows, exponent_rows(self.entries))
        self.steps = jnp.exp2(exponents[:, :LANES].T[:rank]) * (1.0 / LEVELS)

    def rows(self, first, number):
        return self.ref[pl.ds(first, number), :].astype(jnp.int32).astype(F32)

    def proj(self, slot, p):
        entry = self.slots.index(slot) * self.count + p
        return self.rows(entry * self.rank, self.rank) * self.steps[:, entry : entry + 1]

    def gram(self):
        rank = self.rank
        digits = self.rows(self.entries * rank, rank // 2)
        digits = jnp.concatenate([digits[:, : 2 * rank], digits[:, 2 * rank :]], axis=0)
        return (digits[:, :rank] + digits[:, rank:] * (0.5 / LEVELS)) * self.steps[:, self.entries : self.entries + 1]


def encode(values, gram, coded_ref, rank):
    count = len(values)
    lanes = lane_numbers((rank, LANES))
    exponents = jnp.zeros((rank, LANES), F32)
    for p, value in enumerate(values):
        proj = value()
        exponent = row_exponent(proj)
        coded = jnp.floor(proj * (LEVELS / jnp.exp2(exponent)) + 0.5)
        coded_ref[pl.ds(p * rank, rank), :] = coded.astype(jnp.int32).astype(jnp.int16)
        exponents = jnp.where(lanes == p, exponent, exponents)
    end = count * rank
    if gram is not None:
        exponent = row_exponent(gram)
        scaled = gram * (LEVELS / jnp.exp2(exponent))
        whole = jnp.floor(scaled + 0.5)
        rest = jnp.floor((scaled - whole) * (2 * LEVELS) + 0.5)
        digits = jnp.concatenate([whole, rest], axis=1)
        digits = jnp.concatenate([digits[: rank // 2], digits[rank // 2 :]], axis=1)
        coded_ref[pl.ds(end, rank // 2), :] = digits.astype(jnp.int32).astype(jnp.int16)
        exponents = jnp.where(lanes == count, exponent, exponents)
        end += rank // 2
    rows = exponent_rows(count)
    last = jnp.concatenate([exponents.T[:rows], jnp.zeros((rows, coded_ref.shape[1] - rank), F32)], axis=1)
    coded_ref[pl.ds(end, rows), :] = last.astype(jnp.int32).astype(jnp.int16)


def first_projection_kernel(slots, place, v_hbm, visits_ref, coded_ref, v_ref, buffers, sems, v_sem):
    count = buffers.shape[1]
    v_copy = pltpu.make_async_copy(v_hbm, v_ref, v_sem)
    v_copy.start()
    copies = [
        pltpu.make_async_copy(visits_ref.at[feature_of(place) ^ slot, pl.ds(0, count)], buffers.at[i], sems.at[i])
        for i, slot in enumerate(slots)
    ]
    for copy in copies:
        copy.start()
    v_copy.wait()
    gram = low_dot(v_ref[...], v_ref[...], ROWS_BY_ROWS)

    def value(i, p):
        if p == 0:
            copies[i].wait()
        return low_dot(v_ref[...], buffers[i, p], ROWS_BY_ROWS)

    values = [functools.partial(value, i, p) for i in range(len(slots)) for p in range(count)]
    encode(values, gram, coded_ref, v_ref.shape[0])


def first_projection(slots, count, place, visits, v_rows):
    width = visits.shape[3]
    rank = v_rows.shape[0]
    return pl.pallas_call(
        functools.partial(first_projection_kernel, slots),
        in_specs=[SMEM_SPEC, HBM_SPEC, HBM_SPEC],
        out_specs=VMEM_SPEC,
        out_shape=jax.ShapeDtypeStruct(payload_shape(len(slots) * count, rank, visits.shape[2], True), jnp.int16),
        scratch_shapes=[
            pltpu.VMEM(v_rows.shape, BF16),
            pltpu.VMEM((len(slots), count) + visits.shape[2:], BF16),
            pltpu.SemaphoreType.DMA((len(slots),)),
            pltpu.SemaphoreType.DMA,
        ],
        compiler_params=parameters(LIMIT),
        cost_estimate=SHORT,
        name="project_first",
    )(place, v_rows, visits)


def next_projection_kernel(slots, first, count, layouts, place, v_ref, visits_ref, *refs):
    coded_ref = refs[-1]
    rank = v_ref.shape[0]
    arrived = [Payload(ref, layout, count, rank, first == 0) for ref, layout in zip(refs, layouts)]

    def value(slot, p):
        proj = low_dot(v_ref[...], visits_ref[feature_of(place) ^ slot, first + p], ROWS_BY_ROWS)
        for payload in arrived:
            proj = proj + payload.proj(slot, p)
        return proj

    gram = None
    if first == 0:
        gram = low_dot(v_ref[...], v_ref[...], ROWS_BY_ROWS)
        for payload in arrived:
            gram = gram + payload.gram()
    encode([functools.partial(value, slot, p) for slot in slots for p in range(count)], gram, coded_ref, rank)


def next_projection(slots, first, count, layouts, place, visits, v_rows, arrived, after):
    rank = v_rows.shape[0]
    return pl.pallas_call(
        functools.partial(next_projection_kernel, slots, first, count, layouts),
        in_specs=[SMEM_SPEC] + [VMEM_SPEC] * (2 + len(arrived)) + [ANY_SPEC] * len(after),
        out_specs=VMEM_SPEC,
        out_shape=jax.ShapeDtypeStruct(payload_shape(len(slots) * count, rank, visits.shape[2], first == 0), jnp.int16),
        compiler_params=parameters(LIMIT),
        cost_estimate=SHORT,
        name="project_next",
    )(place, v_rows, visits, *arrived, *after)


def w_gram_kernel(w_ref, gram_ref):
    gram_ref[...] = high_dot(w_ref[...], w_ref[...], COLS_BY_COLS)


def own_w_gram(w_start):
    rank = w_start.shape[1]
    return pl.pallas_call(
        w_gram_kernel,
        in_specs=[VMEM_SPEC],
        out_specs=VMEM_SPEC,
        out_shape=jax.ShapeDtypeStruct((rank, rank), F32),
        compiler_params=parameters(LIMIT),
        cost_estimate=SHORT,
        name="own_w_gram",
    )(w_start)


def own_projection_kernel(place, v_ref, visits_ref, *refs):
    *proj_refs, v_gram_ref = refs
    count = visits_ref.shape[1] // len(proj_refs)
    for p in range(visits_ref.shape[1]):
        proj_refs[p // count][p % count] = low_dot(v_ref[...], visits_ref[feature_of(place), p], ROWS_BY_ROWS)
    v_gram_ref[...] = low_dot(v_ref[...], v_ref[...], ROWS_BY_ROWS)


def project_own(n_parts, place, visits, v_rows):
    _, share, slots, width = visits.shape
    rank = v_rows.shape[0]
    proj = jax.ShapeDtypeStruct((share // n_parts, rank, slots), F32)
    *own, v_gram = pl.pallas_call(
        own_projection_kernel,
        in_specs=[SMEM_SPEC] + [VMEM_SPEC] * 2,
        out_specs=[VMEM_SPEC] * (n_parts + 1),
        out_shape=[proj] * n_parts + [jax.ShapeDtypeStruct((rank, rank), F32)],
        compiler_params=parameters(LIMIT),
        cost_estimate=SHORT,
        name="project_own",
    )(place, v_rows, visits)
    return own, v_gram


def pair_inverse(a, b, c, d):
    scale = 1.0 / (a * d - b * c)
    return d * scale, b * scale, c * scale, a * scale


def eliminate(table, rank):
    tiles = [table[8 * t : 8 * t + 8] for t in range(rank // 8)]
    rows = lax.broadcasted_iota(jnp.int32, tiles[0].shape, 0)
    for i in range(0, rank, 4):
        columns = [[jnp.broadcast_to(t[:, i + q : i + q + 1], t.shape) for q in range(4)] for t in tiles]
        home, first = i // 8, i % 8
        r0, r1, r2, r3 = (tiles[home][first + q : first + q + 1] for q in range(4))
        m = [[columns[home][q][first + p : first + p + 1] for q in range(4)] for p in range(4)]
        d, b, c, a = pair_inverse(m[0][0], m[0][1], m[1][0], m[1][1])
        q02, q03 = d * m[0][2] - b * m[1][2], d * m[0][3] - b * m[1][3]
        q12, q13 = a * m[1][2] - c * m[0][2], a * m[1][3] - c * m[0][3]
        y0, y1 = d * r0 - b * r1, a * r1 - c * r0
        z2 = r2 - (m[2][0] * y0 + m[2][1] * y1)
        z3 = r3 - (m[3][0] * y0 + m[3][1] * y1)
        d, b, c, a = pair_inverse(
            m[2][2] - (m[2][0] * q02 + m[2][1] * q12),
            m[2][3] - (m[2][0] * q03 + m[2][1] * q13),
            m[3][2] - (m[3][0] * q02 + m[3][1] * q12),
            m[3][3] - (m[3][0] * q03 + m[3][1] * q13),
        )
        n2, n3 = d * z2 - b * z3, a * z3 - c * z2
        new = [y0 - (q02 * n2 + q03 * n3), y1 - (q12 * n2 + q13 * n3), n2, n3]
        for t, (c0, c1, c2, c3) in enumerate(columns):
            tile = tiles[t] - ((c0 * new[0] + c1 * new[1]) + (c2 * new[2] + c3 * new[3]))
            if t == home:
                for q in range(4):
                    tile = jnp.where(rows == first + q, new[q], tile)
            tiles[t] = tile
    return jnp.concatenate(tiles, axis=0)


def inverse_of(gram):
    rank = gram.shape[0]
    eye = (lax.broadcasted_iota(jnp.int32, gram.shape, 0) == lane_numbers(gram.shape)).astype(F32)
    return eliminate(jnp.concatenate([gram, eye], axis=1), rank)[:, rank:]


def total(refs):
    out = refs[0][...]
    for ref in refs[1:]:
        out = out + ref[...]
    return out


def first_inverse_kernel(v_gram_ref, *refs):
    *terms, w_gram_ref, inverse_ref = refs
    w_gram = total(terms)
    w_gram_ref[...] = w_gram
    inverse_ref[...] = inverse_of(w_gram * v_gram_ref[...])


def first_inverse(v_gram, w_grams):
    out = jax.ShapeDtypeStruct(v_gram.shape, F32)
    return pl.pallas_call(
        first_inverse_kernel,
        in_specs=[VMEM_SPEC] * (1 + len(w_grams)),
        out_specs=[VMEM_SPEC] * 2,
        out_shape=[out, out],
        compiler_params=parameters(LIMIT),
        cost_estimate=SHORT,
        name="first_inverse",
    )(v_gram, *w_grams)


def sweep_all(frames, rank, fine):
    patients = range(frames.shape[0])
    if fine:
        both = [jnp.concatenate(two_parts(frames[p]), axis=0) for p in patients]
        blocks = [low_dot(x, x, ROWS_BY_ROWS) for x in both]
        blocks = [x[:rank] + x[rank:] for x in blocks]
        grams = [x + pltpu.roll(x, rank, 1) for x in blocks]
        moved = [low_dot(jnp.concatenate(two_parts(g), axis=0), x) for g, x in zip(grams, both)]
        moved = [x[:rank] + x[rank:] for x in moved]
    else:
        first = [frames[p].astype(BF16) for p in patients]
        grams = [low_dot(x, x, ROWS_BY_ROWS).astype(BF16) for x in first]
        moved = [low_dot(g, x) for g, x in zip(grams, first)]
    for p in patients:
        frames[p] = 1.5 * frames[p] - 0.5 * moved[p]


def frames_kernel(layouts, part, share, place, counts_ref, h_ref, w_ref, v_gram_ref, before_ref, own_ref, *refs):
    coded, refs = refs[: len(layouts)], refs[len(layouts) :]
    frames_ref, terms_ref, v_total_ref, proj, frames = refs
    count, rank, slots = frames.shape
    patients = range(count)
    first = feature_of(place) * share + part * count
    pieces = [own_ref[p] for p in patients]
    v_gram = v_gram_ref[...]
    for code, layout in zip(coded, layouts):
        payload = Payload(code, layout, count, rank, part == 0)
        pieces = [pieces[p] + payload.proj(0, p) for p in patients]
        if part == 0:
            v_gram = v_gram + payload.gram()
    v_total_ref[...] = v_gram
    for p in patients:
        proj[p] = pieces[p]
    weights = [w_ref[pl.ds(first + p, 1), :] for p in patients]
    mixed = [high_dot(h_ref[...] * weights[p], pieces[p]) for p in patients]
    lanes = lane_numbers((rank, slots))
    mixed = [jnp.where(lanes < counts_ref[first + p], mixed[p], 0.0) for p in patients]
    energy = [jnp.sum(jnp.sum(x * x, axis=1, keepdims=True), axis=0, keepdims=True) for x in mixed]
    for p in patients:
        frames[p] = mixed[p] * lax.rsqrt(energy[p] + epsilon)

    def sweep(fine, step, carry):
        sweep_all(frames, rank, fine)
        return carry

    lax.fori_loop(0, COARSE_STEPS, functools.partial(sweep, False), 0, unroll=True)
    lax.fori_loop(COARSE_STEPS, NS_STEPS, functools.partial(sweep, True), 0, unroll=3)
    low = [frames[p].astype(BF16) for p in patients]
    for p in patients:
        frames_ref[p] = low[p]
    products = [jnp.concatenate(three_parts(proj[p]), axis=0) for p in patients]
    products = [low_dot(low[p], products[p], ROWS_BY_ROWS) for p in patients]
    terms = before_ref[...] if part else jnp.zeros((rank, rank), F32)
    for p in patients:
        product = products[p][:, :rank] + (products[p][:, rank : 2 * rank] + products[p][:, 2 * rank :])
        terms = terms + product * weights[p]
    terms_ref[...] = terms


def own_frames(layouts, part, n_parts, place, counts, h_start, w_start, v_gram, before, own, coded):
    count, rank, slots = own.shape
    share = count * n_parts
    return pl.pallas_call(
        functools.partial(frames_kernel, layouts, part, share),
        in_specs=[SMEM_SPEC] * 2 + [VMEM_SPEC] * (5 + len(coded)),
        out_specs=[VMEM_SPEC] * 3,
        out_shape=[
            jax.ShapeDtypeStruct(own.shape, BF16),
            jax.ShapeDtypeStruct((rank, rank), F32),
            jax.ShapeDtypeStruct((rank, rank), F32),
        ],
        scratch_shapes=[pltpu.VMEM(own.shape, F32)] * 2,
        compiler_params=parameters(LIMIT),
        cost_estimate=SHORT,
        name="own_frames",
    )(place, counts, h_start, w_start, v_gram, before, own, *coded)


def projected_kernel(items, place, visits_ref, *refs):
    frames_refs, outs, token_ref = refs[: len(items)], refs[-2 * len(items) - 1 : -1], refs[-1]
    token_ref[...] = jnp.zeros_like(token_ref)
    for i, (slots, first) in enumerate(items):
        total_count, rank, _ = frames_refs[i].shape
        count = total_count // len(slots)
        for p in range(total_count):
            rows = pl.ds(p * rank, rank)
            owner = feature_of(place) ^ slots[p // count]
            product = low_dot(frames_refs[i][p], visits_ref[owner, first + p % count])
            outs[2 * i][rows, :], outs[2 * i + 1][rows, :] = two_parts(product)


def join_kernel(count, *refs):
    out_ref = refs[-1]
    first = 0
    for part in refs[:count]:
        out_ref[first : first + part.shape[0]] = part[...]
        first += part.shape[0]


def join(parts, after):
    if len(parts) == 1:
        return parts[0]
    return pl.pallas_call(
        functools.partial(join_kernel, len(parts)),
        in_specs=[VMEM_SPEC] * len(parts) + [ANY_SPEC] * len(after),
        out_specs=VMEM_SPEC,
        out_shape=jax.ShapeDtypeStruct((sum(x.shape[0] for x in parts),) + parts[0].shape[1:], parts[0].dtype),
        compiler_params=parameters(LIMIT),
        cost_estimate=SHORT,
        name="join_frames",
    )(*parts, *after)


def project_frames(items, place, frames, visits, after):
    width = visits.shape[-1]
    outs = []
    for item in items:
        count, rank, _ = frames[item].shape
        outs += [jax.ShapeDtypeStruct((count * rank, width), BF16)] * 2
    *parts, token = pl.pallas_call(
        functools.partial(projected_kernel, items),
        in_specs=[SMEM_SPEC] + [VMEM_SPEC] * (1 + len(items)) + [ANY_SPEC] * len(after),
        out_specs=[VMEM_SPEC] * (len(outs) + 1),
        out_shape=outs + [jax.ShapeDtypeStruct((8, LANES), F32)],
        compiler_params=parameters(LIMIT),
        cost_estimate=SHORT,
        name="project_frames",
    )(place, visits, *[frames[item] for item in items], *after)
    return {item: parts[2 * i : 2 * i + 2] for i, item in enumerate(items)}, token


def next_h_kernel(n_terms, n_slots, place, *refs):
    inverse_ref, w_ref, _, result_ref, h_ref, factor_ref = refs[n_terms:]
    h_next = high_dot(total(refs[:n_terms]), inverse_ref[...])
    result_ref[...] = h_next
    h_ref[...] = h_next
    rank = h_next.shape[0]
    patients = w_ref.shape[0]
    share = patients // n_slots
    h_rows = h_next.T
    w_rows = jnp.concatenate([w_ref[...], jnp.zeros((LANES - patients, rank), F32)], axis=0)
    w_columns = w_rows.T
    for slot in range(n_slots):
        first = (feature_of(place) ^ slot) * share
        columns = pltpu.roll(w_columns, jnp.where(first == 0, 0, LANES - first), 1)
        factor = jnp.concatenate([h_rows * columns[:, p : p + 1] for p in range(share)], axis=1)
        factor_ref[slot] = jnp.concatenate(three_parts(factor), axis=0)


def next_h(place, terms, inverse, w_start, n_slots, after):
    patients, rank = w_start.shape
    share = patients // n_slots
    return pl.pallas_call(
        functools.partial(next_h_kernel, len(terms), n_slots),
        in_specs=[SMEM_SPEC] + [VMEM_SPEC] * (len(terms) + 2) + [ANY_SPEC],
        out_specs=[VMEM_SPEC] * 3,
        out_shape=[
            jax.ShapeDtypeStruct(inverse.shape, F32),
            jax.ShapeDtypeStruct(inverse.shape, F32),
            jax.ShapeDtypeStruct((n_slots, 3 * rank, share * rank), BF16),
        ],
        compiler_params=parameters(LIMIT),
        cost_estimate=SHORT,
        name="next_h",
    )(place, *terms, inverse, w_start, after)


def second_inverse_kernel(h_ref, w_gram_ref, gram_ref, inverse_ref):
    gram = high_dot(h_ref[...], h_ref[...], COLS_BY_COLS)
    gram_ref[...] = gram
    inverse_ref[...] = inverse_of(gram * w_gram_ref[...])


def second_inverse(h_next, w_gram):
    out = jax.ShapeDtypeStruct(w_gram.shape, F32)
    return pl.pallas_call(
        second_inverse_kernel,
        out_shape=[out, out],
        compiler_params=parameters(LIMIT),
        cost_estimate=SHORT,
        name="second_inverse",
    )(h_next, w_gram)


def v_terms_kernel(items, place, factor_ref, *refs):
    *parts, keep_ref, send_ref, terms_ref = refs
    rank, width = terms_ref.shape
    half = width // 2
    total = None
    for i, (slots, first) in enumerate(items):
        count = parts[2 * i].shape[0] // len(slots)
        columns = pl.ds(first * rank, count)
        for k, slot in enumerate(slots):
            rows = pl.ds(k * count, count)
            large = low_dot(factor_ref[slot, :, columns], parts[2 * i][rows, :])
            small = low_dot(factor_ref[slot, : 2 * rank, columns], parts[2 * i + 1][rows, :])
            terms = large[:rank] + (large[rank : 2 * rank] + small[:rank]) + (large[2 * rank :] + small[rank:])
            total = terms if total is None else total + terms
    terms_ref[...] = total
    keep_ref[...] = terms_ref[:, pl.ds(pl.multiple_of(core_of(place) * half, half), half)]
    send_ref[...] = terms_ref[:, pl.ds(pl.multiple_of((1 - core_of(place)) * half, half), half)]


def all_v_terms(items, place, factor, projected):
    width = projected[0].shape[1]
    rank = factor.shape[1] // 3
    half = (rank, width // 2)
    return pl.pallas_call(
        functools.partial(v_terms_kernel, items),
        in_specs=[SMEM_SPEC] + [VMEM_SPEC] * (1 + len(projected)),
        out_specs=[VMEM_SPEC] * 2,
        out_shape=[jax.ShapeDtypeStruct(half, F32)] * 2,
        scratch_shapes=[pltpu.VMEM((rank, width), F32)],
        compiler_params=parameters(LIMIT),
        cost_estimate=SHORT,
        name="v_terms",
    )(place, factor, *projected)


def next_v_kernel(items, share, place, own_ref, other_ref, inverse_ref, h_ref, *refs):
    *parts, v_ref, sums_ref, v_parts = refs
    rank = inverse_ref.shape[0]
    upper = core_of(place) == 1
    left = jnp.where(upper, other_ref[...], own_ref[...])
    right = jnp.where(upper, own_ref[...], other_ref[...])
    v_rows = high_dot(inverse_ref[...], jnp.concatenate([left, right], axis=1))
    v_ref[...] = v_rows
    v_parts[...] = jnp.concatenate(two_parts(v_rows), axis=0)
    weights = jnp.concatenate([h_ref[...]] * 2, axis=1)
    gram = low_dot(v_parts[...], v_parts[...], ROWS_BY_ROWS)
    gram = gram[:rank, :rank] + (gram[:rank, rank:] + gram[rank:, :rank])
    sums_ref[...] = jnp.concatenate([jnp.zeros((rank, rank), F32), gram], axis=1)
    for i, (slots, done) in enumerate(items):
        seen = low_dot(parts[2 * i][...], v_parts[...], ROWS_BY_ROWS)
        seen = seen + low_dot(parts[2 * i + 1][...], v_parts[...], ROWS_BY_ROWS)
        count = seen.shape[0] // rank // len(slots)
        for p in range(seen.shape[0] // rank):
            patient = (feature_of(place) ^ slots[p // count]) * share + done + p % count
            row = jnp.sum(seen[p * rank : (p + 1) * rank] * weights, axis=0, keepdims=True)
            sums_ref[pl.ds(patient, 1), :rank] = row[:, :rank] + row[:, rank:]


def next_v(items, share, place, own, other, inverse, h_next, projected):
    width = projected[0].shape[1]
    rank = inverse.shape[0]
    return pl.pallas_call(
        functools.partial(next_v_kernel, items, share),
        in_specs=[SMEM_SPEC] + [VMEM_SPEC] * (4 + len(projected)),
        out_specs=[VMEM_SPEC] * 2,
        out_shape=[
            jax.ShapeDtypeStruct((rank, width), F32),
            jax.ShapeDtypeStruct((rank, 2 * rank), F32),
        ],
        scratch_shapes=[pltpu.VMEM((2 * rank, width), BF16)],
        compiler_params=parameters(LIMIT),
        cost_estimate=SHORT,
        name="next_v",
    )(place, own, other, inverse, h_next, *projected)


def next_w_kernel(n_sums, *refs):
    gram_ref, w_ref = refs[n_sums:]
    patients, rank = w_ref.shape
    sums = total(refs[:n_sums])
    table = jnp.concatenate([sums[:, rank:] * gram_ref[...], sums.T[:rank]], axis=1)
    w_ref[...] = eliminate(table, rank).T[rank : rank + patients]


def next_w(sums, h_gram, patients):
    rank = h_gram.shape[0]
    return pl.pallas_call(
        functools.partial(next_w_kernel, len(sums)),
        out_shape=jax.ShapeDtypeStruct((patients, rank), F32),
        compiler_params=parameters(LIMIT),
        cost_estimate=SHORT,
        name="next_w",
    )(*sums, h_gram)


def swap(x, axis, slot):
    pairs = [(i, i ^ slot) for i in range(lax.axis_size(axis))]
    return lax.ppermute(x, axis, pairs)


def all_terms(x, axis):
    n = lax.axis_size(axis)
    if n > 4:
        return [lax.psum(x, axis)]
    return [x] + [swap(x, axis, s) for s in range(1, n)]


def staged_terms(x, axis, after):
    n = lax.axis_size(axis)
    step = 1
    while 2 * step < n:
        x = add(x, swap(x, axis, step), after)
        step *= 2
    return [x, swap(x, axis, step)]


def add_kernel(a_ref, b_ref, *refs):
    refs[-1][...] = a_ref[...] + b_ref[...]


def add(a, b, after):
    return pl.pallas_call(
        add_kernel,
        in_specs=[VMEM_SPEC] * 2 + [ANY_SPEC] * len(after),
        out_specs=VMEM_SPEC,
        out_shape=jax.ShapeDtypeStruct(a.shape, a.dtype),
        compiler_params=parameters(LIMIT),
        cost_estimate=SHORT,
        name="add_terms",
    )(a, b, *after)


def patient_halves(keep, send, after):
    own = add(keep, swap(send, "patient", 1), [])
    step = 2
    while step < lax.axis_size("patient"):
        own = add(own, swap(own, "patient", step), [after])
        step *= 2
    return own, swap(own, "patient", 1)


def on_device(visits, visit_counts, h_start, v_start, w_start):
    n = lax.axis_size("feature")
    patients, slots, width = visits.shape
    share = patients // n
    place = (2 * lax.axis_index("feature") + (lax.axis_index("patient") & 1)).astype(jnp.int32).reshape(1)
    by_owner = visits.reshape(n, share, slots, width)
    in_hbm = pltpu.with_memory_space_constraint(by_owner, pltpu.HBM)
    v_rows = pltpu.with_memory_space_constraint(v_start.T, pltpu.HBM)

    n_parts = 2 if share % 2 == 0 else 1
    count = share // n_parts
    firsts = [part * count for part in range(n_parts)]
    bits = [1 << i for i in range(n.bit_length() - 1)]
    v_near = v_start.T

    def send(bit):
        return [slot for slot in range(n) if slot & bit and not slot & (bit - 1)]

    def receive(bit):
        return [slot ^ bit for slot in send(bit)]

    w_grams = staged_terms(own_w_gram(w_start), "patient", [])
    arrived = [[] for _ in firsts]
    for i, bit in enumerate(bits):
        layouts = [receive(before) for before in bits[:i]]
        for part, first in enumerate(firsts):
            if i == 0 and part == 0:
                code = first_projection(send(bit), count, place, in_hbm, v_rows)
            else:
                after = [w_grams[part]] if i else []
                code = next_projection(
                    send(bit), first, count, layouts, place, by_owner, v_near, arrived[part], after
                )
            arrived[part] = arrived[part] + [swap(code, "feature", bit)]
    own, v_gram = project_own(n_parts, place, by_owner, v_near)
    h_local = v_gram

    layouts = [receive(bit) for bit in bits]
    frames = [[] for _ in firsts]

    def double(part, after):
        for bit in bits[::-1]:
            slots = tuple(slot ^ bit for group, _ in frames[part] for slot in group)
            frames[part].append((slots, swap(join([x for _, x in frames[part]], after), "feature", bit)))

    def project_groups(groups, after):
        arrays = {(frames[part][k][0], firsts[part]): frames[part][k][1] for part, k in groups}
        return project_frames(list(arrays), place, arrays, by_owner, after)

    for part, first in enumerate(firsts):
        low, h_local, v_total = own_frames(
            layouts, part, n_parts, place, visit_counts, h_start, w_start, v_gram, h_local, own[part], arrived[part]
        )
        v_gram = v_total if first == 0 else v_gram
        frames[part].append(((0,), low))
        if part < n_parts - 1:
            double(part, [])

    last = len(bits)
    projected, token = project_groups([(part, 0) for part in range(n_parts)], [])
    w_gram, inverse = first_inverse(v_gram, w_grams)
    h_sums = staged_terms(h_local, "patient", [token])
    h_sum = add(*h_sums, [inverse])
    double(n_parts - 1, [h_sum])
    order = [(part, k) for part in range(n_parts) for k in range(1, last + 1)]
    more, token = project_groups(order[:1], [h_sum])
    projected |= more
    h_terms = staged_terms(h_sum, "feature", [token])
    after = h_terms[:1]
    for group in order[1:]:
        more, token = project_groups([group], after)
        projected |= more
        after = [token]
    h_result, h_next, factor = next_h(place, h_terms, inverse, w_start, n, token)

    items = list(projected)
    flat = [x for item in items for x in projected[item]]
    keep, send = all_v_terms(items, place, factor, flat)
    h_gram, second = second_inverse(h_next, w_gram)
    own_terms, other_terms = patient_halves(keep, send, second)
    v_next, sums = next_v(items, share, place, own_terms, other_terms, second, h_next, flat)
    w_next = next_w(all_terms(sums, "feature"), h_gram, patients)
    return (h_result, v_next.T, w_next)


def solution(mesh):
    return jax.shard_map(
        on_device,
        mesh=mesh,
        in_specs=(
            P(("groups", "patient"), None, "feature"),
            P(("groups", "patient")),
            P(),
            P("feature", None),
            P(("groups", "patient"), None),
        ),
        out_specs=(P(None, "groups"), P("feature", "groups"), P("patient", "groups")),
        check_vma=False,
    )
```

```python
import functools

import jax
import jax.numpy as jnp
from jax import lax
from jax.experimental import pallas as pl
from jax.experimental.pallas import tpu as pltpu
from jax.sharding import PartitionSpec as P

NS_STEPS = 12
LANES = 128
LEVELS = 32000.0
COARSE_STEPS = 3
SHORT = pl.CostEstimate(flops=1000, bytes_accessed=1000, transcendentals=0)

epsilon = 1e-06
HIGH = lax.Precision.HIGHEST
F32 = jnp.float32
BF16 = jnp.bfloat16
MIB = 1024 * 1024

ROWS_BY_COLS = (((1,), (0,)), ((), ()))
ROWS_BY_ROWS = (((1,), (1,)), ((), ()))
COLS_BY_COLS = (((0,), (0,)), ((), ()))


def low_dot(a, b, dims=ROWS_BY_COLS):
    return lax.dot_general(a, b, dims, preferred_element_type=F32)


def high_dot(a, b, dims=ROWS_BY_COLS):
    return lax.dot_general(a, b, dims, precision=HIGH, preferred_element_type=F32)


def two_parts(x):
    first = x.astype(BF16)
    return first, (x - first.astype(F32)).astype(BF16)


def three_parts(x):
    first = x.astype(BF16)
    rest = x - first.astype(F32)
    second = rest.astype(BF16)
    return first, second, (rest - second.astype(F32)).astype(BF16)


def feature_of(place):
    return place[0] >> 1


def core_of(place):
    return place[0] & 1


def lane_numbers(shape):
    return lax.broadcasted_iota(jnp.int32, shape, len(shape) - 1)


ANY_SPEC = pl.BlockSpec(memory_space=pl.ANY)
HBM_SPEC = pl.BlockSpec(memory_space=pltpu.HBM)


def parameters(mib):
    return pltpu.CompilerParams(vmem_limit_bytes=mib * MIB)


LIMIT = 8
VMEM_SPEC = pl.BlockSpec(memory_space=pltpu.VMEM)
SMEM_SPEC = pl.BlockSpec(memory_space=pltpu.SMEM)


def exponent_rows(total_count):
    return -(-(total_count + 1) // 16) * 16


def payload_shape(total_count, rank, slots, with_gram):
    return (total_count * rank + (rank // 2 if with_gram else 0) + exponent_rows(total_count), slots)


def row_exponent(x):
    top = jnp.max(jnp.abs(x), axis=1, keepdims=True)
    return jnp.ceil(jnp.log2(jnp.maximum(top, 1e-30)))


class Payload:
    def __init__(self, ref, slots, count, rank, with_gram):
        self.ref, self.slots, self.count, self.rank, self.with_gram = ref, slots, count, rank, with_gram
        self.entries = len(slots) * count
        gram_rows = rank // 2 if with_gram else 0
        exponents = self.rows(self.entries * rank + gram_rows, exponent_rows(self.entries))
        self.steps = jnp.exp2(exponents[:, :LANES].T[:rank]) * (1.0 / LEVELS)

    def rows(self, first, number):
        return self.ref[pl.ds(first, number), :].astype(jnp.int32).astype(F32)

    def proj(self, slot, p):
        entry = self.slots.index(slot) * self.count + p
        return self.rows(entry * self.rank, self.rank) * self.steps[:, entry : entry + 1]

    def gram(self):
        rank = self.rank
        digits = self.rows(self.entries * rank, rank // 2)
        digits = jnp.concatenate([digits[:, : 2 * rank], digits[:, 2 * rank :]], axis=0)
        return (digits[:, :rank] + digits[:, rank:] * (0.5 / LEVELS)) * self.steps[:, self.entries : self.entries + 1]


def encode(values, gram, coded_ref, rank):
    count = len(values)
    lanes = lane_numbers((rank, LANES))
    exponents = jnp.zeros((rank, LANES), F32)
    for p, value in enumerate(values):
        proj = value()
        exponent = row_exponent(proj)
        coded = jnp.floor(proj * (LEVELS / jnp.exp2(exponent)) + 0.5)
        coded_ref[pl.ds(p * rank, rank), :] = coded.astype(jnp.int32).astype(jnp.int16)
        exponents = jnp.where(lanes == p, exponent, exponents)
    end = count * rank
    if gram is not None:
        exponent = row_exponent(gram)
        scaled = gram * (LEVELS / jnp.exp2(exponent))
        whole = jnp.floor(scaled + 0.5)
        rest = jnp.floor((scaled - whole) * (2 * LEVELS) + 0.5)
        digits = jnp.concatenate([whole, rest], axis=1)
        digits = jnp.concatenate([digits[: rank // 2], digits[rank // 2 :]], axis=1)
        coded_ref[pl.ds(end, rank // 2), :] = digits.astype(jnp.int32).astype(jnp.int16)
        exponents = jnp.where(lanes == count, exponent, exponents)
        end += rank // 2
    rows = exponent_rows(count)
    last = jnp.concatenate([exponents.T[:rows], jnp.zeros((rows, coded_ref.shape[1] - rank), F32)], axis=1)
    coded_ref[pl.ds(end, rows), :] = last.astype(jnp.int32).astype(jnp.int16)


def first_projection_kernel(slots, place, v_hbm, visits_ref, coded_ref, v_ref, buffers, sems, v_sem):
    count = buffers.shape[1]
    v_copy = pltpu.make_async_copy(v_hbm, v_ref, v_sem)
    v_copy.start()
    copies = [
        pltpu.make_async_copy(visits_ref.at[feature_of(place) ^ slot, pl.ds(0, count)], buffers.at[i], sems.at[i])
        for i, slot in enumerate(slots)
    ]
    for copy in copies:
        copy.start()
    v_copy.wait()
    gram = low_dot(v_ref[...], v_ref[...], ROWS_BY_ROWS)

    def value(i, p):
        if p == 0:
            copies[i].wait()
        return low_dot(v_ref[...], buffers[i, p], ROWS_BY_ROWS)

    values = [functools.partial(value, i, p) for i in range(len(slots)) for p in range(count)]
    encode(values, gram, coded_ref, v_ref.shape[0])


def first_projection(slots, count, place, visits, v_rows):
    width = visits.shape[3]
    rank = v_rows.shape[0]
    return pl.pallas_call(
        functools.partial(first_projection_kernel, slots),
        in_specs=[SMEM_SPEC, HBM_SPEC, HBM_SPEC],
        out_specs=VMEM_SPEC,
        out_shape=jax.ShapeDtypeStruct(payload_shape(len(slots) * count, rank, visits.shape[2], True), jnp.int16),
        scratch_shapes=[
            pltpu.VMEM(v_rows.shape, BF16),
            pltpu.VMEM((len(slots), count) + visits.shape[2:], BF16),
            pltpu.SemaphoreType.DMA((len(slots),)),
            pltpu.SemaphoreType.DMA,
        ],
        compiler_params=parameters(LIMIT),
        cost_estimate=SHORT,
        name="project_first",
    )(place, v_rows, visits)


def next_projection_kernel(slots, first, count, layouts, place, v_ref, visits_ref, *refs):
    coded_ref = refs[-1]
    rank = v_ref.shape[0]
    arrived = [Payload(ref, layout, count, rank, first == 0) for ref, layout in zip(refs, layouts)]

    def value(slot, p):
        proj = low_dot(v_ref[...], visits_ref[feature_of(place) ^ slot, first + p], ROWS_BY_ROWS)
        for payload in arrived:
            proj = proj + payload.proj(slot, p)
        return proj

    gram = None
    if first == 0:
        gram = low_dot(v_ref[...], v_ref[...], ROWS_BY_ROWS)
        for payload in arrived:
            gram = gram + payload.gram()
    encode([functools.partial(value, slot, p) for slot in slots for p in range(count)], gram, coded_ref, rank)


def next_projection(slots, first, count, layouts, place, visits, v_rows, arrived, after):
    rank = v_rows.shape[0]
    return pl.pallas_call(
        functools.partial(next_projection_kernel, slots, first, count, layouts),
        in_specs=[SMEM_SPEC] + [VMEM_SPEC] * (2 + len(arrived)) + [ANY_SPEC] * len(after),
        out_specs=VMEM_SPEC,
        out_shape=jax.ShapeDtypeStruct(payload_shape(len(slots) * count, rank, visits.shape[2], first == 0), jnp.int16),
        compiler_params=parameters(LIMIT),
        cost_estimate=SHORT,
        name="project_next",
    )(place, v_rows, visits, *arrived, *after)


def w_gram_kernel(w_ref, gram_ref):
    gram_ref[...] = high_dot(w_ref[...], w_ref[...], COLS_BY_COLS)


def own_w_gram(w_start):
    rank = w_start.shape[1]
    return pl.pallas_call(
        w_gram_kernel,
        in_specs=[VMEM_SPEC],
        out_specs=VMEM_SPEC,
        out_shape=jax.ShapeDtypeStruct((rank, rank), F32),
        compiler_params=parameters(LIMIT),
        cost_estimate=SHORT,
        name="own_w_gram",
    )(w_start)


def own_projection_kernel(place, v_ref, visits_ref, *refs):
    *proj_refs, v_gram_ref = refs
    count = visits_ref.shape[1] // len(proj_refs)
    for p in range(visits_ref.shape[1]):
        proj_refs[p // count][p % count] = low_dot(v_ref[...], visits_ref[feature_of(place), p], ROWS_BY_ROWS)
    v_gram_ref[...] = low_dot(v_ref[...], v_ref[...], ROWS_BY_ROWS)


def project_own(n_parts, place, visits, v_rows):
    _, share, slots, width = visits.shape
    rank = v_rows.shape[0]
    proj = jax.ShapeDtypeStruct((share // n_parts, rank, slots), F32)
    *own, v_gram = pl.pallas_call(
        own_projection_kernel,
        in_specs=[SMEM_SPEC] + [VMEM_SPEC] * 2,
        out_specs=[VMEM_SPEC] * (n_parts + 1),
        out_shape=[proj] * n_parts + [jax.ShapeDtypeStruct((rank, rank), F32)],
        compiler_params=parameters(LIMIT),
        cost_estimate=SHORT,
        name="project_own",
    )(place, v_rows, visits)
    return own, v_gram


def pair_inverse(a, b, c, d):
    scale = 1.0 / (a * d - b * c)
    return d * scale, b * scale, c * scale, a * scale


def eliminate(table, rank):
    tiles = [table[8 * t : 8 * t + 8] for t in range(rank // 8)]
    rows = lax.broadcasted_iota(jnp.int32, tiles[0].shape, 0)
    for i in range(0, rank, 4):
        columns = [[jnp.broadcast_to(t[:, i + q : i + q + 1], t.shape) for q in range(4)] for t in tiles]
        home, first = i // 8, i % 8
        r0, r1, r2, r3 = (tiles[home][first + q : first + q + 1] for q in range(4))
        m = [[columns[home][q][first + p : first + p + 1] for q in range(4)] for p in range(4)]
        d, b, c, a = pair_inverse(m[0][0], m[0][1], m[1][0], m[1][1])
        q02, q03 = d * m[0][2] - b * m[1][2], d * m[0][3] - b * m[1][3]
        q12, q13 = a * m[1][2] - c * m[0][2], a * m[1][3] - c * m[0][3]
        y0, y1 = d * r0 - b * r1, a * r1 - c * r0
        z2 = r2 - (m[2][0] * y0 + m[2][1] * y1)
        z3 = r3 - (m[3][0] * y0 + m[3][1] * y1)
        d, b, c, a = pair_inverse(
            m[2][2] - (m[2][0] * q02 + m[2][1] * q12),
            m[2][3] - (m[2][0] * q03 + m[2][1] * q13),
            m[3][2] - (m[3][0] * q02 + m[3][1] * q12),
            m[3][3] - (m[3][0] * q03 + m[3][1] * q13),
        )
        n2, n3 = d * z2 - b * z3, a * z3 - c * z2
        new = [y0 - (q02 * n2 + q03 * n3), y1 - (q12 * n2 + q13 * n3), n2, n3]
        for t, (c0, c1, c2, c3) in enumerate(columns):
            tile = tiles[t] - ((c0 * new[0] + c1 * new[1]) + (c2 * new[2] + c3 * new[3]))
            if t == home:
                for q in range(4):
                    tile = jnp.where(rows == first + q, new[q], tile)
            tiles[t] = tile
    return jnp.concatenate(tiles, axis=0)


def inverse_of(gram):
    rank = gram.shape[0]
    eye = (lax.broadcasted_iota(jnp.int32, gram.shape, 0) == lane_numbers(gram.shape)).astype(F32)
    return eliminate(jnp.concatenate([gram, eye], axis=1), rank)[:, rank:]


def total(refs):
    out = refs[0][...]
    for ref in refs[1:]:
        out = out + ref[...]
    return out


def first_inverse_kernel(v_gram_ref, *refs):
    *terms, _, w_gram_ref, inverse_ref = refs
    w_gram = total(terms)
    w_gram_ref[...] = w_gram
    inverse_ref[...] = inverse_of(w_gram * v_gram_ref[...])


def first_inverse(v_gram, w_grams, after):
    out = jax.ShapeDtypeStruct(v_gram.shape, F32)
    return pl.pallas_call(
        first_inverse_kernel,
        in_specs=[VMEM_SPEC] * (1 + len(w_grams)) + [ANY_SPEC],
        out_specs=[VMEM_SPEC] * 2,
        out_shape=[out, out],
        compiler_params=parameters(LIMIT),
        cost_estimate=SHORT,
        name="first_inverse",
    )(v_gram, *w_grams, after)


def sweep_all(frames, rank, fine):
    patients = range(frames.shape[0])
    if fine:
        both = [jnp.concatenate(two_parts(frames[p]), axis=0) for p in patients]
        blocks = [low_dot(x, x, ROWS_BY_ROWS) for x in both]
        blocks = [x[:rank] + x[rank:] for x in blocks]
        grams = [x + pltpu.roll(x, rank, 1) for x in blocks]
        moved = [low_dot(jnp.concatenate(two_parts(g), axis=0), x) for g, x in zip(grams, both)]
        moved = [x[:rank] + x[rank:] for x in moved]
    else:
        first = [frames[p].astype(BF16) for p in patients]
        grams = [low_dot(x, x, ROWS_BY_ROWS).astype(BF16) for x in first]
        moved = [low_dot(g, x) for g, x in zip(grams, first)]
    for p in patients:
        frames[p] = 1.5 * frames[p] - 0.5 * moved[p]


def frames_kernel(layouts, part, share, place, counts_ref, h_ref, w_ref, v_gram_ref, before_ref, own_ref, *refs):
    coded, refs = refs[: len(layouts)], refs[len(layouts) :]
    frames_ref, terms_ref, v_total_ref, proj, frames = refs
    count, rank, slots = frames.shape
    patients = range(count)
    first = feature_of(place) * share + part * count
    pieces = [own_ref[p] for p in patients]
    v_gram = v_gram_ref[...]
    for code, layout in zip(coded, layouts):
        payload = Payload(code, layout, count, rank, part == 0)
        pieces = [pieces[p] + payload.proj(0, p) for p in patients]
        if part == 0:
            v_gram = v_gram + payload.gram()
    v_total_ref[...] = v_gram
    for p in patients:
        proj[p] = pieces[p]
    weights = [w_ref[pl.ds(first + p, 1), :] for p in patients]
    mixed = [high_dot(h_ref[...] * weights[p], pieces[p]) for p in patients]
    lanes = lane_numbers((rank, slots))
    mixed = [jnp.where(lanes < counts_ref[first + p], mixed[p], 0.0) for p in patients]
    energy = [jnp.sum(jnp.sum(x * x, axis=1, keepdims=True), axis=0, keepdims=True) for x in mixed]
    for p in patients:
        frames[p] = mixed[p] * lax.rsqrt(energy[p] + epsilon)

    def sweep(fine, step, carry):
        sweep_all(frames, rank, fine)
        return carry

    lax.fori_loop(0, COARSE_STEPS, functools.partial(sweep, False), 0, unroll=True)
    lax.fori_loop(COARSE_STEPS, NS_STEPS, functools.partial(sweep, True), 0, unroll=3)
    low = [frames[p].astype(BF16) for p in patients]
    for p in patients:
        frames_ref[p] = low[p]
    products = [jnp.concatenate(three_parts(proj[p]), axis=0) for p in patients]
    products = [low_dot(low[p], products[p], ROWS_BY_ROWS) for p in patients]
    terms = before_ref[...] if part else jnp.zeros((rank, rank), F32)
    for p in patients:
        product = products[p][:, :rank] + (products[p][:, rank : 2 * rank] + products[p][:, 2 * rank :])
        terms = terms + product * weights[p]
    terms_ref[...] = terms


def own_frames(layouts, part, n_parts, place, counts, h_start, w_start, v_gram, before, own, coded):
    count, rank, slots = own.shape
    share = count * n_parts
    return pl.pallas_call(
        functools.partial(frames_kernel, layouts, part, share),
        in_specs=[SMEM_SPEC] * 2 + [VMEM_SPEC] * (5 + len(coded)),
        out_specs=[VMEM_SPEC] * 3,
        out_shape=[
            jax.ShapeDtypeStruct(own.shape, BF16),
            jax.ShapeDtypeStruct((rank, rank), F32),
            jax.ShapeDtypeStruct((rank, rank), F32),
        ],
        scratch_shapes=[pltpu.VMEM(own.shape, F32)] * 2,
        compiler_params=parameters(LIMIT),
        cost_estimate=SHORT,
        name="own_frames",
    )(place, counts, h_start, w_start, v_gram, before, own, *coded)


def projected_kernel(items, place, visits_ref, *refs):
    frames_refs, outs, token_ref = refs[: len(items)], refs[-2 * len(items) - 1 : -1], refs[-1]
    token_ref[...] = jnp.zeros_like(token_ref)
    for i, (slots, first) in enumerate(items):
        total_count, rank, _ = frames_refs[i].shape
        count = total_count // len(slots)
        for p in range(total_count):
            rows = pl.ds(p * rank, rank)
            owner = feature_of(place) ^ slots[p // count]
            product = low_dot(frames_refs[i][p], visits_ref[owner, first + p % count])
            outs[2 * i][rows, :], outs[2 * i + 1][rows, :] = two_parts(product)


def join_kernel(count, *refs):
    out_ref = refs[-1]
    first = 0
    for part in refs[:count]:
        out_ref[first : first + part.shape[0]] = part[...]
        first += part.shape[0]


def join(parts, after):
    if len(parts) == 1:
        return parts[0]
    return pl.pallas_call(
        functools.partial(join_kernel, len(parts)),
        in_specs=[VMEM_SPEC] * len(parts) + [ANY_SPEC] * len(after),
        out_specs=VMEM_SPEC,
        out_shape=jax.ShapeDtypeStruct((sum(x.shape[0] for x in parts),) + parts[0].shape[1:], parts[0].dtype),
        compiler_params=parameters(LIMIT),
        cost_estimate=SHORT,
        name="join_frames",
    )(*parts, *after)


def project_frames(items, place, frames, visits, after):
    width = visits.shape[-1]
    outs = []
    for item in items:
        count, rank, _ = frames[item].shape
        outs += [jax.ShapeDtypeStruct((count * rank, width), BF16)] * 2
    *parts, token = pl.pallas_call(
        functools.partial(projected_kernel, items),
        in_specs=[SMEM_SPEC] + [VMEM_SPEC] * (1 + len(items)) + [ANY_SPEC] * len(after),
        out_specs=[VMEM_SPEC] * (len(outs) + 1),
        out_shape=outs + [jax.ShapeDtypeStruct((8, LANES), F32)],
        compiler_params=parameters(LIMIT),
        cost_estimate=SHORT,
        name="project_frames",
    )(place, visits, *[frames[item] for item in items], *after)
    return {item: parts[2 * i : 2 * i + 2] for i, item in enumerate(items)}, token


def next_h_kernel(n_terms, n_slots, place, *refs):
    inverse_ref, w_ref, _, result_ref, h_ref, factor_ref = refs[n_terms:]
    h_next = high_dot(total(refs[:n_terms]), inverse_ref[...])
    result_ref[...] = h_next
    h_ref[...] = h_next
    rank = h_next.shape[0]
    patients = w_ref.shape[0]
    share = patients // n_slots
    h_rows = h_next.T
    w_rows = jnp.concatenate([w_ref[...], jnp.zeros((LANES - patients, rank), F32)], axis=0)
    w_columns = w_rows.T
    for slot in range(n_slots):
        first = (feature_of(place) ^ slot) * share
        columns = pltpu.roll(w_columns, jnp.where(first == 0, 0, LANES - first), 1)
        factor = jnp.concatenate([h_rows * columns[:, p : p + 1] for p in range(share)], axis=1)
        factor_ref[slot] = jnp.concatenate(three_parts(factor), axis=0)


def next_h(place, terms, inverse, w_start, n_slots, after):
    patients, rank = w_start.shape
    share = patients // n_slots
    return pl.pallas_call(
        functools.partial(next_h_kernel, len(terms), n_slots),
        in_specs=[SMEM_SPEC] + [VMEM_SPEC] * (len(terms) + 2) + [ANY_SPEC],
        out_specs=[VMEM_SPEC] * 3,
        out_shape=[
            jax.ShapeDtypeStruct(inverse.shape, F32),
            jax.ShapeDtypeStruct(inverse.shape, F32),
            jax.ShapeDtypeStruct((n_slots, 3 * rank, share * rank), BF16),
        ],
        compiler_params=parameters(LIMIT),
        cost_estimate=SHORT,
        name="next_h",
    )(place, *terms, inverse, w_start, after)


def second_inverse_kernel(h_ref, w_gram_ref, gram_ref, inverse_ref):
    gram = high_dot(h_ref[...], h_ref[...], COLS_BY_COLS)
    gram_ref[...] = gram
    inverse_ref[...] = inverse_of(gram * w_gram_ref[...])


def second_inverse(h_next, w_gram):
    out = jax.ShapeDtypeStruct(w_gram.shape, F32)
    return pl.pallas_call(
        second_inverse_kernel,
        out_shape=[out, out],
        compiler_params=parameters(LIMIT),
        cost_estimate=SHORT,
        name="second_inverse",
    )(h_next, w_gram)


def v_terms_kernel(items, place, factor_ref, *refs):
    *parts, keep_ref, send_ref, terms_ref = refs
    rank, width = terms_ref.shape
    half = width // 2
    total = None
    for i, (slots, first) in enumerate(items):
        count = parts[2 * i].shape[0] // len(slots)
        columns = pl.ds(first * rank, count)
        for k, slot in enumerate(slots):
            rows = pl.ds(k * count, count)
            large = low_dot(factor_ref[slot, :, columns], parts[2 * i][rows, :])
            small = low_dot(factor_ref[slot, : 2 * rank, columns], parts[2 * i + 1][rows, :])
            terms = large[:rank] + (large[rank : 2 * rank] + small[:rank]) + (large[2 * rank :] + small[rank:])
            total = terms if total is None else total + terms
    terms_ref[...] = total
    keep_ref[...] = terms_ref[:, pl.ds(pl.multiple_of(core_of(place) * half, half), half)]
    send_ref[...] = terms_ref[:, pl.ds(pl.multiple_of((1 - core_of(place)) * half, half), half)]


def all_v_terms(items, place, factor, projected):
    width = projected[0].shape[1]
    rank = factor.shape[1] // 3
    half = (rank, width // 2)
    return pl.pallas_call(
        functools.partial(v_terms_kernel, items),
        in_specs=[SMEM_SPEC] + [VMEM_SPEC] * (1 + len(projected)),
        out_specs=[VMEM_SPEC] * 2,
        out_shape=[jax.ShapeDtypeStruct(half, F32)] * 2,
        scratch_shapes=[pltpu.VMEM((rank, width), F32)],
        compiler_params=parameters(LIMIT),
        cost_estimate=SHORT,
        name="v_terms",
    )(place, factor, *projected)


def next_v_kernel(items, share, place, own_ref, other_ref, inverse_ref, h_ref, *refs):
    *parts, v_ref, sums_ref, v_parts = refs
    rank = inverse_ref.shape[0]
    upper = core_of(place) == 1
    left = jnp.where(upper, other_ref[...], own_ref[...])
    right = jnp.where(upper, own_ref[...], other_ref[...])
    v_rows = high_dot(inverse_ref[...], jnp.concatenate([left, right], axis=1))
    v_ref[...] = v_rows
    v_parts[...] = jnp.concatenate(two_parts(v_rows), axis=0)
    weights = jnp.concatenate([h_ref[...]] * 2, axis=1)
    gram = low_dot(v_parts[...], v_parts[...], ROWS_BY_ROWS)
    gram = gram[:rank, :rank] + (gram[:rank, rank:] + gram[rank:, :rank])
    sums_ref[...] = jnp.concatenate([jnp.zeros((rank, rank), F32), gram], axis=1)
    for i, (slots, done) in enumerate(items):
        seen = low_dot(parts[2 * i][...], v_parts[...], ROWS_BY_ROWS)
        seen = seen + low_dot(parts[2 * i + 1][...], v_parts[...], ROWS_BY_ROWS)
        count = seen.shape[0] // rank // len(slots)
        for p in range(seen.shape[0] // rank):
            patient = (feature_of(place) ^ slots[p // count]) * share + done + p % count
            row = jnp.sum(seen[p * rank : (p + 1) * rank] * weights, axis=0, keepdims=True)
            sums_ref[pl.ds(patient, 1), :rank] = row[:, :rank] + row[:, rank:]


def next_v(items, share, place, own, other, inverse, h_next, projected):
    width = projected[0].shape[1]
    rank = inverse.shape[0]
    return pl.pallas_call(
        functools.partial(next_v_kernel, items, share),
        in_specs=[SMEM_SPEC] + [VMEM_SPEC] * (4 + len(projected)),
        out_specs=[VMEM_SPEC] * 2,
        out_shape=[
            jax.ShapeDtypeStruct((rank, width), F32),
            jax.ShapeDtypeStruct((rank, 2 * rank), F32),
        ],
        scratch_shapes=[pltpu.VMEM((2 * rank, width), BF16)],
        compiler_params=parameters(LIMIT),
        cost_estimate=SHORT,
        name="next_v",
    )(place, own, other, inverse, h_next, *projected)


def next_w_kernel(n_sums, *refs):
    gram_ref, w_ref = refs[n_sums:]
    patients, rank = w_ref.shape
    sums = total(refs[:n_sums])
    table = jnp.concatenate([sums[:, rank:] * gram_ref[...], sums.T[:rank]], axis=1)
    w_ref[...] = eliminate(table, rank).T[rank : rank + patients]


def next_w(sums, h_gram, patients):
    rank = h_gram.shape[0]
    return pl.pallas_call(
        functools.partial(next_w_kernel, len(sums)),
        out_shape=jax.ShapeDtypeStruct((patients, rank), F32),
        compiler_params=parameters(LIMIT),
        cost_estimate=SHORT,
        name="next_w",
    )(*sums, h_gram)


def swap(x, axis, slot):
    pairs = [(i, i ^ slot) for i in range(lax.axis_size(axis))]
    return lax.ppermute(x, axis, pairs)


def all_terms(x, axis):
    n = lax.axis_size(axis)
    if n > 4:
        return [lax.psum(x, axis)]
    return [x] + [swap(x, axis, s) for s in range(1, n)]


def staged_terms(x, axis, after, far_first=False):
    n = lax.axis_size(axis)
    steps = [1 << i for i in range(n.bit_length() - 1)]
    steps = steps[::-1] if far_first else steps
    for step in steps[:-1]:
        x = add(x, swap(x, axis, step), after)
    return [x, swap(x, axis, steps[-1])]


def add_kernel(a_ref, b_ref, *refs):
    refs[-1][...] = a_ref[...] + b_ref[...]


def add(a, b, after):
    return pl.pallas_call(
        add_kernel,
        in_specs=[VMEM_SPEC] * 2 + [ANY_SPEC] * len(after),
        out_specs=VMEM_SPEC,
        out_shape=jax.ShapeDtypeStruct(a.shape, a.dtype),
        compiler_params=parameters(LIMIT),
        cost_estimate=SHORT,
        name="add_terms",
    )(a, b, *after)


def patient_halves(keep, send, after):
    own = add(keep, swap(send, "patient", 1), [])
    step = 2
    while step < lax.axis_size("patient"):
        own = add(own, swap(own, "patient", step), [after])
        step *= 2
    return own, swap(own, "patient", 1)


def on_device(visits, visit_counts, h_start, v_start, w_start):
    n = lax.axis_size("feature")
    patients, slots, width = visits.shape
    share = patients // n
    place = (2 * lax.axis_index("feature") + (lax.axis_index("patient") & 1)).astype(jnp.int32).reshape(1)
    by_owner = visits.reshape(n, share, slots, width)
    in_hbm = pltpu.with_memory_space_constraint(by_owner, pltpu.HBM)
    v_rows = pltpu.with_memory_space_constraint(v_start.T, pltpu.HBM)

    n_parts = 2 if share % 2 == 0 else 1
    count = share // n_parts
    firsts = [part * count for part in range(n_parts)]
    bits = [1 << i for i in range(n.bit_length() - 1)]
    v_near = v_start.T

    def send(bit):
        return [slot for slot in range(n) if slot & bit and not slot & (bit - 1)]

    def receive(bit):
        return [slot ^ bit for slot in send(bit)]

    w_grams = staged_terms(own_w_gram(w_start), "patient", [])
    arrived = [[] for _ in firsts]
    for i, bit in enumerate(bits):
        layouts = [receive(before) for before in bits[:i]]
        for part, first in enumerate(firsts):
            if i == 0 and part == 0:
                code = first_projection(send(bit), count, place, in_hbm, v_rows)
            else:
                after = [w_grams[part]] if i else []
                code = next_projection(
                    send(bit), first, count, layouts, place, by_owner, v_near, arrived[part], after
                )
            arrived[part] = arrived[part] + [swap(code, "feature", bit)]
    own, v_gram = project_own(n_parts, place, by_owner, v_near)
    h_local = v_gram

    layouts = [receive(bit) for bit in bits]
    frames = [[] for _ in firsts]
    joined = []

    def double(part, after):
        for bit in bits[::-1]:
            slots = tuple(slot ^ bit for group, _ in frames[part] for slot in group)
            joined = join([x for _, x in frames[part]], after)
            frames[part].append((slots, swap(joined, "feature", bit)))
        return [joined]

    def project_groups(groups, after):
        arrays = {(frames[part][k][0], firsts[part]): frames[part][k][1] for part, k in groups}
        return project_frames(list(arrays), place, arrays, by_owner, after)

    for part, first in enumerate(firsts):
        low, h_local, v_total = own_frames(
            layouts, part, n_parts, place, visit_counts, h_start, w_start, v_gram, h_local, own[part], arrived[part]
        )
        v_gram = v_total if first == 0 else v_gram
        frames[part].append(((0,), low))
        if part < n_parts - 1:
            joined = double(part, [])

    last = len(bits)
    projected, token = project_groups([(part, 0) for part in range(n_parts)], joined)
    h_sums = staged_terms(h_local, "patient", [token])
    h_sum = add(*h_sums, [])
    double(n_parts - 1, [h_sum])
    order = [(part, k) for part in range(n_parts) for k in range(1, last + 1)]
    more, token = project_groups(order[:-2], [h_sum])
    projected |= more
    w_gram, inverse = first_inverse(v_gram, w_grams, token)
    h_terms = staged_terms(h_sum, "feature", [inverse], far_first=True)
    after = h_terms[:1]
    for group in order[-2:]:
        more, token = project_groups([group], after)
        projected |= more
        after = [token]
    h_result, h_next, factor = next_h(place, h_terms, inverse, w_start, n, token)

    items = list(projected)
    flat = [x for item in items for x in projected[item]]
    keep, send = all_v_terms(items, place, factor, flat)
    h_gram, second = second_inverse(h_next, w_gram)
    own_terms, other_terms = patient_halves(keep, send, second)
    v_next, sums = next_v(items, share, place, own_terms, other_terms, second, h_next, flat)
    w_next = next_w(all_terms(sums, "feature"), h_gram, patients)
    return (h_result, v_next.T, w_next)


def solution(mesh):
    return jax.shard_map(
        on_device,
        mesh=mesh,
        in_specs=(
            P(("groups", "patient"), None, "feature"),
            P(("groups", "patient")),
            P(),
            P("feature", None),
            P(("groups", "patient"), None),
        ),
        out_specs=(P(None, "groups"), P("feature", "groups"), P("patient", "groups")),
        check_vma=False,
    )
```

```python
import functools

import jax
import jax.numpy as jnp
from jax import lax
from jax.experimental import pallas as pl
from jax.experimental.pallas import tpu as pltpu
from jax.sharding import PartitionSpec as P

NS_STEPS = 12
LANES = 128
LEVELS = 32000.0
COARSE_STEPS = 3
SHORT = pl.CostEstimate(flops=1000, bytes_accessed=1000, transcendentals=0)

epsilon = 1e-06
HIGH = lax.Precision.HIGHEST
F32 = jnp.float32
BF16 = jnp.bfloat16
MIB = 1024 * 1024

ROWS_BY_COLS = (((1,), (0,)), ((), ()))
ROWS_BY_ROWS = (((1,), (1,)), ((), ()))
COLS_BY_COLS = (((0,), (0,)), ((), ()))


def low_dot(a, b, dims=ROWS_BY_COLS):
    return lax.dot_general(a, b, dims, preferred_element_type=F32)


def high_dot(a, b, dims=ROWS_BY_COLS):
    return lax.dot_general(a, b, dims, precision=HIGH, preferred_element_type=F32)


def two_parts(x):
    first = x.astype(BF16)
    return first, (x - first.astype(F32)).astype(BF16)


def three_parts(x):
    first = x.astype(BF16)
    rest = x - first.astype(F32)
    second = rest.astype(BF16)
    return first, second, (rest - second.astype(F32)).astype(BF16)


def feature_of(place):
    return place[0] >> 1


def core_of(place):
    return place[0] & 1


def lane_numbers(shape):
    return lax.broadcasted_iota(jnp.int32, shape, len(shape) - 1)


ANY_SPEC = pl.BlockSpec(memory_space=pl.ANY)
HBM_SPEC = pl.BlockSpec(memory_space=pltpu.HBM)


def parameters(mib):
    return pltpu.CompilerParams(vmem_limit_bytes=mib * MIB)


LIMIT = 8
VMEM_SPEC = pl.BlockSpec(memory_space=pltpu.VMEM)
SMEM_SPEC = pl.BlockSpec(memory_space=pltpu.SMEM)


def exponent_rows(total_count):
    return -(-(total_count + 1) // 16) * 16


def payload_shape(total_count, rank, slots, with_gram):
    return (total_count * rank + (rank // 2 if with_gram else 0) + exponent_rows(total_count), slots)


def row_exponent(x):
    top = jnp.max(jnp.abs(x), axis=1, keepdims=True)
    return jnp.ceil(jnp.log2(jnp.maximum(top, 1e-30)))


class Payload:
    def __init__(self, ref, slots, count, rank, with_gram):
        self.ref, self.slots, self.count, self.rank, self.with_gram = ref, slots, count, rank, with_gram
        self.entries = len(slots) * count
        gram_rows = rank // 2 if with_gram else 0
        exponents = self.rows(self.entries * rank + gram_rows, exponent_rows(self.entries))
        self.steps = jnp.exp2(exponents[:, :LANES].T[:rank]) * (1.0 / LEVELS)

    def rows(self, first, number):
        return self.ref[pl.ds(first, number), :].astype(jnp.int32).astype(F32)

    def proj(self, slot, p):
        entry = self.slots.index(slot) * self.count + p
        return self.rows(entry * self.rank, self.rank) * self.steps[:, entry : entry + 1]

    def gram(self):
        rank = self.rank
        digits = self.rows(self.entries * rank, rank // 2)
        digits = jnp.concatenate([digits[:, : 2 * rank], digits[:, 2 * rank :]], axis=0)
        return (digits[:, :rank] + digits[:, rank:] * (0.5 / LEVELS)) * self.steps[:, self.entries : self.entries + 1]


def encode(values, gram, coded_ref, rank):
    count = len(values)
    lanes = lane_numbers((rank, LANES))
    exponents = jnp.zeros((rank, LANES), F32)
    for p, value in enumerate(values):
        proj = value()
        exponent = row_exponent(proj)
        coded = jnp.floor(proj * (LEVELS / jnp.exp2(exponent)) + 0.5)
        coded_ref[pl.ds(p * rank, rank), :] = coded.astype(jnp.int32).astype(jnp.int16)
        exponents = jnp.where(lanes == p, exponent, exponents)
    end = count * rank
    if gram is not None:
        exponent = row_exponent(gram)
        scaled = gram * (LEVELS / jnp.exp2(exponent))
        whole = jnp.floor(scaled + 0.5)
        rest = jnp.floor((scaled - whole) * (2 * LEVELS) + 0.5)
        digits = jnp.concatenate([whole, rest], axis=1)
        digits = jnp.concatenate([digits[: rank // 2], digits[rank // 2 :]], axis=1)
        coded_ref[pl.ds(end, rank // 2), :] = digits.astype(jnp.int32).astype(jnp.int16)
        exponents = jnp.where(lanes == count, exponent, exponents)
        end += rank // 2
    rows = exponent_rows(count)
    last = jnp.concatenate([exponents.T[:rows], jnp.zeros((rows, coded_ref.shape[1] - rank), F32)], axis=1)
    coded_ref[pl.ds(end, rows), :] = last.astype(jnp.int32).astype(jnp.int16)


def first_projection_kernel(slots, place, v_hbm, visits_ref, coded_ref, v_ref, buffers, sems, v_sem):
    count = buffers.shape[1]
    v_copy = pltpu.make_async_copy(v_hbm, v_ref, v_sem)
    v_copy.start()
    copies = [
        pltpu.make_async_copy(visits_ref.at[feature_of(place) ^ slot, pl.ds(0, count)], buffers.at[i], sems.at[i])
        for i, slot in enumerate(slots)
    ]
    for copy in copies:
        copy.start()
    v_copy.wait()
    gram = low_dot(v_ref[...], v_ref[...], ROWS_BY_ROWS)

    def value(i, p):
        if p == 0:
            copies[i].wait()
        return low_dot(v_ref[...], buffers[i, p], ROWS_BY_ROWS)

    values = [functools.partial(value, i, p) for i in range(len(slots)) for p in range(count)]
    encode(values, gram, coded_ref, v_ref.shape[0])


def first_projection(slots, count, place, visits, v_rows):
    width = visits.shape[3]
    rank = v_rows.shape[0]
    return pl.pallas_call(
        functools.partial(first_projection_kernel, slots),
        in_specs=[SMEM_SPEC, HBM_SPEC, HBM_SPEC],
        out_specs=VMEM_SPEC,
        out_shape=jax.ShapeDtypeStruct(payload_shape(len(slots) * count, rank, visits.shape[2], True), jnp.int16),
        scratch_shapes=[
            pltpu.VMEM(v_rows.shape, BF16),
            pltpu.VMEM((len(slots), count) + visits.shape[2:], BF16),
            pltpu.SemaphoreType.DMA((len(slots),)),
            pltpu.SemaphoreType.DMA,
        ],
        compiler_params=parameters(LIMIT),
        cost_estimate=SHORT,
        name="project_first",
    )(place, v_rows, visits)


def next_projection_kernel(slots, first, count, layouts, place, v_ref, visits_ref, *refs):
    coded_ref = refs[-1]
    rank = v_ref.shape[0]
    arrived = [Payload(ref, layout, count, rank, first == 0) for ref, layout in zip(refs, layouts)]

    def value(slot, p):
        proj = low_dot(v_ref[...], visits_ref[feature_of(place) ^ slot, first + p], ROWS_BY_ROWS)
        for payload in arrived:
            proj = proj + payload.proj(slot, p)
        return proj

    gram = None
    if first == 0:
        gram = low_dot(v_ref[...], v_ref[...], ROWS_BY_ROWS)
        for payload in arrived:
            gram = gram + payload.gram()
    encode([functools.partial(value, slot, p) for slot in slots for p in range(count)], gram, coded_ref, rank)


def next_projection(slots, first, count, layouts, place, visits, v_rows, arrived, after):
    rank = v_rows.shape[0]
    return pl.pallas_call(
        functools.partial(next_projection_kernel, slots, first, count, layouts),
        in_specs=[SMEM_SPEC] + [VMEM_SPEC] * (2 + len(arrived)) + [ANY_SPEC] * len(after),
        out_specs=VMEM_SPEC,
        out_shape=jax.ShapeDtypeStruct(payload_shape(len(slots) * count, rank, visits.shape[2], first == 0), jnp.int16),
        compiler_params=parameters(LIMIT),
        cost_estimate=SHORT,
        name="project_next",
    )(place, v_rows, visits, *arrived, *after)


def w_gram_kernel(w_ref, gram_ref):
    gram_ref[...] = high_dot(w_ref[...], w_ref[...], COLS_BY_COLS)


def own_w_gram(w_start):
    rank = w_start.shape[1]
    return pl.pallas_call(
        w_gram_kernel,
        in_specs=[VMEM_SPEC],
        out_specs=VMEM_SPEC,
        out_shape=jax.ShapeDtypeStruct((rank, rank), F32),
        compiler_params=parameters(LIMIT),
        cost_estimate=SHORT,
        name="own_w_gram",
    )(w_start)


def own_projection_kernel(place, v_ref, visits_ref, *refs):
    *proj_refs, v_gram_ref = refs
    count = visits_ref.shape[1] // len(proj_refs)
    for p in range(visits_ref.shape[1]):
        proj_refs[p // count][p % count] = low_dot(v_ref[...], visits_ref[feature_of(place), p], ROWS_BY_ROWS)
    v_gram_ref[...] = low_dot(v_ref[...], v_ref[...], ROWS_BY_ROWS)


def project_own(n_parts, place, visits, v_rows):
    _, share, slots, width = visits.shape
    rank = v_rows.shape[0]
    proj = jax.ShapeDtypeStruct((share // n_parts, rank, slots), F32)
    *own, v_gram = pl.pallas_call(
        own_projection_kernel,
        in_specs=[SMEM_SPEC] + [VMEM_SPEC] * 2,
        out_specs=[VMEM_SPEC] * (n_parts + 1),
        out_shape=[proj] * n_parts + [jax.ShapeDtypeStruct((rank, rank), F32)],
        compiler_params=parameters(LIMIT),
        cost_estimate=SHORT,
        name="project_own",
    )(place, v_rows, visits)
    return own, v_gram


def solve_tile(columns, tile):
    rows = lax.broadcasted_iota(jnp.int32, tile.shape, 0)
    for a in range(0, 8, 2):
        b = a + 1
        first, second = columns[a], columns[b]
        m_aa, m_ab, m_ba, m_bb = first[a:b], second[a:b], first[b : b + 1], second[b : b + 1]
        scale = 1.0 / (m_aa * m_bb - m_ab * m_ba)
        m_aa, m_ab, m_ba, m_bb = m_aa * scale, m_ab * scale, m_ba * scale, m_bb * scale

        def step(x):
            x_a, x_b = x[a:b], x[b : b + 1]
            new_a, new_b = m_bb * x_a - m_ab * x_b, m_aa * x_b - m_ba * x_a
            x = x - (first * new_a + second * new_b)
            return jnp.where(rows == a, new_a, jnp.where(rows == b, new_b, x))

        tile = step(tile)
        columns = [step(x) if q > b else x for q, x in enumerate(columns)]
    return tile


def eliminate(table, rank):
    tiles = [table[8 * t : 8 * t + 8] for t in range(rank // 8)]
    for home in range(rank // 8):
        first = 8 * home
        columns = [[jnp.broadcast_to(t[:, q : q + 1], t.shape) for q in range(first, first + 8)] for t in tiles]
        solved = solve_tile(columns[home], tiles[home])
        for t, tile in enumerate(tiles):
            terms = [column * solved[q : q + 1] for q, column in enumerate(columns[t])]
            while len(terms) > 1:
                terms = [x + y for x, y in zip(terms[::2], terms[1::2])]
            tiles[t] = solved if t == home else tile - terms[0]
    return jnp.concatenate(tiles, axis=0)


def inverse_of(gram):
    rank = gram.shape[0]
    eye = (lax.broadcasted_iota(jnp.int32, gram.shape, 0) == lane_numbers(gram.shape)).astype(F32)
    return eliminate(jnp.concatenate([gram, eye], axis=1), rank)[:, rank:]


def total(refs):
    out = refs[0][...]
    for ref in refs[1:]:
        out = out + ref[...]
    return out


def first_inverse_kernel(v_gram_ref, *refs):
    *terms, _, w_gram_ref, inverse_ref = refs
    w_gram = total(terms)
    w_gram_ref[...] = w_gram
    inverse_ref[...] = inverse_of(w_gram * v_gram_ref[...])


def first_inverse(v_gram, w_grams, after):
    out = jax.ShapeDtypeStruct(v_gram.shape, F32)
    return pl.pallas_call(
        first_inverse_kernel,
        in_specs=[VMEM_SPEC] * (1 + len(w_grams)) + [ANY_SPEC],
        out_specs=[VMEM_SPEC] * 2,
        out_shape=[out, out],
        compiler_params=parameters(LIMIT),
        cost_estimate=SHORT,
        name="first_inverse",
    )(v_gram, *w_grams, after)


def sweep_all(frames, rank, fine):
    patients = range(frames.shape[0])
    if fine:
        both = [jnp.concatenate(two_parts(frames[p]), axis=0) for p in patients]
        blocks = [low_dot(x, x, ROWS_BY_ROWS) for x in both]
        blocks = [x[:rank] + x[rank:] for x in blocks]
        grams = [x + pltpu.roll(x, rank, 1) for x in blocks]
        moved = [low_dot(jnp.concatenate(two_parts(g), axis=0), x) for g, x in zip(grams, both)]
        moved = [x[:rank] + x[rank:] for x in moved]
    else:
        first = [frames[p].astype(BF16) for p in patients]
        grams = [low_dot(x, x, ROWS_BY_ROWS).astype(BF16) for x in first]
        moved = [low_dot(g, x) for g, x in zip(grams, first)]
    for p in patients:
        frames[p] = 1.5 * frames[p] - 0.5 * moved[p]


def frames_kernel(layouts, part, share, place, counts_ref, h_ref, w_ref, v_gram_ref, before_ref, own_ref, *refs):
    coded, refs = refs[: len(layouts)], refs[len(layouts) :]
    frames_ref, terms_ref, v_total_ref, proj, frames = refs
    count, rank, slots = frames.shape
    patients = range(count)
    first = feature_of(place) * share + part * count
    pieces = [own_ref[p] for p in patients]
    v_gram = v_gram_ref[...]
    for code, layout in zip(coded, layouts):
        payload = Payload(code, layout, count, rank, part == 0)
        pieces = [pieces[p] + payload.proj(0, p) for p in patients]
        if part == 0:
            v_gram = v_gram + payload.gram()
    v_total_ref[...] = v_gram
    for p in patients:
        proj[p] = pieces[p]
    weights = [w_ref[pl.ds(first + p, 1), :] for p in patients]
    mixed = [high_dot(h_ref[...] * weights[p], pieces[p]) for p in patients]
    lanes = lane_numbers((rank, slots))
    mixed = [jnp.where(lanes < counts_ref[first + p], mixed[p], 0.0) for p in patients]
    energy = [jnp.sum(jnp.sum(x * x, axis=1, keepdims=True), axis=0, keepdims=True) for x in mixed]
    for p in patients:
        frames[p] = mixed[p] * lax.rsqrt(energy[p] + epsilon)

    def sweep(fine, step, carry):
        sweep_all(frames, rank, fine)
        return carry

    lax.fori_loop(0, COARSE_STEPS, functools.partial(sweep, False), 0, unroll=True)
    lax.fori_loop(COARSE_STEPS, NS_STEPS, functools.partial(sweep, True), 0, unroll=3)
    low = [frames[p].astype(BF16) for p in patients]
    for p in patients:
        frames_ref[p] = low[p]
    products = [jnp.concatenate(three_parts(proj[p]), axis=0) for p in patients]
    products = [low_dot(low[p], products[p], ROWS_BY_ROWS) for p in patients]
    terms = before_ref[...] if part else jnp.zeros((rank, rank), F32)
    for p in patients:
        product = products[p][:, :rank] + (products[p][:, rank : 2 * rank] + products[p][:, 2 * rank :])
        terms = terms + product * weights[p]
    terms_ref[...] = terms


def own_frames(layouts, part, n_parts, place, counts, h_start, w_start, v_gram, before, own, coded):
    count, rank, slots = own.shape
    share = count * n_parts
    return pl.pallas_call(
        functools.partial(frames_kernel, layouts, part, share),
        in_specs=[SMEM_SPEC] * 2 + [VMEM_SPEC] * (5 + len(coded)),
        out_specs=[VMEM_SPEC] * 3,
        out_shape=[
            jax.ShapeDtypeStruct(own.shape, BF16),
            jax.ShapeDtypeStruct((rank, rank), F32),
            jax.ShapeDtypeStruct((rank, rank), F32),
        ],
        scratch_shapes=[pltpu.VMEM(own.shape, F32)] * 2,
        compiler_params=parameters(LIMIT),
        cost_estimate=SHORT,
        name="own_frames",
    )(place, counts, h_start, w_start, v_gram, before, own, *coded)


def projected_kernel(items, place, visits_ref, *refs):
    frames_refs, outs, token_ref = refs[: len(items)], refs[-2 * len(items) - 1 : -1], refs[-1]
    token_ref[...] = jnp.zeros_like(token_ref)
    for i, (slots, first) in enumerate(items):
        total_count, rank, _ = frames_refs[i].shape
        count = total_count // len(slots)
        for p in range(total_count):
            rows = pl.ds(p * rank, rank)
            owner = feature_of(place) ^ slots[p // count]
            product = low_dot(frames_refs[i][p], visits_ref[owner, first + p % count])
            outs[2 * i][rows, :], outs[2 * i + 1][rows, :] = two_parts(product)


def join_kernel(count, *refs):
    out_ref = refs[-1]
    first = 0
    for part in refs[:count]:
        out_ref[first : first + part.shape[0]] = part[...]
        first += part.shape[0]


def join(parts, after):
    if len(parts) == 1:
        return parts[0]
    return pl.pallas_call(
        functools.partial(join_kernel, len(parts)),
        in_specs=[VMEM_SPEC] * len(parts) + [ANY_SPEC] * len(after),
        out_specs=VMEM_SPEC,
        out_shape=jax.ShapeDtypeStruct((sum(x.shape[0] for x in parts),) + parts[0].shape[1:], parts[0].dtype),
        compiler_params=parameters(LIMIT),
        cost_estimate=SHORT,
        name="join_frames",
    )(*parts, *after)


def project_frames(items, place, frames, visits, after):
    width = visits.shape[-1]
    outs = []
    for item in items:
        count, rank, _ = frames[item].shape
        outs += [jax.ShapeDtypeStruct((count * rank, width), BF16)] * 2
    *parts, token = pl.pallas_call(
        functools.partial(projected_kernel, items),
        in_specs=[SMEM_SPEC] + [VMEM_SPEC] * (1 + len(items)) + [ANY_SPEC] * len(after),
        out_specs=[VMEM_SPEC] * (len(outs) + 1),
        out_shape=outs + [jax.ShapeDtypeStruct((8, LANES), F32)],
        compiler_params=parameters(LIMIT),
        cost_estimate=SHORT,
        name="project_frames",
    )(place, visits, *[frames[item] for item in items], *after)
    return {item: parts[2 * i : 2 * i + 2] for i, item in enumerate(items)}, token


def next_h_kernel(n_terms, n_slots, place, *refs):
    inverse_ref, w_ref, _, result_ref, h_ref, factor_ref = refs[n_terms:]
    h_next = high_dot(total(refs[:n_terms]), inverse_ref[...])
    result_ref[...] = h_next
    h_ref[...] = h_next
    rank = h_next.shape[0]
    patients = w_ref.shape[0]
    share = patients // n_slots
    h_rows = h_next.T
    w_rows = jnp.concatenate([w_ref[...], jnp.zeros((LANES - patients, rank), F32)], axis=0)
    w_columns = w_rows.T
    for slot in range(n_slots):
        first = (feature_of(place) ^ slot) * share
        columns = pltpu.roll(w_columns, jnp.where(first == 0, 0, LANES - first), 1)
        factor = jnp.concatenate([h_rows * columns[:, p : p + 1] for p in range(share)], axis=1)
        factor_ref[slot] = jnp.concatenate(three_parts(factor), axis=0)


def next_h(place, terms, inverse, w_start, n_slots, after):
    patients, rank = w_start.shape
    share = patients // n_slots
    return pl.pallas_call(
        functools.partial(next_h_kernel, len(terms), n_slots),
        in_specs=[SMEM_SPEC] + [VMEM_SPEC] * (len(terms) + 2) + [ANY_SPEC],
        out_specs=[VMEM_SPEC] * 3,
        out_shape=[
            jax.ShapeDtypeStruct(inverse.shape, F32),
            jax.ShapeDtypeStruct(inverse.shape, F32),
            jax.ShapeDtypeStruct((n_slots, 3 * rank, share * rank), BF16),
        ],
        compiler_params=parameters(LIMIT),
        cost_estimate=SHORT,
        name="next_h",
    )(place, *terms, inverse, w_start, after)


def second_inverse_kernel(h_ref, w_gram_ref, gram_ref, inverse_ref):
    gram = high_dot(h_ref[...], h_ref[...], COLS_BY_COLS)
    gram_ref[...] = gram
    inverse_ref[...] = inverse_of(gram * w_gram_ref[...])


def second_inverse(h_next, w_gram):
    out = jax.ShapeDtypeStruct(w_gram.shape, F32)
    return pl.pallas_call(
        second_inverse_kernel,
        out_shape=[out, out],
        compiler_params=parameters(LIMIT),
        cost_estimate=SHORT,
        name="second_inverse",
    )(h_next, w_gram)


def v_terms_kernel(items, place, factor_ref, *refs):
    *parts, keep_ref, send_ref, terms_ref = refs
    rank, width = terms_ref.shape
    half = width // 2
    total = None
    for i, (slots, first) in enumerate(items):
        count = parts[2 * i].shape[0] // len(slots)
        columns = pl.ds(first * rank, count)
        for k, slot in enumerate(slots):
            rows = pl.ds(k * count, count)
            large = low_dot(factor_ref[slot, :, columns], parts[2 * i][rows, :])
            small = low_dot(factor_ref[slot, : 2 * rank, columns], parts[2 * i + 1][rows, :])
            terms = large[:rank] + (large[rank : 2 * rank] + small[:rank]) + (large[2 * rank :] + small[rank:])
            total = terms if total is None else total + terms
    terms_ref[...] = total
    keep_ref[...] = terms_ref[:, pl.ds(pl.multiple_of(core_of(place) * half, half), half)]
    send_ref[...] = terms_ref[:, pl.ds(pl.multiple_of((1 - core_of(place)) * half, half), half)]


def all_v_terms(items, place, factor, projected):
    width = projected[0].shape[1]
    rank = factor.shape[1] // 3
    half = (rank, width // 2)
    return pl.pallas_call(
        functools.partial(v_terms_kernel, items),
        in_specs=[SMEM_SPEC] + [VMEM_SPEC] * (1 + len(projected)),
        out_specs=[VMEM_SPEC] * 2,
        out_shape=[jax.ShapeDtypeStruct(half, F32)] * 2,
        scratch_shapes=[pltpu.VMEM((rank, width), F32)],
        compiler_params=parameters(LIMIT),
        cost_estimate=SHORT,
        name="v_terms",
    )(place, factor, *projected)


def next_v_kernel(items, share, place, own_ref, other_ref, inverse_ref, h_ref, *refs):
    *parts, v_ref, sums_ref, v_parts = refs
    rank = inverse_ref.shape[0]
    upper = core_of(place) == 1
    left = jnp.where(upper, other_ref[...], own_ref[...])
    right = jnp.where(upper, own_ref[...], other_ref[...])
    v_rows = high_dot(inverse_ref[...], jnp.concatenate([left, right], axis=1))
    v_ref[...] = v_rows
    v_parts[...] = jnp.concatenate(two_parts(v_rows), axis=0)
    weights = jnp.concatenate([h_ref[...]] * 2, axis=1)
    gram = low_dot(v_parts[...], v_parts[...], ROWS_BY_ROWS)
    gram = gram[:rank, :rank] + (gram[:rank, rank:] + gram[rank:, :rank])
    sums_ref[...] = jnp.concatenate([jnp.zeros((rank, rank), F32), gram], axis=1)
    for i, (slots, done) in enumerate(items):
        seen = low_dot(parts[2 * i][...], v_parts[...], ROWS_BY_ROWS)
        seen = seen + low_dot(parts[2 * i + 1][...], v_parts[...], ROWS_BY_ROWS)
        count = seen.shape[0] // rank // len(slots)
        for p in range(seen.shape[0] // rank):
            patient = (feature_of(place) ^ slots[p // count]) * share + done + p % count
            row = jnp.sum(seen[p * rank : (p + 1) * rank] * weights, axis=0, keepdims=True)
            sums_ref[pl.ds(patient, 1), :rank] = row[:, :rank] + row[:, rank:]


def next_v(items, share, place, own, other, inverse, h_next, projected):
    width = projected[0].shape[1]
    rank = inverse.shape[0]
    return pl.pallas_call(
        functools.partial(next_v_kernel, items, share),
        in_specs=[SMEM_SPEC] + [VMEM_SPEC] * (4 + len(projected)),
        out_specs=[VMEM_SPEC] * 2,
        out_shape=[
            jax.ShapeDtypeStruct((rank, width), F32),
            jax.ShapeDtypeStruct((rank, 2 * rank), F32),
        ],
        scratch_shapes=[pltpu.VMEM((2 * rank, width), BF16)],
        compiler_params=parameters(LIMIT),
        cost_estimate=SHORT,
        name="next_v",
    )(place, own, other, inverse, h_next, *projected)


def next_w_kernel(n_sums, *refs):
    gram_ref, w_ref = refs[n_sums:]
    patients, rank = w_ref.shape
    sums = total(refs[:n_sums])
    table = jnp.concatenate([sums[:, rank:] * gram_ref[...], sums.T[:rank]], axis=1)
    w_ref[...] = eliminate(table, rank).T[rank : rank + patients]


def next_w(sums, h_gram, patients):
    rank = h_gram.shape[0]
    return pl.pallas_call(
        functools.partial(next_w_kernel, len(sums)),
        out_shape=jax.ShapeDtypeStruct((patients, rank), F32),
        compiler_params=parameters(LIMIT),
        cost_estimate=SHORT,
        name="next_w",
    )(*sums, h_gram)


def swap(x, axis, slot):
    pairs = [(i, i ^ slot) for i in range(lax.axis_size(axis))]
    return lax.ppermute(x, axis, pairs)


def all_terms(x, axis):
    n = lax.axis_size(axis)
    if n > 4:
        return [lax.psum(x, axis)]
    return [x] + [swap(x, axis, s) for s in range(1, n)]


def staged_terms(x, axis, after):
    n = lax.axis_size(axis)
    steps = [1 << i for i in range(n.bit_length() - 1)]
    for step in steps[:-1]:
        x = add(x, swap(x, axis, step), after)
    return [x, swap(x, axis, steps[-1])]


def add_kernel(a_ref, b_ref, *refs):
    refs[-1][...] = a_ref[...] + b_ref[...]


def add(a, b, after):
    return pl.pallas_call(
        add_kernel,
        in_specs=[VMEM_SPEC] * 2 + [ANY_SPEC] * len(after),
        out_specs=VMEM_SPEC,
        out_shape=jax.ShapeDtypeStruct(a.shape, a.dtype),
        compiler_params=parameters(LIMIT),
        cost_estimate=SHORT,
        name="add_terms",
    )(a, b, *after)


def patient_halves(keep, send, after):
    own = add(keep, swap(send, "patient", 1), [])
    step = 2
    while step < lax.axis_size("patient"):
        own = add(own, swap(own, "patient", step), [after])
        step *= 2
    return own, swap(own, "patient", 1)


def on_device(visits, visit_counts, h_start, v_start, w_start):
    n = lax.axis_size("feature")
    patients, slots, width = visits.shape
    share = patients // n
    place = (2 * lax.axis_index("feature") + (lax.axis_index("patient") & 1)).astype(jnp.int32).reshape(1)
    by_owner = visits.reshape(n, share, slots, width)
    in_hbm = pltpu.with_memory_space_constraint(by_owner, pltpu.HBM)
    v_rows = pltpu.with_memory_space_constraint(v_start.T, pltpu.HBM)

    n_parts = 2 if share % 2 == 0 else 1
    count = share // n_parts
    firsts = [part * count for part in range(n_parts)]
    bits = [1 << i for i in range(n.bit_length() - 1)]
    v_near = v_start.T

    def send(bit):
        return [slot for slot in range(n) if slot & bit and not slot & (bit - 1)]

    def receive(bit):
        return [slot ^ bit for slot in send(bit)]

    w_grams = staged_terms(own_w_gram(w_start), "patient", [])
    own, v_gram = project_own(n_parts, place, by_owner, v_near)
    h_local = v_gram
    arrived = [[] for _ in firsts]
    for i, bit in enumerate(bits):
        layouts = [receive(before) for before in bits[:i]]
        for part, first in enumerate(firsts):
            if i == 0 and part == 0:
                code = first_projection(send(bit), count, place, in_hbm, v_rows)
            else:
                after = [w_grams[part]] + [v_gram] * part if i else []
                code = next_projection(
                    send(bit), first, count, layouts, place, by_owner, v_near, arrived[part], after
                )
            arrived[part] = arrived[part] + [swap(code, "feature", bit)]

    layouts = [receive(bit) for bit in bits]
    frames = [[] for _ in firsts]
    joined = []

    def double(part, after):
        for bit in bits[::-1]:
            slots = tuple(slot ^ bit for group, _ in frames[part] for slot in group)
            joined = join([x for _, x in frames[part]], after)
            frames[part].append((slots, swap(joined, "feature", bit)))
        return [joined]

    def project_groups(groups, after):
        arrays = {(frames[part][k][0], firsts[part]): frames[part][k][1] for part, k in groups}
        return project_frames(list(arrays), place, arrays, by_owner, after)

    for part, first in enumerate(firsts):
        low, h_local, v_total = own_frames(
            layouts, part, n_parts, place, visit_counts, h_start, w_start, v_gram, h_local, own[part], arrived[part]
        )
        v_gram = v_total if first == 0 else v_gram
        frames[part].append(((0,), low))
        if part < n_parts - 1:
            joined = double(part, [])

    last = len(bits)
    projected, token = project_groups([(part, 0) for part in range(n_parts)], joined)
    h_sums = staged_terms(h_local, "patient", [token])
    h_sum = add(*h_sums, [])
    double(n_parts - 1, [h_sum])
    order = [(part, k) for part in range(n_parts) for k in range(1, last + 1)]
    h_terms = all_terms(h_sum, "feature")
    more, token = project_groups(order[:-2], [h_sum])
    projected |= more
    w_gram, inverse = first_inverse(v_gram, w_grams, token)
    after = [inverse]
    for group in order[-2:]:
        more, token = project_groups([group], after)
        projected |= more
        after = [token]
    h_result, h_next, factor = next_h(place, h_terms, inverse, w_start, n, token)

    items = list(projected)
    flat = [x for item in items for x in projected[item]]
    keep, send = all_v_terms(items, place, factor, flat)
    h_gram, second = second_inverse(h_next, w_gram)
    own_terms, other_terms = patient_halves(keep, send, second)
    v_next, sums = next_v(items, share, place, own_terms, other_terms, second, h_next, flat)
    w_next = next_w(all_terms(sums, "feature"), h_gram, patients)
    return (h_result, v_next.T, w_next)


def solution(mesh):
    return jax.shard_map(
        on_device,
        mesh=mesh,
        in_specs=(
            P(("groups", "patient"), None, "feature"),
            P(("groups", "patient")),
            P(),
            P("feature", None),
            P(("groups", "patient"), None),
        ),
        out_specs=(P(None, "groups"), P("feature", "groups"), P("patient", "groups")),
        check_vma=False,
    )
```

```python
import functools

import jax
import jax.numpy as jnp
from jax import lax
from jax.experimental import pallas as pl
from jax.experimental.pallas import tpu as pltpu
from jax.sharding import PartitionSpec as P

NS_STEPS = 12
LANES = 128
LEVELS = 32000.0
COARSE_STEPS = 3
SHORT = pl.CostEstimate(flops=1000, bytes_accessed=1000, transcendentals=0)

epsilon = 1e-06
HIGH = lax.Precision.HIGHEST
F32 = jnp.float32
BF16 = jnp.bfloat16
MIB = 1024 * 1024

ROWS_BY_COLS = (((1,), (0,)), ((), ()))
ROWS_BY_ROWS = (((1,), (1,)), ((), ()))
COLS_BY_COLS = (((0,), (0,)), ((), ()))


def low_dot(a, b, dims=ROWS_BY_COLS):
    return lax.dot_general(a, b, dims, preferred_element_type=F32)


def high_dot(a, b, dims=ROWS_BY_COLS):
    return lax.dot_general(a, b, dims, precision=HIGH, preferred_element_type=F32)


def two_parts(x):
    first = x.astype(BF16)
    return first, (x - first.astype(F32)).astype(BF16)


def three_parts(x):
    first = x.astype(BF16)
    rest = x - first.astype(F32)
    second = rest.astype(BF16)
    return first, second, (rest - second.astype(F32)).astype(BF16)


def feature_of(place):
    return place[0] >> 1


def core_of(place):
    return place[0] & 1


def lane_numbers(shape):
    return lax.broadcasted_iota(jnp.int32, shape, len(shape) - 1)


ANY_SPEC = pl.BlockSpec(memory_space=pl.ANY)
HBM_SPEC = pl.BlockSpec(memory_space=pltpu.HBM)


def parameters(mib):
    return pltpu.CompilerParams(vmem_limit_bytes=mib * MIB)


LIMIT = 8
VMEM_SPEC = pl.BlockSpec(memory_space=pltpu.VMEM)
SMEM_SPEC = pl.BlockSpec(memory_space=pltpu.SMEM)


def exponent_rows(total_count):
    return -(-(total_count + 1) // 16) * 16


def payload_shape(total_count, rank, slots, with_gram):
    return (total_count * rank + (rank // 2 if with_gram else 0) + exponent_rows(total_count), slots)


def row_exponent(x):
    top = jnp.max(jnp.abs(x), axis=1, keepdims=True)
    return jnp.ceil(jnp.log2(jnp.maximum(top, 1e-30)))


class Payload:
    def __init__(self, ref, slots, count, rank, with_gram):
        self.ref, self.slots, self.count, self.rank, self.with_gram = ref, slots, count, rank, with_gram
        self.entries = len(slots) * count
        gram_rows = rank // 2 if with_gram else 0
        exponents = self.rows(self.entries * rank + gram_rows, exponent_rows(self.entries))
        self.steps = jnp.exp2(exponents[:, :LANES].T[:rank]) * (1.0 / LEVELS)

    def rows(self, first, number):
        return self.ref[pl.ds(first, number), :].astype(jnp.int32).astype(F32)

    def proj(self, slot, p):
        entry = self.slots.index(slot) * self.count + p
        return self.rows(entry * self.rank, self.rank) * self.steps[:, entry : entry + 1]

    def gram(self):
        rank = self.rank
        digits = self.rows(self.entries * rank, rank // 2)
        digits = jnp.concatenate([digits[:, : 2 * rank], digits[:, 2 * rank :]], axis=0)
        return (digits[:, :rank] + digits[:, rank:] * (0.5 / LEVELS)) * self.steps[:, self.entries : self.entries + 1]


def encode(values, gram, coded_ref, rank):
    count = len(values)
    lanes = lane_numbers((rank, LANES))
    exponents = jnp.zeros((rank, LANES), F32)
    for p, value in enumerate(values):
        proj = value()
        exponent = row_exponent(proj)
        coded = jnp.floor(proj * (LEVELS / jnp.exp2(exponent)) + 0.5)
        coded_ref[pl.ds(p * rank, rank), :] = coded.astype(jnp.int32).astype(jnp.int16)
        exponents = jnp.where(lanes == p, exponent, exponents)
    end = count * rank
    if gram is not None:
        exponent = row_exponent(gram)
        scaled = gram * (LEVELS / jnp.exp2(exponent))
        whole = jnp.floor(scaled + 0.5)
        rest = jnp.floor((scaled - whole) * (2 * LEVELS) + 0.5)
        digits = jnp.concatenate([whole, rest], axis=1)
        digits = jnp.concatenate([digits[: rank // 2], digits[rank // 2 :]], axis=1)
        coded_ref[pl.ds(end, rank // 2), :] = digits.astype(jnp.int32).astype(jnp.int16)
        exponents = jnp.where(lanes == count, exponent, exponents)
        end += rank // 2
    rows = exponent_rows(count)
    last = jnp.concatenate([exponents.T[:rows], jnp.zeros((rows, coded_ref.shape[1] - rank), F32)], axis=1)
    coded_ref[pl.ds(end, rows), :] = last.astype(jnp.int32).astype(jnp.int16)


def first_projection_kernel(slots, with_gram, place, v_hbm, visits_ref, coded_ref, v_ref, buffers, sems, v_sem):
    count = buffers.shape[1]
    v_copy = pltpu.make_async_copy(v_hbm, v_ref, v_sem)
    v_copy.start()
    copies = [
        pltpu.make_async_copy(visits_ref.at[feature_of(place) ^ slot, pl.ds(0, count)], buffers.at[i], sems.at[i])
        for i, slot in enumerate(slots)
    ]
    for copy in copies:
        copy.start()
    v_copy.wait()

    def value(i, p):
        if p == 0:
            copies[i].wait()
        return low_dot(v_ref[...], buffers[i, p], ROWS_BY_ROWS)

    values = [functools.partial(value, i, p) for i in range(len(slots)) for p in range(count)]
    gram = low_dot(v_ref[...], v_ref[...], ROWS_BY_ROWS) if with_gram else None
    encode(values, gram, coded_ref, v_ref.shape[0])


def first_projection(slots, count, with_gram, place, visits, v_rows):
    width = visits.shape[3]
    rank = v_rows.shape[0]
    return pl.pallas_call(
        functools.partial(first_projection_kernel, slots, with_gram),
        in_specs=[SMEM_SPEC, HBM_SPEC, HBM_SPEC],
        out_specs=VMEM_SPEC,
        out_shape=jax.ShapeDtypeStruct(payload_shape(len(slots) * count, rank, visits.shape[2], with_gram), jnp.int16),
        scratch_shapes=[
            pltpu.VMEM(v_rows.shape, BF16),
            pltpu.VMEM((len(slots), count) + visits.shape[2:], BF16),
            pltpu.SemaphoreType.DMA((len(slots),)),
            pltpu.SemaphoreType.DMA,
        ],
        compiler_params=parameters(LIMIT),
        cost_estimate=SHORT,
        name="project_first",
    )(place, v_rows, visits)


def next_projection_kernel(slots, first, count, with_gram, layouts, place, v_ref, visits_ref, *refs):
    coded_ref = refs[-1]
    rank = v_ref.shape[0]
    arrived = [Payload(ref, layout, count, rank, with_gram) for ref, layout in zip(refs, layouts)]

    def value(slot, p):
        proj = low_dot(v_ref[...], visits_ref[feature_of(place) ^ slot, first + p], ROWS_BY_ROWS)
        for payload in arrived:
            proj = proj + payload.proj(slot, p)
        return proj

    gram = None
    if with_gram:
        gram = low_dot(v_ref[...], v_ref[...], ROWS_BY_ROWS)
        for payload in arrived:
            gram = gram + payload.gram()
    encode([functools.partial(value, slot, p) for slot in slots for p in range(count)], gram, coded_ref, rank)


def next_projection(slots, first, count, with_gram, layouts, place, visits, v_rows, arrived, after):
    rank = v_rows.shape[0]
    return pl.pallas_call(
        functools.partial(next_projection_kernel, slots, first, count, with_gram, layouts),
        in_specs=[SMEM_SPEC] + [VMEM_SPEC] * (2 + len(arrived)) + [ANY_SPEC] * len(after),
        out_specs=VMEM_SPEC,
        out_shape=jax.ShapeDtypeStruct(payload_shape(len(slots) * count, rank, visits.shape[2], with_gram), jnp.int16),
        compiler_params=parameters(LIMIT),
        cost_estimate=SHORT,
        name="project_next",
    )(place, v_rows, visits, *arrived, *after)


def w_gram_kernel(w_ref, gram_ref):
    gram_ref[...] = high_dot(w_ref[...], w_ref[...], COLS_BY_COLS)


def own_w_gram(w_start):
    rank = w_start.shape[1]
    return pl.pallas_call(
        w_gram_kernel,
        in_specs=[VMEM_SPEC],
        out_specs=VMEM_SPEC,
        out_shape=jax.ShapeDtypeStruct((rank, rank), F32),
        compiler_params=parameters(LIMIT),
        cost_estimate=SHORT,
        name="own_w_gram",
    )(w_start)


def own_projection_kernel(place, v_ref, visits_ref, *refs):
    *proj_refs, v_gram_ref = refs
    count = visits_ref.shape[1] // len(proj_refs)
    for p in range(visits_ref.shape[1]):
        proj_refs[p // count][p % count] = low_dot(v_ref[...], visits_ref[feature_of(place), p], ROWS_BY_ROWS)
    v_gram_ref[...] = low_dot(v_ref[...], v_ref[...], ROWS_BY_ROWS)


def project_own(n_parts, place, visits, v_rows):
    _, share, slots, width = visits.shape
    rank = v_rows.shape[0]
    proj = jax.ShapeDtypeStruct((share // n_parts, rank, slots), F32)
    *own, v_gram = pl.pallas_call(
        own_projection_kernel,
        in_specs=[SMEM_SPEC] + [VMEM_SPEC] * 2,
        out_specs=[VMEM_SPEC] * (n_parts + 1),
        out_shape=[proj] * n_parts + [jax.ShapeDtypeStruct((rank, rank), F32)],
        compiler_params=parameters(LIMIT),
        cost_estimate=SHORT,
        name="project_own",
    )(place, v_rows, visits)
    return own, v_gram


def solve_tile(columns, tile):
    rows = lax.broadcasted_iota(jnp.int32, tile.shape, 0)
    for a in range(0, 8, 2):
        b = a + 1
        first, second = columns[a], columns[b]
        m_aa, m_ab, m_ba, m_bb = first[a:b], second[a:b], first[b : b + 1], second[b : b + 1]
        scale = 1.0 / (m_aa * m_bb - m_ab * m_ba)
        m_aa, m_ab, m_ba, m_bb = m_aa * scale, m_ab * scale, m_ba * scale, m_bb * scale

        def step(x):
            x_a, x_b = x[a:b], x[b : b + 1]
            new_a, new_b = m_bb * x_a - m_ab * x_b, m_aa * x_b - m_ba * x_a
            x = x - (first * new_a + second * new_b)
            return jnp.where(rows == a, new_a, jnp.where(rows == b, new_b, x))

        tile = step(tile)
        columns = [step(x) if q > b else x for q, x in enumerate(columns)]
    return tile


def eliminate(table, rank):
    tiles = [table[8 * t : 8 * t + 8] for t in range(rank // 8)]
    for home in range(rank // 8):
        first = 8 * home
        columns = [[jnp.broadcast_to(t[:, q : q + 1], t.shape) for q in range(first, first + 8)] for t in tiles]
        solved = solve_tile(columns[home], tiles[home])
        for t, tile in enumerate(tiles):
            terms = [column * solved[q : q + 1] for q, column in enumerate(columns[t])]
            while len(terms) > 1:
                terms = [x + y for x, y in zip(terms[::2], terms[1::2])]
            tiles[t] = solved if t == home else tile - terms[0]
    return jnp.concatenate(tiles, axis=0)


def inverse_of(gram):
    rank = gram.shape[0]
    eye = (lax.broadcasted_iota(jnp.int32, gram.shape, 0) == lane_numbers(gram.shape)).astype(F32)
    return eliminate(jnp.concatenate([gram, eye], axis=1), rank)[:, rank:]


def total(refs):
    out = refs[0][...]
    for ref in refs[1:]:
        out = out + ref[...]
    return out


def first_inverse_kernel(v_gram_ref, *refs):
    *terms, _, w_gram_ref, inverse_ref = refs
    w_gram = total(terms)
    w_gram_ref[...] = w_gram
    inverse_ref[...] = inverse_of(w_gram * v_gram_ref[...])


def first_inverse(v_gram, w_grams, after):
    out = jax.ShapeDtypeStruct(v_gram.shape, F32)
    return pl.pallas_call(
        first_inverse_kernel,
        in_specs=[VMEM_SPEC] * (1 + len(w_grams)) + [ANY_SPEC],
        out_specs=[VMEM_SPEC] * 2,
        out_shape=[out, out],
        compiler_params=parameters(LIMIT),
        cost_estimate=SHORT,
        name="first_inverse",
    )(v_gram, *w_grams, after)


def sweep_all(frames, rank, fine):
    patients = range(frames.shape[0])
    if fine:
        both = [jnp.concatenate(two_parts(frames[p]), axis=0) for p in patients]
        blocks = [low_dot(x, x, ROWS_BY_ROWS) for x in both]
        blocks = [x[:rank] + x[rank:] for x in blocks]
        grams = [x + pltpu.roll(x, rank, 1) for x in blocks]
        moved = [low_dot(jnp.concatenate(two_parts(g), axis=0), x) for g, x in zip(grams, both)]
        moved = [x[:rank] + x[rank:] for x in moved]
    else:
        first = [frames[p].astype(BF16) for p in patients]
        grams = [low_dot(x, x, ROWS_BY_ROWS).astype(BF16) for x in first]
        moved = [low_dot(g, x) for g, x in zip(grams, first)]
    for p in patients:
        frames[p] = 1.5 * frames[p] - 0.5 * moved[p]


def frames_kernel(layouts, part, share, place, counts_ref, h_ref, w_ref, v_gram_ref, before_ref, own_ref, *refs):
    coded, refs = refs[: len(layouts)], refs[len(layouts) :]
    frames_ref, terms_ref, v_total_ref, proj, frames = refs
    count, rank, slots = frames.shape
    patients = range(count)
    first = feature_of(place) * share + part * count
    pieces = [own_ref[p] for p in patients]
    v_gram = v_gram_ref[...]
    for code, layout in zip(coded, layouts):
        payload = Payload(code, layout, count, rank, (part + 1) * count == share)
        pieces = [pieces[p] + payload.proj(0, p) for p in patients]
        if payload.with_gram:
            v_gram = v_gram + payload.gram()
    v_total_ref[...] = v_gram
    for p in patients:
        proj[p] = pieces[p]
    weights = [w_ref[pl.ds(first + p, 1), :] for p in patients]
    mixed = [high_dot(h_ref[...] * weights[p], pieces[p]) for p in patients]
    lanes = lane_numbers((rank, slots))
    mixed = [jnp.where(lanes < counts_ref[first + p], mixed[p], 0.0) for p in patients]
    energy = [jnp.sum(jnp.sum(x * x, axis=1, keepdims=True), axis=0, keepdims=True) for x in mixed]
    for p in patients:
        frames[p] = mixed[p] * lax.rsqrt(energy[p] + epsilon)

    def sweep(fine, step, carry):
        sweep_all(frames, rank, fine)
        return carry

    lax.fori_loop(0, COARSE_STEPS, functools.partial(sweep, False), 0, unroll=True)
    lax.fori_loop(COARSE_STEPS, NS_STEPS, functools.partial(sweep, True), 0, unroll=3)
    low = [frames[p].astype(BF16) for p in patients]
    for p in patients:
        frames_ref[p] = low[p]
    products = [jnp.concatenate(three_parts(proj[p]), axis=0) for p in patients]
    products = [low_dot(low[p], products[p], ROWS_BY_ROWS) for p in patients]
    terms = before_ref[...] if part else jnp.zeros((rank, rank), F32)
    for p in patients:
        product = products[p][:, :rank] + (products[p][:, rank : 2 * rank] + products[p][:, 2 * rank :])
        terms = terms + product * weights[p]
    terms_ref[...] = terms


def own_frames(layouts, part, n_parts, place, counts, h_start, w_start, v_gram, before, own, coded):
    count, rank, slots = own.shape
    share = count * n_parts
    return pl.pallas_call(
        functools.partial(frames_kernel, layouts, part, share),
        in_specs=[SMEM_SPEC] * 2 + [VMEM_SPEC] * (5 + len(coded)),
        out_specs=[VMEM_SPEC] * 3,
        out_shape=[
            jax.ShapeDtypeStruct(own.shape, BF16),
            jax.ShapeDtypeStruct((rank, rank), F32),
            jax.ShapeDtypeStruct((rank, rank), F32),
        ],
        scratch_shapes=[pltpu.VMEM(own.shape, F32)] * 2,
        compiler_params=parameters(LIMIT),
        cost_estimate=SHORT,
        name="own_frames",
    )(place, counts, h_start, w_start, v_gram, before, own, *coded)


def projected_kernel(items, place, visits_ref, *refs):
    frames_refs, outs, token_ref = refs[: len(items)], refs[-2 * len(items) - 1 : -1], refs[-1]
    token_ref[...] = jnp.zeros_like(token_ref)
    for i, (slots, first) in enumerate(items):
        total_count, rank, _ = frames_refs[i].shape
        count = total_count // len(slots)
        for p in range(total_count):
            rows = pl.ds(p * rank, rank)
            owner = feature_of(place) ^ slots[p // count]
            product = low_dot(frames_refs[i][p], visits_ref[owner, first + p % count])
            outs[2 * i][rows, :], outs[2 * i + 1][rows, :] = two_parts(product)


def join_kernel(count, *refs):
    out_ref = refs[-1]
    first = 0
    for part in refs[:count]:
        out_ref[first : first + part.shape[0]] = part[...]
        first += part.shape[0]


def join(parts, after):
    if len(parts) == 1:
        return parts[0]
    return pl.pallas_call(
        functools.partial(join_kernel, len(parts)),
        in_specs=[VMEM_SPEC] * len(parts) + [ANY_SPEC] * len(after),
        out_specs=VMEM_SPEC,
        out_shape=jax.ShapeDtypeStruct((sum(x.shape[0] for x in parts),) + parts[0].shape[1:], parts[0].dtype),
        compiler_params=parameters(LIMIT),
        cost_estimate=SHORT,
        name="join_frames",
    )(*parts, *after)


def project_frames(items, place, frames, visits, after):
    width = visits.shape[-1]
    outs = []
    for item in items:
        count, rank, _ = frames[item].shape
        outs += [jax.ShapeDtypeStruct((count * rank, width), BF16)] * 2
    *parts, token = pl.pallas_call(
        functools.partial(projected_kernel, items),
        in_specs=[SMEM_SPEC] + [VMEM_SPEC] * (1 + len(items)) + [ANY_SPEC] * len(after),
        out_specs=[VMEM_SPEC] * (len(outs) + 1),
        out_shape=outs + [jax.ShapeDtypeStruct((8, LANES), F32)],
        compiler_params=parameters(LIMIT),
        cost_estimate=SHORT,
        name="project_frames",
    )(place, visits, *[frames[item] for item in items], *after)
    return {item: parts[2 * i : 2 * i + 2] for i, item in enumerate(items)}, token


def next_h_kernel(n_terms, n_slots, place, *refs):
    inverse_ref, w_ref, _, result_ref, h_ref, factor_ref = refs[n_terms:]
    h_next = high_dot(total(refs[:n_terms]), inverse_ref[...])
    result_ref[...] = h_next
    h_ref[...] = h_next
    rank = h_next.shape[0]
    patients = w_ref.shape[0]
    share = patients // n_slots
    h_rows = h_next.T
    w_rows = jnp.concatenate([w_ref[...], jnp.zeros((LANES - patients, rank), F32)], axis=0)
    w_columns = w_rows.T
    for slot in range(n_slots):
        first = (feature_of(place) ^ slot) * share
        columns = pltpu.roll(w_columns, jnp.where(first == 0, 0, LANES - first), 1)
        factor = jnp.concatenate([h_rows * columns[:, p : p + 1] for p in range(share)], axis=1)
        factor_ref[slot] = jnp.concatenate(three_parts(factor), axis=0)


def next_h(place, terms, inverse, w_start, n_slots, after):
    patients, rank = w_start.shape
    share = patients // n_slots
    return pl.pallas_call(
        functools.partial(next_h_kernel, len(terms), n_slots),
        in_specs=[SMEM_SPEC] + [VMEM_SPEC] * (len(terms) + 2) + [ANY_SPEC],
        out_specs=[VMEM_SPEC] * 3,
        out_shape=[
            jax.ShapeDtypeStruct(inverse.shape, F32),
            jax.ShapeDtypeStruct(inverse.shape, F32),
            jax.ShapeDtypeStruct((n_slots, 3 * rank, share * rank), BF16),
        ],
        compiler_params=parameters(LIMIT),
        cost_estimate=SHORT,
        name="next_h",
    )(place, *terms, inverse, w_start, after)


def second_inverse_kernel(h_ref, w_gram_ref, gram_ref, inverse_ref):
    gram = high_dot(h_ref[...], h_ref[...], COLS_BY_COLS)
    gram_ref[...] = gram
    inverse_ref[...] = inverse_of(gram * w_gram_ref[...])


def second_inverse(h_next, w_gram):
    out = jax.ShapeDtypeStruct(w_gram.shape, F32)
    return pl.pallas_call(
        second_inverse_kernel,
        out_shape=[out, out],
        compiler_params=parameters(LIMIT),
        cost_estimate=SHORT,
        name="second_inverse",
    )(h_next, w_gram)


def v_terms_kernel(items, place, factor_ref, *refs):
    *parts, keep_ref, send_ref, terms_ref = refs
    rank, width = terms_ref.shape
    half = width // 2
    total = None
    for i, (slots, first) in enumerate(items):
        count = parts[2 * i].shape[0] // len(slots)
        columns = pl.ds(first * rank, count)
        for k, slot in enumerate(slots):
            rows = pl.ds(k * count, count)
            large = low_dot(factor_ref[slot, :, columns], parts[2 * i][rows, :])
            small = low_dot(factor_ref[slot, : 2 * rank, columns], parts[2 * i + 1][rows, :])
            terms = large[:rank] + (large[rank : 2 * rank] + small[:rank]) + (large[2 * rank :] + small[rank:])
            total = terms if total is None else total + terms
    terms_ref[...] = total
    keep_ref[...] = terms_ref[:, pl.ds(pl.multiple_of(core_of(place) * half, half), half)]
    send_ref[...] = terms_ref[:, pl.ds(pl.multiple_of((1 - core_of(place)) * half, half), half)]


def all_v_terms(items, place, factor, projected):
    width = projected[0].shape[1]
    rank = factor.shape[1] // 3
    half = (rank, width // 2)
    return pl.pallas_call(
        functools.partial(v_terms_kernel, items),
        in_specs=[SMEM_SPEC] + [VMEM_SPEC] * (1 + len(projected)),
        out_specs=[VMEM_SPEC] * 2,
        out_shape=[jax.ShapeDtypeStruct(half, F32)] * 2,
        scratch_shapes=[pltpu.VMEM((rank, width), F32)],
        compiler_params=parameters(LIMIT),
        cost_estimate=SHORT,
        name="v_terms",
    )(place, factor, *projected)


def next_v_kernel(items, share, place, own_ref, other_ref, inverse_ref, h_ref, *refs):
    *parts, v_ref, sums_ref, v_parts = refs
    rank = inverse_ref.shape[0]
    upper = core_of(place) == 1
    left = jnp.where(upper, other_ref[...], own_ref[...])
    right = jnp.where(upper, own_ref[...], other_ref[...])
    v_rows = high_dot(inverse_ref[...], jnp.concatenate([left, right], axis=1))
    v_ref[...] = v_rows
    v_parts[...] = jnp.concatenate(two_parts(v_rows), axis=0)
    weights = jnp.concatenate([h_ref[...]] * 2, axis=1)
    gram = low_dot(v_parts[...], v_parts[...], ROWS_BY_ROWS)
    gram = gram[:rank, :rank] + (gram[:rank, rank:] + gram[rank:, :rank])
    sums_ref[...] = jnp.concatenate([jnp.zeros((rank, rank), F32), gram], axis=1)
    for i, (slots, done) in enumerate(items):
        seen = low_dot(parts[2 * i][...], v_parts[...], ROWS_BY_ROWS)
        seen = seen + low_dot(parts[2 * i + 1][...], v_parts[...], ROWS_BY_ROWS)
        count = seen.shape[0] // rank // len(slots)
        for p in range(seen.shape[0] // rank):
            patient = (feature_of(place) ^ slots[p // count]) * share + done + p % count
            row = jnp.sum(seen[p * rank : (p + 1) * rank] * weights, axis=0, keepdims=True)
            sums_ref[pl.ds(patient, 1), :rank] = row[:, :rank] + row[:, rank:]


def next_v(items, share, place, own, other, inverse, h_next, projected):
    width = projected[0].shape[1]
    rank = inverse.shape[0]
    return pl.pallas_call(
        functools.partial(next_v_kernel, items, share),
        in_specs=[SMEM_SPEC] + [VMEM_SPEC] * (4 + len(projected)),
        out_specs=[VMEM_SPEC] * 2,
        out_shape=[
            jax.ShapeDtypeStruct((rank, width), F32),
            jax.ShapeDtypeStruct((rank, 2 * rank), F32),
        ],
        scratch_shapes=[pltpu.VMEM((2 * rank, width), BF16)],
        compiler_params=parameters(LIMIT),
        cost_estimate=SHORT,
        name="next_v",
    )(place, own, other, inverse, h_next, *projected)


def next_w_kernel(n_sums, *refs):
    gram_ref, w_ref = refs[n_sums:]
    patients, rank = w_ref.shape
    sums = total(refs[:n_sums])
    table = jnp.concatenate([sums[:, rank:] * gram_ref[...], sums.T[:rank]], axis=1)
    w_ref[...] = eliminate(table, rank).T[rank : rank + patients]


def next_w(sums, h_gram, patients):
    rank = h_gram.shape[0]
    return pl.pallas_call(
        functools.partial(next_w_kernel, len(sums)),
        out_shape=jax.ShapeDtypeStruct((patients, rank), F32),
        compiler_params=parameters(LIMIT),
        cost_estimate=SHORT,
        name="next_w",
    )(*sums, h_gram)


def swap(x, axis, slot):
    pairs = [(i, i ^ slot) for i in range(lax.axis_size(axis))]
    return lax.ppermute(x, axis, pairs)


def all_terms(x, axis):
    n = lax.axis_size(axis)
    if n > 4:
        return [lax.psum(x, axis)]
    return [x] + [swap(x, axis, s) for s in range(1, n)]


def staged_terms(x, axis, after):
    n = lax.axis_size(axis)
    steps = [1 << i for i in range(n.bit_length() - 1)]
    for step in steps[:-1]:
        x = add(x, swap(x, axis, step), after)
    return [x, swap(x, axis, steps[-1])]


def add_kernel(a_ref, b_ref, *refs):
    refs[-1][...] = a_ref[...] + b_ref[...]


def add(a, b, after):
    return pl.pallas_call(
        add_kernel,
        in_specs=[VMEM_SPEC] * 2 + [ANY_SPEC] * len(after),
        out_specs=VMEM_SPEC,
        out_shape=jax.ShapeDtypeStruct(a.shape, a.dtype),
        compiler_params=parameters(LIMIT),
        cost_estimate=SHORT,
        name="add_terms",
    )(a, b, *after)


def patient_halves(keep, send, after):
    own = add(keep, swap(send, "patient", 1), [])
    step = 2
    while step < lax.axis_size("patient"):
        own = add(own, swap(own, "patient", step), [after])
        step *= 2
    return own, swap(own, "patient", 1)


def on_device(visits, visit_counts, h_start, v_start, w_start):
    n = lax.axis_size("feature")
    patients, slots, width = visits.shape
    share = patients // n
    place = (2 * lax.axis_index("feature") + (lax.axis_index("patient") & 1)).astype(jnp.int32).reshape(1)
    by_owner = visits.reshape(n, share, slots, width)
    in_hbm = pltpu.with_memory_space_constraint(by_owner, pltpu.HBM)
    v_rows = pltpu.with_memory_space_constraint(v_start.T, pltpu.HBM)

    n_parts = 2 if share % 2 == 0 else 1
    count = share // n_parts
    firsts = [part * count for part in range(n_parts)]
    bits = [1 << i for i in range(n.bit_length() - 1)]
    v_near = v_start.T

    def send(bit):
        return [slot for slot in range(n) if slot & bit and not slot & (bit - 1)]

    def receive(bit):
        return [slot ^ bit for slot in send(bit)]

    w_grams = staged_terms(own_w_gram(w_start), "patient", [])
    own, v_gram = project_own(n_parts, place, by_owner, v_near)
    h_local = v_gram
    arrived = [[] for _ in firsts]
    for i, bit in enumerate(bits):
        layouts = [receive(before) for before in bits[:i]]
        for part, first in enumerate(firsts):
            if i == 0 and part == 0:
                code = first_projection(send(bit), count, n_parts == 1, place, in_hbm, v_rows)
            else:
                after = [w_grams[part]] + [v_gram] * part if i else []
                code = next_projection(
                    send(bit), first, count, part == n_parts - 1, layouts, place, by_owner, v_near, arrived[part], after
                )
            arrived[part] = arrived[part] + [swap(code, "feature", bit)]

    layouts = [receive(bit) for bit in bits]
    frames = [[] for _ in firsts]
    joined = []

    def double(part, after):
        for bit in bits[::-1]:
            slots = tuple(slot ^ bit for group, _ in frames[part] for slot in group)
            joined = join([x for _, x in frames[part]], after)
            frames[part].append((slots, swap(joined, "feature", bit)))
        return [joined]

    def project_groups(groups, after):
        arrays = {(frames[part][k][0], firsts[part]): frames[part][k][1] for part, k in groups}
        return project_frames(list(arrays), place, arrays, by_owner, after)

    for part, first in enumerate(firsts):
        low, h_local, v_total = own_frames(
            layouts, part, n_parts, place, visit_counts, h_start, w_start, v_gram, h_local, own[part], arrived[part]
        )
        v_gram = v_total
        frames[part].append(((0,), low))

    last = len(bits)
    for part in range(n_parts - 1):
        joined = double(part, [frames[-1][0][1]])
    projected, token = project_groups([(part, 0) for part in range(n_parts)], joined)
    early = [(part, k) for part in range(n_parts - 1) for k in range(1, last + 1)]
    h_sums = staged_terms(h_local, "patient", [token])
    more, token = project_groups(early, h_sums[:1])
    projected |= more
    h_sum = add(*h_sums, [token])
    joined = double(n_parts - 1, [h_sum])
    h_terms = all_terms(h_sum, "feature")
    w_gram, inverse = first_inverse(v_gram, w_grams, joined[0])
    after = [inverse]
    for k in range(1, last + 1):
        more, token = project_groups([(n_parts - 1, k)], after)
        projected |= more
        after = [token]
    h_result, h_next, factor = next_h(place, h_terms, inverse, w_start, n, token)

    items = list(projected)
    flat = [x for item in items for x in projected[item]]
    keep, send = all_v_terms(items, place, factor, flat)
    h_gram, second = second_inverse(h_next, w_gram)
    own_terms, other_terms = patient_halves(keep, send, second)
    v_next, sums = next_v(items, share, place, own_terms, other_terms, second, h_next, flat)
    w_next = next_w(all_terms(sums, "feature"), h_gram, patients)
    return (h_result, v_next.T, w_next)


def solution(mesh):
    return jax.shard_map(
        on_device,
        mesh=mesh,
        in_specs=(
            P(("groups", "patient"), None, "feature"),
            P(("groups", "patient")),
            P(),
            P("feature", None),
            P(("groups", "patient"), None),
        ),
        out_specs=(P(None, "groups"), P("feature", "groups"), P("patient", "groups")),
        check_vma=False,
    )
```

```python
import functools

import jax
import jax.numpy as jnp
from jax import lax
from jax.experimental import pallas as pl
from jax.experimental.pallas import tpu as pltpu
from jax.sharding import PartitionSpec as P

NS_STEPS = 12
LANES = 128
LEVELS = 32000.0
COARSE_STEPS = 3
SHORT = pl.CostEstimate(flops=1000, bytes_accessed=1000, transcendentals=0)

epsilon = 1e-06
HIGH = lax.Precision.HIGHEST
F32 = jnp.float32
BF16 = jnp.bfloat16
MIB = 1024 * 1024

ROWS_BY_COLS = (((1,), (0,)), ((), ()))
ROWS_BY_ROWS = (((1,), (1,)), ((), ()))
COLS_BY_COLS = (((0,), (0,)), ((), ()))


def low_dot(a, b, dims=ROWS_BY_COLS):
    return lax.dot_general(a, b, dims, preferred_element_type=F32)


def high_dot(a, b, dims=ROWS_BY_COLS):
    return lax.dot_general(a, b, dims, precision=HIGH, preferred_element_type=F32)


def two_parts(x):
    first = x.astype(BF16)
    return first, (x - first.astype(F32)).astype(BF16)


def three_parts(x):
    first = x.astype(BF16)
    rest = x - first.astype(F32)
    second = rest.astype(BF16)
    return first, second, (rest - second.astype(F32)).astype(BF16)


def feature_of(place):
    return place[0] >> 1


def core_of(place):
    return place[0] & 1


def lane_numbers(shape):
    return lax.broadcasted_iota(jnp.int32, shape, len(shape) - 1)


ANY_SPEC = pl.BlockSpec(memory_space=pl.ANY)
HBM_SPEC = pl.BlockSpec(memory_space=pltpu.HBM)


def parameters(mib):
    return pltpu.CompilerParams(vmem_limit_bytes=mib * MIB)


LIMIT = 8
VMEM_SPEC = pl.BlockSpec(memory_space=pltpu.VMEM)
SMEM_SPEC = pl.BlockSpec(memory_space=pltpu.SMEM)


def exponent_rows(total_count):
    return -(-(total_count + 1) // 16) * 16


def payload_shape(total_count, rank, slots, with_gram):
    return (total_count * rank + (rank // 2 if with_gram else 0) + exponent_rows(total_count), slots)


def row_exponent(x):
    top = jnp.max(jnp.abs(x), axis=1, keepdims=True)
    return jnp.ceil(jnp.log2(jnp.maximum(top, 1e-30)))


class Payload:
    def __init__(self, ref, slots, count, rank, with_gram):
        self.ref, self.slots, self.count, self.rank, self.with_gram = ref, slots, count, rank, with_gram
        self.entries = len(slots) * count
        gram_rows = rank // 2 if with_gram else 0
        exponents = self.rows(self.entries * rank + gram_rows, exponent_rows(self.entries))
        self.steps = jnp.exp2(exponents[:, :LANES].T[:rank]) * (1.0 / LEVELS)

    def rows(self, first, number):
        return self.ref[pl.ds(first, number), :].astype(jnp.int32).astype(F32)

    def proj(self, slot, p):
        entry = self.slots.index(slot) * self.count + p
        return self.rows(entry * self.rank, self.rank) * self.steps[:, entry : entry + 1]

    def gram(self):
        rank = self.rank
        digits = self.rows(self.entries * rank, rank // 2)
        digits = jnp.concatenate([digits[:, : 2 * rank], digits[:, 2 * rank :]], axis=0)
        return (digits[:, :rank] + digits[:, rank:] * (0.5 / LEVELS)) * self.steps[:, self.entries : self.entries + 1]


def encode(values, gram, coded_ref, rank):
    count = len(values)
    lanes = lane_numbers((rank, LANES))
    exponents = jnp.zeros((rank, LANES), F32)
    for p, value in enumerate(values):
        proj = value()
        exponent = row_exponent(proj)
        coded = jnp.floor(proj * (LEVELS / jnp.exp2(exponent)) + 0.5)
        coded_ref[pl.ds(p * rank, rank), :] = coded.astype(jnp.int32).astype(jnp.int16)
        exponents = jnp.where(lanes == p, exponent, exponents)
    end = count * rank
    if gram is not None:
        exponent = row_exponent(gram)
        scaled = gram * (LEVELS / jnp.exp2(exponent))
        whole = jnp.floor(scaled + 0.5)
        rest = jnp.floor((scaled - whole) * (2 * LEVELS) + 0.5)
        digits = jnp.concatenate([whole, rest], axis=1)
        digits = jnp.concatenate([digits[: rank // 2], digits[rank // 2 :]], axis=1)
        coded_ref[pl.ds(end, rank // 2), :] = digits.astype(jnp.int32).astype(jnp.int16)
        exponents = jnp.where(lanes == count, exponent, exponents)
        end += rank // 2
    rows = exponent_rows(count)
    last = jnp.concatenate([exponents.T[:rows], jnp.zeros((rows, coded_ref.shape[1] - rank), F32)], axis=1)
    coded_ref[pl.ds(end, rows), :] = last.astype(jnp.int32).astype(jnp.int16)


def first_projection_kernel(slots, with_gram, place, v_hbm, visits_ref, coded_ref, v_ref, buffers, sems, v_sem):
    count = buffers.shape[1]
    v_copy = pltpu.make_async_copy(v_hbm, v_ref, v_sem)
    v_copy.start()
    copies = [
        pltpu.make_async_copy(visits_ref.at[feature_of(place) ^ slot, pl.ds(0, count)], buffers.at[i], sems.at[i])
        for i, slot in enumerate(slots)
    ]
    for copy in copies:
        copy.start()
    v_copy.wait()

    def value(i, p):
        if p == 0:
            copies[i].wait()
        return low_dot(v_ref[...], buffers[i, p], ROWS_BY_ROWS)

    values = [functools.partial(value, i, p) for i in range(len(slots)) for p in range(count)]
    gram = low_dot(v_ref[...], v_ref[...], ROWS_BY_ROWS) if with_gram else None
    encode(values, gram, coded_ref, v_ref.shape[0])


def first_projection(slots, count, with_gram, place, visits, v_rows):
    width = visits.shape[3]
    rank = v_rows.shape[0]
    return pl.pallas_call(
        functools.partial(first_projection_kernel, slots, with_gram),
        in_specs=[SMEM_SPEC, HBM_SPEC, HBM_SPEC],
        out_specs=VMEM_SPEC,
        out_shape=jax.ShapeDtypeStruct(payload_shape(len(slots) * count, rank, visits.shape[2], with_gram), jnp.int16),
        scratch_shapes=[
            pltpu.VMEM(v_rows.shape, BF16),
            pltpu.VMEM((len(slots), count) + visits.shape[2:], BF16),
            pltpu.SemaphoreType.DMA((len(slots),)),
            pltpu.SemaphoreType.DMA,
        ],
        compiler_params=parameters(LIMIT),
        cost_estimate=SHORT,
        name="project_first",
    )(place, v_rows, visits)


def next_projection_kernel(slots, first, count, with_gram, layouts, place, v_ref, visits_ref, *refs):
    coded_ref = refs[-1]
    rank = v_ref.shape[0]
    arrived = [Payload(ref, layout, count, rank, with_gram) for ref, layout in zip(refs, layouts)]

    def value(slot, p):
        proj = low_dot(v_ref[...], visits_ref[feature_of(place) ^ slot, first + p], ROWS_BY_ROWS)
        for payload in arrived:
            proj = proj + payload.proj(slot, p)
        return proj

    gram = None
    if with_gram:
        gram = low_dot(v_ref[...], v_ref[...], ROWS_BY_ROWS)
        for payload in arrived:
            gram = gram + payload.gram()
    encode([functools.partial(value, slot, p) for slot in slots for p in range(count)], gram, coded_ref, rank)


def next_projection(slots, first, count, with_gram, layouts, place, visits, v_rows, arrived, after):
    rank = v_rows.shape[0]
    return pl.pallas_call(
        functools.partial(next_projection_kernel, slots, first, count, with_gram, layouts),
        in_specs=[SMEM_SPEC] + [VMEM_SPEC] * (2 + len(arrived)) + [ANY_SPEC] * len(after),
        out_specs=VMEM_SPEC,
        out_shape=jax.ShapeDtypeStruct(payload_shape(len(slots) * count, rank, visits.shape[2], with_gram), jnp.int16),
        compiler_params=parameters(LIMIT),
        cost_estimate=SHORT,
        name="project_next",
    )(place, v_rows, visits, *arrived, *after)


def w_gram_kernel(w_ref, gram_ref):
    gram_ref[...] = high_dot(w_ref[...], w_ref[...], COLS_BY_COLS)


def own_w_gram(w_start):
    rank = w_start.shape[1]
    return pl.pallas_call(
        w_gram_kernel,
        in_specs=[VMEM_SPEC],
        out_specs=VMEM_SPEC,
        out_shape=jax.ShapeDtypeStruct((rank, rank), F32),
        compiler_params=parameters(LIMIT),
        cost_estimate=SHORT,
        name="own_w_gram",
    )(w_start)


def own_projection_kernel(place, v_ref, visits_ref, *refs):
    *proj_refs, v_gram_ref = refs
    count = visits_ref.shape[1] // len(proj_refs)
    for p in range(visits_ref.shape[1]):
        proj_refs[p // count][p % count] = low_dot(v_ref[...], visits_ref[feature_of(place), p], ROWS_BY_ROWS)
    v_gram_ref[...] = low_dot(v_ref[...], v_ref[...], ROWS_BY_ROWS)


def project_own(n_parts, place, visits, v_rows):
    _, share, slots, width = visits.shape
    rank = v_rows.shape[0]
    proj = jax.ShapeDtypeStruct((share // n_parts, rank, slots), F32)
    *own, v_gram = pl.pallas_call(
        own_projection_kernel,
        in_specs=[SMEM_SPEC] + [VMEM_SPEC] * 2,
        out_specs=[VMEM_SPEC] * (n_parts + 1),
        out_shape=[proj] * n_parts + [jax.ShapeDtypeStruct((rank, rank), F32)],
        compiler_params=parameters(LIMIT),
        cost_estimate=SHORT,
        name="project_own",
    )(place, v_rows, visits)
    return own, v_gram


def solve_tile(columns, tile):
    rows = lax.broadcasted_iota(jnp.int32, tile.shape, 0)
    for a in range(0, 8, 2):
        b = a + 1
        first, second = columns[a], columns[b]
        m_aa, m_ab, m_ba, m_bb = first[a:b], second[a:b], first[b : b + 1], second[b : b + 1]
        scale = 1.0 / (m_aa * m_bb - m_ab * m_ba)
        m_aa, m_ab, m_ba, m_bb = m_aa * scale, m_ab * scale, m_ba * scale, m_bb * scale

        def step(x):
            x_a, x_b = x[a:b], x[b : b + 1]
            new_a, new_b = m_bb * x_a - m_ab * x_b, m_aa * x_b - m_ba * x_a
            x = x - (first * new_a + second * new_b)
            return jnp.where(rows == a, new_a, jnp.where(rows == b, new_b, x))

        tile = step(tile)
        columns = [step(x) if q > b else x for q, x in enumerate(columns)]
    return tile


def eliminate(table, rank):
    tiles = [table[8 * t : 8 * t + 8] for t in range(rank // 8)]
    for home in range(rank // 8):
        first = 8 * home
        columns = [[jnp.broadcast_to(t[:, q : q + 1], t.shape) for q in range(first, first + 8)] for t in tiles]
        solved = solve_tile(columns[home], tiles[home])
        for t, tile in enumerate(tiles):
            terms = [column * solved[q : q + 1] for q, column in enumerate(columns[t])]
            while len(terms) > 1:
                terms = [x + y for x, y in zip(terms[::2], terms[1::2])]
            tiles[t] = solved if t == home else tile - terms[0]
    return jnp.concatenate(tiles, axis=0)


def inverse_of(gram):
    rank = gram.shape[0]
    eye = (lax.broadcasted_iota(jnp.int32, gram.shape, 0) == lane_numbers(gram.shape)).astype(F32)
    return eliminate(jnp.concatenate([gram, eye], axis=1), rank)[:, rank:]


def total(refs):
    out = refs[0][...]
    for ref in refs[1:]:
        out = out + ref[...]
    return out


def first_inverse_kernel(v_gram_ref, *refs):
    *terms, _, w_gram_ref, inverse_ref = refs
    w_gram = total(terms)
    w_gram_ref[...] = w_gram
    inverse_ref[...] = inverse_of(w_gram * v_gram_ref[...])


def first_inverse(v_gram, w_grams, after):
    out = jax.ShapeDtypeStruct(v_gram.shape, F32)
    return pl.pallas_call(
        first_inverse_kernel,
        in_specs=[VMEM_SPEC] * (1 + len(w_grams)) + [ANY_SPEC],
        out_specs=[VMEM_SPEC] * 2,
        out_shape=[out, out],
        compiler_params=parameters(LIMIT),
        cost_estimate=SHORT,
        name="first_inverse",
    )(v_gram, *w_grams, after)


def sweep_all(frames, rank, fine):
    patients = range(frames.shape[0])
    if fine:
        both = [jnp.concatenate(two_parts(frames[p]), axis=0) for p in patients]
        blocks = [low_dot(x, x, ROWS_BY_ROWS) for x in both]
        blocks = [x[:rank] + x[rank:] for x in blocks]
        grams = [x + pltpu.roll(x, rank, 1) for x in blocks]
        moved = [low_dot(jnp.concatenate(two_parts(g), axis=0), x) for g, x in zip(grams, both)]
        moved = [x[:rank] + x[rank:] for x in moved]
    else:
        first = [frames[p].astype(BF16) for p in patients]
        grams = [low_dot(x, x, ROWS_BY_ROWS).astype(BF16) for x in first]
        moved = [low_dot(g, x) for g, x in zip(grams, first)]
    for p in patients:
        frames[p] = 1.5 * frames[p] - 0.5 * moved[p]


def frames_kernel(layouts, part, share, place, counts_ref, h_ref, w_ref, v_gram_ref, before_ref, own_ref, *refs):
    coded, refs = refs[: len(layouts)], refs[len(layouts) :]
    frames_ref, terms_ref, v_total_ref, proj, frames = refs
    count, rank, slots = frames.shape
    patients = range(count)
    first = feature_of(place) * share + part * count
    pieces = [own_ref[p] for p in patients]
    v_gram = v_gram_ref[...]
    for code, layout in zip(coded, layouts):
        payload = Payload(code, layout, count, rank, (part + 1) * count == share)
        pieces = [pieces[p] + payload.proj(0, p) for p in patients]
        if payload.with_gram:
            v_gram = v_gram + payload.gram()
    v_total_ref[...] = v_gram
    for p in patients:
        proj[p] = pieces[p]
    weights = [w_ref[pl.ds(first + p, 1), :] for p in patients]
    mixed = [high_dot(h_ref[...] * weights[p], pieces[p]) for p in patients]
    lanes = lane_numbers((rank, slots))
    mixed = [jnp.where(lanes < counts_ref[first + p], mixed[p], 0.0) for p in patients]
    energy = [jnp.sum(jnp.sum(x * x, axis=1, keepdims=True), axis=0, keepdims=True) for x in mixed]
    for p in patients:
        frames[p] = mixed[p] * lax.rsqrt(energy[p] + epsilon)

    def sweep(fine, step, carry):
        sweep_all(frames, rank, fine)
        return carry

    lax.fori_loop(0, COARSE_STEPS, functools.partial(sweep, False), 0, unroll=True)
    lax.fori_loop(COARSE_STEPS, NS_STEPS, functools.partial(sweep, True), 0, unroll=3)
    low = [frames[p].astype(BF16) for p in patients]
    for p in patients:
        frames_ref[p] = low[p]
    products = [jnp.concatenate(three_parts(proj[p]), axis=0) for p in patients]
    products = [low_dot(low[p], products[p], ROWS_BY_ROWS) for p in patients]
    terms = before_ref[...] if part else jnp.zeros((rank, rank), F32)
    for p in patients:
        product = products[p][:, :rank] + (products[p][:, rank : 2 * rank] + products[p][:, 2 * rank :])
        terms = terms + product * weights[p]
    terms_ref[...] = terms


def own_frames(layouts, part, n_parts, place, counts, h_start, w_start, v_gram, before, own, coded):
    count, rank, slots = own.shape
    share = count * n_parts
    return pl.pallas_call(
        functools.partial(frames_kernel, layouts, part, share),
        in_specs=[SMEM_SPEC] * 2 + [VMEM_SPEC] * (5 + len(coded)),
        out_specs=[VMEM_SPEC] * 3,
        out_shape=[
            jax.ShapeDtypeStruct(own.shape, BF16),
            jax.ShapeDtypeStruct((rank, rank), F32),
            jax.ShapeDtypeStruct((rank, rank), F32),
        ],
        scratch_shapes=[pltpu.VMEM(own.shape, F32)] * 2,
        compiler_params=parameters(LIMIT),
        cost_estimate=SHORT,
        name="own_frames",
    )(place, counts, h_start, w_start, v_gram, before, own, *coded)


def projected_kernel(items, place, visits_ref, *refs):
    frames_refs, outs, token_ref = refs[: len(items)], refs[-2 * len(items) - 1 : -1], refs[-1]
    token_ref[...] = jnp.zeros_like(token_ref)
    for i, (slots, first) in enumerate(items):
        total_count, rank, _ = frames_refs[i].shape
        count = total_count // len(slots)
        for p in range(total_count):
            rows = pl.ds(p * rank, rank)
            owner = feature_of(place) ^ slots[p // count]
            product = low_dot(frames_refs[i][p], visits_ref[owner, first + p % count])
            outs[2 * i][rows, :], outs[2 * i + 1][rows, :] = two_parts(product)


def join_kernel(count, *refs):
    out_ref = refs[-1]
    first = 0
    for part in refs[:count]:
        out_ref[first : first + part.shape[0]] = part[...]
        first += part.shape[0]


def join(parts, after):
    if len(parts) == 1:
        return parts[0]
    return pl.pallas_call(
        functools.partial(join_kernel, len(parts)),
        in_specs=[VMEM_SPEC] * len(parts) + [ANY_SPEC] * len(after),
        out_specs=VMEM_SPEC,
        out_shape=jax.ShapeDtypeStruct((sum(x.shape[0] for x in parts),) + parts[0].shape[1:], parts[0].dtype),
        compiler_params=parameters(LIMIT),
        cost_estimate=SHORT,
        name="join_frames",
    )(*parts, *after)


def project_frames(items, place, frames, visits, after):
    width = visits.shape[-1]
    outs = []
    for item in items:
        count, rank, _ = frames[item].shape
        outs += [jax.ShapeDtypeStruct((count * rank, width), BF16)] * 2
    *parts, token = pl.pallas_call(
        functools.partial(projected_kernel, items),
        in_specs=[SMEM_SPEC] + [VMEM_SPEC] * (1 + len(items)) + [ANY_SPEC] * len(after),
        out_specs=[VMEM_SPEC] * (len(outs) + 1),
        out_shape=outs + [jax.ShapeDtypeStruct((8, LANES), F32)],
        compiler_params=parameters(LIMIT),
        cost_estimate=SHORT,
        name="project_frames",
    )(place, visits, *[frames[item] for item in items], *after)
    return {item: parts[2 * i : 2 * i + 2] for i, item in enumerate(items)}, token


def next_h_kernel(n_terms, n_slots, place, *refs):
    inverse_ref, w_ref, _, result_ref, h_ref, factor_ref = refs[n_terms:]
    h_next = high_dot(total(refs[:n_terms]), inverse_ref[...])
    result_ref[...] = h_next
    h_ref[...] = h_next
    rank = h_next.shape[0]
    patients = w_ref.shape[0]
    share = patients // n_slots
    h_rows = h_next.T
    w_rows = jnp.concatenate([w_ref[...], jnp.zeros((LANES - patients, rank), F32)], axis=0)
    w_columns = w_rows.T
    for slot in range(n_slots):
        first = (feature_of(place) ^ slot) * share
        columns = pltpu.roll(w_columns, jnp.where(first == 0, 0, LANES - first), 1)
        factor = jnp.concatenate([h_rows * columns[:, p : p + 1] for p in range(share)], axis=1)
        factor_ref[slot] = jnp.concatenate(three_parts(factor), axis=0)


def next_h(place, terms, inverse, w_start, n_slots, after):
    patients, rank = w_start.shape
    share = patients // n_slots
    return pl.pallas_call(
        functools.partial(next_h_kernel, len(terms), n_slots),
        in_specs=[SMEM_SPEC] + [VMEM_SPEC] * (len(terms) + 2) + [ANY_SPEC],
        out_specs=[VMEM_SPEC] * 3,
        out_shape=[
            jax.ShapeDtypeStruct(inverse.shape, F32),
            jax.ShapeDtypeStruct(inverse.shape, F32),
            jax.ShapeDtypeStruct((n_slots, 3 * rank, share * rank), BF16),
        ],
        compiler_params=parameters(LIMIT),
        cost_estimate=SHORT,
        name="next_h",
    )(place, *terms, inverse, w_start, after)


def second_inverse_kernel(h_ref, w_gram_ref, gram_ref, inverse_ref):
    gram = high_dot(h_ref[...], h_ref[...], COLS_BY_COLS)
    gram_ref[...] = gram
    inverse_ref[...] = inverse_of(gram * w_gram_ref[...])


def second_inverse(h_next, w_gram):
    out = jax.ShapeDtypeStruct(w_gram.shape, F32)
    return pl.pallas_call(
        second_inverse_kernel,
        out_shape=[out, out],
        compiler_params=parameters(LIMIT),
        cost_estimate=SHORT,
        name="second_inverse",
    )(h_next, w_gram)


def v_terms_kernel(items, sent, place, factor_ref, *refs):
    parts, terms_ref = refs[: 2 * len(items)], refs[-1]
    rank, half = terms_ref.shape
    upper = core_of(place) ^ 1 if sent else core_of(place)
    features = pl.ds(pl.multiple_of(upper * half, half), half)
    total = None
    for i, (slots, first) in enumerate(items):
        count = parts[2 * i].shape[0] // len(slots)
        columns = pl.ds(first * rank, count)
        for k, slot in enumerate(slots):
            rows = pl.ds(k * count, count)
            large = low_dot(factor_ref[slot, :, columns], parts[2 * i][rows, features])
            small = low_dot(factor_ref[slot, : 2 * rank, columns], parts[2 * i + 1][rows, features])
            terms = large[:rank] + (large[rank : 2 * rank] + small[:rank]) + (large[2 * rank :] + small[rank:])
            total = terms if total is None else total + terms
    terms_ref[...] = total


def half_v_terms(items, sent, place, factor, projected, after):
    width = projected[0].shape[1]
    rank = factor.shape[1] // 3
    return pl.pallas_call(
        functools.partial(v_terms_kernel, items, sent),
        in_specs=[SMEM_SPEC] + [VMEM_SPEC] * (1 + len(projected)) + [ANY_SPEC] * len(after),
        out_specs=VMEM_SPEC,
        out_shape=jax.ShapeDtypeStruct((rank, width // 2), F32),
        compiler_params=parameters(LIMIT),
        cost_estimate=SHORT,
        name="v_terms",
    )(place, factor, *projected, *after)


def next_v_kernel(items, share, place, own_ref, other_ref, inverse_ref, h_ref, *refs):
    *parts, v_ref, sums_ref, v_parts = refs
    rank = inverse_ref.shape[0]
    upper = core_of(place) == 1
    left = jnp.where(upper, other_ref[...], own_ref[...])
    right = jnp.where(upper, own_ref[...], other_ref[...])
    v_rows = high_dot(inverse_ref[...], jnp.concatenate([left, right], axis=1))
    v_ref[...] = v_rows
    v_parts[...] = jnp.concatenate(two_parts(v_rows), axis=0)
    weights = jnp.concatenate([h_ref[...]] * 2, axis=1)
    gram = low_dot(v_parts[...], v_parts[...], ROWS_BY_ROWS)
    gram = gram[:rank, :rank] + (gram[:rank, rank:] + gram[rank:, :rank])
    sums_ref[...] = jnp.concatenate([jnp.zeros((rank, rank), F32), gram], axis=1)
    for i, (slots, done) in enumerate(items):
        seen = low_dot(parts[2 * i][...], v_parts[...], ROWS_BY_ROWS)
        seen = seen + low_dot(parts[2 * i + 1][...], v_parts[...], ROWS_BY_ROWS)
        count = seen.shape[0] // rank // len(slots)
        for p in range(seen.shape[0] // rank):
            patient = (feature_of(place) ^ slots[p // count]) * share + done + p % count
            row = jnp.sum(seen[p * rank : (p + 1) * rank] * weights, axis=0, keepdims=True)
            sums_ref[pl.ds(patient, 1), :rank] = row[:, :rank] + row[:, rank:]


def next_v(items, share, place, own, other, inverse, h_next, projected):
    width = projected[0].shape[1]
    rank = inverse.shape[0]
    return pl.pallas_call(
        functools.partial(next_v_kernel, items, share),
        in_specs=[SMEM_SPEC] + [VMEM_SPEC] * (4 + len(projected)),
        out_specs=[VMEM_SPEC] * 2,
        out_shape=[
            jax.ShapeDtypeStruct((rank, width), F32),
            jax.ShapeDtypeStruct((rank, 2 * rank), F32),
        ],
        scratch_shapes=[pltpu.VMEM((2 * rank, width), BF16)],
        compiler_params=parameters(LIMIT),
        cost_estimate=SHORT,
        name="next_v",
    )(place, own, other, inverse, h_next, *projected)


def next_w_kernel(n_sums, *refs):
    gram_ref, w_ref = refs[n_sums:]
    patients, rank = w_ref.shape
    sums = total(refs[:n_sums])
    table = jnp.concatenate([sums[:, rank:] * gram_ref[...], sums.T[:rank]], axis=1)
    w_ref[...] = eliminate(table, rank).T[rank : rank + patients]


def next_w(sums, h_gram, patients):
    rank = h_gram.shape[0]
    return pl.pallas_call(
        functools.partial(next_w_kernel, len(sums)),
        out_shape=jax.ShapeDtypeStruct((patients, rank), F32),
        compiler_params=parameters(LIMIT),
        cost_estimate=SHORT,
        name="next_w",
    )(*sums, h_gram)


def swap(x, axis, slot):
    pairs = [(i, i ^ slot) for i in range(lax.axis_size(axis))]
    return lax.ppermute(x, axis, pairs)


def all_terms(x, axis):
    n = lax.axis_size(axis)
    if n > 4:
        return [lax.psum(x, axis)]
    return [x] + [swap(x, axis, s) for s in range(1, n)]


def staged_terms(x, axis, after):
    n = lax.axis_size(axis)
    steps = [1 << i for i in range(n.bit_length() - 1)]
    for step in steps[:-1]:
        x = add(x, swap(x, axis, step), after)
    return [x, swap(x, axis, steps[-1])]


def add_kernel(a_ref, b_ref, *refs):
    refs[-1][...] = a_ref[...] + b_ref[...]


def add(a, b, after):
    return pl.pallas_call(
        add_kernel,
        in_specs=[VMEM_SPEC] * 2 + [ANY_SPEC] * len(after),
        out_specs=VMEM_SPEC,
        out_shape=jax.ShapeDtypeStruct(a.shape, a.dtype),
        compiler_params=parameters(LIMIT),
        cost_estimate=SHORT,
        name="add_terms",
    )(a, b, *after)


def patient_halves(keep, send, after):
    own = add(keep, swap(send, "patient", 1), [])
    step = 2
    while step < lax.axis_size("patient"):
        own = add(own, swap(own, "patient", step), [after])
        step *= 2
    return own, swap(own, "patient", 1)


def on_device(visits, visit_counts, h_start, v_start, w_start):
    n = lax.axis_size("feature")
    patients, slots, width = visits.shape
    share = patients // n
    place = (2 * lax.axis_index("feature") + (lax.axis_index("patient") & 1)).astype(jnp.int32).reshape(1)
    by_owner = visits.reshape(n, share, slots, width)
    in_hbm = pltpu.with_memory_space_constraint(by_owner, pltpu.HBM)
    v_rows = pltpu.with_memory_space_constraint(v_start.T, pltpu.HBM)

    n_parts = 2 if share % 2 == 0 else 1
    count = share // n_parts
    firsts = [part * count for part in range(n_parts)]
    bits = [1 << i for i in range(n.bit_length() - 1)]
    v_near = v_start.T

    def send(bit):
        return [slot for slot in range(n) if slot & bit and not slot & (bit - 1)]

    def receive(bit):
        return [slot ^ bit for slot in send(bit)]

    w_grams = staged_terms(own_w_gram(w_start), "patient", [])
    own, v_gram = project_own(n_parts, place, by_owner, v_near)
    h_local = v_gram
    arrived = [[] for _ in firsts]
    for i, bit in enumerate(bits):
        layouts = [receive(before) for before in bits[:i]]
        for part, first in enumerate(firsts):
            if i == 0 and part == 0:
                code = first_projection(send(bit), count, n_parts == 1, place, in_hbm, v_rows)
            else:
                after = [w_grams[part]] + [v_gram] * part if i else []
                code = next_projection(
                    send(bit), first, count, part == n_parts - 1, layouts, place, by_owner, v_near, arrived[part], after
                )
            arrived[part] = arrived[part] + [swap(code, "feature", bit)]

    layouts = [receive(bit) for bit in bits]
    frames = [[] for _ in firsts]
    joined = []

    def double(part, after):
        for bit in bits[::-1]:
            slots = tuple(slot ^ bit for group, _ in frames[part] for slot in group)
            joined = join([x for _, x in frames[part]], after)
            frames[part].append((slots, swap(joined, "feature", bit)))
        return [joined]

    def project_groups(groups, after):
        arrays = {(frames[part][k][0], firsts[part]): frames[part][k][1] for part, k in groups}
        return project_frames(list(arrays), place, arrays, by_owner, after)

    for part, first in enumerate(firsts):
        low, h_local, v_total = own_frames(
            layouts, part, n_parts, place, visit_counts, h_start, w_start, v_gram, h_local, own[part], arrived[part]
        )
        v_gram = v_total
        frames[part].append(((0,), low))

    last = len(bits)
    for part in range(n_parts - 1):
        joined = double(part, [frames[-1][0][1]])
    first_groups = [(part, 0) for part in range(n_parts)] + [(part, 1) for part in range(n_parts - 1)]
    early = [(part, k) for part in range(n_parts - 1) for k in range(2, last + 1)]
    projected, token = project_groups(first_groups, joined)
    h_sums = staged_terms(h_local, "patient", [token])
    w_gram, inverse = first_inverse(v_gram, w_grams, h_sums[0])
    h_sum = add(*h_sums, [inverse])
    joined = double(n_parts - 1, [h_sum] + [frames[part][k][1] for part, k in early])
    h_terms = all_terms(h_sum, "feature")
    after = joined
    for groups in [early] + [[(n_parts - 1, k)] for k in range(1, last + 1)]:
        if groups:
            more, token = project_groups(groups, after)
            projected |= more
            after = [token]
    h_result, h_next, factor = next_h(place, h_terms, inverse, w_start, n, token)

    items = list(projected)
    flat = [x for item in items for x in projected[item]]
    send = half_v_terms(items, True, place, factor, flat, [])
    keep = half_v_terms(items, False, place, factor, flat, [send])
    h_gram, second = second_inverse(h_next, w_gram)
    own_terms, other_terms = patient_halves(keep, send, second)
    v_next, sums = next_v(items, share, place, own_terms, other_terms, second, h_next, flat)
    w_next = next_w(all_terms(sums, "feature"), h_gram, patients)
    return (h_result, v_next.T, w_next)


def solution(mesh):
    return jax.shard_map(
        on_device,
        mesh=mesh,
        in_specs=(
            P(("groups", "patient"), None, "feature"),
            P(("groups", "patient")),
            P(),
            P("feature", None),
            P(("groups", "patient"), None),
        ),
        out_specs=(P(None, "groups"), P("feature", "groups"), P("patient", "groups")),
        check_vma=False,
    )
```

```python
import functools

import jax
import jax.numpy as jnp
from jax import lax
from jax.experimental import pallas as pl
from jax.experimental.pallas import tpu as pltpu
from jax.sharding import PartitionSpec as P

NS_STEPS = 12
LANES = 128
LEVELS = 32000.0
COARSE_STEPS = 3
SHORT = pl.CostEstimate(flops=1000, bytes_accessed=1000, transcendentals=0)

epsilon = 1e-06
HIGH = lax.Precision.HIGHEST
F32 = jnp.float32
BF16 = jnp.bfloat16
MIB = 1024 * 1024

ROWS_BY_COLS = (((1,), (0,)), ((), ()))
ROWS_BY_ROWS = (((1,), (1,)), ((), ()))
COLS_BY_COLS = (((0,), (0,)), ((), ()))


def low_dot(a, b, dims=ROWS_BY_COLS):
    return lax.dot_general(a, b, dims, preferred_element_type=F32)


def high_dot(a, b, dims=ROWS_BY_COLS):
    return lax.dot_general(a, b, dims, precision=HIGH, preferred_element_type=F32)


def two_parts(x):
    first = x.astype(BF16)
    return first, (x - first.astype(F32)).astype(BF16)


def three_parts(x):
    first = x.astype(BF16)
    rest = x - first.astype(F32)
    second = rest.astype(BF16)
    return first, second, (rest - second.astype(F32)).astype(BF16)


def feature_of(place):
    return place[0] >> 1


def core_of(place):
    return place[0] & 1


def lane_numbers(shape):
    return lax.broadcasted_iota(jnp.int32, shape, len(shape) - 1)


ANY_SPEC = pl.BlockSpec(memory_space=pl.ANY)
HBM_SPEC = pl.BlockSpec(memory_space=pltpu.HBM)


def parameters(mib):
    return pltpu.CompilerParams(vmem_limit_bytes=mib * MIB)


LIMIT = 8
VMEM_SPEC = pl.BlockSpec(memory_space=pltpu.VMEM)
SMEM_SPEC = pl.BlockSpec(memory_space=pltpu.SMEM)


def exponent_rows(total_count):
    return -(-(total_count + 1) // 16) * 16


def payload_shape(total_count, rank, slots, with_gram):
    return (total_count * rank + (rank // 2 if with_gram else 0) + exponent_rows(total_count), slots)


def row_exponent(x):
    top = jnp.max(jnp.abs(x), axis=1, keepdims=True)
    return jnp.ceil(jnp.log2(jnp.maximum(top, 1e-30)))


class Payload:
    def __init__(self, ref, slots, count, rank, with_gram):
        self.ref, self.slots, self.count, self.rank, self.with_gram = ref, slots, count, rank, with_gram
        self.entries = len(slots) * count
        gram_rows = rank // 2 if with_gram else 0
        exponents = self.rows(self.entries * rank + gram_rows, exponent_rows(self.entries))
        self.steps = jnp.exp2(exponents[:, :LANES].T[:rank]) * (1.0 / LEVELS)

    def rows(self, first, number):
        return self.ref[pl.ds(first, number), :].astype(jnp.int32).astype(F32)

    def proj(self, slot, p):
        entry = self.slots.index(slot) * self.count + p
        return self.rows(entry * self.rank, self.rank) * self.steps[:, entry : entry + 1]

    def gram(self):
        rank = self.rank
        digits = self.rows(self.entries * rank, rank // 2)
        digits = jnp.concatenate([digits[:, : 2 * rank], digits[:, 2 * rank :]], axis=0)
        return (digits[:, :rank] + digits[:, rank:] * (0.5 / LEVELS)) * self.steps[:, self.entries : self.entries + 1]


def encode(values, gram, coded_ref, rank):
    count = len(values)
    lanes = lane_numbers((rank, LANES))
    exponents = jnp.zeros((rank, LANES), F32)
    for p, value in enumerate(values):
        proj = value()
        exponent = row_exponent(proj)
        coded = jnp.floor(proj * (LEVELS / jnp.exp2(exponent)) + 0.5)
        coded_ref[pl.ds(p * rank, rank), :] = coded.astype(jnp.int32).astype(jnp.int16)
        exponents = jnp.where(lanes == p, exponent, exponents)
    end = count * rank
    if gram is not None:
        exponent = row_exponent(gram)
        scaled = gram * (LEVELS / jnp.exp2(exponent))
        whole = jnp.floor(scaled + 0.5)
        rest = jnp.floor((scaled - whole) * (2 * LEVELS) + 0.5)
        digits = jnp.concatenate([whole, rest], axis=1)
        digits = jnp.concatenate([digits[: rank // 2], digits[rank // 2 :]], axis=1)
        coded_ref[pl.ds(end, rank // 2), :] = digits.astype(jnp.int32).astype(jnp.int16)
        exponents = jnp.where(lanes == count, exponent, exponents)
        end += rank // 2
    rows = exponent_rows(count)
    last = jnp.concatenate([exponents.T[:rows], jnp.zeros((rows, coded_ref.shape[1] - rank), F32)], axis=1)
    coded_ref[pl.ds(end, rows), :] = last.astype(jnp.int32).astype(jnp.int16)


def first_projection_kernel(slots, with_gram, place, v_hbm, visits_ref, coded_ref, v_ref, buffers, sems, v_sem):
    count = buffers.shape[1]
    v_copy = pltpu.make_async_copy(v_hbm, v_ref, v_sem)
    v_copy.start()
    copies = [
        pltpu.make_async_copy(visits_ref.at[feature_of(place) ^ slot, pl.ds(0, count)], buffers.at[i], sems.at[i])
        for i, slot in enumerate(slots)
    ]
    for copy in copies:
        copy.start()
    v_copy.wait()

    def value(i, p):
        if p == 0:
            copies[i].wait()
        return low_dot(v_ref[...], buffers[i, p], ROWS_BY_ROWS)

    values = [functools.partial(value, i, p) for i in range(len(slots)) for p in range(count)]
    gram = low_dot(v_ref[...], v_ref[...], ROWS_BY_ROWS) if with_gram else None
    encode(values, gram, coded_ref, v_ref.shape[0])


def first_projection(slots, count, with_gram, place, visits, v_rows):
    width = visits.shape[3]
    rank = v_rows.shape[0]
    return pl.pallas_call(
        functools.partial(first_projection_kernel, slots, with_gram),
        in_specs=[SMEM_SPEC, HBM_SPEC, HBM_SPEC],
        out_specs=VMEM_SPEC,
        out_shape=jax.ShapeDtypeStruct(payload_shape(len(slots) * count, rank, visits.shape[2], with_gram), jnp.int16),
        scratch_shapes=[
            pltpu.VMEM(v_rows.shape, BF16),
            pltpu.VMEM((len(slots), count) + visits.shape[2:], BF16),
            pltpu.SemaphoreType.DMA((len(slots),)),
            pltpu.SemaphoreType.DMA,
        ],
        compiler_params=parameters(LIMIT),
        cost_estimate=SHORT,
        name="project_first",
    )(place, v_rows, visits)


def next_projection_kernel(slots, first, count, with_gram, layouts, place, v_ref, visits_ref, *refs):
    coded_ref = refs[-1]
    rank = v_ref.shape[0]
    arrived = [Payload(ref, layout, count, rank, with_gram) for ref, layout in zip(refs, layouts)]

    def value(slot, p):
        proj = low_dot(v_ref[...], visits_ref[feature_of(place) ^ slot, first + p], ROWS_BY_ROWS)
        for payload in arrived:
            proj = proj + payload.proj(slot, p)
        return proj

    gram = None
    if with_gram:
        gram = low_dot(v_ref[...], v_ref[...], ROWS_BY_ROWS)
        for payload in arrived:
            gram = gram + payload.gram()
    encode([functools.partial(value, slot, p) for slot in slots for p in range(count)], gram, coded_ref, rank)


def next_projection(slots, first, count, with_gram, layouts, place, visits, v_rows, arrived, after):
    rank = v_rows.shape[0]
    return pl.pallas_call(
        functools.partial(next_projection_kernel, slots, first, count, with_gram, layouts),
        in_specs=[SMEM_SPEC] + [VMEM_SPEC] * (2 + len(arrived)) + [ANY_SPEC] * len(after),
        out_specs=VMEM_SPEC,
        out_shape=jax.ShapeDtypeStruct(payload_shape(len(slots) * count, rank, visits.shape[2], with_gram), jnp.int16),
        compiler_params=parameters(LIMIT),
        cost_estimate=SHORT,
        name="project_next",
    )(place, v_rows, visits, *arrived, *after)


def spread_w_kernel(n_slots, place, w_ref, gram_ref, spread_ref):
    gram_ref[...] = high_dot(w_ref[...], w_ref[...], COLS_BY_COLS)
    patients, rank = w_ref.shape
    share = patients // n_slots
    w_rows = jnp.concatenate([w_ref[...], jnp.zeros((LANES - patients, rank), F32)], axis=0)
    w_columns = w_rows.T
    for slot in range(n_slots):
        first = (feature_of(place) ^ slot) * share
        columns = pltpu.roll(w_columns, jnp.where(first == 0, 0, LANES - first), 1)
        spread = [jnp.broadcast_to(columns[:, p : p + 1], (rank, rank)) for p in range(share)]
        spread_ref[slot] = jnp.concatenate(spread, axis=1)


def spread_w(place, w_start, n_slots):
    patients, rank = w_start.shape
    return pl.pallas_call(
        functools.partial(spread_w_kernel, n_slots),
        in_specs=[SMEM_SPEC, VMEM_SPEC],
        out_specs=[VMEM_SPEC] * 2,
        out_shape=[
            jax.ShapeDtypeStruct((rank, rank), F32),
            jax.ShapeDtypeStruct((n_slots, rank, patients // n_slots * rank), F32),
        ],
        compiler_params=parameters(LIMIT),
        cost_estimate=SHORT,
        name="spread_w",
    )(place, w_start)


def own_projection_kernel(place, v_ref, visits_ref, *refs):
    *proj_refs, v_gram_ref = refs
    count = visits_ref.shape[1] // len(proj_refs)
    for p in range(visits_ref.shape[1]):
        proj_refs[p // count][p % count] = low_dot(v_ref[...], visits_ref[feature_of(place), p], ROWS_BY_ROWS)
    v_gram_ref[...] = low_dot(v_ref[...], v_ref[...], ROWS_BY_ROWS)


def project_own(n_parts, place, visits, v_rows):
    _, share, slots, width = visits.shape
    rank = v_rows.shape[0]
    proj = jax.ShapeDtypeStruct((share // n_parts, rank, slots), F32)
    *own, v_gram = pl.pallas_call(
        own_projection_kernel,
        in_specs=[SMEM_SPEC] + [VMEM_SPEC] * 2,
        out_specs=[VMEM_SPEC] * (n_parts + 1),
        out_shape=[proj] * n_parts + [jax.ShapeDtypeStruct((rank, rank), F32)],
        compiler_params=parameters(LIMIT),
        cost_estimate=SHORT,
        name="project_own",
    )(place, v_rows, visits)
    return own, v_gram


def solve_tile(columns, tile):
    rows = lax.broadcasted_iota(jnp.int32, tile.shape, 0)
    for a in range(0, 8, 2):
        b = a + 1
        first, second = columns[a], columns[b]
        m_aa, m_ab, m_ba, m_bb = first[a:b], second[a:b], first[b : b + 1], second[b : b + 1]
        scale = 1.0 / (m_aa * m_bb - m_ab * m_ba)
        m_aa, m_ab, m_ba, m_bb = m_aa * scale, m_ab * scale, m_ba * scale, m_bb * scale

        def step(x):
            x_a, x_b = x[a:b], x[b : b + 1]
            new_a, new_b = m_bb * x_a - m_ab * x_b, m_aa * x_b - m_ba * x_a
            x = x - (first * new_a + second * new_b)
            return jnp.where(rows == a, new_a, jnp.where(rows == b, new_b, x))

        tile = step(tile)
        columns = [step(x) if q > b else x for q, x in enumerate(columns)]
    return tile


def eliminate(table, rank):
    tiles = [table[8 * t : 8 * t + 8] for t in range(rank // 8)]
    for home in range(rank // 8):
        first = 8 * home
        columns = [[jnp.broadcast_to(t[:, q : q + 1], t.shape) for q in range(first, first + 8)] for t in tiles]
        solved = solve_tile(columns[home], tiles[home])
        for t, tile in enumerate(tiles):
            terms = [column * solved[q : q + 1] for q, column in enumerate(columns[t])]
            while len(terms) > 1:
                terms = [x + y for x, y in zip(terms[::2], terms[1::2])]
            tiles[t] = solved if t == home else tile - terms[0]
    return jnp.concatenate(tiles, axis=0)


def inverse_of(gram):
    rank = gram.shape[0]
    eye = (lax.broadcasted_iota(jnp.int32, gram.shape, 0) == lane_numbers(gram.shape)).astype(F32)
    return eliminate(jnp.concatenate([gram, eye], axis=1), rank)[:, rank:]


def total(refs):
    out = refs[0][...]
    for ref in refs[1:]:
        out = out + ref[...]
    return out


def first_inverse_kernel(v_gram_ref, *refs):
    *terms, _, w_gram_ref, inverse_ref = refs
    w_gram = total(terms)
    w_gram_ref[...] = w_gram
    inverse_ref[...] = inverse_of(w_gram * v_gram_ref[...])


def first_inverse(v_gram, w_grams, after):
    out = jax.ShapeDtypeStruct(v_gram.shape, F32)
    return pl.pallas_call(
        first_inverse_kernel,
        in_specs=[VMEM_SPEC] * (1 + len(w_grams)) + [ANY_SPEC],
        out_specs=[VMEM_SPEC] * 2,
        out_shape=[out, out],
        compiler_params=parameters(LIMIT),
        cost_estimate=SHORT,
        name="first_inverse",
    )(v_gram, *w_grams, after)


def sweep_all(frames, rank, fine):
    patients = range(frames.shape[0])
    if fine:
        both = [jnp.concatenate(two_parts(frames[p]), axis=0) for p in patients]
        blocks = [low_dot(x, x, ROWS_BY_ROWS) for x in both]
        blocks = [x[:rank] + x[rank:] for x in blocks]
        grams = [x + pltpu.roll(x, rank, 1) for x in blocks]
        moved = [low_dot(jnp.concatenate(two_parts(g), axis=0), x) for g, x in zip(grams, both)]
        moved = [x[:rank] + x[rank:] for x in moved]
    else:
        first = [frames[p].astype(BF16) for p in patients]
        grams = [low_dot(x, x, ROWS_BY_ROWS).astype(BF16) for x in first]
        moved = [low_dot(g, x) for g, x in zip(grams, first)]
    for p in patients:
        frames[p] = 1.5 * frames[p] - 0.5 * moved[p]


def frames_kernel(layouts, part, share, place, counts_ref, h_ref, w_ref, v_gram_ref, before_ref, own_ref, *refs):
    coded, refs = refs[: len(layouts)], refs[len(layouts) :]
    frames_ref, terms_ref, v_total_ref, proj, frames = refs
    count, rank, slots = frames.shape
    patients = range(count)
    first = feature_of(place) * share + part * count
    pieces = [own_ref[p] for p in patients]
    v_gram = v_gram_ref[...]
    for code, layout in zip(coded, layouts):
        payload = Payload(code, layout, count, rank, (part + 1) * count == share)
        pieces = [pieces[p] + payload.proj(0, p) for p in patients]
        if payload.with_gram:
            v_gram = v_gram + payload.gram()
    v_total_ref[...] = v_gram
    for p in patients:
        proj[p] = pieces[p]
    weights = [w_ref[pl.ds(first + p, 1), :] for p in patients]
    mixed = [high_dot(h_ref[...] * weights[p], pieces[p]) for p in patients]
    lanes = lane_numbers((rank, slots))
    mixed = [jnp.where(lanes < counts_ref[first + p], mixed[p], 0.0) for p in patients]
    energy = [jnp.sum(jnp.sum(x * x, axis=1, keepdims=True), axis=0, keepdims=True) for x in mixed]
    for p in patients:
        frames[p] = mixed[p] * lax.rsqrt(energy[p] + epsilon)

    def sweep(fine, step, carry):
        sweep_all(frames, rank, fine)
        return carry

    lax.fori_loop(0, COARSE_STEPS, functools.partial(sweep, False), 0, unroll=True)
    lax.fori_loop(COARSE_STEPS, NS_STEPS, functools.partial(sweep, True), 0, unroll=True)
    low = [frames[p].astype(BF16) for p in patients]
    for p in patients:
        frames_ref[p] = low[p]
    products = [jnp.concatenate(three_parts(proj[p]), axis=0) for p in patients]
    products = [low_dot(low[p], products[p], ROWS_BY_ROWS) for p in patients]
    terms = before_ref[...] if part else jnp.zeros((rank, rank), F32)
    for p in patients:
        product = products[p][:, :rank] + (products[p][:, rank : 2 * rank] + products[p][:, 2 * rank :])
        terms = terms + product * weights[p]
    terms_ref[...] = terms


def own_frames(layouts, part, n_parts, place, counts, h_start, w_start, v_gram, before, own, coded):
    count, rank, slots = own.shape
    share = count * n_parts
    return pl.pallas_call(
        functools.partial(frames_kernel, layouts, part, share),
        in_specs=[SMEM_SPEC] * 2 + [VMEM_SPEC] * (5 + len(coded)),
        out_specs=[VMEM_SPEC] * 3,
        out_shape=[
            jax.ShapeDtypeStruct(own.shape, BF16),
            jax.ShapeDtypeStruct((rank, rank), F32),
            jax.ShapeDtypeStruct((rank, rank), F32),
        ],
        scratch_shapes=[pltpu.VMEM(own.shape, F32)] * 2,
        compiler_params=parameters(LIMIT),
        cost_estimate=SHORT,
        name="own_frames",
    )(place, counts, h_start, w_start, v_gram, before, own, *coded)


def projected_kernel(items, place, visits_ref, *refs):
    frames_refs, outs, token_ref = refs[: len(items)], refs[-2 * len(items) - 1 : -1], refs[-1]
    token_ref[...] = jnp.zeros_like(token_ref)
    for i, (slots, first) in enumerate(items):
        total_count, rank, _ = frames_refs[i].shape
        count = total_count // len(slots)
        for p in range(total_count):
            rows = pl.ds(p * rank, rank)
            owner = feature_of(place) ^ slots[p // count]
            product = low_dot(frames_refs[i][p], visits_ref[owner, first + p % count])
            outs[2 * i][rows, :], outs[2 * i + 1][rows, :] = two_parts(product)


def join_kernel(count, *refs):
    out_ref = refs[-1]
    first = 0
    for part in refs[:count]:
        out_ref[first : first + part.shape[0]] = part[...]
        first += part.shape[0]


def join(parts, after):
    if len(parts) == 1:
        return parts[0]
    return pl.pallas_call(
        functools.partial(join_kernel, len(parts)),
        in_specs=[VMEM_SPEC] * len(parts) + [ANY_SPEC] * len(after),
        out_specs=VMEM_SPEC,
        out_shape=jax.ShapeDtypeStruct((sum(x.shape[0] for x in parts),) + parts[0].shape[1:], parts[0].dtype),
        compiler_params=parameters(LIMIT),
        cost_estimate=SHORT,
        name="join_frames",
    )(*parts, *after)


def project_frames(items, place, frames, visits, after):
    width = visits.shape[-1]
    outs = []
    for item in items:
        count, rank, _ = frames[item].shape
        outs += [jax.ShapeDtypeStruct((count * rank, width), BF16)] * 2
    *parts, token = pl.pallas_call(
        functools.partial(projected_kernel, items),
        in_specs=[SMEM_SPEC] + [VMEM_SPEC] * (1 + len(items)) + [ANY_SPEC] * len(after),
        out_specs=[VMEM_SPEC] * (len(outs) + 1),
        out_shape=outs + [jax.ShapeDtypeStruct((8, LANES), F32)],
        compiler_params=parameters(LIMIT),
        cost_estimate=SHORT,
        name="project_frames",
    )(place, visits, *[frames[item] for item in items], *after)
    return {item: parts[2 * i : 2 * i + 2] for i, item in enumerate(items)}, token


def next_h_kernel(n_terms, *refs):
    inverse_ref, spread_ref, _, result_ref, h_ref, factor_ref = refs[n_terms:]
    h_next = high_dot(total(refs[:n_terms]), inverse_ref[...])
    result_ref[...] = h_next
    h_ref[...] = h_next
    rank = h_next.shape[0]
    h_rows = h_next.T
    h_rows = jnp.concatenate([h_rows] * (spread_ref.shape[2] // rank), axis=1)
    for slot in range(spread_ref.shape[0]):
        factor_ref[slot] = jnp.concatenate(three_parts(h_rows * spread_ref[slot]), axis=0)


def next_h(terms, inverse, spread, after):
    n_slots, rank, columns = spread.shape
    return pl.pallas_call(
        functools.partial(next_h_kernel, len(terms)),
        in_specs=[VMEM_SPEC] * (len(terms) + 2) + [ANY_SPEC],
        out_specs=[VMEM_SPEC] * 3,
        out_shape=[
            jax.ShapeDtypeStruct(inverse.shape, F32),
            jax.ShapeDtypeStruct(inverse.shape, F32),
            jax.ShapeDtypeStruct((n_slots, 3 * rank, columns), BF16),
        ],
        compiler_params=parameters(LIMIT),
        cost_estimate=SHORT,
        name="next_h",
    )(*terms, inverse, spread, after)


def second_inverse_kernel(h_ref, w_gram_ref, gram_ref, inverse_ref):
    gram = high_dot(h_ref[...], h_ref[...], COLS_BY_COLS)
    gram_ref[...] = gram
    inverse_ref[...] = inverse_of(gram * w_gram_ref[...])


def second_inverse(h_next, w_gram):
    out = jax.ShapeDtypeStruct(w_gram.shape, F32)
    return pl.pallas_call(
        second_inverse_kernel,
        out_shape=[out, out],
        compiler_params=parameters(LIMIT),
        cost_estimate=SHORT,
        name="second_inverse",
    )(h_next, w_gram)


def v_terms_kernel(items, sent, place, factor_ref, *refs):
    parts, terms_ref = refs[: 2 * len(items)], refs[-1]
    rank, half = terms_ref.shape
    upper = core_of(place) ^ 1 if sent else core_of(place)
    features = pl.ds(pl.multiple_of(upper * half, half), half)
    total = None
    for i, (slots, first) in enumerate(items):
        count = parts[2 * i].shape[0] // len(slots)
        columns = pl.ds(first * rank, count)
        for k, slot in enumerate(slots):
            rows = pl.ds(k * count, count)
            large = low_dot(factor_ref[slot, :, columns], parts[2 * i][rows, features])
            small = low_dot(factor_ref[slot, : 2 * rank, columns], parts[2 * i + 1][rows, features])
            terms = large[:rank] + (large[rank : 2 * rank] + small[:rank]) + (large[2 * rank :] + small[rank:])
            total = terms if total is None else total + terms
    terms_ref[...] = total


def half_v_terms(items, sent, place, factor, projected, after):
    width = projected[0].shape[1]
    rank = factor.shape[1] // 3
    return pl.pallas_call(
        functools.partial(v_terms_kernel, items, sent),
        in_specs=[SMEM_SPEC] + [VMEM_SPEC] * (1 + len(projected)) + [ANY_SPEC] * len(after),
        out_specs=VMEM_SPEC,
        out_shape=jax.ShapeDtypeStruct((rank, width // 2), F32),
        compiler_params=parameters(LIMIT),
        cost_estimate=SHORT,
        name="v_terms",
    )(place, factor, *projected, *after)


def next_v_kernel(items, share, later, place, terms_ref, inverse_ref, h_ref, *refs):
    parts, refs = refs[: 2 * len(items)], refs[2 * len(items) :]
    rank, half = terms_ref.shape
    here = pl.multiple_of((core_of(place) ^ 1 if later else core_of(place)) * half, half)
    features = pl.ds(here, half)
    v_rows = high_dot(inverse_ref[...], terms_ref[...])
    if later:
        v_before_ref, before_ref, v_ref, sums_ref, v_parts = refs
        v_ref[:, features] = v_rows
        v_ref[:, pl.ds(pl.multiple_of(half - here, half), half)] = v_before_ref[...]
        sums = before_ref[...]
    else:
        v_ref, sums_ref, v_parts = refs
        v_ref[...] = v_rows
        sums = jnp.zeros((rank, 2 * rank), F32)
    v_parts[...] = jnp.concatenate(two_parts(v_rows), axis=0)
    weights = jnp.concatenate([h_ref[...]] * 2, axis=1)
    gram = low_dot(v_parts[...], v_parts[...], ROWS_BY_ROWS)
    gram = gram[:rank, :rank] + (gram[:rank, rank:] + gram[rank:, :rank])
    sums_ref[...] = sums + jnp.concatenate([jnp.zeros((rank, rank), F32), gram], axis=1)
    for i, (slots, done) in enumerate(items):
        seen = low_dot(parts[2 * i][:, features], v_parts[...], ROWS_BY_ROWS)
        seen = seen + low_dot(parts[2 * i + 1][:, features], v_parts[...], ROWS_BY_ROWS)
        count = seen.shape[0] // rank // len(slots)
        for p in range(seen.shape[0] // rank):
            patient = (feature_of(place) ^ slots[p // count]) * share + done + p % count
            row = jnp.sum(seen[p * rank : (p + 1) * rank] * weights, axis=0, keepdims=True)
            sums_ref[pl.ds(patient, 1), :rank] += row[:, :rank] + row[:, rank:]


def half_v(items, share, place, terms, inverse, h_next, projected, before):
    rank, half = terms.shape
    return pl.pallas_call(
        functools.partial(next_v_kernel, items, share, bool(before)),
        in_specs=[SMEM_SPEC] + [VMEM_SPEC] * (3 + len(projected) + len(before)),
        out_specs=[VMEM_SPEC] * 2,
        out_shape=[
            jax.ShapeDtypeStruct((rank, 2 * half if before else half), F32),
            jax.ShapeDtypeStruct((rank, 2 * rank), F32),
        ],
        scratch_shapes=[pltpu.VMEM((2 * rank, half), BF16)],
        compiler_params=parameters(LIMIT),
        cost_estimate=SHORT,
        name="next_v",
    )(place, terms, inverse, h_next, *projected, *before)


def next_w_kernel(n_sums, *refs):
    gram_ref, w_ref = refs[n_sums:]
    patients, rank = w_ref.shape
    sums = total(refs[:n_sums])
    table = jnp.concatenate([sums[:, rank:] * gram_ref[...], sums.T[:rank]], axis=1)
    w_ref[...] = eliminate(table, rank).T[rank : rank + patients]


def next_w(sums, h_gram, patients):
    rank = h_gram.shape[0]
    return pl.pallas_call(
        functools.partial(next_w_kernel, len(sums)),
        out_shape=jax.ShapeDtypeStruct((patients, rank), F32),
        compiler_params=parameters(LIMIT),
        cost_estimate=SHORT,
        name="next_w",
    )(*sums, h_gram)


def swap(x, axis, slot):
    pairs = [(i, i ^ slot) for i in range(lax.axis_size(axis))]
    return lax.ppermute(x, axis, pairs)


def all_terms(x, axis):
    n = lax.axis_size(axis)
    if n > 4:
        return [lax.psum(x, axis)]
    return [x] + [swap(x, axis, s) for s in range(1, n)]


def staged_terms(x, axis, after):
    n = lax.axis_size(axis)
    steps = [1 << i for i in range(n.bit_length() - 1)]
    for step in steps[:-1]:
        x = add(x, swap(x, axis, step), after)
    return [x, swap(x, axis, steps[-1])]


def add_kernel(a_ref, b_ref, *refs):
    refs[-1][...] = a_ref[...] + b_ref[...]


def add(a, b, after):
    return pl.pallas_call(
        add_kernel,
        in_specs=[VMEM_SPEC] * 2 + [ANY_SPEC] * len(after),
        out_specs=VMEM_SPEC,
        out_shape=jax.ShapeDtypeStruct(a.shape, a.dtype),
        compiler_params=parameters(LIMIT),
        cost_estimate=SHORT,
        name="add_terms",
    )(a, b, *after)


def patient_halves(keep, send, after):
    own = add(keep, swap(send, "patient", 1), [])
    step = 2
    while step < lax.axis_size("patient"):
        own = add(own, swap(own, "patient", step), [after])
        step *= 2
    return own, swap(own, "patient", 1)


def on_device(visits, visit_counts, h_start, v_start, w_start):
    n = lax.axis_size("feature")
    patients, slots, width = visits.shape
    share = patients // n
    place = (2 * lax.axis_index("feature") + (lax.axis_index("patient") & 1)).astype(jnp.int32).reshape(1)
    by_owner = visits.reshape(n, share, slots, width)
    in_hbm = pltpu.with_memory_space_constraint(by_owner, pltpu.HBM)
    v_rows = pltpu.with_memory_space_constraint(v_start.T, pltpu.HBM)

    n_parts = 2 if share % 2 == 0 else 1
    count = share // n_parts
    firsts = [part * count for part in range(n_parts)]
    bits = [1 << i for i in range(n.bit_length() - 1)]
    v_near = v_start.T

    def send(bit):
        return [slot for slot in range(n) if slot & bit and not slot & (bit - 1)]

    def receive(bit):
        return [slot ^ bit for slot in send(bit)]

    w_gram, spread = spread_w(place, w_start, n)
    w_grams = staged_terms(w_gram, "patient", [])
    own, v_gram = project_own(n_parts, place, by_owner, v_near)
    h_local = v_gram
    arrived = [[] for _ in firsts]
    for i, bit in enumerate(bits):
        layouts = [receive(before) for before in bits[:i]]
        for part, first in enumerate(firsts):
            if i == 0 and part == 0:
                code = first_projection(send(bit), count, n_parts == 1, place, in_hbm, v_rows)
            else:
                after = [w_grams[part]] + [v_gram] * part if i else []
                code = next_projection(
                    send(bit), first, count, part == n_parts - 1, layouts, place, by_owner, v_near, arrived[part], after
                )
            arrived[part] = arrived[part] + [swap(code, "feature", bit)]

    layouts = [receive(bit) for bit in bits]
    frames = [[] for _ in firsts]
    joined = []

    def double(part, after):
        for bit in bits[::-1]:
            slots = tuple(slot ^ bit for group, _ in frames[part] for slot in group)
            joined = join([x for _, x in frames[part]], after)
            frames[part].append((slots, swap(joined, "feature", bit)))
        return [joined]

    def project_groups(groups, after):
        arrays = {(frames[part][k][0], firsts[part]): frames[part][k][1] for part, k in groups}
        return project_frames(list(arrays), place, arrays, by_owner, after)

    for part, first in enumerate(firsts):
        low, h_local, v_total = own_frames(
            layouts, part, n_parts, place, visit_counts, h_start, w_start, v_gram, h_local, own[part], arrived[part]
        )
        v_gram = v_total
        frames[part].append(((0,), low))

    last = len(bits)
    for part in range(n_parts - 1):
        joined = double(part, [frames[-1][0][1]])
    first_groups = [(part, 0) for part in range(n_parts)] + [(part, 1) for part in range(n_parts - 1)]
    early = [(part, k) for part in range(n_parts - 1) for k in range(2, last + 1)]
    projected, token = project_groups(first_groups, joined)
    h_sums = staged_terms(h_local, "patient", [token])
    w_gram, inverse = first_inverse(v_gram, w_grams, h_sums[0])
    h_sum = add(*h_sums, [inverse])
    joined = double(n_parts - 1, [h_sum] + [frames[part][k][1] for part, k in early])
    h_terms = all_terms(h_sum, "feature")
    after = joined
    for groups in [early] + [[(n_parts - 1, k)] for k in range(1, last + 1)]:
        if groups:
            more, token = project_groups(groups, after)
            projected |= more
            after = [token]
    h_result, h_next, factor = next_h(h_terms, inverse, spread, token)

    items = list(projected)
    flat = [x for item in items for x in projected[item]]
    send = half_v_terms(items, True, place, factor, flat, [])
    keep = half_v_terms(items, False, place, factor, flat, [send])
    h_gram, second = second_inverse(h_next, w_gram)
    own_terms, other_terms = patient_halves(keep, send, second)
    before = half_v(items, share, place, own_terms, second, h_next, flat, [])
    v_next, sums = half_v(items, share, place, other_terms, second, h_next, flat, before)
    w_next = next_w(all_terms(sums, "feature"), h_gram, patients)
    return (h_result, v_next.T, w_next)


def solution(mesh):
    return jax.shard_map(
        on_device,
        mesh=mesh,
        in_specs=(
            P(("groups", "patient"), None, "feature"),
            P(("groups", "patient")),
            P(),
            P("feature", None),
            P(("groups", "patient"), None),
        ),
        out_specs=(P(None, "groups"), P("feature", "groups"), P("patient", "groups")),
        check_vma=False,
    )
```

```python
import functools

import jax
import jax.numpy as jnp
from jax import lax
from jax.experimental import pallas as pl
from jax.experimental.pallas import tpu as pltpu
from jax.sharding import PartitionSpec as P

NS_STEPS = 12
LANES = 128
LEVELS = 32000.0
COARSE_STEPS = 3
SHORT = pl.CostEstimate(flops=1000, bytes_accessed=1000, transcendentals=0)

epsilon = 1e-06
HIGH = lax.Precision.HIGHEST
F32 = jnp.float32
BF16 = jnp.bfloat16
MIB = 1024 * 1024

ROWS_BY_COLS = (((1,), (0,)), ((), ()))
ROWS_BY_ROWS = (((1,), (1,)), ((), ()))
COLS_BY_COLS = (((0,), (0,)), ((), ()))


def low_dot(a, b, dims=ROWS_BY_COLS):
    return lax.dot_general(a, b, dims, preferred_element_type=F32)


def high_dot(a, b, dims=ROWS_BY_COLS):
    return lax.dot_general(a, b, dims, precision=HIGH, preferred_element_type=F32)


def two_parts(x):
    first = x.astype(BF16)
    return first, (x - first.astype(F32)).astype(BF16)


def three_parts(x):
    first = x.astype(BF16)
    rest = x - first.astype(F32)
    second = rest.astype(BF16)
    return first, second, (rest - second.astype(F32)).astype(BF16)


def feature_of(place):
    return place[0] >> 1


def core_of(place):
    return place[0] & 1


def lane_numbers(shape):
    return lax.broadcasted_iota(jnp.int32, shape, len(shape) - 1)


ANY_SPEC = pl.BlockSpec(memory_space=pl.ANY)
HBM_SPEC = pl.BlockSpec(memory_space=pltpu.HBM)


def parameters(mib):
    return pltpu.CompilerParams(vmem_limit_bytes=mib * MIB)


LIMIT = 8
VMEM_SPEC = pl.BlockSpec(memory_space=pltpu.VMEM)
SMEM_SPEC = pl.BlockSpec(memory_space=pltpu.SMEM)


def exponent_rows(total_count):
    return -(-(total_count + 1) // 16) * 16


def payload_shape(total_count, rank, slots, with_gram):
    return (total_count * rank + (rank // 2 if with_gram else 0) + exponent_rows(total_count), slots)


def row_exponent(x):
    top = jnp.max(jnp.abs(x), axis=1, keepdims=True)
    return jnp.ceil(jnp.log2(jnp.maximum(top, 1e-30)))


class Payload:
    def __init__(self, ref, slots, count, rank, with_gram):
        self.ref, self.slots, self.count, self.rank, self.with_gram = ref, slots, count, rank, with_gram
        self.entries = len(slots) * count
        gram_rows = rank // 2 if with_gram else 0
        exponents = self.rows(self.entries * rank + gram_rows, exponent_rows(self.entries))
        self.steps = jnp.exp2(exponents[:, :LANES].T[:rank]) * (1.0 / LEVELS)

    def rows(self, first, number):
        return self.ref[pl.ds(first, number), :].astype(jnp.int32).astype(F32)

    def proj(self, slot, p):
        entry = self.slots.index(slot) * self.count + p
        return self.rows(entry * self.rank, self.rank) * self.steps[:, entry : entry + 1]

    def gram(self):
        rank = self.rank
        digits = self.rows(self.entries * rank, rank // 2)
        digits = jnp.concatenate([digits[:, : 2 * rank], digits[:, 2 * rank :]], axis=0)
        return (digits[:, :rank] + digits[:, rank:] * (0.5 / LEVELS)) * self.steps[:, self.entries : self.entries + 1]


def encode(values, gram, coded_ref, rank):
    count = len(values)
    lanes = lane_numbers((rank, LANES))
    exponents = jnp.zeros((rank, LANES), F32)
    for p, value in enumerate(values):
        proj = value()
        exponent = row_exponent(proj)
        coded = jnp.floor(proj * (LEVELS / jnp.exp2(exponent)) + 0.5)
        coded_ref[pl.ds(p * rank, rank), :] = coded.astype(jnp.int32).astype(jnp.int16)
        exponents = jnp.where(lanes == p, exponent, exponents)
    end = count * rank
    if gram is not None:
        exponent = row_exponent(gram)
        scaled = gram * (LEVELS / jnp.exp2(exponent))
        whole = jnp.floor(scaled + 0.5)
        rest = jnp.floor((scaled - whole) * (2 * LEVELS) + 0.5)
        digits = jnp.concatenate([whole, rest], axis=1)
        digits = jnp.concatenate([digits[: rank // 2], digits[rank // 2 :]], axis=1)
        coded_ref[pl.ds(end, rank // 2), :] = digits.astype(jnp.int32).astype(jnp.int16)
        exponents = jnp.where(lanes == count, exponent, exponents)
        end += rank // 2
    rows = exponent_rows(count)
    last = jnp.concatenate([exponents.T[:rows], jnp.zeros((rows, coded_ref.shape[1] - rank), F32)], axis=1)
    coded_ref[pl.ds(end, rows), :] = last.astype(jnp.int32).astype(jnp.int16)


def first_projection_kernel(slots, with_gram, place, v_hbm, visits_ref, coded_ref, v_ref, buffers, sems, v_sem):
    count = buffers.shape[1]
    v_copy = pltpu.make_async_copy(v_hbm, v_ref, v_sem)
    v_copy.start()
    copies = [
        pltpu.make_async_copy(visits_ref.at[feature_of(place) ^ slot, pl.ds(0, count)], buffers.at[i], sems.at[i])
        for i, slot in enumerate(slots)
    ]
    for copy in copies:
        copy.start()
    v_copy.wait()

    def value(i, p):
        if p == 0:
            copies[i].wait()
        return low_dot(v_ref[...], buffers[i, p], ROWS_BY_ROWS)

    values = [functools.partial(value, i, p) for i in range(len(slots)) for p in range(count)]
    gram = low_dot(v_ref[...], v_ref[...], ROWS_BY_ROWS) if with_gram else None
    encode(values, gram, coded_ref, v_ref.shape[0])


def first_projection(slots, count, with_gram, place, visits, v_rows):
    width = visits.shape[3]
    rank = v_rows.shape[0]
    return pl.pallas_call(
        functools.partial(first_projection_kernel, slots, with_gram),
        in_specs=[SMEM_SPEC, HBM_SPEC, HBM_SPEC],
        out_specs=VMEM_SPEC,
        out_shape=jax.ShapeDtypeStruct(payload_shape(len(slots) * count, rank, visits.shape[2], with_gram), jnp.int16),
        scratch_shapes=[
            pltpu.VMEM(v_rows.shape, BF16),
            pltpu.VMEM((len(slots), count) + visits.shape[2:], BF16),
            pltpu.SemaphoreType.DMA((len(slots),)),
            pltpu.SemaphoreType.DMA,
        ],
        compiler_params=parameters(LIMIT),
        cost_estimate=SHORT,
        name="project_first",
    )(place, v_rows, visits)


def next_projection_kernel(slots, first, count, with_gram, layouts, place, v_ref, visits_ref, *refs):
    coded_ref = refs[-1]
    rank = v_ref.shape[0]
    arrived = [Payload(ref, layout, count, rank, with_gram) for ref, layout in zip(refs, layouts)]

    def value(slot, p):
        proj = low_dot(v_ref[...], visits_ref[feature_of(place) ^ slot, first + p], ROWS_BY_ROWS)
        for payload in arrived:
            proj = proj + payload.proj(slot, p)
        return proj

    gram = None
    if with_gram:
        gram = low_dot(v_ref[...], v_ref[...], ROWS_BY_ROWS)
        for payload in arrived:
            gram = gram + payload.gram()
    encode([functools.partial(value, slot, p) for slot in slots for p in range(count)], gram, coded_ref, rank)


def next_projection(slots, first, count, with_gram, layouts, place, visits, v_rows, arrived, after):
    rank = v_rows.shape[0]
    return pl.pallas_call(
        functools.partial(next_projection_kernel, slots, first, count, with_gram, layouts),
        in_specs=[SMEM_SPEC] + [VMEM_SPEC] * (2 + len(arrived)) + [ANY_SPEC] * len(after),
        out_specs=VMEM_SPEC,
        out_shape=jax.ShapeDtypeStruct(payload_shape(len(slots) * count, rank, visits.shape[2], with_gram), jnp.int16),
        compiler_params=parameters(LIMIT),
        cost_estimate=SHORT,
        name="project_next",
    )(place, v_rows, visits, *arrived, *after)


def spread_w_kernel(n_slots, place, w_ref, gram_ref, spread_ref):
    gram_ref[...] = high_dot(w_ref[...], w_ref[...], COLS_BY_COLS)
    patients, rank = w_ref.shape
    share = patients // n_slots
    w_rows = jnp.concatenate([w_ref[...], jnp.zeros((LANES - patients, rank), F32)], axis=0)
    w_columns = w_rows.T
    for slot in range(n_slots):
        first = (feature_of(place) ^ slot) * share
        columns = pltpu.roll(w_columns, jnp.where(first == 0, 0, LANES - first), 1)
        spread = [jnp.broadcast_to(columns[:, p : p + 1], (rank, rank)) for p in range(share)]
        spread_ref[slot] = jnp.concatenate(spread, axis=1)


def spread_w(place, w_start, n_slots):
    patients, rank = w_start.shape
    return pl.pallas_call(
        functools.partial(spread_w_kernel, n_slots),
        in_specs=[SMEM_SPEC, VMEM_SPEC],
        out_specs=[VMEM_SPEC] * 2,
        out_shape=[
            jax.ShapeDtypeStruct((rank, rank), F32),
            jax.ShapeDtypeStruct((n_slots, rank, patients // n_slots * rank), F32),
        ],
        compiler_params=parameters(LIMIT),
        cost_estimate=SHORT,
        name="spread_w",
    )(place, w_start)


def own_projection_kernel(place, v_ref, visits_ref, *refs):
    *proj_refs, v_gram_ref = refs
    count = visits_ref.shape[1] // len(proj_refs)
    for p in range(visits_ref.shape[1]):
        proj_refs[p // count][p % count] = low_dot(v_ref[...], visits_ref[feature_of(place), p], ROWS_BY_ROWS)
    v_gram_ref[...] = low_dot(v_ref[...], v_ref[...], ROWS_BY_ROWS)


def project_own(n_parts, place, visits, v_rows):
    _, share, slots, width = visits.shape
    rank = v_rows.shape[0]
    proj = jax.ShapeDtypeStruct((share // n_parts, rank, slots), F32)
    *own, v_gram = pl.pallas_call(
        own_projection_kernel,
        in_specs=[SMEM_SPEC] + [VMEM_SPEC] * 2,
        out_specs=[VMEM_SPEC] * (n_parts + 1),
        out_shape=[proj] * n_parts + [jax.ShapeDtypeStruct((rank, rank), F32)],
        compiler_params=parameters(LIMIT),
        cost_estimate=SHORT,
        name="project_own",
    )(place, v_rows, visits)
    return own, v_gram


def solve_tile(columns, tile):
    rows = lax.broadcasted_iota(jnp.int32, tile.shape, 0)
    for a in range(0, 8, 2):
        b = a + 1
        first, second = columns[a], columns[b]
        m_aa, m_ab, m_ba, m_bb = first[a:b], second[a:b], first[b : b + 1], second[b : b + 1]
        scale = 1.0 / (m_aa * m_bb - m_ab * m_ba)
        m_aa, m_ab, m_ba, m_bb = m_aa * scale, m_ab * scale, m_ba * scale, m_bb * scale

        def step(x):
            x_a, x_b = x[a:b], x[b : b + 1]
            new_a, new_b = m_bb * x_a - m_ab * x_b, m_aa * x_b - m_ba * x_a
            x = x - (first * new_a + second * new_b)
            return jnp.where(rows == a, new_a, jnp.where(rows == b, new_b, x))

        tile = step(tile)
        columns = [step(x) if q > b else x for q, x in enumerate(columns)]
    return tile


def eliminate(table, rank):
    tiles = [table[8 * t : 8 * t + 8] for t in range(rank // 8)]
    for home in range(rank // 8):
        first = 8 * home
        columns = [[jnp.broadcast_to(t[:, q : q + 1], t.shape) for q in range(first, first + 8)] for t in tiles]
        solved = solve_tile(columns[home], tiles[home])
        for t, tile in enumerate(tiles):
            terms = [column * solved[q : q + 1] for q, column in enumerate(columns[t])]
            while len(terms) > 1:
                terms = [x + y for x, y in zip(terms[::2], terms[1::2])]
            tiles[t] = solved if t == home else tile - terms[0]
    return jnp.concatenate(tiles, axis=0)


def inverse_of(gram):
    rank = gram.shape[0]
    eye = (lax.broadcasted_iota(jnp.int32, gram.shape, 0) == lane_numbers(gram.shape)).astype(F32)
    return eliminate(jnp.concatenate([gram, eye], axis=1), rank)[:, rank:]


def total(refs):
    out = refs[0][...]
    for ref in refs[1:]:
        out = out + ref[...]
    return out


def first_inverse_kernel(v_gram_ref, *refs):
    *terms, _, w_gram_ref, inverse_ref = refs
    w_gram = total(terms)
    w_gram_ref[...] = w_gram
    inverse_ref[...] = inverse_of(w_gram * v_gram_ref[...])


def first_inverse(v_gram, w_grams, after):
    out = jax.ShapeDtypeStruct(v_gram.shape, F32)
    return pl.pallas_call(
        first_inverse_kernel,
        in_specs=[VMEM_SPEC] * (1 + len(w_grams)) + [ANY_SPEC],
        out_specs=[VMEM_SPEC] * 2,
        out_shape=[out, out],
        compiler_params=parameters(LIMIT),
        cost_estimate=SHORT,
        name="first_inverse",
    )(v_gram, *w_grams, after)


def sweep_all(frames, rank, fine):
    patients = range(frames.shape[0])
    if fine:
        both = [jnp.concatenate(two_parts(frames[p]), axis=0) for p in patients]
        blocks = [low_dot(x, x, ROWS_BY_ROWS) for x in both]
        blocks = [x[:rank] + x[rank:] for x in blocks]
        grams = [x + pltpu.roll(x, rank, 1) for x in blocks]
        moved = [low_dot(jnp.concatenate(two_parts(g), axis=0), x) for g, x in zip(grams, both)]
        moved = [x[:rank] + x[rank:] for x in moved]
    else:
        first = [frames[p].astype(BF16) for p in patients]
        grams = [low_dot(x, x, ROWS_BY_ROWS).astype(BF16) for x in first]
        moved = [low_dot(g, x) for g, x in zip(grams, first)]
    for p in patients:
        frames[p] = 1.5 * frames[p] - 0.5 * moved[p]


def frames_kernel(layouts, part, share, place, counts_ref, h_ref, w_ref, v_gram_ref, before_ref, own_ref, *refs):
    coded, refs = refs[: len(layouts)], refs[len(layouts) :]
    frames_ref, terms_ref, v_total_ref, proj, frames = refs
    count, rank, slots = frames.shape
    patients = range(count)
    first = feature_of(place) * share + part * count
    pieces = [own_ref[p] for p in patients]
    v_gram = v_gram_ref[...]
    for code, layout in zip(coded, layouts):
        payload = Payload(code, layout, count, rank, (part + 1) * count == share)
        pieces = [pieces[p] + payload.proj(0, p) for p in patients]
        if payload.with_gram:
            v_gram = v_gram + payload.gram()
    v_total_ref[...] = v_gram
    for p in patients:
        proj[p] = pieces[p]
    weights = [w_ref[pl.ds(first + p, 1), :] for p in patients]
    mixed = [high_dot(h_ref[...] * weights[p], pieces[p]) for p in patients]
    lanes = lane_numbers((rank, slots))
    mixed = [jnp.where(lanes < counts_ref[first + p], mixed[p], 0.0) for p in patients]
    energy = [jnp.sum(jnp.sum(x * x, axis=1, keepdims=True), axis=0, keepdims=True) for x in mixed]
    for p in patients:
        frames[p] = mixed[p] * lax.rsqrt(energy[p] + epsilon)

    def sweep(fine, step, carry):
        sweep_all(frames, rank, fine)
        return carry

    lax.fori_loop(0, COARSE_STEPS, functools.partial(sweep, False), 0, unroll=True)
    lax.fori_loop(COARSE_STEPS, NS_STEPS, functools.partial(sweep, True), 0, unroll=True)
    low = [frames[p].astype(BF16) for p in patients]
    for p in patients:
        frames_ref[p] = low[p]
    products = [jnp.concatenate(three_parts(proj[p]), axis=0) for p in patients]
    products = [low_dot(low[p], products[p], ROWS_BY_ROWS) for p in patients]
    terms = before_ref[...] if part else jnp.zeros((rank, rank), F32)
    for p in patients:
        product = products[p][:, :rank] + (products[p][:, rank : 2 * rank] + products[p][:, 2 * rank :])
        terms = terms + product * weights[p]
    terms_ref[...] = terms


def own_frames(layouts, part, n_parts, place, counts, h_start, w_start, v_gram, before, own, coded):
    count, rank, slots = own.shape
    share = count * n_parts
    return pl.pallas_call(
        functools.partial(frames_kernel, layouts, part, share),
        in_specs=[SMEM_SPEC] * 2 + [VMEM_SPEC] * (5 + len(coded)),
        out_specs=[VMEM_SPEC] * 3,
        out_shape=[
            jax.ShapeDtypeStruct(own.shape, BF16),
            jax.ShapeDtypeStruct((rank, rank), F32),
            jax.ShapeDtypeStruct((rank, rank), F32),
        ],
        scratch_shapes=[pltpu.VMEM(own.shape, F32)] * 2,
        compiler_params=parameters(LIMIT),
        cost_estimate=SHORT,
        name="own_frames",
    )(place, counts, h_start, w_start, v_gram, before, own, *coded)


def projected_kernel(items, place, visits_ref, *refs):
    frames_refs, outs, token_ref = refs[: len(items)], refs[-2 * len(items) - 1 : -1], refs[-1]
    token_ref[...] = jnp.zeros_like(token_ref)
    for i, (slots, first) in enumerate(items):
        total_count, rank, _ = frames_refs[i].shape
        count = total_count // len(slots)
        for p in range(total_count):
            rows = pl.ds(p * rank, rank)
            owner = feature_of(place) ^ slots[p // count]
            product = low_dot(frames_refs[i][p], visits_ref[owner, first + p % count])
            outs[2 * i][rows, :], outs[2 * i + 1][rows, :] = two_parts(product)


def join_kernel(count, *refs):
    out_ref = refs[-1]
    first = 0
    for part in refs[:count]:
        out_ref[first : first + part.shape[0]] = part[...]
        first += part.shape[0]


def join(parts, after):
    if len(parts) == 1:
        return parts[0]
    return pl.pallas_call(
        functools.partial(join_kernel, len(parts)),
        in_specs=[VMEM_SPEC] * len(parts) + [ANY_SPEC] * len(after),
        out_specs=VMEM_SPEC,
        out_shape=jax.ShapeDtypeStruct((sum(x.shape[0] for x in parts),) + parts[0].shape[1:], parts[0].dtype),
        compiler_params=parameters(LIMIT),
        cost_estimate=SHORT,
        name="join_frames",
    )(*parts, *after)


def project_frames(items, place, frames, visits, after):
    width = visits.shape[-1]
    outs = []
    for item in items:
        count, rank, _ = frames[item].shape
        outs += [jax.ShapeDtypeStruct((count * rank, width), BF16)] * 2
    *parts, token = pl.pallas_call(
        functools.partial(projected_kernel, items),
        in_specs=[SMEM_SPEC] + [VMEM_SPEC] * (1 + len(items)) + [ANY_SPEC] * len(after),
        out_specs=[VMEM_SPEC] * (len(outs) + 1),
        out_shape=outs + [jax.ShapeDtypeStruct((8, LANES), F32)],
        compiler_params=parameters(LIMIT),
        cost_estimate=SHORT,
        name="project_frames",
    )(place, visits, *[frames[item] for item in items], *after)
    return {item: parts[2 * i : 2 * i + 2] for i, item in enumerate(items)}, token


def next_h_kernel(n_terms, *refs):
    inverse_ref, spread_ref, _, result_ref, h_ref, factor_ref = refs[n_terms:]
    h_next = high_dot(total(refs[:n_terms]), inverse_ref[...])
    result_ref[...] = h_next
    h_ref[...] = h_next
    rank = h_next.shape[0]
    h_rows = h_next.T
    h_rows = jnp.concatenate([h_rows] * (spread_ref.shape[2] // rank), axis=1)
    for slot in range(spread_ref.shape[0]):
        factor_ref[slot] = jnp.concatenate(three_parts(h_rows * spread_ref[slot]), axis=0)


def next_h(terms, inverse, spread, after):
    n_slots, rank, columns = spread.shape
    return pl.pallas_call(
        functools.partial(next_h_kernel, len(terms)),
        in_specs=[VMEM_SPEC] * (len(terms) + 2) + [ANY_SPEC],
        out_specs=[VMEM_SPEC] * 3,
        out_shape=[
            jax.ShapeDtypeStruct(inverse.shape, F32),
            jax.ShapeDtypeStruct(inverse.shape, F32),
            jax.ShapeDtypeStruct((n_slots, 3 * rank, columns), BF16),
        ],
        compiler_params=parameters(LIMIT),
        cost_estimate=SHORT,
        name="next_h",
    )(*terms, inverse, spread, after)


def second_inverse_kernel(h_ref, w_gram_ref, gram_ref, inverse_ref):
    gram = high_dot(h_ref[...], h_ref[...], COLS_BY_COLS)
    gram_ref[...] = gram
    inverse_ref[...] = inverse_of(gram * w_gram_ref[...])


def second_inverse(h_next, w_gram):
    out = jax.ShapeDtypeStruct(w_gram.shape, F32)
    return pl.pallas_call(
        second_inverse_kernel,
        out_shape=[out, out],
        compiler_params=parameters(LIMIT),
        cost_estimate=SHORT,
        name="second_inverse",
    )(h_next, w_gram)


def v_terms_kernel(items, sent, place, factor_ref, *refs):
    parts, terms_ref = refs[: 2 * len(items)], refs[-1]
    rank, half = terms_ref.shape
    upper = core_of(place) ^ 1 if sent else core_of(place)
    features = pl.ds(pl.multiple_of(upper * half, half), half)
    total = None
    for i, (slots, first) in enumerate(items):
        count = parts[2 * i].shape[0] // len(slots)
        columns = pl.ds(first * rank, count)
        for k, slot in enumerate(slots):
            rows = pl.ds(k * count, count)
            large = low_dot(factor_ref[slot, :, columns], parts[2 * i][rows, features])
            small = low_dot(factor_ref[slot, : 2 * rank, columns], parts[2 * i + 1][rows, features])
            terms = large[:rank] + (large[rank : 2 * rank] + small[:rank]) + (large[2 * rank :] + small[rank:])
            total = terms if total is None else total + terms
    terms_ref[...] = total


def half_v_terms(items, sent, place, factor, projected, after):
    width = projected[0].shape[1]
    rank = factor.shape[1] // 3
    return pl.pallas_call(
        functools.partial(v_terms_kernel, items, sent),
        in_specs=[SMEM_SPEC] + [VMEM_SPEC] * (1 + len(projected)) + [ANY_SPEC] * len(after),
        out_specs=VMEM_SPEC,
        out_shape=jax.ShapeDtypeStruct((rank, width // 2), F32),
        compiler_params=parameters(LIMIT),
        cost_estimate=SHORT,
        name="v_terms",
    )(place, factor, *projected, *after)


def next_v_kernel(items, share, later, place, terms_ref, inverse_ref, h_ref, *refs):
    parts, refs = refs[: 2 * len(items)], refs[2 * len(items) :]
    rank, half = terms_ref.shape
    here = pl.multiple_of((core_of(place) ^ 1 if later else core_of(place)) * half, half)
    features = pl.ds(here, half)
    v_rows = high_dot(inverse_ref[...], terms_ref[...])
    *before, v_ref, sums_ref, v_parts = refs
    v_ref[...] = v_rows
    sums = before[0][...] if later else jnp.zeros((rank, 2 * rank), F32)
    v_parts[...] = jnp.concatenate(two_parts(v_rows), axis=0)
    weights = jnp.concatenate([h_ref[...]] * 2, axis=1)
    gram = low_dot(v_parts[...], v_parts[...], ROWS_BY_ROWS)
    gram = gram[:rank, :rank] + (gram[:rank, rank:] + gram[rank:, :rank])
    sums_ref[...] = sums + jnp.concatenate([jnp.zeros((rank, rank), F32), gram], axis=1)
    for i, (slots, done) in enumerate(items):
        seen = low_dot(parts[2 * i][:, features], v_parts[...], ROWS_BY_ROWS)
        seen = seen + low_dot(parts[2 * i + 1][:, features], v_parts[...], ROWS_BY_ROWS)
        count = seen.shape[0] // rank // len(slots)
        for p in range(seen.shape[0] // rank):
            patient = (feature_of(place) ^ slots[p // count]) * share + done + p % count
            row = jnp.sum(seen[p * rank : (p + 1) * rank] * weights, axis=0, keepdims=True)
            sums_ref[pl.ds(patient, 1), :rank] += row[:, :rank] + row[:, rank:]


def half_v(items, share, place, terms, inverse, h_next, projected, before):
    rank, half = terms.shape
    return pl.pallas_call(
        functools.partial(next_v_kernel, items, share, bool(before)),
        in_specs=[SMEM_SPEC] + [VMEM_SPEC] * (3 + len(projected) + len(before)),
        out_specs=[VMEM_SPEC] * 2,
        out_shape=[
            jax.ShapeDtypeStruct((rank, half), F32),
            jax.ShapeDtypeStruct((rank, 2 * rank), F32),
        ],
        scratch_shapes=[pltpu.VMEM((2 * rank, half), BF16)],
        compiler_params=parameters(LIMIT),
        cost_estimate=SHORT,
        name="next_v",
    )(place, terms, inverse, h_next, *projected, *before)


def whole_v_kernel(place, own_ref, other_ref, v_ref, token_ref):
    half = own_ref.shape[1]
    upper = core_of(place) == 1
    v_ref[:, :half] = jnp.where(upper, other_ref[...], own_ref[...])
    v_ref[:, half:] = jnp.where(upper, own_ref[...], other_ref[...])
    token_ref[...] = jnp.zeros_like(token_ref)


def whole_v(place, own, other):
    rank, half = own.shape
    return pl.pallas_call(
        whole_v_kernel,
        in_specs=[SMEM_SPEC] + [VMEM_SPEC] * 2,
        out_specs=[VMEM_SPEC] * 2,
        out_shape=[jax.ShapeDtypeStruct((rank, 2 * half), F32), jax.ShapeDtypeStruct((8, LANES), F32)],
        compiler_params=parameters(LIMIT),
        cost_estimate=SHORT,
        name="whole_v",
    )(place, own, other)


def next_w_kernel(n_sums, *refs):
    gram_ref, _, w_ref = refs[n_sums:]
    patients, rank = w_ref.shape
    sums = total(refs[:n_sums])
    table = jnp.concatenate([sums[:, rank:] * gram_ref[...], sums.T[:rank]], axis=1)
    w_ref[...] = eliminate(table, rank).T[rank : rank + patients]


def next_w(sums, h_gram, patients, after):
    rank = h_gram.shape[0]
    return pl.pallas_call(
        functools.partial(next_w_kernel, len(sums)),
        in_specs=[VMEM_SPEC] * (len(sums) + 1) + [ANY_SPEC],
        out_specs=VMEM_SPEC,
        out_shape=jax.ShapeDtypeStruct((patients, rank), F32),
        compiler_params=parameters(LIMIT),
        cost_estimate=SHORT,
        name="next_w",
    )(*sums, h_gram, after)


def swap(x, axis, slot):
    pairs = [(i, i ^ slot) for i in range(lax.axis_size(axis))]
    return lax.ppermute(x, axis, pairs)


def all_terms(x, axis):
    n = lax.axis_size(axis)
    if n > 4:
        return [lax.psum(x, axis)]
    return [x] + [swap(x, axis, s) for s in range(1, n)]


def staged_terms(x, axis, after):
    n = lax.axis_size(axis)
    steps = [1 << i for i in range(n.bit_length() - 1)]
    for step in steps[:-1]:
        x = add(x, swap(x, axis, step), after)
    return [x, swap(x, axis, steps[-1])]


def add_kernel(a_ref, b_ref, *refs):
    refs[-1][...] = a_ref[...] + b_ref[...]


def add(a, b, after):
    return pl.pallas_call(
        add_kernel,
        in_specs=[VMEM_SPEC] * 2 + [ANY_SPEC] * len(after),
        out_specs=VMEM_SPEC,
        out_shape=jax.ShapeDtypeStruct(a.shape, a.dtype),
        compiler_params=parameters(LIMIT),
        cost_estimate=SHORT,
        name="add_terms",
    )(a, b, *after)


def patient_halves(keep, send, after):
    own = add(keep, swap(send, "patient", 1), [])
    step = 2
    while step < lax.axis_size("patient"):
        own = add(own, swap(own, "patient", step), [after])
        step *= 2
    return own, swap(own, "patient", 1)


def on_device(visits, visit_counts, h_start, v_start, w_start):
    n = lax.axis_size("feature")
    patients, slots, width = visits.shape
    share = patients // n
    place = (2 * lax.axis_index("feature") + (lax.axis_index("patient") & 1)).astype(jnp.int32).reshape(1)
    by_owner = visits.reshape(n, share, slots, width)
    in_hbm = pltpu.with_memory_space_constraint(by_owner, pltpu.HBM)
    v_rows = pltpu.with_memory_space_constraint(v_start.T, pltpu.HBM)

    n_parts = 2 if share % 2 == 0 else 1
    count = share // n_parts
    firsts = [part * count for part in range(n_parts)]
    bits = [1 << i for i in range(n.bit_length() - 1)]
    v_near = v_start.T

    def send(bit):
        return [slot for slot in range(n) if slot & bit and not slot & (bit - 1)]

    def receive(bit):
        return [slot ^ bit for slot in send(bit)]

    w_gram, spread = spread_w(place, w_start, n)
    w_grams = staged_terms(w_gram, "patient", [])
    own, v_gram = project_own(n_parts, place, by_owner, v_near)
    h_local = v_gram
    arrived = [[] for _ in firsts]
    for i, bit in enumerate(bits):
        layouts = [receive(before) for before in bits[:i]]
        for part, first in enumerate(firsts):
            if i == 0 and part == 0:
                code = first_projection(send(bit), count, n_parts == 1, place, in_hbm, v_rows)
            else:
                after = [w_grams[part]] + [v_gram] * part if i else []
                code = next_projection(
                    send(bit), first, count, part == n_parts - 1, layouts, place, by_owner, v_near, arrived[part], after
                )
            arrived[part] = arrived[part] + [swap(code, "feature", bit)]

    layouts = [receive(bit) for bit in bits]
    frames = [[] for _ in firsts]
    joined = []

    def double(part, after):
        for bit in bits[::-1]:
            slots = tuple(slot ^ bit for group, _ in frames[part] for slot in group)
            joined = join([x for _, x in frames[part]], after)
            frames[part].append((slots, swap(joined, "feature", bit)))
        return [joined]

    def project_groups(groups, after):
        arrays = {(frames[part][k][0], firsts[part]): frames[part][k][1] for part, k in groups}
        return project_frames(list(arrays), place, arrays, by_owner, after)

    for part, first in enumerate(firsts):
        low, h_local, v_total = own_frames(
            layouts, part, n_parts, place, visit_counts, h_start, w_start, v_gram, h_local, own[part], arrived[part]
        )
        v_gram = v_total
        frames[part].append(((0,), low))

    last = len(bits)
    for part in range(n_parts - 1):
        joined = double(part, [frames[-1][0][1]])
    first_groups = [(part, 0) for part in range(n_parts)] + [(part, 1) for part in range(n_parts - 1)]
    early = [(part, k) for part in range(n_parts - 1) for k in range(2, last + 1)]
    projected, token = project_groups(first_groups, joined)
    h_sums = staged_terms(h_local, "patient", [token])
    w_gram, inverse = first_inverse(v_gram, w_grams, h_sums[0])
    after = double(n_parts - 1, [inverse])
    if early:
        more, token = project_groups(early, after)
        projected |= more
        after = [token]
    h_sum = add(*h_sums, after)
    h_terms = all_terms(h_sum, "feature")
    for k in range(1, last + 1):
        more, token = project_groups([(n_parts - 1, k)], [h_sum] if k == 1 else [token])
        projected |= more
    h_result, h_next, factor = next_h(h_terms, inverse, spread, token)

    items = list(projected)
    flat = [x for item in items for x in projected[item]]
    send = half_v_terms(items, True, place, factor, flat, [])
    keep = half_v_terms(items, False, place, factor, flat, [send])
    h_gram, second = second_inverse(h_next, w_gram)
    own_terms, other_terms = patient_halves(keep, send, second)
    v_own, before = half_v(items, share, place, own_terms, second, h_next, flat, [])
    v_other, sums = half_v(items, share, place, other_terms, second, h_next, flat, [before])
    v_next, token = whole_v(place, v_own, v_other)
    w_next = next_w(all_terms(sums, "feature"), h_gram, patients, token)
    return (h_result, v_next.T, w_next)


def solution(mesh):
    return jax.shard_map(
        on_device,
        mesh=mesh,
        in_specs=(
            P(("groups", "patient"), None, "feature"),
            P(("groups", "patient")),
            P(),
            P("feature", None),
            P(("groups", "patient"), None),
        ),
        out_specs=(P(None, "groups"), P("feature", "groups"), P("patient", "groups")),
        check_vma=False,
    )
```

```python
import functools

import jax
import jax.numpy as jnp
from jax import lax
from jax.experimental import pallas as pl
from jax.experimental.pallas import tpu as pltpu
from jax.sharding import PartitionSpec as P

NS_STEPS = 12
LANES = 128
LEVELS = 32000.0
COARSE_STEPS = 3
SHORT = pl.CostEstimate(flops=1000, bytes_accessed=1000, transcendentals=0)

epsilon = 1e-06
HIGH = lax.Precision.HIGHEST
F32 = jnp.float32
BF16 = jnp.bfloat16
MIB = 1024 * 1024

ROWS_BY_COLS = (((1,), (0,)), ((), ()))
ROWS_BY_ROWS = (((1,), (1,)), ((), ()))
COLS_BY_COLS = (((0,), (0,)), ((), ()))


def low_dot(a, b, dims=ROWS_BY_COLS):
    return lax.dot_general(a, b, dims, preferred_element_type=F32)


def high_dot(a, b, dims=ROWS_BY_COLS):
    return lax.dot_general(a, b, dims, precision=HIGH, preferred_element_type=F32)


def two_parts(x):
    first = x.astype(BF16)
    return first, (x - first.astype(F32)).astype(BF16)


def three_parts(x):
    first = x.astype(BF16)
    rest = x - first.astype(F32)
    second = rest.astype(BF16)
    return first, second, (rest - second.astype(F32)).astype(BF16)


def feature_of(place):
    return place[0] >> 1


def core_of(place):
    return place[0] & 1


def lane_numbers(shape):
    return lax.broadcasted_iota(jnp.int32, shape, len(shape) - 1)


ANY_SPEC = pl.BlockSpec(memory_space=pl.ANY)
HBM_SPEC = pl.BlockSpec(memory_space=pltpu.HBM)


def parameters(mib):
    return pltpu.CompilerParams(vmem_limit_bytes=mib * MIB)


LIMIT = 8
VMEM_SPEC = pl.BlockSpec(memory_space=pltpu.VMEM)
SMEM_SPEC = pl.BlockSpec(memory_space=pltpu.SMEM)


def exponent_rows(total_count):
    return -(-(total_count + 1) // 16) * 16


def payload_shape(total_count, rank, slots, with_gram):
    return (total_count * rank + (rank // 2 if with_gram else 0) + exponent_rows(total_count), slots)


def row_exponent(x):
    top = jnp.max(jnp.abs(x), axis=1, keepdims=True)
    return jnp.ceil(jnp.log2(jnp.maximum(top, 1e-30)))


class Payload:
    def __init__(self, ref, slots, count, rank, with_gram):
        self.ref, self.slots, self.count, self.rank, self.with_gram = ref, slots, count, rank, with_gram
        self.entries = len(slots) * count
        gram_rows = rank // 2 if with_gram else 0
        exponents = self.rows(self.entries * rank + gram_rows, exponent_rows(self.entries))
        self.steps = jnp.exp2(exponents[:, :LANES].T[:rank]) * (1.0 / LEVELS)

    def rows(self, first, number):
        return self.ref[pl.ds(first, number), :].astype(jnp.int32).astype(F32)

    def proj(self, slot, p):
        entry = self.slots.index(slot) * self.count + p
        return self.rows(entry * self.rank, self.rank) * self.steps[:, entry : entry + 1]

    def gram(self):
        rank = self.rank
        digits = self.rows(self.entries * rank, rank // 2)
        digits = jnp.concatenate([digits[:, : 2 * rank], digits[:, 2 * rank :]], axis=0)
        return (digits[:, :rank] + digits[:, rank:] * (0.5 / LEVELS)) * self.steps[:, self.entries : self.entries + 1]


def encode(values, gram, coded_ref, rank):
    count = len(values)
    lanes = lane_numbers((rank, LANES))
    exponents = jnp.zeros((rank, LANES), F32)
    for p, value in enumerate(values):
        proj = value()
        exponent = row_exponent(proj)
        coded = jnp.floor(proj * (LEVELS / jnp.exp2(exponent)) + 0.5)
        coded_ref[pl.ds(p * rank, rank), :] = coded.astype(jnp.int32).astype(jnp.int16)
        exponents = jnp.where(lanes == p, exponent, exponents)
    end = count * rank
    if gram is not None:
        exponent = row_exponent(gram)
        scaled = gram * (LEVELS / jnp.exp2(exponent))
        whole = jnp.floor(scaled + 0.5)
        rest = jnp.floor((scaled - whole) * (2 * LEVELS) + 0.5)
        digits = jnp.concatenate([whole, rest], axis=1)
        digits = jnp.concatenate([digits[: rank // 2], digits[rank // 2 :]], axis=1)
        coded_ref[pl.ds(end, rank // 2), :] = digits.astype(jnp.int32).astype(jnp.int16)
        exponents = jnp.where(lanes == count, exponent, exponents)
        end += rank // 2
    rows = exponent_rows(count)
    last = jnp.concatenate([exponents.T[:rows], jnp.zeros((rows, coded_ref.shape[1] - rank), F32)], axis=1)
    coded_ref[pl.ds(end, rows), :] = last.astype(jnp.int32).astype(jnp.int16)


def first_projection_kernel(slots, with_gram, place, v_hbm, visits_ref, coded_ref, v_ref, buffers, sems, v_sem):
    count = buffers.shape[1]
    v_copy = pltpu.make_async_copy(v_hbm, v_ref, v_sem)
    v_copy.start()
    copies = [
        pltpu.make_async_copy(visits_ref.at[feature_of(place) ^ slot, pl.ds(0, count)], buffers.at[i], sems.at[i])
        for i, slot in enumerate(slots)
    ]
    for copy in copies:
        copy.start()
    v_copy.wait()

    def value(i, p):
        if p == 0:
            copies[i].wait()
        return low_dot(v_ref[...], buffers[i, p], ROWS_BY_ROWS)

    values = [functools.partial(value, i, p) for i in range(len(slots)) for p in range(count)]
    gram = low_dot(v_ref[...], v_ref[...], ROWS_BY_ROWS) if with_gram else None
    encode(values, gram, coded_ref, v_ref.shape[0])


def first_projection(slots, count, with_gram, place, visits, v_rows):
    width = visits.shape[3]
    rank = v_rows.shape[0]
    return pl.pallas_call(
        functools.partial(first_projection_kernel, slots, with_gram),
        in_specs=[SMEM_SPEC, HBM_SPEC, HBM_SPEC],
        out_specs=VMEM_SPEC,
        out_shape=jax.ShapeDtypeStruct(payload_shape(len(slots) * count, rank, visits.shape[2], with_gram), jnp.int16),
        scratch_shapes=[
            pltpu.VMEM(v_rows.shape, BF16),
            pltpu.VMEM((len(slots), count) + visits.shape[2:], BF16),
            pltpu.SemaphoreType.DMA((len(slots),)),
            pltpu.SemaphoreType.DMA,
        ],
        compiler_params=parameters(LIMIT),
        cost_estimate=SHORT,
        name="project_first",
    )(place, v_rows, visits)


def next_projection_kernel(slots, first, count, with_gram, layouts, place, v_ref, visits_ref, *refs):
    coded_ref = refs[-1]
    rank = v_ref.shape[0]
    arrived = [Payload(ref, layout, count, rank, with_gram) for ref, layout in zip(refs, layouts)]

    def value(slot, p):
        proj = low_dot(v_ref[...], visits_ref[feature_of(place) ^ slot, first + p], ROWS_BY_ROWS)
        for payload in arrived:
            proj = proj + payload.proj(slot, p)
        return proj

    gram = None
    if with_gram:
        gram = low_dot(v_ref[...], v_ref[...], ROWS_BY_ROWS)
        for payload in arrived:
            gram = gram + payload.gram()
    encode([functools.partial(value, slot, p) for slot in slots for p in range(count)], gram, coded_ref, rank)


def next_projection(slots, first, count, with_gram, layouts, place, visits, v_rows, arrived, after):
    rank = v_rows.shape[0]
    return pl.pallas_call(
        functools.partial(next_projection_kernel, slots, first, count, with_gram, layouts),
        in_specs=[SMEM_SPEC] + [VMEM_SPEC] * (2 + len(arrived)) + [ANY_SPEC] * len(after),
        out_specs=VMEM_SPEC,
        out_shape=jax.ShapeDtypeStruct(payload_shape(len(slots) * count, rank, visits.shape[2], with_gram), jnp.int16),
        compiler_params=parameters(LIMIT),
        cost_estimate=SHORT,
        name="project_next",
    )(place, v_rows, visits, *arrived, *after)


def spread_w_kernel(n_slots, place, w_ref, gram_ref, spread_ref):
    gram_ref[...] = high_dot(w_ref[...], w_ref[...], COLS_BY_COLS)
    patients, rank = w_ref.shape
    share = patients // n_slots
    w_rows = jnp.concatenate([w_ref[...], jnp.zeros((LANES - patients, rank), F32)], axis=0)
    w_columns = w_rows.T
    for slot in range(n_slots):
        first = (feature_of(place) ^ slot) * share
        columns = pltpu.roll(w_columns, jnp.where(first == 0, 0, LANES - first), 1)
        spread = [jnp.broadcast_to(columns[:, p : p + 1], (rank, rank)) for p in range(share)]
        spread_ref[slot] = jnp.concatenate(spread, axis=1)


def spread_w(place, w_start, n_slots):
    patients, rank = w_start.shape
    return pl.pallas_call(
        functools.partial(spread_w_kernel, n_slots),
        in_specs=[SMEM_SPEC, VMEM_SPEC],
        out_specs=[VMEM_SPEC] * 2,
        out_shape=[
            jax.ShapeDtypeStruct((rank, rank), F32),
            jax.ShapeDtypeStruct((n_slots, rank, patients // n_slots * rank), F32),
        ],
        compiler_params=parameters(LIMIT),
        cost_estimate=SHORT,
        name="spread_w",
    )(place, w_start)


def own_projection_kernel(place, v_ref, visits_ref, *refs):
    *proj_refs, v_gram_ref = refs
    count = visits_ref.shape[1] // len(proj_refs)
    for p in range(visits_ref.shape[1]):
        proj_refs[p // count][p % count] = low_dot(v_ref[...], visits_ref[feature_of(place), p], ROWS_BY_ROWS)
    v_gram_ref[...] = low_dot(v_ref[...], v_ref[...], ROWS_BY_ROWS)


def project_own(n_parts, place, visits, v_rows):
    _, share, slots, width = visits.shape
    rank = v_rows.shape[0]
    proj = jax.ShapeDtypeStruct((share // n_parts, rank, slots), F32)
    *own, v_gram = pl.pallas_call(
        own_projection_kernel,
        in_specs=[SMEM_SPEC] + [VMEM_SPEC] * 2,
        out_specs=[VMEM_SPEC] * (n_parts + 1),
        out_shape=[proj] * n_parts + [jax.ShapeDtypeStruct((rank, rank), F32)],
        compiler_params=parameters(LIMIT),
        cost_estimate=SHORT,
        name="project_own",
    )(place, v_rows, visits)
    return own, v_gram


def solve_tile(columns, tile):
    rows = lax.broadcasted_iota(jnp.int32, tile.shape, 0)
    for a in range(0, 8, 2):
        b = a + 1
        first, second = columns[a], columns[b]
        m_aa, m_ab, m_ba, m_bb = first[a:b], second[a:b], first[b : b + 1], second[b : b + 1]
        scale = 1.0 / (m_aa * m_bb - m_ab * m_ba)
        m_aa, m_ab, m_ba, m_bb = m_aa * scale, m_ab * scale, m_ba * scale, m_bb * scale

        def step(x):
            x_a, x_b = x[a:b], x[b : b + 1]
            new_a, new_b = m_bb * x_a - m_ab * x_b, m_aa * x_b - m_ba * x_a
            x = x - (first * new_a + second * new_b)
            return jnp.where(rows == a, new_a, jnp.where(rows == b, new_b, x))

        tile = step(tile)
        columns = [step(x) if q > b else x for q, x in enumerate(columns)]
    return tile


def eliminate(table, rank):
    tiles = [table[8 * t : 8 * t + 8] for t in range(rank // 8)]
    for home in range(rank // 8):
        first = 8 * home
        columns = [[jnp.broadcast_to(t[:, q : q + 1], t.shape) for q in range(first, first + 8)] for t in tiles]
        solved = solve_tile(columns[home], tiles[home])
        for t, tile in enumerate(tiles):
            terms = [column * solved[q : q + 1] for q, column in enumerate(columns[t])]
            while len(terms) > 1:
                terms = [x + y for x, y in zip(terms[::2], terms[1::2])]
            tiles[t] = solved if t == home else tile - terms[0]
    return jnp.concatenate(tiles, axis=0)


def inverse_of(gram):
    rank = gram.shape[0]
    eye = (lax.broadcasted_iota(jnp.int32, gram.shape, 0) == lane_numbers(gram.shape)).astype(F32)
    return eliminate(jnp.concatenate([gram, eye], axis=1), rank)[:, rank:]


def total(refs):
    out = refs[0][...]
    for ref in refs[1:]:
        out = out + ref[...]
    return out


def first_inverse_kernel(v_gram_ref, *refs):
    *terms, _, w_gram_ref, inverse_ref = refs
    w_gram = total(terms)
    w_gram_ref[...] = w_gram
    inverse_ref[...] = inverse_of(w_gram * v_gram_ref[...])


def first_inverse(v_gram, w_grams, after):
    out = jax.ShapeDtypeStruct(v_gram.shape, F32)
    return pl.pallas_call(
        first_inverse_kernel,
        in_specs=[VMEM_SPEC] * (1 + len(w_grams)) + [ANY_SPEC],
        out_specs=[VMEM_SPEC] * 2,
        out_shape=[out, out],
        compiler_params=parameters(LIMIT),
        cost_estimate=SHORT,
        name="first_inverse",
    )(v_gram, *w_grams, after)


def sweep_all(frames, rank, fine):
    patients = range(frames.shape[0])
    if fine:
        both = [jnp.concatenate(two_parts(frames[p]), axis=0) for p in patients]
        blocks = [low_dot(x, x, ROWS_BY_ROWS) for x in both]
        blocks = [x[:rank] + x[rank:] for x in blocks]
        grams = [x + pltpu.roll(x, rank, 1) for x in blocks]
        moved = [low_dot(jnp.concatenate(two_parts(g), axis=0), x) for g, x in zip(grams, both)]
        moved = [x[:rank] + x[rank:] for x in moved]
    else:
        first = [frames[p].astype(BF16) for p in patients]
        grams = [low_dot(x, x, ROWS_BY_ROWS).astype(BF16) for x in first]
        moved = [low_dot(g, x) for g, x in zip(grams, first)]
    for p in patients:
        frames[p] = 1.5 * frames[p] - 0.5 * moved[p]


def frames_kernel(layouts, part, share, place, counts_ref, h_ref, w_ref, v_gram_ref, before_ref, own_ref, *refs):
    coded, refs = refs[: len(layouts)], refs[len(layouts) :]
    frames_ref, terms_ref, v_total_ref, proj, frames = refs
    count, rank, slots = frames.shape
    patients = range(count)
    first = feature_of(place) * share + part * count
    pieces = [own_ref[p] for p in patients]
    v_gram = v_gram_ref[...]
    for code, layout in zip(coded, layouts):
        payload = Payload(code, layout, count, rank, (part + 1) * count == share)
        pieces = [pieces[p] + payload.proj(0, p) for p in patients]
        if payload.with_gram:
            v_gram = v_gram + payload.gram()
    v_total_ref[...] = v_gram
    for p in patients:
        proj[p] = pieces[p]
    weights = [w_ref[pl.ds(first + p, 1), :] for p in patients]
    mixed = [high_dot(h_ref[...] * weights[p], pieces[p]) for p in patients]
    lanes = lane_numbers((rank, slots))
    mixed = [jnp.where(lanes < counts_ref[first + p], mixed[p], 0.0) for p in patients]
    energy = [jnp.sum(jnp.sum(x * x, axis=1, keepdims=True), axis=0, keepdims=True) for x in mixed]
    for p in patients:
        frames[p] = mixed[p] * lax.rsqrt(energy[p] + epsilon)

    def sweep(fine, step, carry):
        sweep_all(frames, rank, fine)
        return carry

    lax.fori_loop(0, COARSE_STEPS, functools.partial(sweep, False), 0, unroll=True)
    lax.fori_loop(COARSE_STEPS, NS_STEPS, functools.partial(sweep, True), 0, unroll=True)
    low = [frames[p].astype(BF16) for p in patients]
    for p in patients:
        frames_ref[p] = low[p]
    products = [jnp.concatenate(three_parts(proj[p]), axis=0) for p in patients]
    products = [low_dot(low[p], products[p], ROWS_BY_ROWS) for p in patients]
    terms = before_ref[...] if part else jnp.zeros((rank, rank), F32)
    for p in patients:
        product = products[p][:, :rank] + (products[p][:, rank : 2 * rank] + products[p][:, 2 * rank :])
        terms = terms + product * weights[p]
    terms_ref[...] = terms


def own_frames(layouts, part, n_parts, place, counts, h_start, w_start, v_gram, before, own, coded):
    count, rank, slots = own.shape
    share = count * n_parts
    return pl.pallas_call(
        functools.partial(frames_kernel, layouts, part, share),
        in_specs=[SMEM_SPEC] * 2 + [VMEM_SPEC] * (5 + len(coded)),
        out_specs=[VMEM_SPEC] * 3,
        out_shape=[
            jax.ShapeDtypeStruct(own.shape, BF16),
            jax.ShapeDtypeStruct((rank, rank), F32),
            jax.ShapeDtypeStruct((rank, rank), F32),
        ],
        scratch_shapes=[pltpu.VMEM(own.shape, F32)] * 2,
        compiler_params=parameters(LIMIT),
        cost_estimate=SHORT,
        name="own_frames",
    )(place, counts, h_start, w_start, v_gram, before, own, *coded)


def projected_kernel(items, place, visits_ref, *refs):
    frames_refs, outs, token_ref = refs[: len(items)], refs[-2 * len(items) - 1 : -1], refs[-1]
    token_ref[...] = jnp.zeros_like(token_ref)
    for i, (slots, first) in enumerate(items):
        total_count, rank, _ = frames_refs[i].shape
        count = total_count // len(slots)
        for p in range(total_count):
            rows = pl.ds(p * rank, rank)
            owner = feature_of(place) ^ slots[p // count]
            product = low_dot(frames_refs[i][p], visits_ref[owner, first + p % count])
            outs[2 * i][rows, :], outs[2 * i + 1][rows, :] = two_parts(product)


def join_kernel(count, *refs):
    out_ref = refs[-1]
    first = 0
    for part in refs[:count]:
        out_ref[first : first + part.shape[0]] = part[...]
        first += part.shape[0]


def join(parts, after):
    if len(parts) == 1:
        return parts[0]
    return pl.pallas_call(
        functools.partial(join_kernel, len(parts)),
        in_specs=[VMEM_SPEC] * len(parts) + [ANY_SPEC] * len(after),
        out_specs=VMEM_SPEC,
        out_shape=jax.ShapeDtypeStruct((sum(x.shape[0] for x in parts),) + parts[0].shape[1:], parts[0].dtype),
        compiler_params=parameters(LIMIT),
        cost_estimate=SHORT,
        name="join_frames",
    )(*parts, *after)


def project_frames(items, place, frames, visits, after):
    width = visits.shape[-1]
    outs = []
    for item in items:
        count, rank, _ = frames[item].shape
        outs += [jax.ShapeDtypeStruct((count * rank, width), BF16)] * 2
    *parts, token = pl.pallas_call(
        functools.partial(projected_kernel, items),
        in_specs=[SMEM_SPEC] + [VMEM_SPEC] * (1 + len(items)) + [ANY_SPEC] * len(after),
        out_specs=[VMEM_SPEC] * (len(outs) + 1),
        out_shape=outs + [jax.ShapeDtypeStruct((8, LANES), F32)],
        compiler_params=parameters(LIMIT),
        cost_estimate=SHORT,
        name="project_frames",
    )(place, visits, *[frames[item] for item in items], *after)
    return {item: parts[2 * i : 2 * i + 2] for i, item in enumerate(items)}, token


def next_h_kernel(n_terms, *refs):
    inverse_ref, spread_ref, _, result_ref, h_ref, factor_ref = refs[n_terms:]
    h_next = high_dot(total(refs[:n_terms]), inverse_ref[...])
    result_ref[...] = h_next
    h_ref[...] = h_next
    rank = h_next.shape[0]
    h_rows = h_next.T
    h_rows = jnp.concatenate([h_rows] * (spread_ref.shape[2] // rank), axis=1)
    for slot in range(spread_ref.shape[0]):
        factor_ref[slot] = jnp.concatenate(three_parts(h_rows * spread_ref[slot]), axis=0)


def next_h(terms, inverse, spread, after):
    n_slots, rank, columns = spread.shape
    return pl.pallas_call(
        functools.partial(next_h_kernel, len(terms)),
        in_specs=[VMEM_SPEC] * (len(terms) + 2) + [ANY_SPEC],
        out_specs=[VMEM_SPEC] * 3,
        out_shape=[
            jax.ShapeDtypeStruct(inverse.shape, F32),
            jax.ShapeDtypeStruct(inverse.shape, F32),
            jax.ShapeDtypeStruct((n_slots, 3 * rank, columns), BF16),
        ],
        compiler_params=parameters(LIMIT),
        cost_estimate=SHORT,
        name="next_h",
    )(*terms, inverse, spread, after)


def second_inverse_kernel(h_ref, w_gram_ref, gram_ref, inverse_ref):
    gram = high_dot(h_ref[...], h_ref[...], COLS_BY_COLS)
    gram_ref[...] = gram
    inverse_ref[...] = inverse_of(gram * w_gram_ref[...])


def second_inverse(h_next, w_gram):
    out = jax.ShapeDtypeStruct(w_gram.shape, F32)
    return pl.pallas_call(
        second_inverse_kernel,
        out_shape=[out, out],
        compiler_params=parameters(LIMIT),
        cost_estimate=SHORT,
        name="second_inverse",
    )(h_next, w_gram)


def v_terms_kernel(items, sent, place, factor_ref, *refs):
    parts, terms_ref = refs[: 2 * len(items)], refs[-1]
    rank, half = terms_ref.shape
    upper = core_of(place) ^ 1 if sent else core_of(place)
    features = pl.ds(pl.multiple_of(upper * half, half), half)
    total = None
    for i, (slots, first) in enumerate(items):
        count = parts[2 * i].shape[0] // len(slots)
        columns = pl.ds(first * rank, count)
        for k, slot in enumerate(slots):
            rows = pl.ds(k * count, count)
            large = low_dot(factor_ref[slot, :, columns], parts[2 * i][rows, features])
            small = low_dot(factor_ref[slot, : 2 * rank, columns], parts[2 * i + 1][rows, features])
            terms = large[:rank] + (large[rank : 2 * rank] + small[:rank]) + (large[2 * rank :] + small[rank:])
            total = terms if total is None else total + terms
    terms_ref[...] = total


def half_v_terms(items, sent, place, factor, projected, after):
    width = projected[0].shape[1]
    rank = factor.shape[1] // 3
    return pl.pallas_call(
        functools.partial(v_terms_kernel, items, sent),
        in_specs=[SMEM_SPEC] + [VMEM_SPEC] * (1 + len(projected)) + [ANY_SPEC] * len(after),
        out_specs=VMEM_SPEC,
        out_shape=jax.ShapeDtypeStruct((rank, width // 2), F32),
        compiler_params=parameters(LIMIT),
        cost_estimate=SHORT,
        name="v_terms",
    )(place, factor, *projected, *after)


def next_v_kernel(items, share, later, place, terms_ref, inverse_ref, h_ref, *refs):
    parts, refs = refs[: 2 * len(items)], refs[2 * len(items) :]
    rank, half = terms_ref.shape
    here = pl.multiple_of((core_of(place) ^ 1 if later else core_of(place)) * half, half)
    features = pl.ds(here, half)
    v_rows = high_dot(inverse_ref[...], terms_ref[...])
    *before, v_ref, sums_ref, v_parts = refs
    v_ref[...] = v_rows
    sums = before[0][...] if later else jnp.zeros((rank, 2 * rank), F32)
    v_parts[...] = jnp.concatenate(two_parts(v_rows), axis=0)
    weights = jnp.concatenate([h_ref[...]] * 2, axis=1)
    gram = low_dot(v_parts[...], v_parts[...], ROWS_BY_ROWS)
    gram = gram[:rank, :rank] + (gram[:rank, rank:] + gram[rank:, :rank])
    sums_ref[...] = sums + jnp.concatenate([jnp.zeros((rank, rank), F32), gram], axis=1)
    for i, (slots, done) in enumerate(items):
        seen = low_dot(parts[2 * i][:, features], v_parts[...], ROWS_BY_ROWS)
        seen = seen + low_dot(parts[2 * i + 1][:, features], v_parts[...], ROWS_BY_ROWS)
        count = seen.shape[0] // rank // len(slots)
        for p in range(seen.shape[0] // rank):
            patient = (feature_of(place) ^ slots[p // count]) * share + done + p % count
            row = jnp.sum(seen[p * rank : (p + 1) * rank] * weights, axis=0, keepdims=True)
            sums_ref[pl.ds(patient, 1), :rank] += row[:, :rank] + row[:, rank:]


def half_v(items, share, place, terms, inverse, h_next, projected, before):
    rank, half = terms.shape
    return pl.pallas_call(
        functools.partial(next_v_kernel, items, share, bool(before)),
        in_specs=[SMEM_SPEC] + [VMEM_SPEC] * (3 + len(projected) + len(before)),
        out_specs=[VMEM_SPEC] * 2,
        out_shape=[
            jax.ShapeDtypeStruct((rank, half), F32),
            jax.ShapeDtypeStruct((rank, 2 * rank), F32),
        ],
        scratch_shapes=[pltpu.VMEM((2 * rank, half), BF16)],
        compiler_params=parameters(LIMIT),
        cost_estimate=SHORT,
        name="next_v",
    )(place, terms, inverse, h_next, *projected, *before)


def whole_v_kernel(place, own_ref, other_ref, v_ref, token_ref):
    half = own_ref.shape[1]
    upper = core_of(place) == 1
    v_ref[:, :half] = jnp.where(upper, other_ref[...], own_ref[...])
    v_ref[:, half:] = jnp.where(upper, own_ref[...], other_ref[...])
    token_ref[...] = jnp.zeros_like(token_ref)


def whole_v(place, own, other):
    rank, half = own.shape
    return pl.pallas_call(
        whole_v_kernel,
        in_specs=[SMEM_SPEC] + [VMEM_SPEC] * 2,
        out_specs=[VMEM_SPEC] * 2,
        out_shape=[jax.ShapeDtypeStruct((rank, 2 * half), F32), jax.ShapeDtypeStruct((8, LANES), F32)],
        compiler_params=parameters(LIMIT),
        cost_estimate=SHORT,
        name="whole_v",
    )(place, own, other)


def next_w_kernel(n_sums, *refs):
    gram_ref, _, w_ref = refs[n_sums:]
    patients, rank = w_ref.shape
    sums = total(refs[:n_sums])
    table = jnp.concatenate([sums[:, rank:] * gram_ref[...], sums.T[:rank]], axis=1)
    w_ref[...] = eliminate(table, rank).T[rank : rank + patients]


def next_w(sums, h_gram, patients, after):
    rank = h_gram.shape[0]
    return pl.pallas_call(
        functools.partial(next_w_kernel, len(sums)),
        in_specs=[VMEM_SPEC] * (len(sums) + 1) + [ANY_SPEC],
        out_specs=VMEM_SPEC,
        out_shape=jax.ShapeDtypeStruct((patients, rank), F32),
        compiler_params=parameters(LIMIT),
        cost_estimate=SHORT,
        name="next_w",
    )(*sums, h_gram, after)


def swap(x, axis, slot):
    pairs = [(i, i ^ slot) for i in range(lax.axis_size(axis))]
    return lax.ppermute(x, axis, pairs)


def all_terms(x, axis):
    n = lax.axis_size(axis)
    if n > 4:
        return [lax.psum(x, axis)]
    return [x] + [swap(x, axis, s) for s in range(1, n)]


def staged_terms(x, axis, after):
    n = lax.axis_size(axis)
    steps = [1 << i for i in range(n.bit_length() - 1)]
    for step in steps[:-1]:
        x = add(x, swap(x, axis, step), after)
    return [x, swap(x, axis, steps[-1])]


def add_kernel(a_ref, b_ref, *refs):
    refs[-1][...] = a_ref[...] + b_ref[...]


def add(a, b, after):
    return pl.pallas_call(
        add_kernel,
        in_specs=[VMEM_SPEC] * 2 + [ANY_SPEC] * len(after),
        out_specs=VMEM_SPEC,
        out_shape=jax.ShapeDtypeStruct(a.shape, a.dtype),
        compiler_params=parameters(LIMIT),
        cost_estimate=SHORT,
        name="add_terms",
    )(a, b, *after)


def patient_halves(keep, send, after):
    own = add(keep, swap(send, "patient", 1), [])
    step = 2
    while step < lax.axis_size("patient"):
        own = add(own, swap(own, "patient", step), [after])
        step *= 2
    return own, swap(own, "patient", 1)


def on_device(visits, visit_counts, h_start, v_start, w_start):
    n = lax.axis_size("feature")
    patients, slots, width = visits.shape
    share = patients // n
    place = (2 * lax.axis_index("feature") + (lax.axis_index("patient") & 1)).astype(jnp.int32).reshape(1)
    by_owner = visits.reshape(n, share, slots, width)
    in_hbm = pltpu.with_memory_space_constraint(by_owner, pltpu.HBM)
    v_rows = pltpu.with_memory_space_constraint(v_start.T, pltpu.HBM)

    n_parts = 2 if share % 2 == 0 else 1
    count = share // n_parts
    firsts = [part * count for part in range(n_parts)]
    bits = [1 << i for i in range(n.bit_length() - 1)]
    v_near = v_start.T

    def send(bit):
        return [slot for slot in range(n) if slot & bit and not slot & (bit - 1)]

    def receive(bit):
        return [slot ^ bit for slot in send(bit)]

    w_gram, spread = spread_w(place, w_start, n)
    w_grams = staged_terms(w_gram, "patient", [])
    own, v_gram = project_own(n_parts, place, by_owner, v_near)
    h_local = v_gram
    arrived = [[] for _ in firsts]
    for i, bit in enumerate(bits):
        layouts = [receive(before) for before in bits[:i]]
        for part, first in enumerate(firsts):
            if i == 0 and part == 0:
                code = first_projection(send(bit), count, n_parts == 1, place, in_hbm, v_rows)
            else:
                after = [w_grams[part]] + [v_gram] * part if i else []
                code = next_projection(
                    send(bit), first, count, part == n_parts - 1, layouts, place, by_owner, v_near, arrived[part], after
                )
            arrived[part] = arrived[part] + [swap(code, "feature", bit)]

    layouts = [receive(bit) for bit in bits]
    frames = [[] for _ in firsts]
    joined = []

    def double(part, after):
        for bit in bits[::-1]:
            slots = tuple(slot ^ bit for group, _ in frames[part] for slot in group)
            joined = join([x for _, x in frames[part]], after)
            frames[part].append((slots, swap(joined, "feature", bit)))
        return [joined]

    def project_groups(groups, after):
        arrays = {(frames[part][k][0], firsts[part]): frames[part][k][1] for part, k in groups}
        return project_frames(list(arrays), place, arrays, by_owner, after)

    for part, first in enumerate(firsts):
        low, h_local, v_total = own_frames(
            layouts, part, n_parts, place, visit_counts, h_start, w_start, v_gram, h_local, own[part], arrived[part]
        )
        v_gram = v_total
        frames[part].append(((0,), low))

    last = len(bits)
    for part in range(n_parts - 1):
        joined = double(part, [frames[-1][0][1]])
    first_groups = [(part, 0) for part in range(n_parts)] + [(part, 1) for part in range(n_parts - 1)]
    early = [(part, k) for part in range(n_parts - 1) for k in range(2, last + 1)]
    projected, token = project_groups(first_groups, joined)
    h_sums = staged_terms(h_local, "patient", [token])
    w_gram, inverse = first_inverse(v_gram, w_grams, h_sums[0])
    h_sum = add(*h_sums, [inverse])
    joined = double(n_parts - 1, [h_sum] + [frames[part][k][1] for part, k in early])
    h_terms = all_terms(h_sum, "feature")
    after = joined
    for groups in [early] + [[(n_parts - 1, k)] for k in range(1, last + 1)]:
        if groups:
            more, token = project_groups(groups, after)
            projected |= more
            after = [token]
    h_result, h_next, factor = next_h(h_terms, inverse, spread, token)

    items = list(projected)
    flat = [x for item in items for x in projected[item]]
    send = half_v_terms(items, True, place, factor, flat, [])
    keep = half_v_terms(items, False, place, factor, flat, [send])
    h_gram, second = second_inverse(h_next, w_gram)
    own_terms, other_terms = patient_halves(keep, send, second)
    v_own, before = half_v(items, share, place, own_terms, second, h_next, flat, [])
    v_other, sums = half_v(items, share, place, other_terms, second, h_next, flat, [before])
    v_next, token = whole_v(place, v_own, v_other)
    w_next = next_w(all_terms(sums, "feature"), h_gram, patients, token)
    return (h_result, v_next.T, w_next)


def solution(mesh):
    return jax.shard_map(
        on_device,
        mesh=mesh,
        in_specs=(
            P(("groups", "patient"), None, "feature"),
            P(("groups", "patient")),
            P(),
            P("feature", None),
            P(("groups", "patient"), None),
        ),
        out_specs=(P(None, "groups"), P("feature", "groups"), P("patient", "groups")),
        check_vma=False,
    )
```

```python
import functools

import jax
import jax.numpy as jnp
from jax import lax
from jax.experimental import pallas as pl
from jax.experimental.pallas import tpu as pltpu
from jax.sharding import PartitionSpec as P

NS_STEPS = 12
LANES = 128
LEVELS = 32000.0
COARSE_STEPS = 3
SHORT = pl.CostEstimate(flops=1000, bytes_accessed=1000, transcendentals=0)

epsilon = 1e-06
HIGH = lax.Precision.HIGHEST
F32 = jnp.float32
BF16 = jnp.bfloat16
MIB = 1024 * 1024

ROWS_BY_COLS = (((1,), (0,)), ((), ()))
ROWS_BY_ROWS = (((1,), (1,)), ((), ()))
COLS_BY_COLS = (((0,), (0,)), ((), ()))


def low_dot(a, b, dims=ROWS_BY_COLS):
    return lax.dot_general(a, b, dims, preferred_element_type=F32)


def high_dot(a, b, dims=ROWS_BY_COLS):
    return lax.dot_general(a, b, dims, precision=HIGH, preferred_element_type=F32)


def two_parts(x):
    first = x.astype(BF16)
    return first, (x - first.astype(F32)).astype(BF16)


def three_parts(x):
    first = x.astype(BF16)
    rest = x - first.astype(F32)
    second = rest.astype(BF16)
    return first, second, (rest - second.astype(F32)).astype(BF16)


def feature_of(place):
    return place[0] >> 1


def core_of(place):
    return place[0] & 1


def lane_numbers(shape):
    return lax.broadcasted_iota(jnp.int32, shape, len(shape) - 1)


ANY_SPEC = pl.BlockSpec(memory_space=pl.ANY)
HBM_SPEC = pl.BlockSpec(memory_space=pltpu.HBM)


def parameters(mib):
    return pltpu.CompilerParams(vmem_limit_bytes=mib * MIB)


LIMIT = 8
VMEM_SPEC = pl.BlockSpec(memory_space=pltpu.VMEM)
SMEM_SPEC = pl.BlockSpec(memory_space=pltpu.SMEM)


def exponent_rows(total_count):
    return -(-(total_count + 1) // 16) * 16


def payload_shape(total_count, rank, slots, with_gram):
    return (total_count * rank + (rank // 2 if with_gram else 0) + exponent_rows(total_count), slots)


def row_exponent(x):
    top = jnp.max(jnp.abs(x), axis=1, keepdims=True)
    return jnp.ceil(jnp.log2(jnp.maximum(top, 1e-30)))


class Payload:
    def __init__(self, ref, slots, count, rank, with_gram):
        self.ref, self.slots, self.count, self.rank, self.with_gram = ref, slots, count, rank, with_gram
        self.entries = len(slots) * count
        gram_rows = rank // 2 if with_gram else 0
        exponents = self.rows(self.entries * rank + gram_rows, exponent_rows(self.entries))
        self.steps = jnp.exp2(exponents[:, :LANES].T[:rank]) * (1.0 / LEVELS)

    def rows(self, first, number):
        return self.ref[pl.ds(first, number), :].astype(jnp.int32).astype(F32)

    def proj(self, slot, p):
        entry = self.slots.index(slot) * self.count + p
        return self.rows(entry * self.rank, self.rank) * self.steps[:, entry : entry + 1]

    def gram(self):
        rank = self.rank
        digits = self.rows(self.entries * rank, rank // 2)
        digits = jnp.concatenate([digits[:, : 2 * rank], digits[:, 2 * rank :]], axis=0)
        return (digits[:, :rank] + digits[:, rank:] * (0.5 / LEVELS)) * self.steps[:, self.entries : self.entries + 1]


def encode(values, gram, coded_ref, rank):
    count = len(values)
    lanes = lane_numbers((rank, LANES))
    exponents = jnp.zeros((rank, LANES), F32)
    for p, value in enumerate(values):
        proj = value()
        exponent = row_exponent(proj)
        coded = jnp.floor(proj * (LEVELS / jnp.exp2(exponent)) + 0.5)
        coded_ref[pl.ds(p * rank, rank), :] = coded.astype(jnp.int32).astype(jnp.int16)
        exponents = jnp.where(lanes == p, exponent, exponents)
    end = count * rank
    if gram is not None:
        exponent = row_exponent(gram)
        scaled = gram * (LEVELS / jnp.exp2(exponent))
        whole = jnp.floor(scaled + 0.5)
        rest = jnp.floor((scaled - whole) * (2 * LEVELS) + 0.5)
        digits = jnp.concatenate([whole, rest], axis=1)
        digits = jnp.concatenate([digits[: rank // 2], digits[rank // 2 :]], axis=1)
        coded_ref[pl.ds(end, rank // 2), :] = digits.astype(jnp.int32).astype(jnp.int16)
        exponents = jnp.where(lanes == count, exponent, exponents)
        end += rank // 2
    rows = exponent_rows(count)
    last = jnp.concatenate([exponents.T[:rows], jnp.zeros((rows, coded_ref.shape[1] - rank), F32)], axis=1)
    coded_ref[pl.ds(end, rows), :] = last.astype(jnp.int32).astype(jnp.int16)


def first_projection_kernel(slots, with_gram, place, v_hbm, visits_ref, coded_ref, v_ref, buffers, sems, v_sem):
    count = buffers.shape[1]
    v_copy = pltpu.make_async_copy(v_hbm, v_ref, v_sem)
    v_copy.start()
    pieces = sems.shape[1]
    piece = count // pieces
    copies = []
    for i, slot in enumerate(slots):
        for j in range(pieces):
            rows = pl.ds(j * piece, piece)
            source = visits_ref.at[feature_of(place) ^ slot, rows]
            copies.append(pltpu.make_async_copy(source, buffers.at[i, rows], sems.at[i, j]))
            copies[-1].start()
    v_copy.wait()

    def value(i, p):
        if p % piece == 0:
            copies[i * pieces + p // piece].wait()
        return low_dot(v_ref[...], buffers[i, p], ROWS_BY_ROWS)

    values = [functools.partial(value, i, p) for i in range(len(slots)) for p in range(count)]
    gram = low_dot(v_ref[...], v_ref[...], ROWS_BY_ROWS) if with_gram else None
    encode(values, gram, coded_ref, v_ref.shape[0])


def first_projection(slots, count, with_gram, place, visits, v_rows):
    width = visits.shape[3]
    rank = v_rows.shape[0]
    return pl.pallas_call(
        functools.partial(first_projection_kernel, slots, with_gram),
        in_specs=[SMEM_SPEC, HBM_SPEC, HBM_SPEC],
        out_specs=VMEM_SPEC,
        out_shape=jax.ShapeDtypeStruct(payload_shape(len(slots) * count, rank, visits.shape[2], with_gram), jnp.int16),
        scratch_shapes=[
            pltpu.VMEM(v_rows.shape, BF16),
            pltpu.VMEM((len(slots), count) + visits.shape[2:], BF16),
            pltpu.SemaphoreType.DMA((len(slots), 2 if count % 2 == 0 else 1)),
            pltpu.SemaphoreType.DMA,
        ],
        compiler_params=parameters(LIMIT),
        cost_estimate=SHORT,
        name="project_first",
    )(place, v_rows, visits)


def next_projection_kernel(slots, first, count, with_gram, layouts, place, v_ref, visits_ref, *refs):
    coded_ref = refs[-1]
    rank = v_ref.shape[0]
    arrived = [Payload(ref, layout, count, rank, with_gram) for ref, layout in zip(refs, layouts)]

    def value(slot, p):
        proj = low_dot(v_ref[...], visits_ref[feature_of(place) ^ slot, first + p], ROWS_BY_ROWS)
        for payload in arrived:
            proj = proj + payload.proj(slot, p)
        return proj

    gram = None
    if with_gram:
        gram = low_dot(v_ref[...], v_ref[...], ROWS_BY_ROWS)
        for payload in arrived:
            gram = gram + payload.gram()
    encode([functools.partial(value, slot, p) for slot in slots for p in range(count)], gram, coded_ref, rank)


def next_projection(slots, first, count, with_gram, layouts, place, visits, v_rows, arrived, after):
    rank = v_rows.shape[0]
    return pl.pallas_call(
        functools.partial(next_projection_kernel, slots, first, count, with_gram, layouts),
        in_specs=[SMEM_SPEC] + [VMEM_SPEC] * (2 + len(arrived)) + [ANY_SPEC] * len(after),
        out_specs=VMEM_SPEC,
        out_shape=jax.ShapeDtypeStruct(payload_shape(len(slots) * count, rank, visits.shape[2], with_gram), jnp.int16),
        compiler_params=parameters(LIMIT),
        cost_estimate=SHORT,
        name="project_next",
    )(place, v_rows, visits, *arrived, *after)


def spread_w_kernel(n_slots, place, w_ref, gram_ref, spread_ref):
    gram_ref[...] = high_dot(w_ref[...], w_ref[...], COLS_BY_COLS)
    patients, rank = w_ref.shape
    share = patients // n_slots
    w_rows = jnp.concatenate([w_ref[...], jnp.zeros((LANES - patients, rank), F32)], axis=0)
    w_columns = w_rows.T
    for slot in range(n_slots):
        first = (feature_of(place) ^ slot) * share
        columns = pltpu.roll(w_columns, jnp.where(first == 0, 0, LANES - first), 1)
        spread = [jnp.broadcast_to(columns[:, p : p + 1], (rank, rank)) for p in range(share)]
        spread_ref[slot] = jnp.concatenate(spread, axis=1)


def spread_w(place, w_start, n_slots):
    patients, rank = w_start.shape
    return pl.pallas_call(
        functools.partial(spread_w_kernel, n_slots),
        in_specs=[SMEM_SPEC, VMEM_SPEC],
        out_specs=[VMEM_SPEC] * 2,
        out_shape=[
            jax.ShapeDtypeStruct((rank, rank), F32),
            jax.ShapeDtypeStruct((n_slots, rank, patients // n_slots * rank), F32),
        ],
        compiler_params=parameters(LIMIT),
        cost_estimate=SHORT,
        name="spread_w",
    )(place, w_start)


def own_projection_kernel(layout, place, v_ref, visits_ref, arrived_ref, *refs):
    *proj_refs, v_gram_ref = refs
    count, rank, _ = proj_refs[0].shape
    payload = Payload(arrived_ref, layout, count, rank, len(proj_refs) == 1)
    for p in range(visits_ref.shape[1]):
        proj = low_dot(v_ref[...], visits_ref[feature_of(place), p], ROWS_BY_ROWS)
        proj_refs[p // count][p % count] = proj + payload.proj(0, p) if p < count else proj
    gram = low_dot(v_ref[...], v_ref[...], ROWS_BY_ROWS)
    v_gram_ref[...] = gram + payload.gram() if payload.with_gram else gram


def project_own(n_parts, layout, place, visits, v_rows, arrived):
    _, share, slots, width = visits.shape
    rank = v_rows.shape[0]
    proj = jax.ShapeDtypeStruct((share // n_parts, rank, slots), F32)
    *own, v_gram = pl.pallas_call(
        functools.partial(own_projection_kernel, layout),
        in_specs=[SMEM_SPEC] + [VMEM_SPEC] * 3,
        out_specs=[VMEM_SPEC] * (n_parts + 1),
        out_shape=[proj] * n_parts + [jax.ShapeDtypeStruct((rank, rank), F32)],
        compiler_params=parameters(LIMIT),
        cost_estimate=SHORT,
        name="project_own",
    )(place, v_rows, visits, arrived)
    return own, v_gram


def solve_tile(columns, tile):
    rows = lax.broadcasted_iota(jnp.int32, tile.shape, 0)
    for a in range(0, 8, 2):
        b = a + 1
        first, second = columns[a], columns[b]
        m_aa, m_ab, m_ba, m_bb = first[a:b], second[a:b], first[b : b + 1], second[b : b + 1]
        scale = 1.0 / (m_aa * m_bb - m_ab * m_ba)
        m_aa, m_ab, m_ba, m_bb = m_aa * scale, m_ab * scale, m_ba * scale, m_bb * scale

        def step(x):
            x_a, x_b = x[a:b], x[b : b + 1]
            new_a, new_b = m_bb * x_a - m_ab * x_b, m_aa * x_b - m_ba * x_a
            x = x - (first * new_a + second * new_b)
            return jnp.where(rows == a, new_a, jnp.where(rows == b, new_b, x))

        tile = step(tile)
        columns = [step(x) if q > b else x for q, x in enumerate(columns)]
    return tile


def eliminate(table, rank):
    tiles = [table[8 * t : 8 * t + 8] for t in range(rank // 8)]
    for home in range(rank // 8):
        first = 8 * home
        columns = [[jnp.broadcast_to(t[:, q : q + 1], t.shape) for q in range(first, first + 8)] for t in tiles]
        solved = solve_tile(columns[home], tiles[home])
        for t, tile in enumerate(tiles):
            terms = [column * solved[q : q + 1] for q, column in enumerate(columns[t])]
            while len(terms) > 1:
                terms = [x + y for x, y in zip(terms[::2], terms[1::2])]
            tiles[t] = solved if t == home else tile - terms[0]
    return jnp.concatenate(tiles, axis=0)


def inverse_of(gram):
    rank = gram.shape[0]
    eye = (lax.broadcasted_iota(jnp.int32, gram.shape, 0) == lane_numbers(gram.shape)).astype(F32)
    return eliminate(jnp.concatenate([gram, eye], axis=1), rank)[:, rank:]


def total(refs):
    out = refs[0][...]
    for ref in refs[1:]:
        out = out + ref[...]
    return out


def first_inverse_kernel(v_gram_ref, *refs):
    *terms, _, w_gram_ref, inverse_ref = refs
    w_gram = total(terms)
    w_gram_ref[...] = w_gram
    inverse_ref[...] = inverse_of(w_gram * v_gram_ref[...])


def first_inverse(v_gram, w_grams, after):
    out = jax.ShapeDtypeStruct(v_gram.shape, F32)
    return pl.pallas_call(
        first_inverse_kernel,
        in_specs=[VMEM_SPEC] * (1 + len(w_grams)) + [ANY_SPEC],
        out_specs=[VMEM_SPEC] * 2,
        out_shape=[out, out],
        compiler_params=parameters(LIMIT),
        cost_estimate=SHORT,
        name="first_inverse",
    )(v_gram, *w_grams, after)


def sweep_all(frames, rank, fine):
    patients = range(frames.shape[0])
    if fine:
        both = [jnp.concatenate(two_parts(frames[p]), axis=0) for p in patients]
        blocks = [low_dot(x, x, ROWS_BY_ROWS) for x in both]
        blocks = [x[:rank] + x[rank:] for x in blocks]
        grams = [x + pltpu.roll(x, rank, 1) for x in blocks]
        moved = [low_dot(jnp.concatenate(two_parts(g), axis=0), x) for g, x in zip(grams, both)]
        moved = [x[:rank] + x[rank:] for x in moved]
    else:
        first = [frames[p].astype(BF16) for p in patients]
        grams = [low_dot(x, x, ROWS_BY_ROWS).astype(BF16) for x in first]
        moved = [low_dot(g, x) for g, x in zip(grams, first)]
    for p in patients:
        frames[p] = 1.5 * frames[p] - 0.5 * moved[p]


def frames_kernel(layouts, part, share, place, counts_ref, h_ref, w_ref, v_gram_ref, before_ref, own_ref, *refs):
    coded, refs = refs[: len(layouts)], refs[len(layouts) :]
    frames_ref, terms_ref, v_total_ref, proj, frames = refs
    count, rank, slots = frames.shape
    patients = range(count)
    first = feature_of(place) * share + part * count
    pieces = [own_ref[p] for p in patients]
    v_gram = v_gram_ref[...]
    for code, layout in zip(coded, layouts):
        payload = Payload(code, layout, count, rank, (part + 1) * count == share)
        pieces = [pieces[p] + payload.proj(0, p) for p in patients]
        if payload.with_gram:
            v_gram = v_gram + payload.gram()
    v_total_ref[...] = v_gram
    for p in patients:
        proj[p] = pieces[p]
    weights = [w_ref[pl.ds(first + p, 1), :] for p in patients]
    mixed = [high_dot(h_ref[...] * weights[p], pieces[p]) for p in patients]
    lanes = lane_numbers((rank, slots))
    mixed = [jnp.where(lanes < counts_ref[first + p], mixed[p], 0.0) for p in patients]
    energy = [jnp.sum(jnp.sum(x * x, axis=1, keepdims=True), axis=0, keepdims=True) for x in mixed]
    for p in patients:
        frames[p] = mixed[p] * lax.rsqrt(energy[p] + epsilon)

    def sweep(fine, step, carry):
        sweep_all(frames, rank, fine)
        return carry

    lax.fori_loop(0, COARSE_STEPS, functools.partial(sweep, False), 0, unroll=True)
    lax.fori_loop(COARSE_STEPS, NS_STEPS, functools.partial(sweep, True), 0, unroll=True)
    low = [frames[p].astype(BF16) for p in patients]
    for p in patients:
        frames_ref[p] = low[p]
    products = [jnp.concatenate(three_parts(proj[p]), axis=0) for p in patients]
    products = [low_dot(low[p], products[p], ROWS_BY_ROWS) for p in patients]
    terms = before_ref[...] if part else jnp.zeros((rank, rank), F32)
    for p in patients:
        product = products[p][:, :rank] + (products[p][:, rank : 2 * rank] + products[p][:, 2 * rank :])
        terms = terms + product * weights[p]
    terms_ref[...] = terms


def own_frames(layouts, part, n_parts, place, counts, h_start, w_start, v_gram, before, own, coded):
    count, rank, slots = own.shape
    share = count * n_parts
    return pl.pallas_call(
        functools.partial(frames_kernel, layouts, part, share),
        in_specs=[SMEM_SPEC] * 2 + [VMEM_SPEC] * (5 + len(coded)),
        out_specs=[VMEM_SPEC] * 3,
        out_shape=[
            jax.ShapeDtypeStruct(own.shape, BF16),
            jax.ShapeDtypeStruct((rank, rank), F32),
            jax.ShapeDtypeStruct((rank, rank), F32),
        ],
        scratch_shapes=[pltpu.VMEM(own.shape, F32)] * 2,
        compiler_params=parameters(LIMIT),
        cost_estimate=SHORT,
        name="own_frames",
    )(place, counts, h_start, w_start, v_gram, before, own, *coded)


def projected_kernel(items, place, visits_ref, *refs):
    frames_refs, outs, token_ref = refs[: len(items)], refs[-2 * len(items) - 1 : -1], refs[-1]
    token_ref[...] = jnp.zeros_like(token_ref)
    for i, (slots, first) in enumerate(items):
        total_count, rank, _ = frames_refs[i].shape
        count = total_count // len(slots)
        for p in range(total_count):
            rows = pl.ds(p * rank, rank)
            owner = feature_of(place) ^ slots[p // count]
            product = low_dot(frames_refs[i][p], visits_ref[owner, first + p % count])
            outs[2 * i][rows, :], outs[2 * i + 1][rows, :] = two_parts(product)


def join_kernel(count, *refs):
    out_ref = refs[-1]
    first = 0
    for part in refs[:count]:
        out_ref[first : first + part.shape[0]] = part[...]
        first += part.shape[0]


def join(parts, after):
    if len(parts) == 1:
        return parts[0]
    return pl.pallas_call(
        functools.partial(join_kernel, len(parts)),
        in_specs=[VMEM_SPEC] * len(parts) + [ANY_SPEC] * len(after),
        out_specs=VMEM_SPEC,
        out_shape=jax.ShapeDtypeStruct((sum(x.shape[0] for x in parts),) + parts[0].shape[1:], parts[0].dtype),
        compiler_params=parameters(LIMIT),
        cost_estimate=SHORT,
        name="join_frames",
    )(*parts, *after)


def project_frames(items, place, frames, visits, after):
    width = visits.shape[-1]
    outs = []
    for item in items:
        count, rank, _ = frames[item].shape
        outs += [jax.ShapeDtypeStruct((count * rank, width), BF16)] * 2
    *parts, token = pl.pallas_call(
        functools.partial(projected_kernel, items),
        in_specs=[SMEM_SPEC] + [VMEM_SPEC] * (1 + len(items)) + [ANY_SPEC] * len(after),
        out_specs=[VMEM_SPEC] * (len(outs) + 1),
        out_shape=outs + [jax.ShapeDtypeStruct((8, LANES), F32)],
        compiler_params=parameters(LIMIT),
        cost_estimate=SHORT,
        name="project_frames",
    )(place, visits, *[frames[item] for item in items], *after)
    return {item: parts[2 * i : 2 * i + 2] for i, item in enumerate(items)}, token


def next_h_kernel(n_terms, *refs):
    inverse_ref, spread_ref, _, result_ref, h_ref, factor_ref = refs[n_terms:]
    h_next = high_dot(total(refs[:n_terms]), inverse_ref[...])
    result_ref[...] = h_next
    h_ref[...] = h_next
    rank = h_next.shape[0]
    h_rows = h_next.T
    h_rows = jnp.concatenate([h_rows] * (spread_ref.shape[2] // rank), axis=1)
    for slot in range(spread_ref.shape[0]):
        factor_ref[slot] = jnp.concatenate(three_parts(h_rows * spread_ref[slot]), axis=0)


def next_h(terms, inverse, spread, after):
    n_slots, rank, columns = spread.shape
    return pl.pallas_call(
        functools.partial(next_h_kernel, len(terms)),
        in_specs=[VMEM_SPEC] * (len(terms) + 2) + [ANY_SPEC],
        out_specs=[VMEM_SPEC] * 3,
        out_shape=[
            jax.ShapeDtypeStruct(inverse.shape, F32),
            jax.ShapeDtypeStruct(inverse.shape, F32),
            jax.ShapeDtypeStruct((n_slots, 3 * rank, columns), BF16),
        ],
        compiler_params=parameters(LIMIT),
        cost_estimate=SHORT,
        name="next_h",
    )(*terms, inverse, spread, after)


def second_inverse_kernel(h_ref, w_gram_ref, gram_ref, inverse_ref):
    gram = high_dot(h_ref[...], h_ref[...], COLS_BY_COLS)
    gram_ref[...] = gram
    inverse_ref[...] = inverse_of(gram * w_gram_ref[...])


def second_inverse(h_next, w_gram):
    out = jax.ShapeDtypeStruct(w_gram.shape, F32)
    return pl.pallas_call(
        second_inverse_kernel,
        out_shape=[out, out],
        compiler_params=parameters(LIMIT),
        cost_estimate=SHORT,
        name="second_inverse",
    )(h_next, w_gram)


def v_terms_kernel(items, sent, place, factor_ref, *refs):
    parts, terms_ref = refs[: 2 * len(items)], refs[-1]
    rank, half = terms_ref.shape
    upper = core_of(place) ^ 1 if sent else core_of(place)
    features = pl.ds(pl.multiple_of(upper * half, half), half)
    total = None
    for i, (slots, first) in enumerate(items):
        count = parts[2 * i].shape[0] // len(slots)
        columns = pl.ds(first * rank, count)
        for k, slot in enumerate(slots):
            rows = pl.ds(k * count, count)
            large = low_dot(factor_ref[slot, :, columns], parts[2 * i][rows, features])
            small = low_dot(factor_ref[slot, : 2 * rank, columns], parts[2 * i + 1][rows, features])
            terms = large[:rank] + (large[rank : 2 * rank] + small[:rank]) + (large[2 * rank :] + small[rank:])
            total = terms if total is None else total + terms
    terms_ref[...] = total


def half_v_terms(items, sent, place, factor, projected, after):
    width = projected[0].shape[1]
    rank = factor.shape[1] // 3
    return pl.pallas_call(
        functools.partial(v_terms_kernel, items, sent),
        in_specs=[SMEM_SPEC] + [VMEM_SPEC] * (1 + len(projected)) + [ANY_SPEC] * len(after),
        out_specs=VMEM_SPEC,
        out_shape=jax.ShapeDtypeStruct((rank, width // 2), F32),
        compiler_params=parameters(LIMIT),
        cost_estimate=SHORT,
        name="v_terms",
    )(place, factor, *projected, *after)


def next_v_kernel(items, share, later, place, terms_ref, inverse_ref, h_ref, *refs):
    parts, refs = refs[: 2 * len(items)], refs[2 * len(items) :]
    rank, half = terms_ref.shape
    here = pl.multiple_of((core_of(place) ^ 1 if later else core_of(place)) * half, half)
    features = pl.ds(here, half)
    v_rows = high_dot(inverse_ref[...], terms_ref[...])
    *before, v_ref, sums_ref, v_parts = refs
    v_ref[...] = v_rows
    sums = before[0][...] if later else jnp.zeros((rank, 2 * rank), F32)
    v_parts[...] = jnp.concatenate(two_parts(v_rows), axis=0)
    weights = jnp.concatenate([h_ref[...]] * 2, axis=1)
    gram = low_dot(v_parts[...], v_parts[...], ROWS_BY_ROWS)
    gram = gram[:rank, :rank] + (gram[:rank, rank:] + gram[rank:, :rank])
    sums_ref[...] = sums + jnp.concatenate([jnp.zeros((rank, rank), F32), gram], axis=1)
    for i, (slots, done) in enumerate(items):
        seen = low_dot(parts[2 * i][:, features], v_parts[...], ROWS_BY_ROWS)
        seen = seen + low_dot(parts[2 * i + 1][:, features], v_parts[...], ROWS_BY_ROWS)
        count = seen.shape[0] // rank // len(slots)
        for p in range(seen.shape[0] // rank):
            patient = (feature_of(place) ^ slots[p // count]) * share + done + p % count
            row = jnp.sum(seen[p * rank : (p + 1) * rank] * weights, axis=0, keepdims=True)
            sums_ref[pl.ds(patient, 1), :rank] += row[:, :rank] + row[:, rank:]


def half_v(items, share, place, terms, inverse, h_next, projected, before):
    rank, half = terms.shape
    return pl.pallas_call(
        functools.partial(next_v_kernel, items, share, bool(before)),
        in_specs=[SMEM_SPEC] + [VMEM_SPEC] * (3 + len(projected) + len(before)),
        out_specs=[VMEM_SPEC] * 2,
        out_shape=[
            jax.ShapeDtypeStruct((rank, half), F32),
            jax.ShapeDtypeStruct((rank, 2 * rank), F32),
        ],
        scratch_shapes=[pltpu.VMEM((2 * rank, half), BF16)],
        compiler_params=parameters(LIMIT),
        cost_estimate=SHORT,
        name="next_v",
    )(place, terms, inverse, h_next, *projected, *before)


def whole_v_kernel(place, own_ref, other_ref, v_ref, token_ref):
    half = own_ref.shape[1]
    upper = core_of(place) == 1
    v_ref[:, :half] = jnp.where(upper, other_ref[...], own_ref[...])
    v_ref[:, half:] = jnp.where(upper, own_ref[...], other_ref[...])
    token_ref[...] = jnp.zeros_like(token_ref)


def whole_v(place, own, other):
    rank, half = own.shape
    return pl.pallas_call(
        whole_v_kernel,
        in_specs=[SMEM_SPEC] + [VMEM_SPEC] * 2,
        out_specs=[VMEM_SPEC] * 2,
        out_shape=[jax.ShapeDtypeStruct((rank, 2 * half), F32), jax.ShapeDtypeStruct((8, LANES), F32)],
        compiler_params=parameters(LIMIT),
        cost_estimate=SHORT,
        name="whole_v",
    )(place, own, other)


def next_w_kernel(n_sums, *refs):
    gram_ref, _, w_ref = refs[n_sums:]
    patients, rank = w_ref.shape
    sums = total(refs[:n_sums])
    table = jnp.concatenate([sums[:, rank:] * gram_ref[...], sums.T[:rank]], axis=1)
    w_ref[...] = eliminate(table, rank).T[rank : rank + patients]


def next_w(sums, h_gram, patients, after):
    rank = h_gram.shape[0]
    return pl.pallas_call(
        functools.partial(next_w_kernel, len(sums)),
        in_specs=[VMEM_SPEC] * (len(sums) + 1) + [ANY_SPEC],
        out_specs=VMEM_SPEC,
        out_shape=jax.ShapeDtypeStruct((patients, rank), F32),
        compiler_params=parameters(LIMIT),
        cost_estimate=SHORT,
        name="next_w",
    )(*sums, h_gram, after)


def swap(x, axis, slot):
    pairs = [(i, i ^ slot) for i in range(lax.axis_size(axis))]
    return lax.ppermute(x, axis, pairs)


def all_terms(x, axis):
    n = lax.axis_size(axis)
    if n > 4:
        return [lax.psum(x, axis)]
    return [x] + [swap(x, axis, s) for s in range(1, n)]


def staged_terms(x, axis, after):
    n = lax.axis_size(axis)
    steps = [1 << i for i in range(n.bit_length() - 1)]
    for step in steps[:-1]:
        x = add(x, swap(x, axis, step), after)
    return [x, swap(x, axis, steps[-1])]


def add_kernel(a_ref, b_ref, *refs):
    refs[-1][...] = a_ref[...] + b_ref[...]


def add(a, b, after):
    return pl.pallas_call(
        add_kernel,
        in_specs=[VMEM_SPEC] * 2 + [ANY_SPEC] * len(after),
        out_specs=VMEM_SPEC,
        out_shape=jax.ShapeDtypeStruct(a.shape, a.dtype),
        compiler_params=parameters(LIMIT),
        cost_estimate=SHORT,
        name="add_terms",
    )(a, b, *after)


def patient_halves(keep, send, after):
    own = add(keep, swap(send, "patient", 1), [])
    step = 2
    while step < lax.axis_size("patient"):
        own = add(own, swap(own, "patient", step), [after])
        step *= 2
    return own, swap(own, "patient", 1)


def on_device(visits, visit_counts, h_start, v_start, w_start):
    n = lax.axis_size("feature")
    patients, slots, width = visits.shape
    share = patients // n
    place = (2 * lax.axis_index("feature") + (lax.axis_index("patient") & 1)).astype(jnp.int32).reshape(1)
    by_owner = visits.reshape(n, share, slots, width)
    in_hbm = pltpu.with_memory_space_constraint(by_owner, pltpu.HBM)
    v_rows = pltpu.with_memory_space_constraint(v_start.T, pltpu.HBM)

    n_parts = 2 if share % 2 == 0 else 1
    count = share // n_parts
    firsts = [part * count for part in range(n_parts)]
    bits = [1 << i for i in range(n.bit_length() - 1)]
    v_near = v_start.T

    def send(bit):
        return [slot for slot in range(n) if slot & bit and not slot & (bit - 1)]

    def receive(bit):
        return [slot ^ bit for slot in send(bit)]

    w_gram, spread = spread_w(place, w_start, n)
    w_grams = staged_terms(w_gram, "patient", [])
    arrived = [[] for _ in firsts]
    for i, bit in enumerate(bits):
        layouts = [receive(before) for before in bits[:i]]
        for part, first in enumerate(firsts):
            if i == 0 and part == 0:
                code = first_projection(send(bit), count, n_parts == 1, place, in_hbm, v_rows)
            else:
                after = [w_grams[part]] + [v_gram] * part if i else []
                code = next_projection(
                    send(bit), first, count, part == n_parts - 1, layouts, place, by_owner, v_near, arrived[part], after
                )
            arrived[part] = arrived[part] + [swap(code, "feature", bit)]
        if i == 0:
            own, v_gram = project_own(n_parts, receive(bit), place, by_owner, v_near, arrived[0][0])

    layouts = [receive(bit) for bit in bits]
    frames = [[] for _ in firsts]
    joined = []

    def double(part, after):
        for bit in bits[::-1]:
            slots = tuple(slot ^ bit for group, _ in frames[part] for slot in group)
            joined = join([x for _, x in frames[part]], after)
            frames[part].append((slots, swap(joined, "feature", bit)))
        return [joined]

    def project_groups(groups, after):
        arrays = {(frames[part][k][0], firsts[part]): frames[part][k][1] for part, k in groups}
        return project_frames(list(arrays), place, arrays, by_owner, after)

    h_local = v_gram
    for part, first in enumerate(firsts):
        low, h_local, v_total = own_frames(
            layouts[part == 0 :],
            part,
            n_parts,
            place,
            visit_counts,
            h_start,
            w_start,
            v_gram,
            h_local,
            own[part],
            arrived[part][part == 0 :],
        )
        v_gram = v_total
        frames[part].append(((0,), low))

    last = len(bits)
    for part in range(n_parts - 1):
        joined = double(part, [frames[-1][0][1]])
    first_groups = [(part, 0) for part in range(n_parts)] + [(part, 1) for part in range(n_parts - 1)]
    early = [(part, k) for part in range(n_parts - 1) for k in range(2, last + 1)]
    projected, token = project_groups(first_groups, joined)
    h_sums = staged_terms(h_local, "patient", [token])
    w_gram, inverse = first_inverse(v_gram, w_grams, h_sums[0])
    h_sum = add(*h_sums, [inverse])
    joined = double(n_parts - 1, [h_sum] + [frames[part][k][1] for part, k in early])
    h_terms = all_terms(h_sum, "feature")
    after = joined
    for groups in [early] + [[(n_parts - 1, k)] for k in range(1, last + 1)]:
        if groups:
            more, token = project_groups(groups, after)
            projected |= more
            after = [token]
    h_result, h_next, factor = next_h(h_terms, inverse, spread, token)

    items = list(projected)
    flat = [x for item in items for x in projected[item]]
    send = half_v_terms(items, True, place, factor, flat, [])
    keep = half_v_terms(items, False, place, factor, flat, [send])
    h_gram, second = second_inverse(h_next, w_gram)
    own_terms, other_terms = patient_halves(keep, send, second)
    v_own, before = half_v(items, share, place, own_terms, second, h_next, flat, [])
    v_other, sums = half_v(items, share, place, other_terms, second, h_next, flat, [before])
    v_next, token = whole_v(place, v_own, v_other)
    w_next = next_w(all_terms(sums, "feature"), h_gram, patients, token)
    return (h_result, v_next.T, w_next)


def solution(mesh):
    return jax.shard_map(
        on_device,
        mesh=mesh,
        in_specs=(
            P(("groups", "patient"), None, "feature"),
            P(("groups", "patient")),
            P(),
            P("feature", None),
            P(("groups", "patient"), None),
        ),
        out_specs=(P(None, "groups"), P("feature", "groups"), P("patient", "groups")),
        check_vma=False,
    )
```

```python
import functools

import jax
import jax.numpy as jnp
from jax import lax
from jax.experimental import pallas as pl
from jax.experimental.pallas import tpu as pltpu
from jax.sharding import PartitionSpec as P

NS_STEPS = 12
LANES = 128
LEVELS = 32000.0
COARSE_STEPS = 3
SHORT = pl.CostEstimate(flops=1000, bytes_accessed=1000, transcendentals=0)

epsilon = 1e-06
HIGH = lax.Precision.HIGHEST
F32 = jnp.float32
BF16 = jnp.bfloat16
MIB = 1024 * 1024

ROWS_BY_COLS = (((1,), (0,)), ((), ()))
ROWS_BY_ROWS = (((1,), (1,)), ((), ()))
COLS_BY_COLS = (((0,), (0,)), ((), ()))


def low_dot(a, b, dims=ROWS_BY_COLS):
    return lax.dot_general(a, b, dims, preferred_element_type=F32)


def high_dot(a, b, dims=ROWS_BY_COLS):
    return lax.dot_general(a, b, dims, precision=HIGH, preferred_element_type=F32)


def two_parts(x):
    first = x.astype(BF16)
    return first, (x - first.astype(F32)).astype(BF16)


def three_parts(x):
    first = x.astype(BF16)
    rest = x - first.astype(F32)
    second = rest.astype(BF16)
    return first, second, (rest - second.astype(F32)).astype(BF16)


def feature_of(place):
    return place[0] >> 1


def core_of(place):
    return place[0] & 1


def lane_numbers(shape):
    return lax.broadcasted_iota(jnp.int32, shape, len(shape) - 1)


ANY_SPEC = pl.BlockSpec(memory_space=pl.ANY)
HBM_SPEC = pl.BlockSpec(memory_space=pltpu.HBM)


def parameters(mib):
    return pltpu.CompilerParams(vmem_limit_bytes=mib * MIB)


LIMIT = 8
VMEM_SPEC = pl.BlockSpec(memory_space=pltpu.VMEM)
SMEM_SPEC = pl.BlockSpec(memory_space=pltpu.SMEM)


def exponent_rows(total_count):
    return -(-(total_count + 1) // 16) * 16


def payload_shape(total_count, rank, slots, with_gram):
    return (total_count * rank + (rank // 2 if with_gram else 0) + exponent_rows(total_count), slots)


def row_exponent(x):
    top = jnp.max(jnp.abs(x), axis=1, keepdims=True)
    return jnp.ceil(jnp.log2(jnp.maximum(top, 1e-30)))


class Payload:
    def __init__(self, ref, slots, count, rank, with_gram):
        self.ref, self.slots, self.count, self.rank, self.with_gram = ref, slots, count, rank, with_gram
        self.entries = len(slots) * count
        gram_rows = rank // 2 if with_gram else 0
        exponents = self.rows(self.entries * rank + gram_rows, exponent_rows(self.entries))
        self.steps = jnp.exp2(exponents[:, :LANES].T[:rank]) * (1.0 / LEVELS)

    def rows(self, first, number):
        return self.ref[pl.ds(first, number), :].astype(jnp.int32).astype(F32)

    def proj(self, slot, p):
        entry = self.slots.index(slot) * self.count + p
        return self.rows(entry * self.rank, self.rank) * self.steps[:, entry : entry + 1]

    def gram(self):
        rank = self.rank
        digits = self.rows(self.entries * rank, rank // 2)
        digits = jnp.concatenate([digits[:, : 2 * rank], digits[:, 2 * rank :]], axis=0)
        return (digits[:, :rank] + digits[:, rank:] * (0.5 / LEVELS)) * self.steps[:, self.entries : self.entries + 1]


def encode(values, gram, coded_ref, rank):
    count = len(values)
    lanes = lane_numbers((rank, LANES))
    exponents = jnp.zeros((rank, LANES), F32)
    for p, value in enumerate(values):
        proj = value()
        exponent = row_exponent(proj)
        coded = jnp.floor(proj * (LEVELS / jnp.exp2(exponent)) + 0.5)
        coded_ref[pl.ds(p * rank, rank), :] = coded.astype(jnp.int32).astype(jnp.int16)
        exponents = jnp.where(lanes == p, exponent, exponents)
    end = count * rank
    if gram is not None:
        exponent = row_exponent(gram)
        scaled = gram * (LEVELS / jnp.exp2(exponent))
        whole = jnp.floor(scaled + 0.5)
        rest = jnp.floor((scaled - whole) * (2 * LEVELS) + 0.5)
        digits = jnp.concatenate([whole, rest], axis=1)
        digits = jnp.concatenate([digits[: rank // 2], digits[rank // 2 :]], axis=1)
        coded_ref[pl.ds(end, rank // 2), :] = digits.astype(jnp.int32).astype(jnp.int16)
        exponents = jnp.where(lanes == count, exponent, exponents)
        end += rank // 2
    rows = exponent_rows(count)
    last = jnp.concatenate([exponents.T[:rows], jnp.zeros((rows, coded_ref.shape[1] - rank), F32)], axis=1)
    coded_ref[pl.ds(end, rows), :] = last.astype(jnp.int32).astype(jnp.int16)


def first_projection_kernel(slots, place, v_hbm, visits_ref, coded_ref, v_ref, buffers, sems, v_sem):
    count = buffers.shape[1]
    v_copy = pltpu.make_async_copy(v_hbm, v_ref, v_sem)
    v_copy.start()
    pieces = sems.shape[1]
    piece = count // pieces
    copies = []
    for i, slot in enumerate(slots):
        for j in range(pieces):
            rows = pl.ds(j * piece, piece)
            source = visits_ref.at[feature_of(place) ^ slot, rows]
            copies.append(pltpu.make_async_copy(source, buffers.at[i, rows], sems.at[i, j]))
            copies[-1].start()
    v_copy.wait()

    def value(i, p):
        if p % piece == 0:
            copies[i * pieces + p // piece].wait()
        return low_dot(v_ref[...], buffers[i, p], ROWS_BY_ROWS)

    values = [functools.partial(value, i, p) for i in range(len(slots)) for p in range(count)]
    gram = low_dot(v_ref[...], v_ref[...], ROWS_BY_ROWS)
    encode(values, gram, coded_ref, v_ref.shape[0])


def first_projection(slots, count, place, visits, v_rows):
    width = visits.shape[3]
    rank = v_rows.shape[0]
    return pl.pallas_call(
        functools.partial(first_projection_kernel, slots),
        in_specs=[SMEM_SPEC, HBM_SPEC, HBM_SPEC],
        out_specs=VMEM_SPEC,
        out_shape=jax.ShapeDtypeStruct(payload_shape(len(slots) * count, rank, visits.shape[2], True), jnp.int16),
        scratch_shapes=[
            pltpu.VMEM(v_rows.shape, BF16),
            pltpu.VMEM((len(slots), count) + visits.shape[2:], BF16),
            pltpu.SemaphoreType.DMA((len(slots), 1)),
            pltpu.SemaphoreType.DMA,
        ],
        compiler_params=parameters(LIMIT),
        cost_estimate=SHORT,
        name="project_first",
    )(place, v_rows, visits)


def next_projection_kernel(slots, first, count, with_gram, layouts, place, v_ref, visits_ref, *refs):
    coded_ref = refs[-1]
    rank = v_ref.shape[0]
    arrived = [Payload(ref, layout, count, rank, carried) for ref, (layout, carried) in zip(refs, layouts)]

    def value(slot, p):
        proj = low_dot(v_ref[...], visits_ref[feature_of(place) ^ slot, first + p], ROWS_BY_ROWS)
        for payload in arrived:
            proj = proj + payload.proj(slot, p)
        return proj

    gram = None
    if with_gram:
        gram = low_dot(v_ref[...], v_ref[...], ROWS_BY_ROWS)
        for payload in arrived:
            gram = gram + payload.gram()
    encode([functools.partial(value, slot, p) for slot in slots for p in range(count)], gram, coded_ref, rank)


def next_projection(slots, first, count, with_gram, layouts, place, visits, v_rows, arrived, after):
    rank = v_rows.shape[0]
    return pl.pallas_call(
        functools.partial(next_projection_kernel, slots, first, count, with_gram, layouts),
        in_specs=[SMEM_SPEC] + [VMEM_SPEC] * (2 + len(arrived)) + [ANY_SPEC] * len(after),
        out_specs=VMEM_SPEC,
        out_shape=jax.ShapeDtypeStruct(payload_shape(len(slots) * count, rank, visits.shape[2], with_gram), jnp.int16),
        compiler_params=parameters(LIMIT),
        cost_estimate=SHORT,
        name="project_next",
    )(place, v_rows, visits, *arrived, *after)


def spread_w_kernel(n_slots, place, w_ref, gram_ref, spread_ref):
    gram_ref[...] = high_dot(w_ref[...], w_ref[...], COLS_BY_COLS)
    patients, rank = w_ref.shape
    share = patients // n_slots
    w_rows = jnp.concatenate([w_ref[...], jnp.zeros((LANES - patients, rank), F32)], axis=0)
    w_columns = w_rows.T
    for slot in range(n_slots):
        first = (feature_of(place) ^ slot) * share
        columns = pltpu.roll(w_columns, jnp.where(first == 0, 0, LANES - first), 1)
        spread = [jnp.broadcast_to(columns[:, p : p + 1], (rank, rank)) for p in range(share)]
        spread_ref[slot] = jnp.concatenate(spread, axis=1)


def spread_w(place, w_start, n_slots):
    patients, rank = w_start.shape
    return pl.pallas_call(
        functools.partial(spread_w_kernel, n_slots),
        in_specs=[SMEM_SPEC, VMEM_SPEC],
        out_specs=[VMEM_SPEC] * 2,
        out_shape=[
            jax.ShapeDtypeStruct((rank, rank), F32),
            jax.ShapeDtypeStruct((n_slots, rank, patients // n_slots * rank), F32),
        ],
        compiler_params=parameters(LIMIT),
        cost_estimate=SHORT,
        name="spread_w",
    )(place, w_start)


def own_projection_kernel(layout, place, v_ref, visits_ref, arrived_ref, *refs):
    *proj_refs, v_gram_ref = refs
    count, rank, _ = proj_refs[0].shape
    payload = Payload(arrived_ref, layout, count, rank, True)
    for p in range(visits_ref.shape[1]):
        proj = low_dot(v_ref[...], visits_ref[feature_of(place), p], ROWS_BY_ROWS)
        proj_refs[p // count][p % count] = proj + payload.proj(0, p) if p < count else proj
    v_gram_ref[...] = low_dot(v_ref[...], v_ref[...], ROWS_BY_ROWS) + payload.gram()


def project_own(n_parts, layout, place, visits, v_rows, arrived):
    _, share, slots, width = visits.shape
    rank = v_rows.shape[0]
    proj = jax.ShapeDtypeStruct((share // n_parts, rank, slots), F32)
    *own, v_gram = pl.pallas_call(
        functools.partial(own_projection_kernel, layout),
        in_specs=[SMEM_SPEC] + [VMEM_SPEC] * 3,
        out_specs=[VMEM_SPEC] * (n_parts + 1),
        out_shape=[proj] * n_parts + [jax.ShapeDtypeStruct((rank, rank), F32)],
        compiler_params=parameters(LIMIT),
        cost_estimate=SHORT,
        name="project_own",
    )(place, v_rows, visits, arrived)
    return own, v_gram


def solve_tile(columns, tile):
    rows = lax.broadcasted_iota(jnp.int32, tile.shape, 0)
    for a in range(0, 8, 2):
        b = a + 1
        first, second = columns[a], columns[b]
        m_aa, m_ab, m_ba, m_bb = first[a:b], second[a:b], first[b : b + 1], second[b : b + 1]
        scale = 1.0 / (m_aa * m_bb - m_ab * m_ba)
        m_aa, m_ab, m_ba, m_bb = m_aa * scale, m_ab * scale, m_ba * scale, m_bb * scale

        def step(x):
            x_a, x_b = x[a:b], x[b : b + 1]
            new_a, new_b = m_bb * x_a - m_ab * x_b, m_aa * x_b - m_ba * x_a
            x = x - (first * new_a + second * new_b)
            return jnp.where(rows == a, new_a, jnp.where(rows == b, new_b, x))

        tile = step(tile)
        columns = [step(x) if q > b else x for q, x in enumerate(columns)]
    return tile


def eliminate(table, rank):
    tiles = [table[8 * t : 8 * t + 8] for t in range(rank // 8)]
    for home in range(rank // 8):
        first = 8 * home
        columns = [[jnp.broadcast_to(t[:, q : q + 1], t.shape) for q in range(first, first + 8)] for t in tiles]
        solved = solve_tile(columns[home], tiles[home])
        for t, tile in enumerate(tiles):
            terms = [column * solved[q : q + 1] for q, column in enumerate(columns[t])]
            while len(terms) > 1:
                terms = [x + y for x, y in zip(terms[::2], terms[1::2])]
            tiles[t] = solved if t == home else tile - terms[0]
    return jnp.concatenate(tiles, axis=0)


def inverse_of(gram):
    rank = gram.shape[0]
    eye = (lax.broadcasted_iota(jnp.int32, gram.shape, 0) == lane_numbers(gram.shape)).astype(F32)
    return eliminate(jnp.concatenate([gram, eye], axis=1), rank)[:, rank:]


def total(refs):
    out = refs[0][...]
    for ref in refs[1:]:
        out = out + ref[...]
    return out


def first_inverse_kernel(v_gram_ref, *refs):
    *terms, _, w_gram_ref, inverse_ref = refs
    w_gram = total(terms)
    w_gram_ref[...] = w_gram
    inverse_ref[...] = inverse_of(w_gram * v_gram_ref[...])


def first_inverse(v_gram, w_grams, after):
    out = jax.ShapeDtypeStruct(v_gram.shape, F32)
    return pl.pallas_call(
        first_inverse_kernel,
        in_specs=[VMEM_SPEC] * (1 + len(w_grams)) + [ANY_SPEC],
        out_specs=[VMEM_SPEC] * 2,
        out_shape=[out, out],
        compiler_params=parameters(LIMIT),
        cost_estimate=SHORT,
        name="first_inverse",
    )(v_gram, *w_grams, after)


def sweep_all(frames, rank, fine):
    patients = range(frames.shape[0])
    if fine:
        both = [jnp.concatenate(two_parts(frames[p]), axis=0) for p in patients]
        blocks = [low_dot(x, x, ROWS_BY_ROWS) for x in both]
        blocks = [x[:rank] + x[rank:] for x in blocks]
        grams = [x + pltpu.roll(x, rank, 1) for x in blocks]
        moved = [low_dot(jnp.concatenate(two_parts(g), axis=0), x) for g, x in zip(grams, both)]
        moved = [x[:rank] + x[rank:] for x in moved]
    else:
        first = [frames[p].astype(BF16) for p in patients]
        grams = [low_dot(x, x, ROWS_BY_ROWS).astype(BF16) for x in first]
        moved = [low_dot(g, x) for g, x in zip(grams, first)]
    for p in patients:
        frames[p] = 1.5 * frames[p] - 0.5 * moved[p]


def frames_kernel(layouts, part, share, place, counts_ref, h_ref, w_ref, v_gram_ref, before_ref, own_ref, *refs):
    coded, refs = refs[: len(layouts)], refs[len(layouts) :]
    frames_ref, terms_ref, v_total_ref, proj, frames = refs
    count, rank, slots = frames.shape
    patients = range(count)
    first = feature_of(place) * share + part * count
    pieces = [own_ref[p] for p in patients]
    v_gram = v_gram_ref[...]
    for code, (layout, carried) in zip(coded, layouts):
        payload = Payload(code, layout, count, rank, carried)
        pieces = [pieces[p] + payload.proj(0, p) for p in patients]
        if payload.with_gram:
            v_gram = v_gram + payload.gram()
    v_total_ref[...] = v_gram
    for p in patients:
        proj[p] = pieces[p]
    weights = [w_ref[pl.ds(first + p, 1), :] for p in patients]
    mixed = [high_dot(h_ref[...] * weights[p], pieces[p]) for p in patients]
    lanes = lane_numbers((rank, slots))
    mixed = [jnp.where(lanes < counts_ref[first + p], mixed[p], 0.0) for p in patients]
    energy = [jnp.sum(jnp.sum(x * x, axis=1, keepdims=True), axis=0, keepdims=True) for x in mixed]
    for p in patients:
        frames[p] = mixed[p] * lax.rsqrt(energy[p] + epsilon)

    def sweep(fine, step, carry):
        sweep_all(frames, rank, fine)
        return carry

    lax.fori_loop(0, COARSE_STEPS, functools.partial(sweep, False), 0, unroll=True)
    lax.fori_loop(COARSE_STEPS, NS_STEPS, functools.partial(sweep, True), 0, unroll=True)
    low = [frames[p].astype(BF16) for p in patients]
    for p in patients:
        frames_ref[p] = low[p]
    products = [jnp.concatenate(three_parts(proj[p]), axis=0) for p in patients]
    products = [low_dot(low[p], products[p], ROWS_BY_ROWS) for p in patients]
    terms = before_ref[...] if part else jnp.zeros((rank, rank), F32)
    for p in patients:
        product = products[p][:, :rank] + (products[p][:, rank : 2 * rank] + products[p][:, 2 * rank :])
        terms = terms + product * weights[p]
    terms_ref[...] = terms


def own_frames(layouts, part, n_parts, place, counts, h_start, w_start, v_gram, before, own, coded):
    count, rank, slots = own.shape
    share = count * n_parts
    return pl.pallas_call(
        functools.partial(frames_kernel, layouts, part, share),
        in_specs=[SMEM_SPEC] * 2 + [VMEM_SPEC] * (5 + len(coded)),
        out_specs=[VMEM_SPEC] * 3,
        out_shape=[
            jax.ShapeDtypeStruct(own.shape, BF16),
            jax.ShapeDtypeStruct((rank, rank), F32),
            jax.ShapeDtypeStruct((rank, rank), F32),
        ],
        scratch_shapes=[pltpu.VMEM(own.shape, F32)] * 2,
        compiler_params=parameters(LIMIT),
        cost_estimate=SHORT,
        name="own_frames",
    )(place, counts, h_start, w_start, v_gram, before, own, *coded)


def projected_kernel(items, place, visits_ref, *refs):
    frames_refs, outs, token_ref = refs[: len(items)], refs[-2 * len(items) - 1 : -1], refs[-1]
    token_ref[...] = jnp.zeros_like(token_ref)
    for i, (slots, first) in enumerate(items):
        total_count, rank, _ = frames_refs[i].shape
        count = total_count // len(slots)
        for p in range(total_count):
            rows = pl.ds(p * rank, rank)
            owner = feature_of(place) ^ slots[p // count]
            product = low_dot(frames_refs[i][p], visits_ref[owner, first + p % count])
            outs[2 * i][rows, :], outs[2 * i + 1][rows, :] = two_parts(product)


def join_kernel(count, *refs):
    out_ref = refs[-1]
    first = 0
    for part in refs[:count]:
        out_ref[first : first + part.shape[0]] = part[...]
        first += part.shape[0]


def join(parts, after):
    if len(parts) == 1:
        return parts[0]
    return pl.pallas_call(
        functools.partial(join_kernel, len(parts)),
        in_specs=[VMEM_SPEC] * len(parts) + [ANY_SPEC] * len(after),
        out_specs=VMEM_SPEC,
        out_shape=jax.ShapeDtypeStruct((sum(x.shape[0] for x in parts),) + parts[0].shape[1:], parts[0].dtype),
        compiler_params=parameters(LIMIT),
        cost_estimate=SHORT,
        name="join_frames",
    )(*parts, *after)


def project_frames(items, place, frames, visits, after):
    width = visits.shape[-1]
    outs = []
    for item in items:
        count, rank, _ = frames[item].shape
        outs += [jax.ShapeDtypeStruct((count * rank, width), BF16)] * 2
    *parts, token = pl.pallas_call(
        functools.partial(projected_kernel, items),
        in_specs=[SMEM_SPEC] + [VMEM_SPEC] * (1 + len(items)) + [ANY_SPEC] * len(after),
        out_specs=[VMEM_SPEC] * (len(outs) + 1),
        out_shape=outs + [jax.ShapeDtypeStruct((8, LANES), F32)],
        compiler_params=parameters(LIMIT),
        cost_estimate=SHORT,
        name="project_frames",
    )(place, visits, *[frames[item] for item in items], *after)
    return {item: parts[2 * i : 2 * i + 2] for i, item in enumerate(items)}, token


def next_h_kernel(n_terms, *refs):
    inverse_ref, spread_ref, _, result_ref, h_ref, factor_ref = refs[n_terms:]
    h_next = high_dot(total(refs[:n_terms]), inverse_ref[...])
    result_ref[...] = h_next
    h_ref[...] = h_next
    rank = h_next.shape[0]
    h_rows = h_next.T
    h_rows = jnp.concatenate([h_rows] * (spread_ref.shape[2] // rank), axis=1)
    for slot in range(spread_ref.shape[0]):
        factor_ref[slot] = jnp.concatenate(three_parts(h_rows * spread_ref[slot]), axis=0)


def next_h(terms, inverse, spread, after):
    n_slots, rank, columns = spread.shape
    return pl.pallas_call(
        functools.partial(next_h_kernel, len(terms)),
        in_specs=[VMEM_SPEC] * (len(terms) + 2) + [ANY_SPEC],
        out_specs=[VMEM_SPEC] * 3,
        out_shape=[
            jax.ShapeDtypeStruct(inverse.shape, F32),
            jax.ShapeDtypeStruct(inverse.shape, F32),
            jax.ShapeDtypeStruct((n_slots, 3 * rank, columns), BF16),
        ],
        compiler_params=parameters(LIMIT),
        cost_estimate=SHORT,
        name="next_h",
    )(*terms, inverse, spread, after)


def second_inverse_kernel(h_ref, w_gram_ref, gram_ref, inverse_ref):
    gram = high_dot(h_ref[...], h_ref[...], COLS_BY_COLS)
    gram_ref[...] = gram
    inverse_ref[...] = inverse_of(gram * w_gram_ref[...])


def second_inverse(h_next, w_gram):
    out = jax.ShapeDtypeStruct(w_gram.shape, F32)
    return pl.pallas_call(
        second_inverse_kernel,
        out_shape=[out, out],
        compiler_params=parameters(LIMIT),
        cost_estimate=SHORT,
        name="second_inverse",
    )(h_next, w_gram)


def v_terms_kernel(items, sent, place, factor_ref, *refs):
    parts, terms_ref = refs[: 2 * len(items)], refs[-1]
    rank, half = terms_ref.shape
    upper = core_of(place) ^ 1 if sent else core_of(place)
    features = pl.ds(pl.multiple_of(upper * half, half), half)
    total = None
    for i, (slots, first) in enumerate(items):
        count = parts[2 * i].shape[0] // len(slots)
        columns = pl.ds(first * rank, count)
        for k, slot in enumerate(slots):
            rows = pl.ds(k * count, count)
            large = low_dot(factor_ref[slot, :, columns], parts[2 * i][rows, features])
            small = low_dot(factor_ref[slot, : 2 * rank, columns], parts[2 * i + 1][rows, features])
            terms = large[:rank] + (large[rank : 2 * rank] + small[:rank]) + (large[2 * rank :] + small[rank:])
            total = terms if total is None else total + terms
    terms_ref[...] = total


def half_v_terms(items, sent, place, factor, projected, after):
    width = projected[0].shape[1]
    rank = factor.shape[1] // 3
    return pl.pallas_call(
        functools.partial(v_terms_kernel, items, sent),
        in_specs=[SMEM_SPEC] + [VMEM_SPEC] * (1 + len(projected)) + [ANY_SPEC] * len(after),
        out_specs=VMEM_SPEC,
        out_shape=jax.ShapeDtypeStruct((rank, width // 2), F32),
        compiler_params=parameters(LIMIT),
        cost_estimate=SHORT,
        name="v_terms",
    )(place, factor, *projected, *after)


def next_v_kernel(items, share, later, place, terms_ref, inverse_ref, h_ref, *refs):
    parts, refs = refs[: 2 * len(items)], refs[2 * len(items) :]
    rank, half = terms_ref.shape
    here = pl.multiple_of((core_of(place) ^ 1 if later else core_of(place)) * half, half)
    features = pl.ds(here, half)
    v_rows = high_dot(inverse_ref[...], terms_ref[...])
    *before, v_ref, sums_ref, v_parts = refs
    v_ref[...] = v_rows
    sums = before[0][...] if later else jnp.zeros((rank, 2 * rank), F32)
    v_parts[...] = jnp.concatenate(two_parts(v_rows), axis=0)
    weights = jnp.concatenate([h_ref[...]] * 2, axis=1)
    gram = low_dot(v_parts[...], v_parts[...], ROWS_BY_ROWS)
    gram = gram[:rank, :rank] + (gram[:rank, rank:] + gram[rank:, :rank])
    sums_ref[...] = sums + jnp.concatenate([jnp.zeros((rank, rank), F32), gram], axis=1)
    for i, (slots, done) in enumerate(items):
        seen = low_dot(parts[2 * i][:, features], v_parts[...], ROWS_BY_ROWS)
        seen = seen + low_dot(parts[2 * i + 1][:, features], v_parts[...], ROWS_BY_ROWS)
        count = seen.shape[0] // rank // len(slots)
        for p in range(seen.shape[0] // rank):
            patient = (feature_of(place) ^ slots[p // count]) * share + done + p % count
            row = jnp.sum(seen[p * rank : (p + 1) * rank] * weights, axis=0, keepdims=True)
            sums_ref[pl.ds(patient, 1), :rank] += row[:, :rank] + row[:, rank:]


def half_v(items, share, place, terms, inverse, h_next, projected, before):
    rank, half = terms.shape
    return pl.pallas_call(
        functools.partial(next_v_kernel, items, share, bool(before)),
        in_specs=[SMEM_SPEC] + [VMEM_SPEC] * (3 + len(projected) + len(before)),
        out_specs=[VMEM_SPEC] * 2,
        out_shape=[
            jax.ShapeDtypeStruct((rank, half), F32),
            jax.ShapeDtypeStruct((rank, 2 * rank), F32),
        ],
        scratch_shapes=[pltpu.VMEM((2 * rank, half), BF16)],
        compiler_params=parameters(LIMIT),
        cost_estimate=SHORT,
        name="next_v",
    )(place, terms, inverse, h_next, *projected, *before)


def whole_v_kernel(place, own_ref, other_ref, v_ref, token_ref):
    half = own_ref.shape[1]
    upper = core_of(place) == 1
    v_ref[:, :half] = jnp.where(upper, other_ref[...], own_ref[...])
    v_ref[:, half:] = jnp.where(upper, own_ref[...], other_ref[...])
    token_ref[...] = jnp.zeros_like(token_ref)


def whole_v(place, own, other):
    rank, half = own.shape
    return pl.pallas_call(
        whole_v_kernel,
        in_specs=[SMEM_SPEC] + [VMEM_SPEC] * 2,
        out_specs=[VMEM_SPEC] * 2,
        out_shape=[jax.ShapeDtypeStruct((rank, 2 * half), F32), jax.ShapeDtypeStruct((8, LANES), F32)],
        compiler_params=parameters(LIMIT),
        cost_estimate=SHORT,
        name="whole_v",
    )(place, own, other)


def next_w_kernel(n_sums, *refs):
    gram_ref, _, w_ref = refs[n_sums:]
    patients, rank = w_ref.shape
    sums = total(refs[:n_sums])
    table = jnp.concatenate([sums[:, rank:] * gram_ref[...], sums.T[:rank]], axis=1)
    w_ref[...] = eliminate(table, rank).T[rank : rank + patients]


def next_w(sums, h_gram, patients, after):
    rank = h_gram.shape[0]
    return pl.pallas_call(
        functools.partial(next_w_kernel, len(sums)),
        in_specs=[VMEM_SPEC] * (len(sums) + 1) + [ANY_SPEC],
        out_specs=VMEM_SPEC,
        out_shape=jax.ShapeDtypeStruct((patients, rank), F32),
        compiler_params=parameters(LIMIT),
        cost_estimate=SHORT,
        name="next_w",
    )(*sums, h_gram, after)


def swap(x, axis, slot):
    pairs = [(i, i ^ slot) for i in range(lax.axis_size(axis))]
    return lax.ppermute(x, axis, pairs)


def all_terms(x, axis):
    n = lax.axis_size(axis)
    if n > 4:
        return [lax.psum(x, axis)]
    return [x] + [swap(x, axis, s) for s in range(1, n)]


def staged_terms(x, axis, after):
    n = lax.axis_size(axis)
    steps = [1 << i for i in range(n.bit_length() - 1)]
    for step in steps[:-1]:
        x = add(x, swap(x, axis, step), after)
    return [x, swap(x, axis, steps[-1])]


def add_kernel(a_ref, b_ref, *refs):
    refs[-1][...] = a_ref[...] + b_ref[...]


def add(a, b, after):
    return pl.pallas_call(
        add_kernel,
        in_specs=[VMEM_SPEC] * 2 + [ANY_SPEC] * len(after),
        out_specs=VMEM_SPEC,
        out_shape=jax.ShapeDtypeStruct(a.shape, a.dtype),
        compiler_params=parameters(LIMIT),
        cost_estimate=SHORT,
        name="add_terms",
    )(a, b, *after)


def patient_halves(keep, send, after):
    own = add(keep, swap(send, "patient", 1), [])
    step = 2
    while step < lax.axis_size("patient"):
        own = add(own, swap(own, "patient", step), [after])
        step *= 2
    return own, swap(own, "patient", 1)


def on_device(visits, visit_counts, h_start, v_start, w_start):
    n = lax.axis_size("feature")
    patients, slots, width = visits.shape
    share = patients // n
    place = (2 * lax.axis_index("feature") + (lax.axis_index("patient") & 1)).astype(jnp.int32).reshape(1)
    by_owner = visits.reshape(n, share, slots, width)
    in_hbm = pltpu.with_memory_space_constraint(by_owner, pltpu.HBM)
    v_rows = pltpu.with_memory_space_constraint(v_start.T, pltpu.HBM)

    n_parts = 2 if share % 2 == 0 else 1
    count = share // n_parts
    firsts = [part * count for part in range(n_parts)]
    bits = [1 << i for i in range(n.bit_length() - 1)]
    v_near = v_start.T

    def send(bit):
        return [slot for slot in range(n) if slot & bit and not slot & (bit - 1)]

    def receive(bit):
        return [slot ^ bit for slot in send(bit)]

    w_gram, spread = spread_w(place, w_start, n)
    w_grams = staged_terms(w_gram, "patient", [])
    def layouts(stages, part):
        return [(receive(bit), part == 0) for bit in bits[:stages]]

    arrived = [[] for _ in firsts]
    for i, bit in enumerate(bits):
        for part, first in enumerate(firsts):
            if i == 0 and part == 0:
                code = first_projection(send(bit), count, place, in_hbm, v_rows)
            else:
                after = [w_grams[part]] + [v_gram] * part if i else []
                code = next_projection(
                    send(bit),
                    first,
                    count,
                    part == 0,
                    layouts(i, part),
                    place,
                    by_owner,
                    v_near,
                    arrived[part],
                    after,
                )
            arrived[part] = arrived[part] + [swap(code, "feature", bit)]
        if i == 0:
            own, v_gram = project_own(n_parts, receive(bit), place, by_owner, v_near, arrived[0][0])

    frames = [[] for _ in firsts]
    joined = []

    def double(part, after):
        for bit in bits[::-1]:
            slots = tuple(slot ^ bit for group, _ in frames[part] for slot in group)
            joined = join([x for _, x in frames[part]], after)
            frames[part].append((slots, swap(joined, "feature", bit)))
        return [joined]

    def project_groups(groups, after):
        arrays = {(frames[part][k][0], firsts[part]): frames[part][k][1] for part, k in groups}
        return project_frames(list(arrays), place, arrays, by_owner, after)

    h_local = v_gram
    for part, first in enumerate(firsts):
        low, h_local, v_total = own_frames(
            layouts(len(bits), part)[part == 0 :],
            part,
            n_parts,
            place,
            visit_counts,
            h_start,
            w_start,
            v_gram,
            h_local,
            own[part],
            arrived[part][part == 0 :],
        )
        v_gram = v_total
        frames[part].append(((0,), low))

    last = len(bits)
    for part in range(n_parts - 1):
        joined = double(part, [frames[-1][0][1]])
    first_groups = [(part, 0) for part in range(n_parts)] + [(part, 1) for part in range(n_parts - 1)]
    early = [(part, k) for part in range(n_parts - 1) for k in range(2, last + 1)]
    projected, token = project_groups(first_groups, joined)
    h_sums = staged_terms(h_local, "patient", [token])
    w_gram, inverse = first_inverse(v_gram, w_grams, h_sums[0])
    joined = double(n_parts - 1, [inverse])
    h_sum = add(*h_sums, joined + [frames[part][k][1] for part, k in early])
    h_terms = all_terms(h_sum, "feature")
    after = [h_sum]
    for groups in [early] + [[(n_parts - 1, k)] for k in range(1, last + 1)]:
        if groups:
            more, token = project_groups(groups, after)
            projected |= more
            after = [token]
    h_result, h_next, factor = next_h(h_terms, inverse, spread, token)

    items = list(projected)
    flat = [x for item in items for x in projected[item]]
    send = half_v_terms(items, True, place, factor, flat, [])
    keep = half_v_terms(items, False, place, factor, flat, [send])
    h_gram, second = second_inverse(h_next, w_gram)
    own_terms, other_terms = patient_halves(keep, send, second)
    v_own, before = half_v(items, share, place, own_terms, second, h_next, flat, [])
    v_other, sums = half_v(items, share, place, other_terms, second, h_next, flat, [before])
    v_next, token = whole_v(place, v_own, v_other)
    w_next = next_w(all_terms(sums, "feature"), h_gram, patients, token)
    return (h_result, v_next.T, w_next)


def solution(mesh):
    return jax.shard_map(
        on_device,
        mesh=mesh,
        in_specs=(
            P(("groups", "patient"), None, "feature"),
            P(("groups", "patient")),
            P(),
            P("feature", None),
            P(("groups", "patient"), None),
        ),
        out_specs=(P(None, "groups"), P("feature", "groups"), P("patient", "groups")),
        check_vma=False,
    )
```

```python
import functools

import jax
import jax.numpy as jnp
from jax import lax
from jax.experimental import pallas as pl
from jax.experimental.pallas import tpu as pltpu
from jax.sharding import PartitionSpec as P

NS_STEPS = 12
LANES = 128
LEVELS = 32000.0
COARSE_STEPS = 3
SHORT = pl.CostEstimate(flops=1000, bytes_accessed=1000, transcendentals=0)

epsilon = 1e-06
HIGH = lax.Precision.HIGHEST
F32 = jnp.float32
BF16 = jnp.bfloat16
MIB = 1024 * 1024

ROWS_BY_COLS = (((1,), (0,)), ((), ()))
ROWS_BY_ROWS = (((1,), (1,)), ((), ()))
COLS_BY_COLS = (((0,), (0,)), ((), ()))


def low_dot(a, b, dims=ROWS_BY_COLS):
    return lax.dot_general(a, b, dims, preferred_element_type=F32)


def high_dot(a, b, dims=ROWS_BY_COLS):
    return lax.dot_general(a, b, dims, precision=HIGH, preferred_element_type=F32)


def two_parts(x):
    first = x.astype(BF16)
    return first, (x - first.astype(F32)).astype(BF16)


def three_parts(x):
    first = x.astype(BF16)
    rest = x - first.astype(F32)
    second = rest.astype(BF16)
    return first, second, (rest - second.astype(F32)).astype(BF16)


def feature_of(place):
    return place[0] >> 1


def core_of(place):
    return place[0] & 1


def lane_numbers(shape):
    return lax.broadcasted_iota(jnp.int32, shape, len(shape) - 1)


ANY_SPEC = pl.BlockSpec(memory_space=pl.ANY)
HBM_SPEC = pl.BlockSpec(memory_space=pltpu.HBM)


def parameters(mib):
    return pltpu.CompilerParams(vmem_limit_bytes=mib * MIB)


LIMIT = 8
VMEM_SPEC = pl.BlockSpec(memory_space=pltpu.VMEM)
SMEM_SPEC = pl.BlockSpec(memory_space=pltpu.SMEM)


def exponent_rows(total_count):
    return -(-(total_count + 1) // 16) * 16


def payload_shape(total_count, rank, slots, with_gram):
    return (total_count * rank + (rank // 2 if with_gram else 0) + exponent_rows(total_count), slots)


def row_exponent(x):
    top = jnp.max(jnp.abs(x), axis=1, keepdims=True)
    return jnp.ceil(jnp.log2(jnp.maximum(top, 1e-30)))


class Payload:
    def __init__(self, ref, slots, count, rank, with_gram):
        self.ref, self.slots, self.count, self.rank, self.with_gram = ref, slots, count, rank, with_gram
        self.entries = len(slots) * count
        gram_rows = rank // 2 if with_gram else 0
        exponents = self.rows(self.entries * rank + gram_rows, exponent_rows(self.entries))
        self.steps = jnp.exp2(exponents[:, :LANES].T[:rank]) * (1.0 / LEVELS)

    def rows(self, first, number):
        return self.ref[pl.ds(first, number), :].astype(jnp.int32).astype(F32)

    def proj(self, slot, p):
        entry = self.slots.index(slot) * self.count + p
        return self.rows(entry * self.rank, self.rank) * self.steps[:, entry : entry + 1]

    def gram(self):
        rank = self.rank
        digits = self.rows(self.entries * rank, rank // 2)
        digits = jnp.concatenate([digits[:, : 2 * rank], digits[:, 2 * rank :]], axis=0)
        return (digits[:, :rank] + digits[:, rank:] * (0.5 / LEVELS)) * self.steps[:, self.entries : self.entries + 1]


def encode(values, gram, coded_ref, rank):
    count = len(values)
    lanes = lane_numbers((rank, LANES))
    exponents = jnp.zeros((rank, LANES), F32)
    for p, value in enumerate(values):
        proj = value()
        exponent = row_exponent(proj)
        coded = jnp.floor(proj * (LEVELS / jnp.exp2(exponent)) + 0.5)
        coded_ref[pl.ds(p * rank, rank), :] = coded.astype(jnp.int32).astype(jnp.int16)
        exponents = jnp.where(lanes == p, exponent, exponents)
    end = count * rank
    if gram is not None:
        exponent = row_exponent(gram)
        scaled = gram * (LEVELS / jnp.exp2(exponent))
        whole = jnp.floor(scaled + 0.5)
        rest = jnp.floor((scaled - whole) * (2 * LEVELS) + 0.5)
        digits = jnp.concatenate([whole, rest], axis=1)
        digits = jnp.concatenate([digits[: rank // 2], digits[rank // 2 :]], axis=1)
        coded_ref[pl.ds(end, rank // 2), :] = digits.astype(jnp.int32).astype(jnp.int16)
        exponents = jnp.where(lanes == count, exponent, exponents)
        end += rank // 2
    rows = exponent_rows(count)
    last = jnp.concatenate([exponents.T[:rows], jnp.zeros((rows, coded_ref.shape[1] - rank), F32)], axis=1)
    coded_ref[pl.ds(end, rows), :] = last.astype(jnp.int32).astype(jnp.int16)


def first_projection_kernel(slots, with_gram, place, v_hbm, visits_ref, coded_ref, v_ref, buffers, sems, v_sem):
    count = buffers.shape[1]
    v_copy = pltpu.make_async_copy(v_hbm, v_ref, v_sem)
    v_copy.start()
    pieces = sems.shape[1]
    piece = count // pieces
    copies = []
    for i, slot in enumerate(slots):
        for j in range(pieces):
            rows = pl.ds(j * piece, piece)
            source = visits_ref.at[feature_of(place) ^ slot, rows]
            copies.append(pltpu.make_async_copy(source, buffers.at[i, rows], sems.at[i, j]))
            copies[-1].start()
    v_copy.wait()

    def value(i, p):
        if p % piece == 0:
            copies[i * pieces + p // piece].wait()
        return low_dot(v_ref[...], buffers[i, p], ROWS_BY_ROWS)

    values = [functools.partial(value, i, p) for i in range(len(slots)) for p in range(count)]
    gram = low_dot(v_ref[...], v_ref[...], ROWS_BY_ROWS) if with_gram else None
    encode(values, gram, coded_ref, v_ref.shape[0])


def first_projection(slots, count, with_gram, place, visits, v_rows):
    width = visits.shape[3]
    rank = v_rows.shape[0]
    return pl.pallas_call(
        functools.partial(first_projection_kernel, slots, with_gram),
        in_specs=[SMEM_SPEC, HBM_SPEC, HBM_SPEC],
        out_specs=VMEM_SPEC,
        out_shape=jax.ShapeDtypeStruct(payload_shape(len(slots) * count, rank, visits.shape[2], with_gram), jnp.int16),
        scratch_shapes=[
            pltpu.VMEM(v_rows.shape, BF16),
            pltpu.VMEM((len(slots), count) + visits.shape[2:], BF16),
            pltpu.SemaphoreType.DMA((len(slots), 1)),
            pltpu.SemaphoreType.DMA,
        ],
        compiler_params=parameters(LIMIT),
        cost_estimate=SHORT,
        name="project_first",
    )(place, v_rows, visits)


def next_projection_kernel(slots, first, count, with_gram, layouts, place, v_ref, visits_ref, *refs):
    coded_ref = refs[-1]
    rank = v_ref.shape[0]
    arrived = [Payload(ref, layout, count, rank, with_gram) for ref, layout in zip(refs, layouts)]

    def value(slot, p):
        proj = low_dot(v_ref[...], visits_ref[feature_of(place) ^ slot, first + p], ROWS_BY_ROWS)
        for payload in arrived:
            proj = proj + payload.proj(slot, p)
        return proj

    gram = None
    if with_gram:
        gram = low_dot(v_ref[...], v_ref[...], ROWS_BY_ROWS)
        for payload in arrived:
            gram = gram + payload.gram()
    encode([functools.partial(value, slot, p) for slot in slots for p in range(count)], gram, coded_ref, rank)


def next_projection(slots, first, count, with_gram, layouts, place, visits, v_rows, arrived, after):
    rank = v_rows.shape[0]
    return pl.pallas_call(
        functools.partial(next_projection_kernel, slots, first, count, with_gram, layouts),
        in_specs=[SMEM_SPEC] + [VMEM_SPEC] * (2 + len(arrived)) + [ANY_SPEC] * len(after),
        out_specs=VMEM_SPEC,
        out_shape=jax.ShapeDtypeStruct(payload_shape(len(slots) * count, rank, visits.shape[2], with_gram), jnp.int16),
        compiler_params=parameters(LIMIT),
        cost_estimate=SHORT,
        name="project_next",
    )(place, v_rows, visits, *arrived, *after)


def spread_w_kernel(n_slots, place, w_ref, gram_ref, spread_ref):
    gram_ref[...] = high_dot(w_ref[...], w_ref[...], COLS_BY_COLS)
    patients, rank = w_ref.shape
    share = patients // n_slots
    w_rows = jnp.concatenate([w_ref[...], jnp.zeros((LANES - patients, rank), F32)], axis=0)
    w_columns = w_rows.T
    for slot in range(n_slots):
        first = (feature_of(place) ^ slot) * share
        columns = pltpu.roll(w_columns, jnp.where(first == 0, 0, LANES - first), 1)
        spread = [jnp.broadcast_to(columns[:, p : p + 1], (rank, rank)) for p in range(share)]
        spread_ref[slot] = jnp.concatenate(spread, axis=1)


def spread_w(place, w_start, n_slots):
    patients, rank = w_start.shape
    return pl.pallas_call(
        functools.partial(spread_w_kernel, n_slots),
        in_specs=[SMEM_SPEC, VMEM_SPEC],
        out_specs=[VMEM_SPEC] * 2,
        out_shape=[
            jax.ShapeDtypeStruct((rank, rank), F32),
            jax.ShapeDtypeStruct((n_slots, rank, patients // n_slots * rank), F32),
        ],
        compiler_params=parameters(LIMIT),
        cost_estimate=SHORT,
        name="spread_w",
    )(place, w_start)


def own_projection_kernel(layout, place, v_ref, visits_ref, arrived_ref, *refs):
    *proj_refs, v_gram_ref = refs
    count, rank, _ = proj_refs[0].shape
    payload = Payload(arrived_ref, layout, count, rank, len(proj_refs) == 1)
    for p in range(visits_ref.shape[1]):
        proj = low_dot(v_ref[...], visits_ref[feature_of(place), p], ROWS_BY_ROWS)
        proj_refs[p // count][p % count] = proj + payload.proj(0, p) if p < count else proj
    gram = low_dot(v_ref[...], v_ref[...], ROWS_BY_ROWS)
    v_gram_ref[...] = gram + payload.gram() if payload.with_gram else gram


def project_own(n_parts, layout, place, visits, v_rows, arrived):
    _, share, slots, width = visits.shape
    rank = v_rows.shape[0]
    proj = jax.ShapeDtypeStruct((share // n_parts, rank, slots), F32)
    *own, v_gram = pl.pallas_call(
        functools.partial(own_projection_kernel, layout),
        in_specs=[SMEM_SPEC] + [VMEM_SPEC] * 3,
        out_specs=[VMEM_SPEC] * (n_parts + 1),
        out_shape=[proj] * n_parts + [jax.ShapeDtypeStruct((rank, rank), F32)],
        compiler_params=parameters(LIMIT),
        cost_estimate=SHORT,
        name="project_own",
    )(place, v_rows, visits, arrived)
    return own, v_gram


def solve_tile(columns, tile):
    rows = lax.broadcasted_iota(jnp.int32, tile.shape, 0)
    for a in range(0, 8, 2):
        b = a + 1
        first, second = columns[a], columns[b]
        m_aa, m_ab, m_ba, m_bb = first[a:b], second[a:b], first[b : b + 1], second[b : b + 1]
        scale = 1.0 / (m_aa * m_bb - m_ab * m_ba)
        m_aa, m_ab, m_ba, m_bb = m_aa * scale, m_ab * scale, m_ba * scale, m_bb * scale

        def step(x):
            x_a, x_b = x[a:b], x[b : b + 1]
            new_a, new_b = m_bb * x_a - m_ab * x_b, m_aa * x_b - m_ba * x_a
            x = x - (first * new_a + second * new_b)
            return jnp.where(rows == a, new_a, jnp.where(rows == b, new_b, x))

        tile = step(tile)
        columns = [step(x) if q > b else x for q, x in enumerate(columns)]
    return tile


def eliminate(table, rank):
    tiles = [table[8 * t : 8 * t + 8] for t in range(rank // 8)]
    for home in range(rank // 8):
        first = 8 * home
        columns = [[jnp.broadcast_to(t[:, q : q + 1], t.shape) for q in range(first, first + 8)] for t in tiles]
        solved = solve_tile(columns[home], tiles[home])
        for t, tile in enumerate(tiles):
            terms = [column * solved[q : q + 1] for q, column in enumerate(columns[t])]
            while len(terms) > 1:
                terms = [x + y for x, y in zip(terms[::2], terms[1::2])]
            tiles[t] = solved if t == home else tile - terms[0]
    return jnp.concatenate(tiles, axis=0)


def inverse_of(gram):
    rank = gram.shape[0]
    eye = (lax.broadcasted_iota(jnp.int32, gram.shape, 0) == lane_numbers(gram.shape)).astype(F32)
    return eliminate(jnp.concatenate([gram, eye], axis=1), rank)[:, rank:]


def total(refs):
    out = refs[0][...]
    for ref in refs[1:]:
        out = out + ref[...]
    return out


def first_inverse_kernel(v_gram_ref, *refs):
    *terms, _, w_gram_ref, inverse_ref = refs
    w_gram = total(terms)
    w_gram_ref[...] = w_gram
    inverse_ref[...] = inverse_of(w_gram * v_gram_ref[...])


def first_inverse(v_gram, w_grams, after):
    out = jax.ShapeDtypeStruct(v_gram.shape, F32)
    return pl.pallas_call(
        first_inverse_kernel,
        in_specs=[VMEM_SPEC] * (1 + len(w_grams)) + [ANY_SPEC],
        out_specs=[VMEM_SPEC] * 2,
        out_shape=[out, out],
        compiler_params=parameters(LIMIT),
        cost_estimate=SHORT,
        name="first_inverse",
    )(v_gram, *w_grams, after)


def sweep_all(frames, rank, fine):
    patients = range(frames.shape[0])
    if fine:
        both = [jnp.concatenate(two_parts(frames[p]), axis=0) for p in patients]
        blocks = [low_dot(x, x, ROWS_BY_ROWS) for x in both]
        blocks = [x[:rank] + x[rank:] for x in blocks]
        grams = [x + pltpu.roll(x, rank, 1) for x in blocks]
        moved = [low_dot(jnp.concatenate(two_parts(g), axis=0), x) for g, x in zip(grams, both)]
        moved = [x[:rank] + x[rank:] for x in moved]
    else:
        first = [frames[p].astype(BF16) for p in patients]
        grams = [low_dot(x, x, ROWS_BY_ROWS).astype(BF16) for x in first]
        moved = [low_dot(g, x) for g, x in zip(grams, first)]
    for p in patients:
        frames[p] = 1.5 * frames[p] - 0.5 * moved[p]


def frames_kernel(layouts, part, share, place, counts_ref, h_ref, w_ref, v_gram_ref, before_ref, own_ref, *refs):
    coded, refs = refs[: len(layouts)], refs[len(layouts) :]
    frames_ref, terms_ref, v_total_ref, proj, frames = refs
    count, rank, slots = frames.shape
    patients = range(count)
    first = feature_of(place) * share + part * count
    pieces = [own_ref[p] for p in patients]
    v_gram = v_gram_ref[...]
    for code, layout in zip(coded, layouts):
        payload = Payload(code, layout, count, rank, (part + 1) * count == share)
        pieces = [pieces[p] + payload.proj(0, p) for p in patients]
        if payload.with_gram:
            v_gram = v_gram + payload.gram()
    v_total_ref[...] = v_gram
    for p in patients:
        proj[p] = pieces[p]
    weights = [w_ref[pl.ds(first + p, 1), :] for p in patients]
    mixed = [high_dot(h_ref[...] * weights[p], pieces[p]) for p in patients]
    lanes = lane_numbers((rank, slots))
    mixed = [jnp.where(lanes < counts_ref[first + p], mixed[p], 0.0) for p in patients]
    energy = [jnp.sum(jnp.sum(x * x, axis=1, keepdims=True), axis=0, keepdims=True) for x in mixed]
    for p in patients:
        frames[p] = mixed[p] * lax.rsqrt(energy[p] + epsilon)

    def sweep(fine, step, carry):
        sweep_all(frames, rank, fine)
        return carry

    lax.fori_loop(0, COARSE_STEPS, functools.partial(sweep, False), 0, unroll=True)
    lax.fori_loop(COARSE_STEPS, NS_STEPS, functools.partial(sweep, True), 0, unroll=True)
    low = [frames[p].astype(BF16) for p in patients]
    for p in patients:
        frames_ref[p] = low[p]
    products = [jnp.concatenate(three_parts(proj[p]), axis=0) for p in patients]
    products = [low_dot(low[p], products[p], ROWS_BY_ROWS) for p in patients]
    terms = before_ref[...] if part else jnp.zeros((rank, rank), F32)
    for p in patients:
        product = products[p][:, :rank] + (products[p][:, rank : 2 * rank] + products[p][:, 2 * rank :])
        terms = terms + product * weights[p]
    terms_ref[...] = terms


def own_frames(layouts, part, n_parts, place, counts, h_start, w_start, v_gram, before, own, coded):
    count, rank, slots = own.shape
    share = count * n_parts
    return pl.pallas_call(
        functools.partial(frames_kernel, layouts, part, share),
        in_specs=[SMEM_SPEC] * 2 + [VMEM_SPEC] * (5 + len(coded)),
        out_specs=[VMEM_SPEC] * 3,
        out_shape=[
            jax.ShapeDtypeStruct(own.shape, BF16),
            jax.ShapeDtypeStruct((rank, rank), F32),
            jax.ShapeDtypeStruct((rank, rank), F32),
        ],
        scratch_shapes=[pltpu.VMEM(own.shape, F32)] * 2,
        compiler_params=parameters(LIMIT),
        cost_estimate=SHORT,
        name="own_frames",
    )(place, counts, h_start, w_start, v_gram, before, own, *coded)


def projected_kernel(items, place, visits_ref, *refs):
    frames_refs, outs, token_ref = refs[: len(items)], refs[-2 * len(items) - 1 : -1], refs[-1]
    token_ref[...] = jnp.zeros_like(token_ref)
    for i, (slots, first) in enumerate(items):
        total_count, rank, _ = frames_refs[i].shape
        count = total_count // len(slots)
        for p in range(total_count):
            rows = pl.ds(p * rank, rank)
            owner = feature_of(place) ^ slots[p // count]
            product = low_dot(frames_refs[i][p], visits_ref[owner, first + p % count])
            outs[2 * i][rows, :], outs[2 * i + 1][rows, :] = two_parts(product)


def join_kernel(count, *refs):
    out_ref = refs[-1]
    first = 0
    for part in refs[:count]:
        out_ref[first : first + part.shape[0]] = part[...]
        first += part.shape[0]


def join(parts, after):
    if len(parts) == 1:
        return parts[0]
    return pl.pallas_call(
        functools.partial(join_kernel, len(parts)),
        in_specs=[VMEM_SPEC] * len(parts) + [ANY_SPEC] * len(after),
        out_specs=VMEM_SPEC,
        out_shape=jax.ShapeDtypeStruct((sum(x.shape[0] for x in parts),) + parts[0].shape[1:], parts[0].dtype),
        compiler_params=parameters(LIMIT),
        cost_estimate=SHORT,
        name="join_frames",
    )(*parts, *after)


def project_frames(items, place, frames, visits, after):
    width = visits.shape[-1]
    outs = []
    for item in items:
        count, rank, _ = frames[item].shape
        outs += [jax.ShapeDtypeStruct((count * rank, width), BF16)] * 2
    *parts, token = pl.pallas_call(
        functools.partial(projected_kernel, items),
        in_specs=[SMEM_SPEC] + [VMEM_SPEC] * (1 + len(items)) + [ANY_SPEC] * len(after),
        out_specs=[VMEM_SPEC] * (len(outs) + 1),
        out_shape=outs + [jax.ShapeDtypeStruct((8, LANES), F32)],
        compiler_params=parameters(LIMIT),
        cost_estimate=SHORT,
        name="project_frames",
    )(place, visits, *[frames[item] for item in items], *after)
    return {item: parts[2 * i : 2 * i + 2] for i, item in enumerate(items)}, token


def next_h_kernel(n_terms, *refs):
    inverse_ref, spread_ref, _, result_ref, h_ref, factor_ref = refs[n_terms:]
    h_next = high_dot(total(refs[:n_terms]), inverse_ref[...])
    result_ref[...] = h_next
    h_ref[...] = h_next
    rank = h_next.shape[0]
    h_rows = h_next.T
    h_rows = jnp.concatenate([h_rows] * (spread_ref.shape[2] // rank), axis=1)
    for slot in range(spread_ref.shape[0]):
        factor_ref[slot] = jnp.concatenate(three_parts(h_rows * spread_ref[slot]), axis=0)


def next_h(terms, inverse, spread, after):
    n_slots, rank, columns = spread.shape
    return pl.pallas_call(
        functools.partial(next_h_kernel, len(terms)),
        in_specs=[VMEM_SPEC] * (len(terms) + 2) + [ANY_SPEC],
        out_specs=[VMEM_SPEC] * 3,
        out_shape=[
            jax.ShapeDtypeStruct(inverse.shape, F32),
            jax.ShapeDtypeStruct(inverse.shape, F32),
            jax.ShapeDtypeStruct((n_slots, 3 * rank, columns), BF16),
        ],
        compiler_params=parameters(LIMIT),
        cost_estimate=SHORT,
        name="next_h",
    )(*terms, inverse, spread, after)


def second_inverse_kernel(h_ref, w_gram_ref, gram_ref, inverse_ref):
    gram = high_dot(h_ref[...], h_ref[...], COLS_BY_COLS)
    gram_ref[...] = gram
    inverse_ref[...] = inverse_of(gram * w_gram_ref[...])


def second_inverse(h_next, w_gram):
    out = jax.ShapeDtypeStruct(w_gram.shape, F32)
    return pl.pallas_call(
        second_inverse_kernel,
        out_shape=[out, out],
        compiler_params=parameters(LIMIT),
        cost_estimate=SHORT,
        name="second_inverse",
    )(h_next, w_gram)


def v_terms_kernel(items, sent, place, factor_ref, *refs):
    parts, terms_ref = refs[: 2 * len(items)], refs[-1]
    rank, half = terms_ref.shape
    upper = core_of(place) ^ 1 if sent else core_of(place)
    features = pl.ds(pl.multiple_of(upper * half, half), half)
    total = None
    for i, (slots, first) in enumerate(items):
        count = parts[2 * i].shape[0] // len(slots)
        columns = pl.ds(first * rank, count)
        for k, slot in enumerate(slots):
            rows = pl.ds(k * count, count)
            large = low_dot(factor_ref[slot, :, columns], parts[2 * i][rows, features])
            small = low_dot(factor_ref[slot, : 2 * rank, columns], parts[2 * i + 1][rows, features])
            terms = large[:rank] + (large[rank : 2 * rank] + small[:rank]) + (large[2 * rank :] + small[rank:])
            total = terms if total is None else total + terms
    terms_ref[...] = total


def half_v_terms(items, sent, place, factor, projected, after):
    width = projected[0].shape[1]
    rank = factor.shape[1] // 3
    return pl.pallas_call(
        functools.partial(v_terms_kernel, items, sent),
        in_specs=[SMEM_SPEC] + [VMEM_SPEC] * (1 + len(projected)) + [ANY_SPEC] * len(after),
        out_specs=VMEM_SPEC,
        out_shape=jax.ShapeDtypeStruct((rank, width // 2), F32),
        compiler_params=parameters(LIMIT),
        cost_estimate=SHORT,
        name="v_terms",
    )(place, factor, *projected, *after)


def next_v_kernel(items, share, later, place, terms_ref, inverse_ref, h_ref, *refs):
    parts, refs = refs[: 2 * len(items)], refs[2 * len(items) :]
    rank, half = terms_ref.shape
    here = pl.multiple_of((core_of(place) ^ 1 if later else core_of(place)) * half, half)
    features = pl.ds(here, half)
    v_rows = high_dot(inverse_ref[...], terms_ref[...])
    *before, v_ref, sums_ref, v_parts = refs
    v_ref[...] = v_rows
    sums = before[0][...] if later else jnp.zeros((rank, 2 * rank), F32)
    v_parts[...] = jnp.concatenate(two_parts(v_rows), axis=0)
    weights = jnp.concatenate([h_ref[...]] * 2, axis=1)
    gram = low_dot(v_parts[...], v_parts[...], ROWS_BY_ROWS)
    gram = gram[:rank, :rank] + (gram[:rank, rank:] + gram[rank:, :rank])
    sums_ref[...] = sums + jnp.concatenate([jnp.zeros((rank, rank), F32), gram], axis=1)
    for i, (slots, done) in enumerate(items):
        seen = low_dot(parts[2 * i][:, features], v_parts[...], ROWS_BY_ROWS)
        seen = seen + low_dot(parts[2 * i + 1][:, features], v_parts[...], ROWS_BY_ROWS)
        count = seen.shape[0] // rank // len(slots)
        for p in range(seen.shape[0] // rank):
            patient = (feature_of(place) ^ slots[p // count]) * share + done + p % count
            row = jnp.sum(seen[p * rank : (p + 1) * rank] * weights, axis=0, keepdims=True)
            sums_ref[pl.ds(patient, 1), :rank] += row[:, :rank] + row[:, rank:]


def half_v(items, share, place, terms, inverse, h_next, projected, before):
    rank, half = terms.shape
    return pl.pallas_call(
        functools.partial(next_v_kernel, items, share, bool(before)),
        in_specs=[SMEM_SPEC] + [VMEM_SPEC] * (3 + len(projected) + len(before)),
        out_specs=[VMEM_SPEC] * 2,
        out_shape=[
            jax.ShapeDtypeStruct((rank, half), F32),
            jax.ShapeDtypeStruct((rank, 2 * rank), F32),
        ],
        scratch_shapes=[pltpu.VMEM((2 * rank, half), BF16)],
        compiler_params=parameters(LIMIT),
        cost_estimate=SHORT,
        name="next_v",
    )(place, terms, inverse, h_next, *projected, *before)


def whole_v_kernel(place, own_ref, other_ref, v_ref, token_ref):
    half = own_ref.shape[1]
    upper = core_of(place) == 1
    v_ref[:, :half] = jnp.where(upper, other_ref[...], own_ref[...])
    v_ref[:, half:] = jnp.where(upper, own_ref[...], other_ref[...])
    token_ref[...] = jnp.zeros_like(token_ref)


def whole_v(place, own, other):
    rank, half = own.shape
    return pl.pallas_call(
        whole_v_kernel,
        in_specs=[SMEM_SPEC] + [VMEM_SPEC] * 2,
        out_specs=[VMEM_SPEC] * 2,
        out_shape=[jax.ShapeDtypeStruct((rank, 2 * half), F32), jax.ShapeDtypeStruct((8, LANES), F32)],
        compiler_params=parameters(LIMIT),
        cost_estimate=SHORT,
        name="whole_v",
    )(place, own, other)


def next_w_kernel(n_sums, *refs):
    gram_ref, _, w_ref = refs[n_sums:]
    patients, rank = w_ref.shape
    sums = total(refs[:n_sums])
    table = jnp.concatenate([sums[:, rank:] * gram_ref[...], sums.T[:rank]], axis=1)
    w_ref[...] = eliminate(table, rank).T[rank : rank + patients]


def next_w(sums, h_gram, patients, after):
    rank = h_gram.shape[0]
    return pl.pallas_call(
        functools.partial(next_w_kernel, len(sums)),
        in_specs=[VMEM_SPEC] * (len(sums) + 1) + [ANY_SPEC],
        out_specs=VMEM_SPEC,
        out_shape=jax.ShapeDtypeStruct((patients, rank), F32),
        compiler_params=parameters(LIMIT),
        cost_estimate=SHORT,
        name="next_w",
    )(*sums, h_gram, after)


def swap(x, axis, slot):
    pairs = [(i, i ^ slot) for i in range(lax.axis_size(axis))]
    return lax.ppermute(x, axis, pairs)


def all_terms(x, axis):
    n = lax.axis_size(axis)
    if n > 4:
        return [lax.psum(x, axis)]
    return [x] + [swap(x, axis, s) for s in range(1, n)]


def staged_terms(x, axis, after):
    n = lax.axis_size(axis)
    steps = [1 << i for i in range(n.bit_length() - 1)]
    for step in steps[:-1]:
        x = add(x, swap(x, axis, step), after)
    return [x, swap(x, axis, steps[-1])]


def add_kernel(a_ref, b_ref, *refs):
    refs[-1][...] = a_ref[...] + b_ref[...]


def add(a, b, after):
    return pl.pallas_call(
        add_kernel,
        in_specs=[VMEM_SPEC] * 2 + [ANY_SPEC] * len(after),
        out_specs=VMEM_SPEC,
        out_shape=jax.ShapeDtypeStruct(a.shape, a.dtype),
        compiler_params=parameters(LIMIT),
        cost_estimate=SHORT,
        name="add_terms",
    )(a, b, *after)


def patient_halves(keep, send, after):
    own = add(keep, swap(send, "patient", 1), [])
    step = 2
    while step < lax.axis_size("patient"):
        own = add(own, swap(own, "patient", step), [after])
        step *= 2
    return own, swap(own, "patient", 1)


def on_device(visits, visit_counts, h_start, v_start, w_start):
    n = lax.axis_size("feature")
    patients, slots, width = visits.shape
    share = patients // n
    place = (2 * lax.axis_index("feature") + (lax.axis_index("patient") & 1)).astype(jnp.int32).reshape(1)
    by_owner = visits.reshape(n, share, slots, width)
    in_hbm = pltpu.with_memory_space_constraint(by_owner, pltpu.HBM)
    v_rows = pltpu.with_memory_space_constraint(v_start.T, pltpu.HBM)

    n_parts = 2 if share % 2 == 0 else 1
    count = share // n_parts
    firsts = [part * count for part in range(n_parts)]
    bits = [1 << i for i in range(n.bit_length() - 1)]
    v_near = v_start.T

    def send(bit):
        return [slot for slot in range(n) if slot & bit and not slot & (bit - 1)]

    def receive(bit):
        return [slot ^ bit for slot in send(bit)]

    w_gram, spread = spread_w(place, w_start, n)
    w_grams = staged_terms(w_gram, "patient", [])
    arrived = [[] for _ in firsts]
    for i, bit in enumerate(bits):
        layouts = [receive(before) for before in bits[:i]]
        for part, first in enumerate(firsts):
            if i == 0 and part == 0:
                code = first_projection(send(bit), count, n_parts == 1, place, in_hbm, v_rows)
            else:
                after = [w_grams[part]] + [v_gram] * part if i else []
                code = next_projection(
                    send(bit), first, count, part == n_parts - 1, layouts, place, by_owner, v_near, arrived[part], after
                )
            arrived[part] = arrived[part] + [swap(code, "feature", bit)]
        if i == 0:
            own, v_gram = project_own(n_parts, receive(bit), place, by_owner, v_near, arrived[0][0])

    layouts = [receive(bit) for bit in bits]
    frames = [[] for _ in firsts]
    joined = []

    def double(part, after):
        for bit in bits[::-1]:
            slots = tuple(slot ^ bit for group, _ in frames[part] for slot in group)
            joined = join([x for _, x in frames[part]], after)
            frames[part].append((slots, swap(joined, "feature", bit)))
        return [joined]

    def project_groups(groups, after):
        arrays = {(frames[part][k][0], firsts[part]): frames[part][k][1] for part, k in groups}
        return project_frames(list(arrays), place, arrays, by_owner, after)

    h_local = v_gram
    for part, first in enumerate(firsts):
        low, h_local, v_total = own_frames(
            layouts[part == 0 :],
            part,
            n_parts,
            place,
            visit_counts,
            h_start,
            w_start,
            v_gram,
            h_local,
            own[part],
            arrived[part][part == 0 :],
        )
        v_gram = v_total
        frames[part].append(((0,), low))

    last = len(bits)
    for part in range(n_parts - 1):
        joined = double(part, [frames[-1][0][1]])
    first_groups = [(part, 0) for part in range(n_parts)] + [(part, 1) for part in range(n_parts - 1)]
    early = [(part, k) for part in range(n_parts - 1) for k in range(2, last + 1)]
    projected, token = project_groups(first_groups, joined)
    h_sums = staged_terms(h_local, "patient", [token])
    w_gram, inverse = first_inverse(v_gram, w_grams, h_sums[0])
    h_sum = add(*h_sums, [inverse])
    joined = double(n_parts - 1, [h_sum] + [frames[part][k][1] for part, k in early])
    h_terms = all_terms(h_sum, "feature")
    after = joined
    for groups in [early] + [[(n_parts - 1, k)] for k in range(1, last + 1)]:
        if groups:
            more, token = project_groups(groups, after)
            projected |= more
            after = [token]
    h_result, h_next, factor = next_h(h_terms, inverse, spread, token)

    items = list(projected)
    flat = [x for item in items for x in projected[item]]
    send = half_v_terms(items, True, place, factor, flat, [])
    keep = half_v_terms(items, False, place, factor, flat, [send])
    h_gram, second = second_inverse(h_next, w_gram)
    own_terms, other_terms = patient_halves(keep, send, second)
    v_own, before = half_v(items, share, place, own_terms, second, h_next, flat, [])
    v_other, sums = half_v(items, share, place, other_terms, second, h_next, flat, [before])
    v_next, token = whole_v(place, v_own, v_other)
    w_next = next_w(all_terms(sums, "feature"), h_gram, patients, token)
    return (h_result, v_next.T, w_next)


def solution(mesh):
    return jax.shard_map(
        on_device,
        mesh=mesh,
        in_specs=(
            P(("groups", "patient"), None, "feature"),
            P(("groups", "patient")),
            P(),
            P("feature", None),
            P(("groups", "patient"), None),
        ),
        out_specs=(P(None, "groups"), P("feature", "groups"), P("patient", "groups")),
        check_vma=False,
    )
```

```python
import functools

import jax
import jax.numpy as jnp
from jax import lax
from jax.experimental import pallas as pl
from jax.experimental.pallas import tpu as pltpu
from jax.sharding import PartitionSpec as P

NS_STEPS = 12
LANES = 128
LEVELS = 32000.0
COARSE_STEPS = 3
SHORT = pl.CostEstimate(flops=1000, bytes_accessed=1000, transcendentals=0)

epsilon = 1e-06
HIGH = lax.Precision.HIGHEST
F32 = jnp.float32
BF16 = jnp.bfloat16
MIB = 1024 * 1024

ROWS_BY_COLS = (((1,), (0,)), ((), ()))
ROWS_BY_ROWS = (((1,), (1,)), ((), ()))
COLS_BY_COLS = (((0,), (0,)), ((), ()))


def low_dot(a, b, dims=ROWS_BY_COLS):
    return lax.dot_general(a, b, dims, preferred_element_type=F32)


def high_dot(a, b, dims=ROWS_BY_COLS):
    return lax.dot_general(a, b, dims, precision=HIGH, preferred_element_type=F32)


def two_parts(x):
    first = x.astype(BF16)
    return first, (x - first.astype(F32)).astype(BF16)


def three_parts(x):
    first = x.astype(BF16)
    rest = x - first.astype(F32)
    second = rest.astype(BF16)
    return first, second, (rest - second.astype(F32)).astype(BF16)


def stacked_dot(a, b):
    n = a.shape[0]
    a_first, a_second, a_third = three_parts(a)
    b_first, b_second, b_third = three_parts(b)
    x = low_dot(jnp.concatenate([a_first, a_second, a_third], axis=0), b_first)
    y = low_dot(jnp.concatenate([a_first, a_second], axis=0), b_second)
    z = low_dot(a_first, b_third)
    return x[:n] + ((x[n : 2 * n] + y[:n]) + ((x[2 * n :] + y[n:]) + z))


def feature_of(place):
    return place[0] >> 1


def core_of(place):
    return place[0] & 1


def lane_numbers(shape):
    return lax.broadcasted_iota(jnp.int32, shape, len(shape) - 1)


ANY_SPEC = pl.BlockSpec(memory_space=pl.ANY)
HBM_SPEC = pl.BlockSpec(memory_space=pltpu.HBM)


def parameters(mib):
    return pltpu.CompilerParams(vmem_limit_bytes=mib * MIB)


LIMIT = 8
VMEM_SPEC = pl.BlockSpec(memory_space=pltpu.VMEM)
SMEM_SPEC = pl.BlockSpec(memory_space=pltpu.SMEM)


def exponent_rows(total_count):
    return -(-(total_count + 1) // 16) * 16


def payload_shape(total_count, rank, slots, with_gram):
    return (total_count * rank + (rank // 2 if with_gram else 0) + exponent_rows(total_count), slots)


def row_exponent(x):
    top = jnp.max(jnp.abs(x), axis=1, keepdims=True)
    return jnp.ceil(jnp.log2(jnp.maximum(top, 1e-30)))


class Payload:
    def __init__(self, ref, slots, count, rank, with_gram):
        self.ref, self.slots, self.count, self.rank, self.with_gram = ref, slots, count, rank, with_gram
        self.entries = len(slots) * count
        gram_rows = rank // 2 if with_gram else 0
        exponents = self.rows(self.entries * rank + gram_rows, exponent_rows(self.entries))
        self.steps = jnp.exp2(exponents[:, :LANES].T[:rank]) * (1.0 / LEVELS)

    def rows(self, first, number):
        return self.ref[pl.ds(first, number), :].astype(jnp.int32).astype(F32)

    def proj(self, slot, p):
        entry = self.slots.index(slot) * self.count + p
        return self.rows(entry * self.rank, self.rank) * self.steps[:, entry : entry + 1]

    def gram(self):
        rank = self.rank
        digits = self.rows(self.entries * rank, rank // 2)
        digits = jnp.concatenate([digits[:, : 2 * rank], digits[:, 2 * rank :]], axis=0)
        return (digits[:, :rank] + digits[:, rank:] * (0.5 / LEVELS)) * self.steps[:, self.entries : self.entries + 1]


def encode(values, gram, coded_ref, rank):
    count = len(values)
    lanes = lane_numbers((rank, LANES))
    exponents = jnp.zeros((rank, LANES), F32)
    for p, value in enumerate(values):
        proj = value()
        exponent = row_exponent(proj)
        coded = jnp.floor(proj * (LEVELS / jnp.exp2(exponent)) + 0.5)
        coded_ref[pl.ds(p * rank, rank), :] = coded.astype(jnp.int32).astype(jnp.int16)
        exponents = jnp.where(lanes == p, exponent, exponents)
    end = count * rank
    if gram is not None:
        exponent = row_exponent(gram)
        scaled = gram * (LEVELS / jnp.exp2(exponent))
        whole = jnp.floor(scaled + 0.5)
        rest = jnp.floor((scaled - whole) * (2 * LEVELS) + 0.5)
        digits = jnp.concatenate([whole, rest], axis=1)
        digits = jnp.concatenate([digits[: rank // 2], digits[rank // 2 :]], axis=1)
        coded_ref[pl.ds(end, rank // 2), :] = digits.astype(jnp.int32).astype(jnp.int16)
        exponents = jnp.where(lanes == count, exponent, exponents)
        end += rank // 2
    rows = exponent_rows(count)
    last = jnp.concatenate([exponents.T[:rows], jnp.zeros((rows, coded_ref.shape[1] - rank), F32)], axis=1)
    coded_ref[pl.ds(end, rows), :] = last.astype(jnp.int32).astype(jnp.int16)


def first_projection_kernel(slots, with_gram, place, v_hbm, visits_ref, coded_ref, v_ref, buffers, sems, v_sem):
    count = buffers.shape[1]
    v_copy = pltpu.make_async_copy(v_hbm, v_ref, v_sem)
    v_copy.start()
    pieces = sems.shape[1]
    piece = count // pieces
    copies = []
    for i, slot in enumerate(slots):
        for j in range(pieces):
            rows = pl.ds(j * piece, piece)
            source = visits_ref.at[feature_of(place) ^ slot, rows]
            copies.append(pltpu.make_async_copy(source, buffers.at[i, rows], sems.at[i, j]))
            copies[-1].start()
    v_copy.wait()

    def value(i, p):
        if p % piece == 0:
            copies[i * pieces + p // piece].wait()
        return low_dot(v_ref[...], buffers[i, p], ROWS_BY_ROWS)

    values = [functools.partial(value, i, p) for i in range(len(slots)) for p in range(count)]
    gram = low_dot(v_ref[...], v_ref[...], ROWS_BY_ROWS) if with_gram else None
    encode(values, gram, coded_ref, v_ref.shape[0])


def first_projection(slots, count, with_gram, place, visits, v_rows):
    width = visits.shape[3]
    rank = v_rows.shape[0]
    return pl.pallas_call(
        functools.partial(first_projection_kernel, slots, with_gram),
        in_specs=[SMEM_SPEC, HBM_SPEC, HBM_SPEC],
        out_specs=VMEM_SPEC,
        out_shape=jax.ShapeDtypeStruct(payload_shape(len(slots) * count, rank, visits.shape[2], with_gram), jnp.int16),
        scratch_shapes=[
            pltpu.VMEM(v_rows.shape, BF16),
            pltpu.VMEM((len(slots), count) + visits.shape[2:], BF16),
            pltpu.SemaphoreType.DMA((len(slots), 1)),
            pltpu.SemaphoreType.DMA,
        ],
        compiler_params=parameters(LIMIT),
        cost_estimate=SHORT,
        name="project_first",
    )(place, v_rows, visits)


def next_projection_kernel(slots, first, count, with_gram, layouts, place, v_ref, visits_ref, *refs):
    coded_ref = refs[-1]
    rank = v_ref.shape[0]
    arrived = [Payload(ref, layout, count, rank, with_gram) for ref, layout in zip(refs, layouts)]

    def value(slot, p):
        proj = low_dot(v_ref[...], visits_ref[feature_of(place) ^ slot, first + p], ROWS_BY_ROWS)
        for payload in arrived:
            proj = proj + payload.proj(slot, p)
        return proj

    gram = None
    if with_gram:
        gram = low_dot(v_ref[...], v_ref[...], ROWS_BY_ROWS)
        for payload in arrived:
            gram = gram + payload.gram()
    encode([functools.partial(value, slot, p) for slot in slots for p in range(count)], gram, coded_ref, rank)


def next_projection(slots, first, count, with_gram, layouts, place, visits, v_rows, arrived, after):
    rank = v_rows.shape[0]
    return pl.pallas_call(
        functools.partial(next_projection_kernel, slots, first, count, with_gram, layouts),
        in_specs=[SMEM_SPEC] + [VMEM_SPEC] * (2 + len(arrived)) + [ANY_SPEC] * len(after),
        out_specs=VMEM_SPEC,
        out_shape=jax.ShapeDtypeStruct(payload_shape(len(slots) * count, rank, visits.shape[2], with_gram), jnp.int16),
        compiler_params=parameters(LIMIT),
        cost_estimate=SHORT,
        name="project_next",
    )(place, v_rows, visits, *arrived, *after)


def spread_w_kernel(n_slots, place, w_ref, gram_ref, spread_ref):
    gram_ref[...] = high_dot(w_ref[...], w_ref[...], COLS_BY_COLS)
    patients, rank = w_ref.shape
    share = patients // n_slots
    w_rows = jnp.concatenate([w_ref[...], jnp.zeros((LANES - patients, rank), F32)], axis=0)
    w_columns = w_rows.T
    for slot in range(n_slots):
        first = (feature_of(place) ^ slot) * share
        columns = pltpu.roll(w_columns, jnp.where(first == 0, 0, LANES - first), 1)
        spread = [jnp.broadcast_to(columns[:, p : p + 1], (rank, rank)) for p in range(share)]
        spread_ref[slot] = jnp.concatenate(spread, axis=1)


def spread_w(place, w_start, n_slots):
    patients, rank = w_start.shape
    return pl.pallas_call(
        functools.partial(spread_w_kernel, n_slots),
        in_specs=[SMEM_SPEC, VMEM_SPEC],
        out_specs=[VMEM_SPEC] * 2,
        out_shape=[
            jax.ShapeDtypeStruct((rank, rank), F32),
            jax.ShapeDtypeStruct((n_slots, rank, patients // n_slots * rank), F32),
        ],
        compiler_params=parameters(LIMIT),
        cost_estimate=SHORT,
        name="spread_w",
    )(place, w_start)


def own_projection_kernel(layout, place, v_ref, visits_ref, arrived_ref, *refs):
    *proj_refs, v_gram_ref = refs
    count, rank, _ = proj_refs[0].shape
    payload = Payload(arrived_ref, layout, count, rank, len(proj_refs) == 1)
    for p in range(visits_ref.shape[1]):
        proj = low_dot(v_ref[...], visits_ref[feature_of(place), p], ROWS_BY_ROWS)
        proj_refs[p // count][p % count] = proj + payload.proj(0, p) if p < count else proj
    gram = low_dot(v_ref[...], v_ref[...], ROWS_BY_ROWS)
    v_gram_ref[...] = gram + payload.gram() if payload.with_gram else gram


def project_own(n_parts, layout, place, visits, v_rows, arrived):
    _, share, slots, width = visits.shape
    rank = v_rows.shape[0]
    proj = jax.ShapeDtypeStruct((share // n_parts, rank, slots), F32)
    *own, v_gram = pl.pallas_call(
        functools.partial(own_projection_kernel, layout),
        in_specs=[SMEM_SPEC] + [VMEM_SPEC] * 3,
        out_specs=[VMEM_SPEC] * (n_parts + 1),
        out_shape=[proj] * n_parts + [jax.ShapeDtypeStruct((rank, rank), F32)],
        compiler_params=parameters(LIMIT),
        cost_estimate=SHORT,
        name="project_own",
    )(place, v_rows, visits, arrived)
    return own, v_gram


def solve_tile(columns, tile):
    rows = lax.broadcasted_iota(jnp.int32, tile.shape, 0)
    for a in range(0, 8, 2):
        b = a + 1
        first, second = columns[a], columns[b]
        m_aa, m_ab, m_ba, m_bb = first[a:b], second[a:b], first[b : b + 1], second[b : b + 1]
        scale = 1.0 / (m_aa * m_bb - m_ab * m_ba)
        m_aa, m_ab, m_ba, m_bb = m_aa * scale, m_ab * scale, m_ba * scale, m_bb * scale

        def step(x):
            x_a, x_b = x[a:b], x[b : b + 1]
            new_a, new_b = m_bb * x_a - m_ab * x_b, m_aa * x_b - m_ba * x_a
            x = x - (first * new_a + second * new_b)
            return jnp.where(rows == a, new_a, jnp.where(rows == b, new_b, x))

        tile = step(tile)
        columns = [step(x) if q > b else x for q, x in enumerate(columns)]
    return tile


def eliminate(table, rank):
    tiles = [table[8 * t : 8 * t + 8] for t in range(rank // 8)]
    for home in range(rank // 8):
        first = 8 * home
        columns = [[jnp.broadcast_to(t[:, q : q + 1], t.shape) for q in range(first, first + 8)] for t in tiles]
        solved = solve_tile(columns[home], tiles[home])
        for t, tile in enumerate(tiles):
            terms = [column * solved[q : q + 1] for q, column in enumerate(columns[t])]
            while len(terms) > 1:
                terms = [x + y for x, y in zip(terms[::2], terms[1::2])]
            tiles[t] = solved if t == home else tile - terms[0]
    return jnp.concatenate(tiles, axis=0)


def inverse_of(gram):
    rank = gram.shape[0]
    eye = (lax.broadcasted_iota(jnp.int32, gram.shape, 0) == lane_numbers(gram.shape)).astype(F32)
    return eliminate(jnp.concatenate([gram, eye], axis=1), rank)[:, rank:]


def total(refs):
    out = refs[0][...]
    for ref in refs[1:]:
        out = out + ref[...]
    return out


def first_inverse_kernel(v_gram_ref, *refs):
    *terms, _, w_gram_ref, inverse_ref = refs
    w_gram = total(terms)
    w_gram_ref[...] = w_gram
    inverse_ref[...] = inverse_of(w_gram * v_gram_ref[...])


def first_inverse(v_gram, w_grams, after):
    out = jax.ShapeDtypeStruct(v_gram.shape, F32)
    return pl.pallas_call(
        first_inverse_kernel,
        in_specs=[VMEM_SPEC] * (1 + len(w_grams)) + [ANY_SPEC],
        out_specs=[VMEM_SPEC] * 2,
        out_shape=[out, out],
        compiler_params=parameters(LIMIT),
        cost_estimate=SHORT,
        name="first_inverse",
    )(v_gram, *w_grams, after)


def sweep_all(frames, rank, fine):
    patients = range(frames.shape[0])
    if fine:
        both = [jnp.concatenate(two_parts(frames[p]), axis=0) for p in patients]
        blocks = [low_dot(x, x, ROWS_BY_ROWS) for x in both]
        blocks = [x[:rank] + x[rank:] for x in blocks]
        grams = [x + pltpu.roll(x, rank, 1) for x in blocks]
        moved = [low_dot(jnp.concatenate(two_parts(g), axis=0), x) for g, x in zip(grams, both)]
        moved = [x[:rank] + x[rank:] for x in moved]
    else:
        first = [frames[p].astype(BF16) for p in patients]
        grams = [low_dot(x, x, ROWS_BY_ROWS).astype(BF16) for x in first]
        moved = [low_dot(g, x) for g, x in zip(grams, first)]
    for p in patients:
        frames[p] = 1.5 * frames[p] - 0.5 * moved[p]


def frames_kernel(layouts, part, share, place, counts_ref, h_ref, w_ref, v_gram_ref, before_ref, own_ref, *refs):
    coded, refs = refs[: len(layouts)], refs[len(layouts) :]
    frames_ref, terms_ref, v_total_ref, proj, frames = refs
    count, rank, slots = frames.shape
    patients = range(count)
    first = feature_of(place) * share + part * count
    pieces = [own_ref[p] for p in patients]
    v_gram = v_gram_ref[...]
    for code, layout in zip(coded, layouts):
        payload = Payload(code, layout, count, rank, (part + 1) * count == share)
        pieces = [pieces[p] + payload.proj(0, p) for p in patients]
        if payload.with_gram:
            v_gram = v_gram + payload.gram()
    v_total_ref[...] = v_gram
    for p in patients:
        proj[p] = pieces[p]
    weights = [w_ref[pl.ds(first + p, 1), :] for p in patients]
    mixed = [stacked_dot(h_ref[...] * weights[p], pieces[p]) for p in patients]
    lanes = lane_numbers((rank, slots))
    mixed = [jnp.where(lanes < counts_ref[first + p], mixed[p], 0.0) for p in patients]
    energy = [jnp.sum(jnp.sum(x * x, axis=1, keepdims=True), axis=0, keepdims=True) for x in mixed]
    for p in patients:
        frames[p] = mixed[p] * lax.rsqrt(energy[p] + epsilon)

    def sweep(fine, step, carry):
        sweep_all(frames, rank, fine)
        return carry

    lax.fori_loop(0, COARSE_STEPS, functools.partial(sweep, False), 0, unroll=True)
    lax.fori_loop(COARSE_STEPS, NS_STEPS, functools.partial(sweep, True), 0, unroll=True)
    low = [frames[p].astype(BF16) for p in patients]
    for p in patients:
        frames_ref[p] = low[p]
    products = [jnp.concatenate(three_parts(proj[p]), axis=0) for p in patients]
    products = [low_dot(low[p], products[p], ROWS_BY_ROWS) for p in patients]
    terms = before_ref[...] if part else jnp.zeros((rank, rank), F32)
    for p in patients:
        product = products[p][:, :rank] + (products[p][:, rank : 2 * rank] + products[p][:, 2 * rank :])
        terms = terms + product * weights[p]
    terms_ref[...] = terms


def own_frames(layouts, part, n_parts, place, counts, h_start, w_start, v_gram, before, own, coded):
    count, rank, slots = own.shape
    share = count * n_parts
    return pl.pallas_call(
        functools.partial(frames_kernel, layouts, part, share),
        in_specs=[SMEM_SPEC] * 2 + [VMEM_SPEC] * (5 + len(coded)),
        out_specs=[VMEM_SPEC] * 3,
        out_shape=[
            jax.ShapeDtypeStruct(own.shape, BF16),
            jax.ShapeDtypeStruct((rank, rank), F32),
            jax.ShapeDtypeStruct((rank, rank), F32),
        ],
        scratch_shapes=[pltpu.VMEM(own.shape, F32)] * 2,
        compiler_params=parameters(LIMIT),
        cost_estimate=SHORT,
        name="own_frames",
    )(place, counts, h_start, w_start, v_gram, before, own, *coded)


def projected_kernel(items, place, visits_ref, *refs):
    frames_refs, outs, token_ref = refs[: len(items)], refs[-2 * len(items) - 1 : -1], refs[-1]
    token_ref[...] = jnp.zeros_like(token_ref)
    for i, (slots, first) in enumerate(items):
        total_count, rank, _ = frames_refs[i].shape
        count = total_count // len(slots)
        for p in range(total_count):
            rows = pl.ds(p * rank, rank)
            owner = feature_of(place) ^ slots[p // count]
            product = low_dot(frames_refs[i][p], visits_ref[owner, first + p % count])
            outs[2 * i][rows, :], outs[2 * i + 1][rows, :] = two_parts(product)


def join_kernel(count, *refs):
    out_ref = refs[-1]
    first = 0
    for part in refs[:count]:
        out_ref[first : first + part.shape[0]] = part[...]
        first += part.shape[0]


def join(parts, after):
    if len(parts) == 1:
        return parts[0]
    return pl.pallas_call(
        functools.partial(join_kernel, len(parts)),
        in_specs=[VMEM_SPEC] * len(parts) + [ANY_SPEC] * len(after),
        out_specs=VMEM_SPEC,
        out_shape=jax.ShapeDtypeStruct((sum(x.shape[0] for x in parts),) + parts[0].shape[1:], parts[0].dtype),
        compiler_params=parameters(LIMIT),
        cost_estimate=SHORT,
        name="join_frames",
    )(*parts, *after)


def project_frames(items, place, frames, visits, after):
    width = visits.shape[-1]
    outs = []
    for item in items:
        count, rank, _ = frames[item].shape
        outs += [jax.ShapeDtypeStruct((count * rank, width), BF16)] * 2
    *parts, token = pl.pallas_call(
        functools.partial(projected_kernel, items),
        in_specs=[SMEM_SPEC] + [VMEM_SPEC] * (1 + len(items)) + [ANY_SPEC] * len(after),
        out_specs=[VMEM_SPEC] * (len(outs) + 1),
        out_shape=outs + [jax.ShapeDtypeStruct((8, LANES), F32)],
        compiler_params=parameters(LIMIT),
        cost_estimate=SHORT,
        name="project_frames",
    )(place, visits, *[frames[item] for item in items], *after)
    return {item: parts[2 * i : 2 * i + 2] for i, item in enumerate(items)}, token


def next_h_kernel(n_terms, *refs):
    inverse_ref, spread_ref, _, result_ref, h_ref, factor_ref = refs[n_terms:]
    h_next = stacked_dot(total(refs[:n_terms]), inverse_ref[...])
    result_ref[...] = h_next
    h_ref[...] = h_next
    rank = h_next.shape[0]
    h_rows = h_next.T
    h_rows = jnp.concatenate([h_rows] * (spread_ref.shape[2] // rank), axis=1)
    for slot in range(spread_ref.shape[0]):
        factor_ref[slot] = jnp.concatenate(three_parts(h_rows * spread_ref[slot]), axis=0)


def next_h(terms, inverse, spread, after):
    n_slots, rank, columns = spread.shape
    return pl.pallas_call(
        functools.partial(next_h_kernel, len(terms)),
        in_specs=[VMEM_SPEC] * (len(terms) + 2) + [ANY_SPEC],
        out_specs=[VMEM_SPEC] * 3,
        out_shape=[
            jax.ShapeDtypeStruct(inverse.shape, F32),
            jax.ShapeDtypeStruct(inverse.shape, F32),
            jax.ShapeDtypeStruct((n_slots, 3 * rank, columns), BF16),
        ],
        compiler_params=parameters(LIMIT),
        cost_estimate=SHORT,
        name="next_h",
    )(*terms, inverse, spread, after)


def second_inverse_kernel(h_ref, w_gram_ref, gram_ref, inverse_ref):
    gram = high_dot(h_ref[...], h_ref[...], COLS_BY_COLS)
    gram_ref[...] = gram
    inverse_ref[...] = inverse_of(gram * w_gram_ref[...])


def second_inverse(h_next, w_gram):
    out = jax.ShapeDtypeStruct(w_gram.shape, F32)
    return pl.pallas_call(
        second_inverse_kernel,
        out_shape=[out, out],
        compiler_params=parameters(LIMIT),
        cost_estimate=SHORT,
        name="second_inverse",
    )(h_next, w_gram)


def v_terms_kernel(items, sent, place, factor_ref, *refs):
    parts, terms_ref = refs[: 2 * len(items)], refs[-1]
    rank, half = terms_ref.shape
    upper = core_of(place) ^ 1 if sent else core_of(place)
    features = pl.ds(pl.multiple_of(upper * half, half), half)
    total = None
    for i, (slots, first) in enumerate(items):
        count = parts[2 * i].shape[0] // len(slots)
        columns = pl.ds(first * rank, count)
        for k, slot in enumerate(slots):
            rows = pl.ds(k * count, count)
            large = low_dot(factor_ref[slot, :, columns], parts[2 * i][rows, features])
            small = low_dot(factor_ref[slot, : 2 * rank, columns], parts[2 * i + 1][rows, features])
            terms = large[:rank] + (large[rank : 2 * rank] + small[:rank]) + (large[2 * rank :] + small[rank:])
            total = terms if total is None else total + terms
    terms_ref[...] = total


def half_v_terms(items, sent, place, factor, projected, after):
    width = projected[0].shape[1]
    rank = factor.shape[1] // 3
    return pl.pallas_call(
        functools.partial(v_terms_kernel, items, sent),
        in_specs=[SMEM_SPEC] + [VMEM_SPEC] * (1 + len(projected)) + [ANY_SPEC] * len(after),
        out_specs=VMEM_SPEC,
        out_shape=jax.ShapeDtypeStruct((rank, width // 2), F32),
        compiler_params=parameters(LIMIT),
        cost_estimate=SHORT,
        name="v_terms",
    )(place, factor, *projected, *after)


def next_v_kernel(items, share, later, place, terms_ref, inverse_ref, h_ref, *refs):
    parts, refs = refs[: 2 * len(items)], refs[2 * len(items) :]
    rank, half = terms_ref.shape
    here = pl.multiple_of((core_of(place) ^ 1 if later else core_of(place)) * half, half)
    features = pl.ds(here, half)
    v_rows = stacked_dot(inverse_ref[...], terms_ref[...])
    *before, v_ref, sums_ref, v_parts = refs
    v_ref[...] = v_rows
    sums = before[0][...] if later else jnp.zeros((rank, 2 * rank), F32)
    v_parts[...] = jnp.concatenate(two_parts(v_rows), axis=0)
    weights = jnp.concatenate([h_ref[...]] * 2, axis=1)
    gram = low_dot(v_parts[...], v_parts[...], ROWS_BY_ROWS)
    gram = gram[:rank, :rank] + (gram[:rank, rank:] + gram[rank:, :rank])
    sums_ref[...] = sums + jnp.concatenate([jnp.zeros((rank, rank), F32), gram], axis=1)
    for i, (slots, done) in enumerate(items):
        seen = low_dot(parts[2 * i][:, features], v_parts[...], ROWS_BY_ROWS)
        seen = seen + low_dot(parts[2 * i + 1][:, features], v_parts[...], ROWS_BY_ROWS)
        count = seen.shape[0] // rank // len(slots)
        for p in range(seen.shape[0] // rank):
            patient = (feature_of(place) ^ slots[p // count]) * share + done + p % count
            row = jnp.sum(seen[p * rank : (p + 1) * rank] * weights, axis=0, keepdims=True)
            sums_ref[pl.ds(patient, 1), :rank] += row[:, :rank] + row[:, rank:]


def half_v(items, share, place, terms, inverse, h_next, projected, before):
    rank, half = terms.shape
    return pl.pallas_call(
        functools.partial(next_v_kernel, items, share, bool(before)),
        in_specs=[SMEM_SPEC] + [VMEM_SPEC] * (3 + len(projected) + len(before)),
        out_specs=[VMEM_SPEC] * 2,
        out_shape=[
            jax.ShapeDtypeStruct((rank, half), F32),
            jax.ShapeDtypeStruct((rank, 2 * rank), F32),
        ],
        scratch_shapes=[pltpu.VMEM((2 * rank, half), BF16)],
        compiler_params=parameters(LIMIT),
        cost_estimate=SHORT,
        name="next_v",
    )(place, terms, inverse, h_next, *projected, *before)


def whole_v_kernel(place, own_ref, other_ref, v_ref, token_ref):
    half = own_ref.shape[1]
    upper = core_of(place) == 1
    v_ref[:, :half] = jnp.where(upper, other_ref[...], own_ref[...])
    v_ref[:, half:] = jnp.where(upper, own_ref[...], other_ref[...])
    token_ref[...] = jnp.zeros_like(token_ref)


def whole_v(place, own, other):
    rank, half = own.shape
    return pl.pallas_call(
        whole_v_kernel,
        in_specs=[SMEM_SPEC] + [VMEM_SPEC] * 2,
        out_specs=[VMEM_SPEC] * 2,
        out_shape=[jax.ShapeDtypeStruct((rank, 2 * half), F32), jax.ShapeDtypeStruct((8, LANES), F32)],
        compiler_params=parameters(LIMIT),
        cost_estimate=SHORT,
        name="whole_v",
    )(place, own, other)


def next_w_kernel(n_sums, *refs):
    gram_ref, _, w_ref = refs[n_sums:]
    patients, rank = w_ref.shape
    sums = total(refs[:n_sums])
    table = jnp.concatenate([sums[:, rank:] * gram_ref[...], sums.T[:rank]], axis=1)
    w_ref[...] = eliminate(table, rank).T[rank : rank + patients]


def next_w(sums, h_gram, patients, after):
    rank = h_gram.shape[0]
    return pl.pallas_call(
        functools.partial(next_w_kernel, len(sums)),
        in_specs=[VMEM_SPEC] * (len(sums) + 1) + [ANY_SPEC],
        out_specs=VMEM_SPEC,
        out_shape=jax.ShapeDtypeStruct((patients, rank), F32),
        compiler_params=parameters(LIMIT),
        cost_estimate=SHORT,
        name="next_w",
    )(*sums, h_gram, after)


def swap(x, axis, slot):
    pairs = [(i, i ^ slot) for i in range(lax.axis_size(axis))]
    return lax.ppermute(x, axis, pairs)


def all_terms(x, axis):
    n = lax.axis_size(axis)
    if n > 4:
        return [lax.psum(x, axis)]
    return [x] + [swap(x, axis, s) for s in range(1, n)]


def staged_terms(x, axis, after):
    n = lax.axis_size(axis)
    steps = [1 << i for i in range(n.bit_length() - 1)]
    for step in steps[:-1]:
        x = add(x, swap(x, axis, step), after)
    return [x, swap(x, axis, steps[-1])]


def add_kernel(a_ref, b_ref, *refs):
    refs[-1][...] = a_ref[...] + b_ref[...]


def add(a, b, after):
    return pl.pallas_call(
        add_kernel,
        in_specs=[VMEM_SPEC] * 2 + [ANY_SPEC] * len(after),
        out_specs=VMEM_SPEC,
        out_shape=jax.ShapeDtypeStruct(a.shape, a.dtype),
        compiler_params=parameters(LIMIT),
        cost_estimate=SHORT,
        name="add_terms",
    )(a, b, *after)


def patient_halves(keep, send, after):
    own = add(keep, swap(send, "patient", 1), [])
    step = 2
    while step < lax.axis_size("patient"):
        own = add(own, swap(own, "patient", step), [after])
        step *= 2
    return own, swap(own, "patient", 1)


def on_device(visits, visit_counts, h_start, v_start, w_start):
    n = lax.axis_size("feature")
    patients, slots, width = visits.shape
    share = patients // n
    place = (2 * lax.axis_index("feature") + (lax.axis_index("patient") & 1)).astype(jnp.int32).reshape(1)
    by_owner = visits.reshape(n, share, slots, width)
    in_hbm = pltpu.with_memory_space_constraint(by_owner, pltpu.HBM)
    v_rows = pltpu.with_memory_space_constraint(v_start.T, pltpu.HBM)

    n_parts = 2 if share % 2 == 0 else 1
    count = share // n_parts
    firsts = [part * count for part in range(n_parts)]
    bits = [1 << i for i in range(n.bit_length() - 1)]
    v_near = v_start.T

    def send(bit):
        return [slot for slot in range(n) if slot & bit and not slot & (bit - 1)]

    def receive(bit):
        return [slot ^ bit for slot in send(bit)]

    w_gram, spread = spread_w(place, w_start, n)
    w_grams = staged_terms(w_gram, "patient", [])
    arrived = [[] for _ in firsts]
    for i, bit in enumerate(bits):
        layouts = [receive(before) for before in bits[:i]]
        for part, first in enumerate(firsts):
            if i == 0 and part == 0:
                code = first_projection(send(bit), count, n_parts == 1, place, in_hbm, v_rows)
            else:
                after = [w_grams[part]] + [v_gram] * part if i else []
                code = next_projection(
                    send(bit), first, count, part == n_parts - 1, layouts, place, by_owner, v_near, arrived[part], after
                )
            arrived[part] = arrived[part] + [swap(code, "feature", bit)]
        if i == 0:
            own, v_gram = project_own(n_parts, receive(bit), place, by_owner, v_near, arrived[0][0])

    layouts = [receive(bit) for bit in bits]
    frames = [[] for _ in firsts]
    joined = []

    def double(part, after):
        for bit in bits[::-1]:
            slots = tuple(slot ^ bit for group, _ in frames[part] for slot in group)
            joined = join([x for _, x in frames[part]], after)
            frames[part].append((slots, swap(joined, "feature", bit)))
        return [joined]

    def project_groups(groups, after):
        arrays = {(frames[part][k][0], firsts[part]): frames[part][k][1] for part, k in groups}
        return project_frames(list(arrays), place, arrays, by_owner, after)

    h_local = v_gram
    for part, first in enumerate(firsts):
        low, h_local, v_total = own_frames(
            layouts[part == 0 :],
            part,
            n_parts,
            place,
            visit_counts,
            h_start,
            w_start,
            v_gram,
            h_local,
            own[part],
            arrived[part][part == 0 :],
        )
        v_gram = v_total
        frames[part].append(((0,), low))

    last = len(bits)
    for part in range(n_parts - 1):
        joined = double(part, [frames[-1][0][1]])
    first_groups = [(part, 0) for part in range(n_parts)] + [(part, 1) for part in range(n_parts - 1)]
    early = [(part, k) for part in range(n_parts - 1) for k in range(2, last + 1)]
    projected, token = project_groups(first_groups, joined)
    h_sums = staged_terms(h_local, "patient", [token])
    w_gram, inverse = first_inverse(v_gram, w_grams, h_sums[0])
    h_sum = add(*h_sums, [inverse])
    joined = double(n_parts - 1, [h_sum] + [frames[part][k][1] for part, k in early])
    h_terms = all_terms(h_sum, "feature")
    after = joined
    for groups in [early] + [[(n_parts - 1, k)] for k in range(1, last + 1)]:
        if groups:
            more, token = project_groups(groups, after)
            projected |= more
            after = [token]
    h_result, h_next, factor = next_h(h_terms, inverse, spread, token)

    items = list(projected)
    flat = [x for item in items for x in projected[item]]
    send = half_v_terms(items, True, place, factor, flat, [])
    keep = half_v_terms(items, False, place, factor, flat, [send])
    h_gram, second = second_inverse(h_next, w_gram)
    own_terms, other_terms = patient_halves(keep, send, second)
    v_own, before = half_v(items, share, place, own_terms, second, h_next, flat, [])
    v_other, sums = half_v(items, share, place, other_terms, second, h_next, flat, [before])
    v_next, token = whole_v(place, v_own, v_other)
    w_next = next_w(all_terms(sums, "feature"), h_gram, patients, token)
    return (h_result, v_next.T, w_next)


def solution(mesh):
    return jax.shard_map(
        on_device,
        mesh=mesh,
        in_specs=(
            P(("groups", "patient"), None, "feature"),
            P(("groups", "patient")),
            P(),
            P("feature", None),
            P(("groups", "patient"), None),
        ),
        out_specs=(P(None, "groups"), P("feature", "groups"), P("patient", "groups")),
        check_vma=False,
    )
```

```python
import functools

import jax
import jax.numpy as jnp
from jax import lax
from jax.experimental import pallas as pl
from jax.experimental.pallas import tpu as pltpu
from jax.sharding import PartitionSpec as P

NS_STEPS = 12
LANES = 128
LEVELS = 32000.0
COARSE_STEPS = 3
SHORT = pl.CostEstimate(flops=1000, bytes_accessed=1000, transcendentals=0)

epsilon = 1e-06
HIGH = lax.Precision.HIGHEST
F32 = jnp.float32
BF16 = jnp.bfloat16
MIB = 1024 * 1024

ROWS_BY_COLS = (((1,), (0,)), ((), ()))
ROWS_BY_ROWS = (((1,), (1,)), ((), ()))
COLS_BY_COLS = (((0,), (0,)), ((), ()))


def low_dot(a, b, dims=ROWS_BY_COLS):
    return lax.dot_general(a, b, dims, preferred_element_type=F32)


def high_dot(a, b, dims=ROWS_BY_COLS):
    return lax.dot_general(a, b, dims, precision=HIGH, preferred_element_type=F32)


def two_parts(x):
    first = x.astype(BF16)
    return first, (x - first.astype(F32)).astype(BF16)


def three_parts(x):
    first = x.astype(BF16)
    rest = x - first.astype(F32)
    second = rest.astype(BF16)
    return first, second, (rest - second.astype(F32)).astype(BF16)


def feature_of(place):
    return place[0] >> 1


def core_of(place):
    return place[0] & 1


def lane_numbers(shape):
    return lax.broadcasted_iota(jnp.int32, shape, len(shape) - 1)


ANY_SPEC = pl.BlockSpec(memory_space=pl.ANY)
HBM_SPEC = pl.BlockSpec(memory_space=pltpu.HBM)


def parameters(mib):
    return pltpu.CompilerParams(vmem_limit_bytes=mib * MIB)


LIMIT = 8
VMEM_SPEC = pl.BlockSpec(memory_space=pltpu.VMEM)
SMEM_SPEC = pl.BlockSpec(memory_space=pltpu.SMEM)


def exponent_rows(total_count):
    return -(-(total_count + 1) // 16) * 16


def payload_shape(total_count, rank, slots, with_gram):
    return (total_count * rank + (rank // 2 if with_gram else 0) + exponent_rows(total_count), slots)


def row_exponent(x):
    top = jnp.max(jnp.abs(x), axis=1, keepdims=True)
    return jnp.ceil(jnp.log2(jnp.maximum(top, 1e-30)))


class Payload:
    def __init__(self, ref, slots, count, rank, with_gram):
        self.ref, self.slots, self.count, self.rank, self.with_gram = ref, slots, count, rank, with_gram
        self.entries = len(slots) * count
        gram_rows = rank // 2 if with_gram else 0
        exponents = self.rows(self.entries * rank + gram_rows, exponent_rows(self.entries))
        self.steps = jnp.exp2(exponents[:, :LANES].T[:rank]) * (1.0 / LEVELS)

    def rows(self, first, number):
        return self.ref[pl.ds(first, number), :].astype(jnp.int32).astype(F32)

    def proj(self, slot, p):
        entry = self.slots.index(slot) * self.count + p
        return self.rows(entry * self.rank, self.rank) * self.steps[:, entry : entry + 1]

    def gram(self):
        rank = self.rank
        digits = self.rows(self.entries * rank, rank // 2)
        digits = jnp.concatenate([digits[:, : 2 * rank], digits[:, 2 * rank :]], axis=0)
        return (digits[:, :rank] + digits[:, rank:] * (0.5 / LEVELS)) * self.steps[:, self.entries : self.entries + 1]


def encode(values, gram, coded_ref, rank):
    count = len(values)
    lanes = lane_numbers((rank, LANES))
    exponents = jnp.zeros((rank, LANES), F32)
    for p, value in enumerate(values):
        proj = value()
        exponent = row_exponent(proj)
        coded = jnp.floor(proj * (LEVELS / jnp.exp2(exponent)) + 0.5)
        coded_ref[pl.ds(p * rank, rank), :] = coded.astype(jnp.int32).astype(jnp.int16)
        exponents = jnp.where(lanes == p, exponent, exponents)
    end = count * rank
    if gram is not None:
        exponent = row_exponent(gram)
        scaled = gram * (LEVELS / jnp.exp2(exponent))
        whole = jnp.floor(scaled + 0.5)
        rest = jnp.floor((scaled - whole) * (2 * LEVELS) + 0.5)
        digits = jnp.concatenate([whole, rest], axis=1)
        digits = jnp.concatenate([digits[: rank // 2], digits[rank // 2 :]], axis=1)
        coded_ref[pl.ds(end, rank // 2), :] = digits.astype(jnp.int32).astype(jnp.int16)
        exponents = jnp.where(lanes == count, exponent, exponents)
        end += rank // 2
    rows = exponent_rows(count)
    last = jnp.concatenate([exponents.T[:rows], jnp.zeros((rows, coded_ref.shape[1] - rank), F32)], axis=1)
    coded_ref[pl.ds(end, rows), :] = last.astype(jnp.int32).astype(jnp.int16)


def first_projection_kernel(slots, with_gram, place, v_hbm, visits_ref, coded_ref, v_ref, buffers, sems, v_sem):
    count = buffers.shape[1]
    v_copy = pltpu.make_async_copy(v_hbm, v_ref, v_sem)
    v_copy.start()
    pieces = sems.shape[1]
    piece = count // pieces
    copies = []
    for i, slot in enumerate(slots):
        for j in range(pieces):
            rows = pl.ds(j * piece, piece)
            source = visits_ref.at[feature_of(place) ^ slot, rows]
            copies.append(pltpu.make_async_copy(source, buffers.at[i, rows], sems.at[i, j]))
            copies[-1].start()
    v_copy.wait()

    def value(i, p):
        if p % piece == 0:
            copies[i * pieces + p // piece].wait()
        return low_dot(v_ref[...], buffers[i, p], ROWS_BY_ROWS)

    values = [functools.partial(value, i, p) for i in range(len(slots)) for p in range(count)]
    gram = low_dot(v_ref[...], v_ref[...], ROWS_BY_ROWS) if with_gram else None
    encode(values, gram, coded_ref, v_ref.shape[0])


def first_projection(slots, count, with_gram, place, visits, v_rows):
    width = visits.shape[3]
    rank = v_rows.shape[0]
    return pl.pallas_call(
        functools.partial(first_projection_kernel, slots, with_gram),
        in_specs=[SMEM_SPEC, HBM_SPEC, HBM_SPEC],
        out_specs=VMEM_SPEC,
        out_shape=jax.ShapeDtypeStruct(payload_shape(len(slots) * count, rank, visits.shape[2], with_gram), jnp.int16),
        scratch_shapes=[
            pltpu.VMEM(v_rows.shape, BF16),
            pltpu.VMEM((len(slots), count) + visits.shape[2:], BF16),
            pltpu.SemaphoreType.DMA((len(slots), 2 if count % 2 == 0 else 1)),
            pltpu.SemaphoreType.DMA,
        ],
        compiler_params=parameters(LIMIT),
        cost_estimate=SHORT,
        name="project_first",
    )(place, v_rows, visits)


def next_projection_kernel(slots, first, count, with_gram, layouts, place, v_ref, visits_ref, *refs):
    coded_ref = refs[-1]
    rank = v_ref.shape[0]
    arrived = [Payload(ref, layout, count, rank, with_gram) for ref, layout in zip(refs, layouts)]

    def value(slot, p):
        proj = low_dot(v_ref[...], visits_ref[feature_of(place) ^ slot, first + p], ROWS_BY_ROWS)
        for payload in arrived:
            proj = proj + payload.proj(slot, p)
        return proj

    gram = None
    if with_gram:
        gram = low_dot(v_ref[...], v_ref[...], ROWS_BY_ROWS)
        for payload in arrived:
            gram = gram + payload.gram()
    encode([functools.partial(value, slot, p) for slot in slots for p in range(count)], gram, coded_ref, rank)


def next_projection(slots, first, count, with_gram, layouts, place, visits, v_rows, arrived, after):
    rank = v_rows.shape[0]
    return pl.pallas_call(
        functools.partial(next_projection_kernel, slots, first, count, with_gram, layouts),
        in_specs=[SMEM_SPEC] + [VMEM_SPEC] * (2 + len(arrived)) + [ANY_SPEC] * len(after),
        out_specs=VMEM_SPEC,
        out_shape=jax.ShapeDtypeStruct(payload_shape(len(slots) * count, rank, visits.shape[2], with_gram), jnp.int16),
        compiler_params=parameters(LIMIT),
        cost_estimate=SHORT,
        name="project_next",
    )(place, v_rows, visits, *arrived, *after)


def spread_w_kernel(n_slots, place, w_ref, gram_ref, spread_ref):
    gram_ref[...] = high_dot(w_ref[...], w_ref[...], COLS_BY_COLS)
    patients, rank = w_ref.shape
    share = patients // n_slots
    w_rows = jnp.concatenate([w_ref[...], jnp.zeros((LANES - patients, rank), F32)], axis=0)
    w_columns = w_rows.T
    for slot in range(n_slots):
        first = (feature_of(place) ^ slot) * share
        columns = pltpu.roll(w_columns, jnp.where(first == 0, 0, LANES - first), 1)
        spread = [jnp.broadcast_to(columns[:, p : p + 1], (rank, rank)) for p in range(share)]
        spread_ref[slot] = jnp.concatenate(spread, axis=1)


def spread_w(place, w_start, n_slots):
    patients, rank = w_start.shape
    return pl.pallas_call(
        functools.partial(spread_w_kernel, n_slots),
        in_specs=[SMEM_SPEC, VMEM_SPEC],
        out_specs=[VMEM_SPEC] * 2,
        out_shape=[
            jax.ShapeDtypeStruct((rank, rank), F32),
            jax.ShapeDtypeStruct((n_slots, rank, patients // n_slots * rank), F32),
        ],
        compiler_params=parameters(LIMIT),
        cost_estimate=SHORT,
        name="spread_w",
    )(place, w_start)


def own_projection_kernel(layout, place, v_ref, visits_ref, arrived_ref, *refs):
    *proj_refs, v_gram_ref = refs
    count, rank, _ = proj_refs[0].shape
    payload = Payload(arrived_ref, layout, count, rank, len(proj_refs) == 1)
    for p in range(visits_ref.shape[1]):
        proj = low_dot(v_ref[...], visits_ref[feature_of(place), p], ROWS_BY_ROWS)
        proj_refs[p // count][p % count] = proj + payload.proj(0, p) if p < count else proj
    gram = low_dot(v_ref[...], v_ref[...], ROWS_BY_ROWS)
    v_gram_ref[...] = gram + payload.gram() if payload.with_gram else gram


def project_own(n_parts, layout, place, visits, v_rows, arrived):
    _, share, slots, width = visits.shape
    rank = v_rows.shape[0]
    proj = jax.ShapeDtypeStruct((share // n_parts, rank, slots), F32)
    *own, v_gram = pl.pallas_call(
        functools.partial(own_projection_kernel, layout),
        in_specs=[SMEM_SPEC] + [VMEM_SPEC] * 3,
        out_specs=[VMEM_SPEC] * (n_parts + 1),
        out_shape=[proj] * n_parts + [jax.ShapeDtypeStruct((rank, rank), F32)],
        compiler_params=parameters(LIMIT),
        cost_estimate=SHORT,
        name="project_own",
    )(place, v_rows, visits, arrived)
    return own, v_gram


def solve_tile(columns, tile):
    rows = lax.broadcasted_iota(jnp.int32, tile.shape, 0)
    for a in range(0, 8, 2):
        b = a + 1
        first, second = columns[a], columns[b]
        m_aa, m_ab, m_ba, m_bb = first[a:b], second[a:b], first[b : b + 1], second[b : b + 1]
        scale = 1.0 / (m_aa * m_bb - m_ab * m_ba)
        m_aa, m_ab, m_ba, m_bb = m_aa * scale, m_ab * scale, m_ba * scale, m_bb * scale

        def step(x):
            x_a, x_b = x[a:b], x[b : b + 1]
            new_a, new_b = m_bb * x_a - m_ab * x_b, m_aa * x_b - m_ba * x_a
            x = x - (first * new_a + second * new_b)
            return jnp.where(rows == a, new_a, jnp.where(rows == b, new_b, x))

        tile = step(tile)
        columns = [step(x) if q > b else x for q, x in enumerate(columns)]
    return tile


def eliminate(table, rank):
    tiles = [table[8 * t : 8 * t + 8] for t in range(rank // 8)]
    for home in range(rank // 8):
        first = 8 * home
        columns = [[jnp.broadcast_to(t[:, q : q + 1], t.shape) for q in range(first, first + 8)] for t in tiles]
        solved = solve_tile(columns[home], tiles[home])
        for t, tile in enumerate(tiles):
            terms = [column * solved[q : q + 1] for q, column in enumerate(columns[t])]
            while len(terms) > 1:
                terms = [x + y for x, y in zip(terms[::2], terms[1::2])]
            tiles[t] = solved if t == home else tile - terms[0]
    return jnp.concatenate(tiles, axis=0)


def inverse_of(gram):
    rank = gram.shape[0]
    eye = (lax.broadcasted_iota(jnp.int32, gram.shape, 0) == lane_numbers(gram.shape)).astype(F32)
    return eliminate(jnp.concatenate([gram, eye], axis=1), rank)[:, rank:]


def total(refs):
    out = refs[0][...]
    for ref in refs[1:]:
        out = out + ref[...]
    return out


def first_inverse_kernel(v_gram_ref, *refs):
    *terms, _, w_gram_ref, inverse_ref = refs
    w_gram = total(terms)
    w_gram_ref[...] = w_gram
    inverse_ref[...] = inverse_of(w_gram * v_gram_ref[...])


def first_inverse(v_gram, w_grams, after):
    out = jax.ShapeDtypeStruct(v_gram.shape, F32)
    return pl.pallas_call(
        first_inverse_kernel,
        in_specs=[VMEM_SPEC] * (1 + len(w_grams)) + [ANY_SPEC],
        out_specs=[VMEM_SPEC] * 2,
        out_shape=[out, out],
        compiler_params=parameters(LIMIT),
        cost_estimate=SHORT,
        name="first_inverse",
    )(v_gram, *w_grams, after)


def sweep_all(frames, rank, fine):
    patients = range(frames.shape[0])
    if fine:
        parts = [two_parts(frames[p]) for p in patients]
        both = [jnp.concatenate(x, axis=0) for x in parts]
        blocks = [low_dot(x, y, ROWS_BY_ROWS) + low_dot(z, y, ROWS_BY_ROWS) for (x, z), y in zip(parts, both)]
        grams = [two_parts(x + pltpu.roll(x, rank, 1)) for x in blocks]
        moved = [low_dot(x, y) + low_dot(z, y) for (x, z), y in zip(grams, both)]
    else:
        first = [frames[p].astype(BF16) for p in patients]
        grams = [low_dot(x, x, ROWS_BY_ROWS).astype(BF16) for x in first]
        moved = [low_dot(g, x) for g, x in zip(grams, first)]
    for p in patients:
        frames[p] = 1.5 * frames[p] - 0.5 * moved[p]


def frames_kernel(layouts, part, share, place, counts_ref, h_ref, w_ref, v_gram_ref, before_ref, own_ref, *refs):
    coded, refs = refs[: len(layouts)], refs[len(layouts) :]
    frames_ref, terms_ref, v_total_ref, proj, frames = refs
    count, rank, slots = frames.shape
    patients = range(count)
    first = feature_of(place) * share + part * count
    pieces = [own_ref[p] for p in patients]
    v_gram = v_gram_ref[...]
    for code, layout in zip(coded, layouts):
        payload = Payload(code, layout, count, rank, (part + 1) * count == share)
        pieces = [pieces[p] + payload.proj(0, p) for p in patients]
        if payload.with_gram:
            v_gram = v_gram + payload.gram()
    v_total_ref[...] = v_gram
    for p in patients:
        proj[p] = pieces[p]
    weights = [w_ref[pl.ds(first + p, 1), :] for p in patients]
    mixed = [high_dot(h_ref[...] * weights[p], pieces[p]) for p in patients]
    lanes = lane_numbers((rank, slots))
    mixed = [jnp.where(lanes < counts_ref[first + p], mixed[p], 0.0) for p in patients]
    energy = [jnp.sum(jnp.sum(x * x, axis=1, keepdims=True), axis=0, keepdims=True) for x in mixed]
    for p in patients:
        frames[p] = mixed[p] * lax.rsqrt(energy[p] + epsilon)

    def sweep(fine, step, carry):
        sweep_all(frames, rank, fine)
        return carry

    lax.fori_loop(0, COARSE_STEPS, functools.partial(sweep, False), 0, unroll=True)
    lax.fori_loop(COARSE_STEPS, NS_STEPS, functools.partial(sweep, True), 0, unroll=True)
    low = [frames[p].astype(BF16) for p in patients]
    for p in patients:
        frames_ref[p] = low[p]
    products = [jnp.concatenate(three_parts(proj[p]), axis=0) for p in patients]
    products = [low_dot(low[p], products[p], ROWS_BY_ROWS) for p in patients]
    terms = before_ref[...] if part else jnp.zeros((rank, rank), F32)
    for p in patients:
        product = products[p][:, :rank] + (products[p][:, rank : 2 * rank] + products[p][:, 2 * rank :])
        terms = terms + product * weights[p]
    terms_ref[...] = terms


def own_frames(layouts, part, n_parts, place, counts, h_start, w_start, v_gram, before, own, coded):
    count, rank, slots = own.shape
    share = count * n_parts
    return pl.pallas_call(
        functools.partial(frames_kernel, layouts, part, share),
        in_specs=[SMEM_SPEC] * 2 + [VMEM_SPEC] * (5 + len(coded)),
        out_specs=[VMEM_SPEC] * 3,
        out_shape=[
            jax.ShapeDtypeStruct(own.shape, BF16),
            jax.ShapeDtypeStruct((rank, rank), F32),
            jax.ShapeDtypeStruct((rank, rank), F32),
        ],
        scratch_shapes=[pltpu.VMEM(own.shape, F32)] * 2,
        compiler_params=parameters(LIMIT),
        cost_estimate=SHORT,
        name="own_frames",
    )(place, counts, h_start, w_start, v_gram, before, own, *coded)


def projected_kernel(items, place, visits_ref, *refs):
    frames_refs, outs, token_ref = refs[: len(items)], refs[-2 * len(items) - 1 : -1], refs[-1]
    token_ref[...] = jnp.zeros_like(token_ref)
    for i, (slots, first) in enumerate(items):
        total_count, rank, _ = frames_refs[i].shape
        count = total_count // len(slots)
        for p in range(total_count):
            rows = pl.ds(p * rank, rank)
            owner = feature_of(place) ^ slots[p // count]
            product = low_dot(frames_refs[i][p], visits_ref[owner, first + p % count])
            outs[2 * i][rows, :], outs[2 * i + 1][rows, :] = two_parts(product)


def join_kernel(count, *refs):
    out_ref = refs[-1]
    first = 0
    for part in refs[:count]:
        out_ref[first : first + part.shape[0]] = part[...]
        first += part.shape[0]


def join(parts, after):
    if len(parts) == 1:
        return parts[0]
    return pl.pallas_call(
        functools.partial(join_kernel, len(parts)),
        in_specs=[VMEM_SPEC] * len(parts) + [ANY_SPEC] * len(after),
        out_specs=VMEM_SPEC,
        out_shape=jax.ShapeDtypeStruct((sum(x.shape[0] for x in parts),) + parts[0].shape[1:], parts[0].dtype),
        compiler_params=parameters(LIMIT),
        cost_estimate=SHORT,
        name="join_frames",
    )(*parts, *after)


def project_frames(items, place, frames, visits, after):
    width = visits.shape[-1]
    outs = []
    for item in items:
        count, rank, _ = frames[item].shape
        outs += [jax.ShapeDtypeStruct((count * rank, width), BF16)] * 2
    *parts, token = pl.pallas_call(
        functools.partial(projected_kernel, items),
        in_specs=[SMEM_SPEC] + [VMEM_SPEC] * (1 + len(items)) + [ANY_SPEC] * len(after),
        out_specs=[VMEM_SPEC] * (len(outs) + 1),
        out_shape=outs + [jax.ShapeDtypeStruct((8, LANES), F32)],
        compiler_params=parameters(LIMIT),
        cost_estimate=SHORT,
        name="project_frames",
    )(place, visits, *[frames[item] for item in items], *after)
    return {item: parts[2 * i : 2 * i + 2] for i, item in enumerate(items)}, token


def next_h_kernel(n_terms, *refs):
    inverse_ref, spread_ref, _, result_ref, h_ref, factor_ref = refs[n_terms:]
    h_next = high_dot(total(refs[:n_terms]), inverse_ref[...])
    result_ref[...] = h_next
    h_ref[...] = h_next
    rank = h_next.shape[0]
    h_rows = h_next.T
    h_rows = jnp.concatenate([h_rows] * (spread_ref.shape[2] // rank), axis=1)
    for slot in range(spread_ref.shape[0]):
        factor_ref[slot] = jnp.concatenate(three_parts(h_rows * spread_ref[slot]), axis=0)


def next_h(terms, inverse, spread, after):
    n_slots, rank, columns = spread.shape
    return pl.pallas_call(
        functools.partial(next_h_kernel, len(terms)),
        in_specs=[VMEM_SPEC] * (len(terms) + 2) + [ANY_SPEC],
        out_specs=[VMEM_SPEC] * 3,
        out_shape=[
            jax.ShapeDtypeStruct(inverse.shape, F32),
            jax.ShapeDtypeStruct(inverse.shape, F32),
            jax.ShapeDtypeStruct((n_slots, 3 * rank, columns), BF16),
        ],
        compiler_params=parameters(LIMIT),
        cost_estimate=SHORT,
        name="next_h",
    )(*terms, inverse, spread, after)


def second_inverse_kernel(h_ref, w_gram_ref, gram_ref, inverse_ref):
    gram = high_dot(h_ref[...], h_ref[...], COLS_BY_COLS)
    gram_ref[...] = gram
    inverse_ref[...] = inverse_of(gram * w_gram_ref[...])


def second_inverse(h_next, w_gram):
    out = jax.ShapeDtypeStruct(w_gram.shape, F32)
    return pl.pallas_call(
        second_inverse_kernel,
        out_shape=[out, out],
        compiler_params=parameters(LIMIT),
        cost_estimate=SHORT,
        name="second_inverse",
    )(h_next, w_gram)


def v_terms_kernel(items, sent, place, factor_ref, *refs):
    parts, terms_ref = refs[: 2 * len(items)], refs[-1]
    rank, half = terms_ref.shape
    upper = core_of(place) ^ 1 if sent else core_of(place)
    features = pl.ds(pl.multiple_of(upper * half, half), half)
    total = None
    for i, (slots, first) in enumerate(items):
        count = parts[2 * i].shape[0] // len(slots)
        columns = pl.ds(first * rank, count)
        for k, slot in enumerate(slots):
            rows = pl.ds(k * count, count)
            large = low_dot(factor_ref[slot, :, columns], parts[2 * i][rows, features])
            small = low_dot(factor_ref[slot, : 2 * rank, columns], parts[2 * i + 1][rows, features])
            terms = large[:rank] + (large[rank : 2 * rank] + small[:rank]) + (large[2 * rank :] + small[rank:])
            total = terms if total is None else total + terms
    terms_ref[...] = total


def half_v_terms(items, sent, place, factor, projected, after):
    width = projected[0].shape[1]
    rank = factor.shape[1] // 3
    return pl.pallas_call(
        functools.partial(v_terms_kernel, items, sent),
        in_specs=[SMEM_SPEC] + [VMEM_SPEC] * (1 + len(projected)) + [ANY_SPEC] * len(after),
        out_specs=VMEM_SPEC,
        out_shape=jax.ShapeDtypeStruct((rank, width // 2), F32),
        compiler_params=parameters(LIMIT),
        cost_estimate=SHORT,
        name="v_terms",
    )(place, factor, *projected, *after)


def next_v_kernel(items, share, later, place, terms_ref, inverse_ref, h_ref, *refs):
    parts, refs = refs[: 2 * len(items)], refs[2 * len(items) :]
    rank, half = terms_ref.shape
    here = pl.multiple_of((core_of(place) ^ 1 if later else core_of(place)) * half, half)
    features = pl.ds(here, half)
    v_rows = high_dot(inverse_ref[...], terms_ref[...])
    *before, v_ref, sums_ref, v_parts = refs
    v_ref[...] = v_rows
    sums = before[0][...] if later else jnp.zeros((rank, 2 * rank), F32)
    v_parts[...] = jnp.concatenate(two_parts(v_rows), axis=0)
    weights = jnp.concatenate([h_ref[...]] * 2, axis=1)
    gram = low_dot(v_parts[...], v_parts[...], ROWS_BY_ROWS)
    gram = gram[:rank, :rank] + (gram[:rank, rank:] + gram[rank:, :rank])
    sums_ref[...] = sums + jnp.concatenate([jnp.zeros((rank, rank), F32), gram], axis=1)
    for i, (slots, done) in enumerate(items):
        seen = low_dot(parts[2 * i][:, features], v_parts[...], ROWS_BY_ROWS)
        seen = seen + low_dot(parts[2 * i + 1][:, features], v_parts[...], ROWS_BY_ROWS)
        count = seen.shape[0] // rank // len(slots)
        for p in range(seen.shape[0] // rank):
            patient = (feature_of(place) ^ slots[p // count]) * share + done + p % count
            row = jnp.sum(seen[p * rank : (p + 1) * rank] * weights, axis=0, keepdims=True)
            sums_ref[pl.ds(patient, 1), :rank] += row[:, :rank] + row[:, rank:]


def half_v(items, share, place, terms, inverse, h_next, projected, before):
    rank, half = terms.shape
    return pl.pallas_call(
        functools.partial(next_v_kernel, items, share, bool(before)),
        in_specs=[SMEM_SPEC] + [VMEM_SPEC] * (3 + len(projected) + len(before)),
        out_specs=[VMEM_SPEC] * 2,
        out_shape=[
            jax.ShapeDtypeStruct((rank, half), F32),
            jax.ShapeDtypeStruct((rank, 2 * rank), F32),
        ],
        scratch_shapes=[pltpu.VMEM((2 * rank, half), BF16)],
        compiler_params=parameters(LIMIT),
        cost_estimate=SHORT,
        name="next_v",
    )(place, terms, inverse, h_next, *projected, *before)


def whole_v_kernel(place, own_ref, other_ref, v_ref, token_ref):
    half = own_ref.shape[1]
    upper = core_of(place) == 1
    v_ref[:, :half] = jnp.where(upper, other_ref[...], own_ref[...])
    v_ref[:, half:] = jnp.where(upper, own_ref[...], other_ref[...])
    token_ref[...] = jnp.zeros_like(token_ref)


def whole_v(place, own, other):
    rank, half = own.shape
    return pl.pallas_call(
        whole_v_kernel,
        in_specs=[SMEM_SPEC] + [VMEM_SPEC] * 2,
        out_specs=[VMEM_SPEC] * 2,
        out_shape=[jax.ShapeDtypeStruct((rank, 2 * half), F32), jax.ShapeDtypeStruct((8, LANES), F32)],
        compiler_params=parameters(LIMIT),
        cost_estimate=SHORT,
        name="whole_v",
    )(place, own, other)


def next_w_kernel(n_sums, *refs):
    gram_ref, _, w_ref = refs[n_sums:]
    patients, rank = w_ref.shape
    sums = total(refs[:n_sums])
    table = jnp.concatenate([sums[:, rank:] * gram_ref[...], sums.T[:rank]], axis=1)
    w_ref[...] = eliminate(table, rank).T[rank : rank + patients]


def next_w(sums, h_gram, patients, after):
    rank = h_gram.shape[0]
    return pl.pallas_call(
        functools.partial(next_w_kernel, len(sums)),
        in_specs=[VMEM_SPEC] * (len(sums) + 1) + [ANY_SPEC],
        out_specs=VMEM_SPEC,
        out_shape=jax.ShapeDtypeStruct((patients, rank), F32),
        compiler_params=parameters(LIMIT),
        cost_estimate=SHORT,
        name="next_w",
    )(*sums, h_gram, after)


def swap(x, axis, slot):
    pairs = [(i, i ^ slot) for i in range(lax.axis_size(axis))]
    return lax.ppermute(x, axis, pairs)


def all_terms(x, axis):
    n = lax.axis_size(axis)
    if n > 4:
        return [lax.psum(x, axis)]
    return [x] + [swap(x, axis, s) for s in range(1, n)]


def staged_terms(x, axis, after):
    n = lax.axis_size(axis)
    steps = [1 << i for i in range(n.bit_length() - 1)]
    for step in steps[:-1]:
        x = add(x, swap(x, axis, step), after)
    return [x, swap(x, axis, steps[-1])]


def add_kernel(a_ref, b_ref, *refs):
    refs[-1][...] = a_ref[...] + b_ref[...]


def add(a, b, after):
    return pl.pallas_call(
        add_kernel,
        in_specs=[VMEM_SPEC] * 2 + [ANY_SPEC] * len(after),
        out_specs=VMEM_SPEC,
        out_shape=jax.ShapeDtypeStruct(a.shape, a.dtype),
        compiler_params=parameters(LIMIT),
        cost_estimate=SHORT,
        name="add_terms",
    )(a, b, *after)


def patient_halves(keep, send, after):
    own = add(keep, swap(send, "patient", 1), [])
    step = 2
    while step < lax.axis_size("patient"):
        own = add(own, swap(own, "patient", step), [after])
        step *= 2
    return own, swap(own, "patient", 1)


def on_device(visits, visit_counts, h_start, v_start, w_start):
    n = lax.axis_size("feature")
    patients, slots, width = visits.shape
    share = patients // n
    place = (2 * lax.axis_index("feature") + (lax.axis_index("patient") & 1)).astype(jnp.int32).reshape(1)
    by_owner = visits.reshape(n, share, slots, width)
    in_hbm = pltpu.with_memory_space_constraint(by_owner, pltpu.HBM)
    v_rows = pltpu.with_memory_space_constraint(v_start.T, pltpu.HBM)

    n_parts = 2 if share % 2 == 0 else 1
    count = share // n_parts
    firsts = [part * count for part in range(n_parts)]
    bits = [1 << i for i in range(n.bit_length() - 1)]
    v_near = v_start.T

    def send(bit):
        return [slot for slot in range(n) if slot & bit and not slot & (bit - 1)]

    def receive(bit):
        return [slot ^ bit for slot in send(bit)]

    w_gram, spread = spread_w(place, w_start, n)
    w_grams = staged_terms(w_gram, "patient", [])
    arrived = [[] for _ in firsts]
    for i, bit in enumerate(bits):
        layouts = [receive(before) for before in bits[:i]]
        for part, first in enumerate(firsts):
            if i == 0 and part == 0:
                code = first_projection(send(bit), count, n_parts == 1, place, in_hbm, v_rows)
            else:
                after = [w_grams[part]] + [v_gram] * part if i else []
                code = next_projection(
                    send(bit), first, count, part == n_parts - 1, layouts, place, by_owner, v_near, arrived[part], after
                )
            arrived[part] = arrived[part] + [swap(code, "feature", bit)]
        if i == 0:
            own, v_gram = project_own(n_parts, receive(bit), place, by_owner, v_near, arrived[0][0])

    layouts = [receive(bit) for bit in bits]
    frames = [[] for _ in firsts]
    joined = []

    def double(part, after):
        for bit in bits[::-1]:
            slots = tuple(slot ^ bit for group, _ in frames[part] for slot in group)
            joined = join([x for _, x in frames[part]], after)
            frames[part].append((slots, swap(joined, "feature", bit)))
        return [joined]

    def project_groups(groups, after):
        arrays = {(frames[part][k][0], firsts[part]): frames[part][k][1] for part, k in groups}
        return project_frames(list(arrays), place, arrays, by_owner, after)

    h_local = v_gram
    for part, first in enumerate(firsts):
        low, h_local, v_total = own_frames(
            layouts[part == 0 :],
            part,
            n_parts,
            place,
            visit_counts,
            h_start,
            w_start,
            v_gram,
            h_local,
            own[part],
            arrived[part][part == 0 :],
        )
        v_gram = v_total
        frames[part].append(((0,), low))

    last = len(bits)
    for part in range(n_parts - 1):
        joined = double(part, [frames[-1][0][1]])
    first_groups = [(part, 0) for part in range(n_parts)] + [(part, 1) for part in range(n_parts - 1)]
    early = [(part, k) for part in range(n_parts - 1) for k in range(2, last + 1)]
    projected, token = project_groups(first_groups, joined)
    h_sums = staged_terms(h_local, "patient", [token])
    w_gram, inverse = first_inverse(v_gram, w_grams, h_sums[0])
    h_sum = add(*h_sums, [inverse])
    joined = double(n_parts - 1, [h_sum] + [frames[part][k][1] for part, k in early])
    h_terms = all_terms(h_sum, "feature")
    after = joined
    for groups in [early] + [[(n_parts - 1, k)] for k in range(1, last + 1)]:
        if groups:
            more, token = project_groups(groups, after)
            projected |= more
            after = [token]
    h_result, h_next, factor = next_h(h_terms, inverse, spread, token)

    items = list(projected)
    flat = [x for item in items for x in projected[item]]
    send = half_v_terms(items, True, place, factor, flat, [])
    keep = half_v_terms(items, False, place, factor, flat, [send])
    h_gram, second = second_inverse(h_next, w_gram)
    own_terms, other_terms = patient_halves(keep, send, second)
    v_own, before = half_v(items, share, place, own_terms, second, h_next, flat, [])
    v_other, sums = half_v(items, share, place, other_terms, second, h_next, flat, [before])
    v_next, token = whole_v(place, v_own, v_other)
    w_next = next_w(all_terms(sums, "feature"), h_gram, patients, token)
    return (h_result, v_next.T, w_next)


def solution(mesh):
    return jax.shard_map(
        on_device,
        mesh=mesh,
        in_specs=(
            P(("groups", "patient"), None, "feature"),
            P(("groups", "patient")),
            P(),
            P("feature", None),
            P(("groups", "patient"), None),
        ),
        out_specs=(P(None, "groups"), P("feature", "groups"), P("patient", "groups")),
        check_vma=False,
    )
```
